128 devices in a mesh: dp: 8 (over x, core), context: 8 (over y, z_lo), tensor: 2 (over z_hi).
Axes of the slice: x: 4, y: 4, z: 4 (z_hi: 2, z_lo: 2; z = z_hi * 2 + z_lo), core: 2. Of those that a mesh axis runs over, the one named last changes fastest.
Arguments:
- tokens_in: float32 [16, 1024, 512], P('dp', 'context'), may hold values from -6 to 6
- cotangent: float32 [16, 1024, 512], P('dp', 'context'), may hold values from -6 to 6
- positions: int32 [16, 1024], P('dp', 'context'), may hold values from 0 to 1023, as said below
- w_qkv: bfloat16 [2, 512, 3, 512], P(None, None, None, 'tensor'), may hold values from -0.25 to 0.25
- b_qkv: float32 [2, 3, 512], P(None, None, 'tensor'), may hold values from -3 to 3
- w_out: bfloat16 [2, 512, 512], P(None, 'tensor'), may hold values from -1.5 to 1.5
- w_up: bfloat16 [2, 512, 2048], P(None, None, 'tensor'), may hold values from -0.25 to 0.25
- b_up: float32 [2, 2048], P(None, 'tensor'), may hold values from -3 to 3
- w_down: bfloat16 [2, 2048, 512], P(None, 'tensor'), may hold values from -0.125 to 0.125
- out_bias: float32 [2, 2, 512], replicated, may hold values from -3 to 3
- ln_gain: float32 [2, 2, 512], replicated, may hold values from 0.5 to 1.5
- ln_bias: float32 [2, 2, 512], replicated, may hold values from -3 to 3
Outputs:
- block_out: float32 [16, 1024, 512], P('dp', 'context')
- in_grad: float32 [16, 1024, 512], P('dp', 'context')
- grad_w_qkv: float32 [2, 512, 3, 512], P(None, None, None, 'tensor')
- grad_b_qkv: float32 [2, 3, 512], P(None, None, 'tensor')
- grad_w_out: float32 [2, 512, 512], P(None, 'tensor')
- grad_w_up: float32 [2, 512, 2048], P(None, None, 'tensor')
- grad_b_up: float32 [2, 2048], P(None, 'tensor')
- grad_w_down: float32 [2, 2048, 512], P(None, 'tensor')
- grad_out_bias: float32 [2, 2, 512], replicated
- grad_ln_gain: float32 [2, 2, 512], replicated
- grad_ln_bias: float32 [2, 2, 512], replicated
The draws below stay inside these ranges and needn't reach their ends.
Inputs may be any that keep to these rules, and one draw needn't show every extreme that they name: Each row is a pack of documents: from token to token the position rises by one, or falls to 0 where a new document begins; the first document of a row may have begun before the row. In each aligned block of 2 rows one row, drawn from the seed, is a single document with positions 0 to 1023.
All inputs are finite; a program needn't handle non-finite values.
Results may differ from the reference program's by a relative error of at most 0.017.
Values may be sent and summed in bfloat16 or wider, within the bound.
No kernel may reach another device: no remote copies, remote signals or barrier semaphores. Data moves between devices by JAX's collectives and lax.ppermute only.
A program may use at most 128 MiB of HBM per device.

```python
import jax
import jax.numpy as jnp
from jax import lax

D = 512
HEADS = 8
FF = 2048
ROT = 16
LAYERS = 2
LENGTH = 1024
SEQ_DEV = 2
SEQS = 16


def draw_positions(key, part):
    key = jax.random.fold_in(key, 7)
    key_docs, key_whole, key_carry = jax.random.split(key, 3)
    token_index = jnp.arange(LENGTH, dtype=jnp.int32)[None, :]
    new_doc = jax.random.randint(key_docs, (SEQS, LENGTH), 0, max(LENGTH // 4, 2)) == 0
    group_pick = jax.random.randint(key_whole, (SEQS // SEQ_DEV,), 0, SEQ_DEV)
    row_slot = jnp.arange(SEQS, dtype=jnp.int32) % SEQ_DEV
    whole_row = (row_slot == jnp.repeat(group_pick, SEQ_DEV))[:, None]
    carried = jax.random.randint(key_carry, (SEQS, 1), 0, LENGTH)
    carried = jnp.where(whole_row, 0, carried)
    forced = token_index == LENGTH - carried
    new_doc = jnp.where(whole_row, token_index == 0, new_doc | forced | (token_index == 0))
    doc_first = lax.cummax(jnp.where(new_doc, token_index, 0), axis=1)
    return (token_index - doc_first + jnp.where(doc_first == 0, carried, 0)).astype(jnp.int32)


def block_levels(key, shape, cuts, smallest, high):
    def one(axis_at, parts):
        heights = jax.random.uniform(jax.random.fold_in(jax.random.fold_in(key, 6), axis_at), (parts,), jnp.float32, smallest / len(cuts), high / len(cuts))
        return jnp.repeat(jnp.exp(heights), shape[axis_at] // parts).reshape((-1,) + (1,) * (len(shape) - axis_at - 1))

    gain = one(*cuts[0])
    for cut in cuts[1:]:
        gain = gain * one(*cut)
    return gain


def gaussian(own_key, extent, scale, most, pieces=(), kind=jnp.bfloat16):
    values = jax.random.normal(own_key, extent, jnp.float32) * scale
    if len(pieces) > 0:
        values = block_levels(own_key, extent, pieces, -0.22, 0.18) * values
    return jnp.clip(values, min=-most, max=most).astype(kind)


def setup_inputs(seed: int = 0) -> dict:
    key_list = jax.random.split(jax.random.key(seed), 13)
    return {
        "tokens_in": gaussian(key_list[0], (SEQS, LENGTH, D), 1.0, 6.0, ((0, 8), (1, 8)), jnp.float32),
        "cotangent": gaussian(key_list[1], (SEQS, LENGTH, D), 1.0, 6.0, ((0, 8), (1, 8)), jnp.float32),
        "positions": draw_positions(jax.random.fold_in(key_list[12], 71), 0),
        "w_qkv": gaussian(key_list[3], (LAYERS, D, 3, D), D ** -0.5, 0.25, ((3, 2),)),
        "b_qkv": gaussian(key_list[4], (LAYERS, 3, D), 0.5, 3.0, ((2, 2),), jnp.float32),
        "w_out": gaussian(key_list[5], (LAYERS, D, D), (D // 32) ** -0.5, 1.5, ((1, 2),)),
        "w_up": gaussian(key_list[6], (LAYERS, D, FF), D ** -0.5, 0.25, ((2, 2),)),
        "b_up": gaussian(key_list[7], (LAYERS, FF), 0.5, 3.0, ((1, 2),), jnp.float32),
        "w_down": gaussian(key_list[8], (LAYERS, FF, D), FF ** -0.5, 0.125, ((1, 2),)),
        "out_bias": gaussian(key_list[9], (LAYERS, 2, D), 0.5, 3.0, (), jnp.float32),
        "ln_gain": jnp.clip(1.0 + 0.1 * jax.random.normal(key_list[10], (LAYERS, 2, D), jnp.float32), 0.5, 1.5),
        "ln_bias": gaussian(key_list[11], (LAYERS, 2, D), 0.5, 3.0, (), jnp.float32),
    }


EPS = 1e-05
HIGH = lax.Precision.HIGHEST

@jax.custom_vjp
def low(v):
    return lax.optimization_barrier(v.astype(jnp.bfloat16)).astype(jnp.float32)

@jax.custom_vjp
def low_back(v):
    return v

def low_keep(v):
    return (low(v), None)

def low_pass(kept, grad):
    return (grad,)

def back_keep(v):
    return (v, None)

def back_low(kept, grad):
    return (low(grad),)
low.defvjp(low_keep, low_pass)
low_back.defvjp(back_keep, back_low)

def rotate(tensor, token_pos):
    half_rot = ROT // 2
    freqs = 10000.0 ** (-jnp.arange(half_rot).astype(jnp.float32) * 2.0 / ROT)
    angles = token_pos.astype(jnp.float32)[..., None] * freqs
    cosine = jnp.concatenate([jnp.cos(angles), jnp.cos(angles)], -1)[..., None, :]
    sine = jnp.concatenate([jnp.sin(angles), jnp.sin(angles)], -1)[..., None, :]
    rotary_part = tensor[..., :ROT]
    turned = jnp.concatenate([-rotary_part[..., half_rot:], rotary_part[..., :half_rot]], -1)
    return jnp.concatenate([rotary_part * cosine + turned * sine, tensor[..., ROT:]], -1)

def attend_one(operands):
    query_rows, key_rows, value_rows, token_pos = operands
    token_index = jnp.arange(LENGTH).astype(jnp.int32)
    doc_start = jnp.maximum(token_index - token_pos.astype(jnp.int32), 0)
    visible = (token_index[None, :] <= token_index[:, None]) & (token_index[None, :] >= doc_start[:, None])
    raw_scores = jnp.einsum('qhd,khd->hqk', query_rows, key_rows, precision=HIGH)
    scores = low_back(raw_scores) * (D // HEADS) ** (-0.5)
    scores = jnp.where(visible[None], scores, -1e+30)
    row_peak = lax.optimization_barrier(jnp.max(scores, -1, keepdims=True))
    shifted = jnp.exp(scores - row_peak)
    probs = shifted / lax.optimization_barrier(jnp.sum(shifted, -1, keepdims=True))
    return jnp.einsum('hqk,khd->qhd', low(probs), value_rows, precision=HIGH)

def block(stream, w_qkv, b_qkv, w_out, w_up, b_up, w_down, out_bias, ln_gain, ln_bias, positions):
    seq_count = stream.shape[0]
    head_dim = D // HEADS
    row_mean = lax.optimization_barrier(jnp.mean(stream, -1, keepdims=True))
    centred = stream - row_mean
    variance = lax.optimization_barrier(jnp.mean(centred * centred, -1, keepdims=True))
    normed = centred * lax.rsqrt(variance + EPS)
    attn_in = low(normed * ln_gain[0] + ln_bias[0])
    mlp_in = low(normed * ln_gain[1] + ln_bias[1])
    joined = low_back(jnp.einsum('nld,dje->nlje', attn_in, w_qkv, precision=HIGH) + b_qkv)
    heads_view = joined.reshape(seq_count, LENGTH, 3, HEADS, head_dim)
    query_r = low(rotate(heads_view[:, :, 0], positions))
    key_r = low(rotate(heads_view[:, :, 1], positions))
    value_b = low(heads_view[:, :, 2])
    attended = lax.map(jax.checkpoint(attend_one), (query_r, key_r, value_b, positions))
    context = low(low_back(attended)).reshape(seq_count, LENGTH, D)
    pre_act = low_back(jnp.einsum('nld,df->nlf', mlp_in, w_up, precision=HIGH) + b_up)
    act = low(jax.nn.gelu(pre_act, approximate=False))
    branch = jnp.einsum('nld,de->nle', context, w_out, precision=HIGH) + jnp.einsum('nlf,fe->nle', act, w_down, precision=HIGH)
    return stream + low_back(branch) + out_bias[0] + out_bias[1]

def reference(tokens_in, cotangent, positions, w_qkv, b_qkv, w_out, w_up, b_up, w_down, out_bias, ln_gain, ln_bias):
    params = (w_qkv.astype(jnp.float32), b_qkv.astype(jnp.float32), w_out.astype(jnp.float32), w_up.astype(jnp.float32), b_up.astype(jnp.float32), w_down.astype(jnp.float32), out_bias.astype(jnp.float32), ln_gain.astype(jnp.float32), ln_bias.astype(jnp.float32))

    def forward(stream, p_qkv, p_bqkv, p_out, p_up, p_bup, p_down, p_obias, p_gain, p_lnb):
        for layer_idx in range(LAYERS):
            stream = block(stream, p_qkv[layer_idx], p_bqkv[layer_idx], p_out[layer_idx], p_up[layer_idx], p_bup[layer_idx], p_down[layer_idx], p_obias[layer_idx], p_gain[layer_idx], p_lnb[layer_idx], positions)
        return stream
    block_out, pullback = jax.vjp(forward, tokens_in.astype(jnp.float32), *params)
    grads = pullback(cotangent.astype(jnp.float32))
    return (block_out, grads[0], grads[1], grads[2], grads[3], grads[4], grads[5], grads[6], grads[7], grads[8], grads[9])
```

```python
from functools import partial

import numpy as np

import jax
import jax.numpy as jnp
from jax import lax
from jax.experimental import pallas as pl
from jax.experimental.pallas import tpu as pltpu
from jax.sharding import PartitionSpec as P

EPS = 1e-05
HALF = 8
HEAD = 64
BLK = 128
CHUNK = 256
NEG = -1e30
BF = jnp.bfloat16
F32 = jnp.float32

FREQS = (10000.0 ** (-np.arange(HALF, dtype=np.float64) * 2.0 / 16.0)).astype(np.float32)


def mm(a, b, ca=1, cb=0):
    return lax.dot_general(a, b, (((ca,), (cb,)), ((), ())), preferred_element_type=F32)


def call(body, out_shape, args, name, scratch=(), smem_first=False):
    specs = [pl.BlockSpec(memory_space=pltpu.VMEM) for _ in args]
    if smem_first:
        specs[0] = pl.BlockSpec(memory_space=pltpu.SMEM)
    return pl.pallas_call(
        body,
        out_shape=[jax.ShapeDtypeStruct(s, d) for s, d in out_shape],
        in_specs=specs,
        out_specs=[pl.BlockSpec(memory_space=pltpu.VMEM) for _ in out_shape],
        scratch_shapes=list(scratch),
        compiler_params=pltpu.CompilerParams(vmem_limit_bytes=56 * 1024 * 1024),
        name=name,
    )(*args)


def norm_rows(x):
    mean = jnp.mean(x, -1, keepdims=True)
    cen = x - mean
    inv = lax.rsqrt(jnp.mean(cen * cen, -1, keepdims=True) + EPS)
    return cen * inv, inv


def turn(t, cos, sin):
    a, b = t[:HALF], t[HALF : 2 * HALF]
    return jnp.concatenate([a * cos - b * sin, b * cos + a * sin, t[2 * HALF :]], 0)


def turn_back(u, cos, sin):
    a, b = u[:HALF], u[HALF : 2 * HALF]
    return jnp.concatenate([a * cos + b * sin, b * cos - a * sin, u[2 * HALF :]], 0)


def send_qkv(send, attn_in, w_qkv, b_qkv, cs):
    qkv = mm(attn_in, w_qkv[...]) + b_qkv[...]
    qkv_t = qkv.T
    wide = w_qkv.shape[1] // 3
    heads = wide // HEAD
    for s in range(2):
        cos, sin = cs[s, 0], cs[s, 1]
        cols = slice(s * BLK, (s + 1) * BLK)
        for h in range(heads):
            j = s * heads + h
            for e in range(3):
                part = qkv_t[e * wide + h * HEAD : e * wide + (h + 1) * HEAD, cols]
                if e < 2:
                    part = turn(part, cos, sin)
                if e == 0:
                    part = part * (HEAD**-0.5)
                send[j, e * HEAD : (e + 1) * HEAD, :] = part.astype(BF)


def feed_forward(mlp_in, w_up, b_up, w_down, act, slope):
    width = w_up.shape[1]
    total = None
    for c in range(0, width, 256):
        cols = slice(c, c + 256)
        pre = mm(mlp_in, w_up[:, cols]) + b_up[:, cols]
        cdf = 0.5 + 0.5 * lax.erf(pre * np.float32(0.7071067811865476))
        a = (pre * cdf).astype(BF)
        act[:, cols] = a
        slope[:, cols] = cdf + pre * (jnp.exp(-0.5 * pre * pre) * np.float32(0.3989422804014327))
        term = mm(a, w_down[cols, :])
        total = term if total is None else total + term
    return total


def feed_back(g_b, act, slope, mlp_in, w_up, w_down, d_up, d_down, d_b_up):
    width = w_up.shape[1]
    total = None
    mlp_t = mlp_in.astype(F32).T.astype(BF)
    for c in range(0, width, 256):
        cols = slice(c, c + 256)
        d_act = mm(g_b, w_down[cols, :], 1, 1)
        d_pre = d_act * slope[:, cols]
        d_pre_b = d_pre.astype(BF)
        d_b_up[:, cols] = jnp.sum(d_pre_b.astype(F32), 0, keepdims=True)
        d_up(c // 256, mm(mlp_t, d_pre_b))
        d_down(c, mm(act[:, cols].astype(F32).T.astype(BF), g_b))
        term = mm(d_pre_b, w_up[:, cols], 1, 1)
        total = term if total is None else total + term
    return total


def pack_up(out, row):
    def put(c, value):
        for p in range(8):
            out[p, row + 64 * c : row + 64 * (c + 1), :] = value[64 * p : 64 * (p + 1)].astype(BF)

    return put


def pack_down(out, row):
    def put(c, value):
        for half in range(2):
            for k in range(2):
                out[c // 128 + k, row + 128 * half : row + 128 * (half + 1), :] = value[
                    128 * k : 128 * (k + 1), 256 * half : 256 * (half + 1)
                ].astype(BF)

    return put


def pack_qkv(out, row, value):
    for p in range(8):
        for c in range(3):
            out[p, row + 64 * c : row + 64 * (c + 1), :] = value[
                64 * p : 64 * (p + 1), 256 * c : 256 * (c + 1)
            ].astype(BF)


def pack_out(out, row, value):
    for p in range(8):
        for half in range(2):
            out[p, row + 32 * half : row + 32 * (half + 1), :] = value[
                32 * p : 32 * (p + 1), 256 * half : 256 * (half + 1)
            ].astype(BF)


def first_body(
    at, pos, freqs, x, gain, bias, w_qkv, b_qkv, w_up, b_up, w_down, send, part, act, slope, cs
):
    for s in range(2):
        p = pos[s : s + 1, :].astype(F32)
        angle = freqs[...] * p
        cs[s, 0] = jnp.cos(angle)
        cs[s, 1] = jnp.sin(angle)
    normed, _ = norm_rows(x[...])
    attn_in = (normed * gain[0, 0:1] + bias[0, 0:1]).astype(BF)
    mlp_in = (normed * gain[0, 1:2] + bias[0, 1:2]).astype(BF)
    send_qkv(send, attn_in, w_qkv, b_qkv, cs)
    heads = w_qkv.shape[1] // 3 // HEAD
    row = lax.broadcasted_iota(jnp.int32, (16, BLK), 0)
    token = at[0] * BLK + lax.broadcasted_iota(jnp.int32, (1, BLK), 1)
    for s in range(2):
        start = jnp.maximum(token - pos[s : s + 1, :], 0)
        high = (start // 8).astype(F32)
        low = (start % 8).astype(F32)
        block = jnp.where(row == 0, high, jnp.where(row == 1, low, 0.0)).astype(BF)
        for h in range(heads):
            send[s * heads + h, 3 * HEAD : 3 * HEAD + 16, :] = block
    part[...] = feed_forward(mlp_in, w_up, b_up, w_down, act, slope).astype(BF)


def load_rows(recv, lo, hi):
    return jnp.concatenate([recv[i, lo:hi, :] for i in range(8)], 1)


def starts_of(recv):
    rows = load_rows(recv, 3 * HEAD, 3 * HEAD + 16).astype(F32)
    return rows[0:1] * 8.0 + rows[1:2]


def visible_of(start, c, length):
    key = lax.broadcasted_iota(jnp.int32, (length, CHUNK), 0)
    query = lax.broadcasted_iota(jnp.int32, (length, CHUNK), 1) + c * CHUNK
    return (key <= query) & (key >= start[:, c * CHUNK : (c + 1) * CHUNK])


def attend_body(recv, send, lse, ctx, start_out):
    q = load_rows(recv, 0, HEAD)
    k_t = load_rows(recv, HEAD, 2 * HEAD)
    v_t = load_rows(recv, 2 * HEAD, 3 * HEAD)
    k = k_t.astype(F32).T.astype(BF)
    start = starts_of(recv).astype(jnp.int32)
    start_out[...] = start
    for c in range(4):
        cols = slice(c * CHUNK, (c + 1) * CHUNK)
        length = (c + 1) * CHUNK
        scores = mm(k[:length], q[:, cols])
        scores = jnp.where(visible_of(start, c, length), scores, NEG)
        peak = jnp.max(scores, 0, keepdims=True)
        shifted = jnp.exp(scores - peak)
        total = jnp.sum(shifted, 0, keepdims=True)
        lse[:, cols] = peak + jnp.log(total)
        out = mm(v_t[:, :length], shifted.astype(BF)) / total
        ctx[:, cols] = out
        for i in range(CHUNK // BLK):
            block = out[:, i * BLK : (i + 1) * BLK].astype(BF)
            for t in range(2):
                send[c * (CHUNK // BLK) + i, t] = block


def attend_both_body(recv, start, send, dk, dv):
    q = load_rows(recv, 0, HEAD)
    k_t = load_rows(recv, HEAD, 2 * HEAD)
    v_t = load_rows(recv, 2 * HEAD, 3 * HEAD)
    d_ctx = load_rows(recv, 3 * HEAD, 4 * HEAD)
    k = k_t.astype(F32).T.astype(BF)
    v = v_t.astype(F32).T.astype(BF)
    dk[...] = jnp.zeros_like(dk)
    dv[...] = jnp.zeros_like(dv)
    for c in range(4):
        cols = slice(c * CHUNK, (c + 1) * CHUNK)
        length = (c + 1) * CHUNK
        scores = mm(k[:length], q[:, cols])
        scores = jnp.where(visible_of(start[...], c, length), scores, NEG)
        peak = jnp.max(scores, 0, keepdims=True)
        shifted = jnp.exp(scores - peak)
        probs = shifted * (1.0 / jnp.sum(shifted, 0, keepdims=True))
        probs_b = probs.astype(BF)
        out = mm(v_t[:, :length], probs_b)
        dq = backward_chunk(q, k_t, v, d_ctx, probs, probs_b, out, cols, length, dk, dv)
        for i in range(CHUNK // BLK):
            b = c * (CHUNK // BLK) + i
            for t in range(2):
                send[b, t, 0:HEAD] = out[:, i * BLK : (i + 1) * BLK].astype(BF)
                send[b, t, HEAD : 2 * HEAD] = dq[:, i * BLK : (i + 1) * BLK].astype(BF)
    put_kv(send, dk, dv, 2 * HEAD)


def backward_chunk(q, k_t, v, d_ctx, probs, probs_b, out, cols, length, dk, dv):
    d_out = d_ctx[:, cols]
    d_probs = mm(v[:length], d_out)
    delta = jnp.sum(d_out.astype(F32) * out, 0, keepdims=True)
    d_scores = (probs * (d_probs - delta)).astype(BF)
    dk[:, :length] += mm(q[:, cols], d_scores, 1, 1)
    dv[:, :length] += mm(d_out, probs_b, 1, 1)
    return mm(k_t[:, :length], d_scores) * (HEAD**-0.5)


def put_kv(send, dk, dv, row):
    for b in range(8):
        for t in range(2):
            send[b, t, row : row + HEAD] = dk[:, b * BLK : (b + 1) * BLK].astype(BF)
            send[b, t, row + HEAD : row + 2 * HEAD] = dv[:, b * BLK : (b + 1) * BLK].astype(BF)


def attend_back_body(recv, recv_d, start, lse, ctx, send, dk, dv):
    q = load_rows(recv, 0, HEAD)
    k_t = load_rows(recv, HEAD, 2 * HEAD)
    v_t = load_rows(recv, 2 * HEAD, 3 * HEAD)
    d_ctx = load_rows(recv_d, 0, HEAD)
    k = k_t.astype(F32).T.astype(BF)
    v = v_t.astype(F32).T.astype(BF)
    dk[...] = jnp.zeros_like(dk)
    dv[...] = jnp.zeros_like(dv)
    for c in range(4):
        cols = slice(c * CHUNK, (c + 1) * CHUNK)
        length = (c + 1) * CHUNK
        scores = mm(k[:length], q[:, cols])
        scores = jnp.where(visible_of(start[...], c, length), scores, NEG)
        probs = jnp.exp(scores - lse[:, cols])
        probs_b = probs.astype(BF)
        dq = backward_chunk(q, k_t, v, d_ctx, probs, probs_b, ctx[:, cols], cols, length, dk, dv)
        for i in range(CHUNK // BLK):
            for t in range(2):
                send[c * (CHUNK // BLK) + i, t, 0:HEAD] = dq[:, i * BLK : (i + 1) * BLK].astype(BF)
    put_kv(send, dk, dv, HEAD)


def gather_ctx(recv, s):
    return jnp.concatenate([recv[s * 4 + h, t, 0:HEAD, :] for t in range(2) for h in range(4)], 0)


def ordered(t, own, other):
    first = jnp.where(t == 0, own[...], other[...])
    second = jnp.where(t == 0, other[...], own[...])
    return first, second


def branch_of(t, recv, w_own, w_other):
    first, second = ordered(t, w_own, w_other)
    w = jnp.concatenate([first, second], 0)
    rows = []
    for s in range(2):
        rows.append(mm(gather_ctx(recv, s).astype(F32).T.astype(BF), w))
    return jnp.concatenate(rows, 0)


def middle_body(
    at, x, part, part_other, recv, w_out_own, w_out_other, out_bias, gain, bias,
    w_qkv, b_qkv, w_up, b_up, w_down, w_out, cot, cs,
    stream, send, grads, parts, d_b_up, d_sum, act, slope,
):
    branch = part[...].astype(F32) + part_other[...].astype(F32)
    branch = branch + branch_of(at[1], recv, w_out_own, w_out_other)
    out = x[...] + branch + out_bias[0, 0:1] + out_bias[0, 1:2]
    stream[...] = out
    normed, _ = norm_rows(out)
    attn_in = (normed * gain[1, 0:1] + bias[1, 0:1]).astype(BF)
    mlp_in = (normed * gain[1, 1:2] + bias[1, 1:2]).astype(BF)
    send_qkv(send, attn_in, w_qkv, b_qkv, cs)
    g_b = cot[...].astype(BF)
    d_ctx = mm(w_out[...], g_b, 1, 1)
    for s in range(2):
        for h in range(4):
            send[s * 4 + h, 3 * HEAD : 4 * HEAD, :] = d_ctx[
                h * HEAD : (h + 1) * HEAD, s * BLK : (s + 1) * BLK
            ].astype(BF)
    d_sum[...] = jnp.sum(cot[...], 0, keepdims=True)
    parts[0:256] = feed_forward(mlp_in, w_up, b_up, w_down, act, slope).astype(BF)
    parts[256:512] = feed_back(
        g_b, act, slope, mlp_in, w_up, w_down, pack_up(grads, 0), pack_down(grads, 256), d_b_up
    ).astype(BF)


def norm_back(
    t, x, g, d_mlp_in, recv, row, w_own, w_other, cs, gain, bias, layer, d_qkv, d_b_qkv, d_norm
):
    normed, inv = norm_rows(x)
    attn_in = (normed * gain[layer, 0:1] + bias[layer, 0:1]).astype(BF)
    halves = [[], []]
    for tt in range(2):
        for e in range(3):
            for h in range(4):
                pieces = []
                for s in range(2):
                    lo = row + e * HEAD
                    u = recv[s * 4 + h, tt, lo : lo + HEAD, :]
                    if e < 2:
                        u = turn_back(u.astype(F32), cs[s, 0], cs[s, 1]).astype(BF)
                    pieces.append(u)
                halves[tt].append(jnp.concatenate(pieces, 1))
    halves = [jnp.concatenate(half, 0) for half in halves]
    first, second = ordered(t, w_own, w_other)
    d_attn_t = mm(first, halves[0]) + mm(second, halves[1])
    d_attn_in = d_attn_t.T
    own = jnp.where(t == 0, halves[0], halves[1])
    d_qkv(mm(attn_in.astype(F32).T.astype(BF), own, 1, 1))
    d_b_qkv[...] = mm(jnp.ones((8, own.shape[1]), BF), own, 1, 1)[0:1]
    d_norm[0:1] = jnp.sum(d_attn_in * normed, 0, keepdims=True)
    d_norm[1:2] = jnp.sum(d_mlp_in * normed, 0, keepdims=True)
    d_norm[2:3] = jnp.sum(d_attn_in, 0, keepdims=True)
    d_norm[3:4] = jnp.sum(d_mlp_in, 0, keepdims=True)
    d_normed = d_attn_in * gain[layer, 0:1] + d_mlp_in * gain[layer, 1:2]
    return g + inv * (
        d_normed
        - jnp.mean(d_normed, -1, keepdims=True)
        - normed * jnp.mean(d_normed * normed, -1, keepdims=True)
    )


def turn_point_body(
    at, stream, parts, parts_other, recv, w_out_own, w_out_other, w_qkv, w_qkv_other, out_bias,
    gain, bias, cot, cs, x, act, slope, w_up, w_down, w_out, recv_first,
    block_out, g_out, send, grads, part, d_b_up, d_b_qkv, d_norm, d_sum,
):
    t = at[1]
    branch = parts[0:256].astype(F32) + parts_other[0:256].astype(F32)
    branch = branch + branch_of(t, recv, w_out_own, w_out_other)
    block_out[...] = stream[...] + branch + out_bias[1, 0:1] + out_bias[1, 1:2]
    d_mlp_in = parts[256:512].astype(F32) + parts_other[256:512].astype(F32)
    g = norm_back(
        t, stream[...], cot[...], d_mlp_in, recv, HEAD, w_qkv, w_qkv_other, cs, gain, bias, 1,
        lambda value: pack_qkv(grads, 0, value), d_b_qkv, d_norm,
    )
    g_out[...] = g
    g_b = g.astype(BF)
    d_sum[...] = jnp.sum(g, 0, keepdims=True)
    d_ctx = mm(w_out[...], g_b, 1, 1)
    for s in range(2):
        for h in range(4):
            send[s * 4 + h] = d_ctx[h * HEAD : (h + 1) * HEAD, s * BLK : (s + 1) * BLK].astype(BF)
    cot_b = cot[...].astype(BF)
    for which, (source, upstream, place) in enumerate(
        ((recv, cot_b, 192), (recv_first, g_b, 768))
    ):
        full = [gather_ctx(source, s) for s in range(2)]
        full = jnp.concatenate(full, 1)
        own = jnp.where(t == 0, full[0:256], full[256:512])
        pack_out(grads, place, mm(own, upstream))
    normed, _ = norm_rows(x[...])
    mlp_in = (normed * gain[0, 1:2] + bias[0, 1:2]).astype(BF)
    part[...] = feed_back(
        g_b, act, slope, mlp_in, w_up, w_down, pack_up(grads, 256), pack_down(grads, 512), d_b_up
    ).astype(BF)


def last_body(
    at, x, g, part, part_other, recv, w_qkv, w_qkv_other, cs, gain, bias,
    in_grad, grads, d_b_qkv, d_norm,
):
    d_mlp_in = part[...].astype(F32) + part_other[...].astype(F32)
    in_grad[...] = norm_back(
        at[1], x[...], g[...], d_mlp_in, recv, 0, w_qkv, w_qkv_other, cs, gain, bias, 0,
        lambda value: pack_qkv(grads, 0, value), d_b_qkv, d_norm,
    )


def swap(value):
    return lax.ppermute(value, "tensor", [(0, 1), (1, 0)])


def exchange(value, axes):
    return lax.all_to_all(value, axes, 0, 0)


def both(value):
    flat = value.reshape((16,) + value.shape[2:])
    return exchange(flat, ("context", "tensor")).reshape(value.shape)


def reduce_all(packed):
    rows = packed.shape[1]
    got = exchange(packed, "dp")
    one = jnp.sum(got.astype(F32), 0).astype(BF)
    got = exchange(one.reshape(8, rows // 8, 256), "context")
    one = jnp.sum(got.astype(F32), 0).astype(BF)
    back = exchange(jnp.broadcast_to(one[None], (8,) + one.shape), "context").reshape(rows, 256)
    return exchange(jnp.broadcast_to(back[None], (8,) + back.shape), "dp")


def shards(
    tokens_in, cotangent, positions, w_qkv, b_qkv, w_out, w_up, b_up, w_down, out_bias, ln_gain, ln_bias
):
    rows, width = 256, 512
    x = tokens_in.reshape(rows, width)
    cot = cotangent.reshape(rows, width)
    wq = w_qkv.reshape(2, width, 768)
    bq = b_qkv.reshape(2, 1, 768)
    bu = b_up.reshape(2, 1, 1024)
    at = jnp.stack([lax.axis_index("context"), lax.axis_index("tensor")]).astype(jnp.int32)
    freqs = jnp.asarray(FREQS).reshape(HALF, 1)
    w_out_other = swap(w_out)
    wq_other = swap(wq)

    send, part, act, slope, cs = call(
        first_body,
        [
            ((8, 208, BLK), BF),
            ((rows, width), BF),
            ((rows, 1024), BF),
            ((rows, 1024), F32),
            ((2, 2, HALF, BLK), F32),
        ],
        (at, positions, freqs, x, ln_gain, ln_bias, wq[0], bq[0], w_up[0], bu[0], w_down[0]),
        "norm_qkv_feed",
        smem_first=True,
    )
    part_other = swap(part)
    recv = exchange(send, "context")
    ctx_send, lse, ctx, start = call(
        attend_body,
        [((8, 2, HEAD, BLK), BF), ((1, 1024), F32), ((HEAD, 1024), F32), ((1, 1024), jnp.int32)],
        (recv,),
        "attend",
    )
    recv_ctx = both(ctx_send)
    stream, send, grads_a, parts, d_b_up1, d_sum1 = call(
        middle_body,
        [
            ((rows, width), F32),
            ((8, 256, BLK), BF),
            ((8, 512, 256), BF),
            ((2 * rows, width), BF),
            ((1, 1024), F32),
            ((1, width), F32),
        ],
        (
            at, x, part, part_other, recv_ctx, w_out[0], w_out_other[0], out_bias, ln_gain, ln_bias,
            wq[1], bq[1], w_up[1], bu[1], w_down[1], w_out[1], cot, cs,
        ),
        "middle",
        scratch=[pltpu.VMEM((rows, 1024), BF), pltpu.VMEM((rows, 1024), F32)],
        smem_first=True,
    )
    parts_other = swap(parts)
    recv_both = exchange(send, "context")
    (both_send,) = call(
        attend_both_body,
        [((8, 2, 256, BLK), BF)],
        (recv_both, start),
        "attend_both",
        scratch=[pltpu.VMEM((HEAD, 1024), F32), pltpu.VMEM((HEAD, 1024), F32)],
    )
    recv_grad = both(both_send)
    block_out, g, send, grads_b, part_g, d_b_up0, d_b_qkv1, d_norm1, d_sum0 = call(
        turn_point_body,
        [
            ((rows, width), F32),
            ((rows, width), F32),
            ((8, HEAD, BLK), BF),
            ((8, 832, 256), BF),
            ((rows, width), BF),
            ((1, 1024), F32),
            ((1, 768), F32),
            ((4, width), F32),
            ((1, width), F32),
        ],
        (
            at, stream, parts, parts_other, recv_grad, w_out[1], w_out_other[1], wq[1], wq_other[1],
            out_bias, ln_gain, ln_bias, cot, cs, x, act, slope, w_up[0], w_down[0], w_out[0], recv_ctx,
        ),
        "turn_point",
        smem_first=True,
    )
    part_g_other = swap(part_g)
    recv_d = exchange(send, "context")
    (back_send,) = call(
        attend_back_body,
        [((8, 2, 192, BLK), BF)],
        (recv, recv_d, start, lse, ctx),
        "attend_back",
        scratch=[pltpu.VMEM((HEAD, 1024), F32), pltpu.VMEM((HEAD, 1024), F32)],
    )
    recv_grad0 = both(back_send)
    in_grad, grads_c, d_b_qkv0, d_norm0 = call(
        last_body,
        [((rows, width), F32), ((8, 192, 256), BF), ((1, 768), F32), ((4, width), F32)],
        (at, x, g, part_g, part_g_other, recv_grad0, wq[0], wq_other[0], cs, ln_gain, ln_bias),
        "last",
        smem_first=True,
    )

    small = jnp.concatenate(
        [
            v.reshape(-1)
            for v in (d_b_up0, d_b_up1, d_b_qkv0, d_b_qkv1, d_sum0, d_sum1, d_norm0, d_norm1)
        ]
    )
    used = small.shape[0]
    small = jnp.pad(small, (0, 8 * 16 * 256 - used)).astype(BF).reshape(8, 16, 256)
    pad = jnp.zeros((8, 48, 256), BF)
    packed = jnp.concatenate([grads_a, grads_b, grads_c, small, pad], 1)
    total = reduce_all(packed)

    def up(row):
        v = total[:, row : row + 256].reshape(8, 4, 64, 256)
        return jnp.transpose(v, (0, 2, 1, 3)).reshape(512, 1024)

    def down(row):
        v = total[:, row : row + 256].reshape(8, 2, 128, 256)
        return jnp.transpose(v, (0, 2, 1, 3)).reshape(1024, 512)

    def qkv(row):
        v = total[:, row : row + 192].reshape(8, 3, 64, 256)
        return jnp.transpose(v, (0, 2, 1, 3)).reshape(512, 3, 256)

    def out(row):
        v = total[:, row : row + 64].reshape(8, 2, 32, 256)
        return jnp.transpose(v, (0, 2, 1, 3)).reshape(256, 512)

    def pair(first, second):
        return jnp.stack([first, second]).astype(F32)

    base = 512
    tiny = total[:, 1536:1552].reshape(-1).astype(F32)
    g_b_up = tiny[0:2048].reshape(2, 1024)
    g_b_qkv = tiny[2048:3584].reshape(2, 3, 256)
    g_sum = tiny[3584:4608].reshape(2, 1, 512)
    g_norm = tiny[4608:8704].reshape(2, 2, 2, 512)
    return (
        block_out.reshape(tokens_in.shape),
        in_grad.reshape(tokens_in.shape),
        pair(qkv(1344), qkv(base)),
        g_b_qkv,
        pair(out(base + 768), out(base + 192)),
        pair(up(base + 256), up(0)),
        g_b_up,
        pair(down(base + 512), down(256)),
        jnp.concatenate([g_sum, g_sum], 1),
        g_norm[:, 0],
        g_norm[:, 1],
    )


def solution(mesh):
    return jax.shard_map(
        shards,
        mesh=mesh,
        in_specs=(
            P("dp", "context", None),
            P("dp", "context", None),
            P("dp", "context"),
            P(None, None, None, "tensor"),
            P(None, None, "tensor"),
            P(None, "tensor", None),
            P(None, None, "tensor"),
            P(None, "tensor"),
            P(None, "tensor", None),
            P(),
            P(),
            P(),
        ),
        out_specs=(
            P("dp", "context", None),
            P("dp", "context", None),
            P(None, None, None, "tensor"),
            P(None, None, "tensor"),
            P(None, "tensor", None),
            P(None, None, "tensor"),
            P(None, "tensor"),
            P(None, "tensor", None),
            P(),
            P(),
            P(),
        ),
        check_vma=False,
    )
```

```python
from functools import partial

import numpy as np

import jax
import jax.numpy as jnp
from jax import lax
from jax.experimental import pallas as pl
from jax.experimental.pallas import tpu as pltpu
from jax.sharding import PartitionSpec as P

EPS = 1e-05
HALF = 8
HEAD = 64
BLK = 128
CHUNK = 256
NEG = -1e30
BF = jnp.bfloat16
F32 = jnp.float32

FREQS = (10000.0 ** (-np.arange(HALF, dtype=np.float64) * 2.0 / 16.0)).astype(np.float32)


def mm(a, b, ca=1, cb=0):
    return lax.dot_general(a, b, (((ca,), (cb,)), ((), ())), preferred_element_type=F32)


class Layer:
    def __init__(self, array, index):
        self.array, self.index = array, index

    def spec(self):
        rest = self.array.shape[1:]
        place = (self.index,) + (0,) * len(rest)
        return pl.BlockSpec((None,) + rest, lambda i: place)


def whole(shape):
    return pl.BlockSpec(shape, lambda i: (0,) * len(shape))


def call(body, out_shape, args, name, scratch=(), smem_first=False):
    specs = [
        a.spec() if isinstance(a, Layer) else whole(a.shape) for a in args
    ]
    args = [a.array if isinstance(a, Layer) else a for a in args]
    if smem_first:
        specs[0] = pl.BlockSpec(memory_space=pltpu.SMEM)
    return pl.pallas_call(
        body,
        grid=(1,),
        out_shape=[jax.ShapeDtypeStruct(s, d) for s, d in out_shape],
        in_specs=specs,
        out_specs=[whole(s) for s, _ in out_shape],
        scratch_shapes=list(scratch),
        compiler_params=pltpu.CompilerParams(vmem_limit_bytes=56 * 1024 * 1024),
        name=name,
    )(*args)


def norm_rows(x):
    mean = jnp.mean(x, -1, keepdims=True)
    cen = x - mean
    inv = lax.rsqrt(jnp.mean(cen * cen, -1, keepdims=True) + EPS)
    return cen * inv, inv


def turn(t, cos, sin):
    a, b = t[:HALF], t[HALF : 2 * HALF]
    return jnp.concatenate([a * cos - b * sin, b * cos + a * sin, t[2 * HALF :]], 0)


def turn_back(u, cos, sin):
    a, b = u[:HALF], u[HALF : 2 * HALF]
    return jnp.concatenate([a * cos + b * sin, b * cos - a * sin, u[2 * HALF :]], 0)


def send_qkv(send, attn_in, w_qkv, b_qkv, layer, cs):
    for e in range(3):
        turned = (mm(attn_in, w_qkv[e]) + b_qkv[e, layer : layer + 1]).T
        for s in range(2):
            cos, sin = cs[s, 0], cs[s, 1]
            for h in range(4):
                j = s * 4 + h
                part = turned[h * HEAD : (h + 1) * HEAD, s * BLK : (s + 1) * BLK]
                if e < 2:
                    part = turn(part, cos, sin)
                if e == 0:
                    part = part * (HEAD**-0.5)
                send[j, e * HEAD : (e + 1) * HEAD, :] = part.astype(BF)


def feed_forward(mlp_in, w_up, b_up, layer, w_down, act, slope):
    width = w_up.shape[1]
    total = None
    for c in range(0, width, 256):
        cols = slice(c, c + 256)
        pre = mm(mlp_in, w_up[:, cols]) + b_up[layer : layer + 1, cols]
        cdf = 0.5 + 0.5 * lax.erf(pre * np.float32(0.7071067811865476))
        a = (pre * cdf).astype(BF)
        act[:, cols] = a
        slope[:, cols] = cdf + pre * (jnp.exp(-0.5 * pre * pre) * np.float32(0.3989422804014327))
        term = mm(a, w_down[cols, :])
        total = term if total is None else total + term
    return total


def feed_back(g_b, act, slope, mlp_in, w_up, w_down, d_up, d_down, d_b_up):
    width = w_up.shape[1]
    total = None
    mlp_t = mlp_in.astype(F32).T.astype(BF)
    for c in range(0, width, 256):
        cols = slice(c, c + 256)
        d_act = mm(g_b, w_down[cols, :], 1, 1)
        d_pre = d_act * slope[:, cols]
        d_pre_b = d_pre.astype(BF)
        d_b_up[:, cols] = jnp.sum(d_pre_b.astype(F32), 0, keepdims=True)
        d_up(c // 256, mm(mlp_t, d_pre_b))
        d_down(c, mm(act[:, cols].astype(F32).T.astype(BF), g_b))
        term = mm(d_pre_b, w_up[:, cols], 1, 1)
        total = term if total is None else total + term
    return total


def pack_up(out, row):
    def put(c, value):
        for p in range(8):
            out[p, row + 64 * c : row + 64 * (c + 1), :] = value[64 * p : 64 * (p + 1)].astype(BF)

    return put


def pack_down(out, row):
    def put(c, value):
        for half in range(2):
            for k in range(2):
                out[c // 128 + k, row + 128 * half : row + 128 * (half + 1), :] = value[
                    128 * k : 128 * (k + 1), 256 * half : 256 * (half + 1)
                ].astype(BF)

    return put


def pack_qkv(out, row):
    def put(e, value):
        for p in range(8):
            out[p, row + 64 * e : row + 64 * (e + 1), :] = value[64 * p : 64 * (p + 1)].astype(BF)

    return put


def own_ctx(t, recv):
    full = jnp.concatenate([gather_ctx(recv, s) for s in range(2)], 1)
    return jnp.where(t == 0, full[0:256], full[256:512])


def pack_out(out, row, ctx, upstream):
    value = mm(ctx, upstream)
    for p in range(8):
        for half in range(2):
            out[p, row + 32 * half : row + 32 * (half + 1), :] = value[
                32 * p : 32 * (p + 1), 256 * half : 256 * (half + 1)
            ].astype(BF)


def first_body(
    at, pos, freqs, x, gain, bias, w_qkv, b_qkv, w_up, b_up, w_down, send, part, act, slope, cs
):
    for s in range(2):
        p = pos[s : s + 1, :].astype(F32)
        angle = freqs[...] * p
        cs[s, 0] = jnp.cos(angle)
        cs[s, 1] = jnp.sin(angle)
    normed, _ = norm_rows(x[...])
    attn_in = (normed * gain[0, 0:1] + bias[0, 0:1]).astype(BF)
    mlp_in = (normed * gain[0, 1:2] + bias[0, 1:2]).astype(BF)
    send_qkv(send, attn_in, w_qkv, b_qkv, 0, cs)
    row = lax.broadcasted_iota(jnp.int32, (16, BLK), 0)
    token = at[0] * BLK + lax.broadcasted_iota(jnp.int32, (1, BLK), 1)
    for s in range(2):
        start = jnp.maximum(token - pos[s : s + 1, :], 0)
        high = (start // 8).astype(F32)
        low = (start % 8).astype(F32)
        block = jnp.where(row == 0, high, jnp.where(row == 1, low, 0.0)).astype(BF)
        for h in range(4):
            send[s * 4 + h, 3 * HEAD : 3 * HEAD + 16, :] = block
    part[...] = feed_forward(mlp_in, w_up, b_up, 0, w_down, act, slope).astype(BF)


def load_rows(recv, lo, hi):
    return jnp.concatenate([recv[i, lo:hi, :] for i in range(8)], 1)


def starts_of(recv):
    rows = load_rows(recv, 3 * HEAD, 3 * HEAD + 16).astype(F32)
    return rows[0:1] * 8.0 + rows[1:2]


def visible_of(start, c, length):
    key = lax.broadcasted_iota(jnp.int32, (length, CHUNK), 0)
    query = lax.broadcasted_iota(jnp.int32, (length, CHUNK), 1) + c * CHUNK
    return (key <= query) & (key >= start[:, c * CHUNK : (c + 1) * CHUNK])


def attend_body(recv, send, lse, ctx, start_out):
    q = load_rows(recv, 0, HEAD)
    k_t = load_rows(recv, HEAD, 2 * HEAD)
    v_t = load_rows(recv, 2 * HEAD, 3 * HEAD)
    k = k_t.astype(F32).T.astype(BF)
    start = starts_of(recv).astype(jnp.int32)
    start_out[...] = start
    for c in range(4):
        cols = slice(c * CHUNK, (c + 1) * CHUNK)
        length = (c + 1) * CHUNK
        scores = mm(k[:length], q[:, cols])
        scores = jnp.where(visible_of(start, c, length), scores, NEG)
        peak = jnp.max(scores, 0, keepdims=True)
        shifted = jnp.exp(scores - peak)
        total = jnp.sum(shifted, 0, keepdims=True)
        lse[:, cols] = peak + jnp.log(total)
        out = mm(v_t[:, :length], shifted.astype(BF)) / total
        ctx[:, cols] = out
        for i in range(CHUNK // BLK):
            block = out[:, i * BLK : (i + 1) * BLK].astype(BF)
            for t in range(2):
                send[c * (CHUNK // BLK) + i, t] = block


def attend_both_body(recv, start, send, dk, dv):
    q = load_rows(recv, 0, HEAD)
    k_t = load_rows(recv, HEAD, 2 * HEAD)
    v_t = load_rows(recv, 2 * HEAD, 3 * HEAD)
    d_ctx = load_rows(recv, 3 * HEAD, 4 * HEAD)
    k = k_t.astype(F32).T.astype(BF)
    v = v_t.astype(F32).T.astype(BF)
    dk[...] = jnp.zeros_like(dk)
    dv[...] = jnp.zeros_like(dv)
    for c in range(4):
        cols = slice(c * CHUNK, (c + 1) * CHUNK)
        length = (c + 1) * CHUNK
        scores = mm(k[:length], q[:, cols])
        scores = jnp.where(visible_of(start[...], c, length), scores, NEG)
        peak = jnp.max(scores, 0, keepdims=True)
        shifted = jnp.exp(scores - peak)
        probs = shifted * (1.0 / jnp.sum(shifted, 0, keepdims=True))
        probs_b = probs.astype(BF)
        out = mm(v_t[:, :length], probs_b)
        dq = backward_chunk(q, k_t, v, d_ctx, probs, probs_b, out, cols, length, dk, dv)
        for i in range(CHUNK // BLK):
            b = c * (CHUNK // BLK) + i
            for t in range(2):
                send[b, t, 0:HEAD] = out[:, i * BLK : (i + 1) * BLK].astype(BF)
                send[b, t, HEAD : 2 * HEAD] = dq[:, i * BLK : (i + 1) * BLK].astype(BF)
    put_kv(send, dk, dv, 2 * HEAD)


def backward_chunk(q, k_t, v, d_ctx, probs, probs_b, out, cols, length, dk, dv):
    d_out = d_ctx[:, cols]
    d_probs = mm(v[:length], d_out)
    delta = jnp.sum(d_out.astype(F32) * out, 0, keepdims=True)
    d_scores = (probs * (d_probs - delta)).astype(BF)
    dk[:, :length] += mm(q[:, cols], d_scores, 1, 1)
    dv[:, :length] += mm(d_out, probs_b, 1, 1)
    return mm(k_t[:, :length], d_scores) * (HEAD**-0.5)


def put_kv(send, dk, dv, row):
    for b in range(8):
        for t in range(2):
            send[b, t, row : row + HEAD] = dk[:, b * BLK : (b + 1) * BLK].astype(BF)
            send[b, t, row + HEAD : row + 2 * HEAD] = dv[:, b * BLK : (b + 1) * BLK].astype(BF)


def attend_back_body(recv, recv_d, start, lse, ctx, send, dk, dv):
    q = load_rows(recv, 0, HEAD)
    k_t = load_rows(recv, HEAD, 2 * HEAD)
    v_t = load_rows(recv, 2 * HEAD, 3 * HEAD)
    d_ctx = load_rows(recv_d, 0, HEAD)
    k = k_t.astype(F32).T.astype(BF)
    v = v_t.astype(F32).T.astype(BF)
    dk[...] = jnp.zeros_like(dk)
    dv[...] = jnp.zeros_like(dv)
    for c in range(4):
        cols = slice(c * CHUNK, (c + 1) * CHUNK)
        length = (c + 1) * CHUNK
        scores = mm(k[:length], q[:, cols])
        scores = jnp.where(visible_of(start[...], c, length), scores, NEG)
        probs = jnp.exp(scores - lse[:, cols])
        probs_b = probs.astype(BF)
        dq = backward_chunk(q, k_t, v, d_ctx, probs, probs_b, ctx[:, cols], cols, length, dk, dv)
        for i in range(CHUNK // BLK):
            for t in range(2):
                send[c * (CHUNK // BLK) + i, t, 0:HEAD] = dq[:, i * BLK : (i + 1) * BLK].astype(BF)
    put_kv(send, dk, dv, HEAD)


def gather_ctx(recv, s):
    return jnp.concatenate([recv[s * 4 + h, t, 0:HEAD, :] for t in range(2) for h in range(4)], 0)


def ordered(t, own, other):
    return jnp.where(t == 0, own, other), jnp.where(t == 0, other, own)


def out_other(others):
    halves = [
        jnp.concatenate([others[3, 64 * p + 32 * c : 64 * p + 32 * (c + 1), :] for p in range(8)], 0)
        for c in range(2)
    ]
    return jnp.concatenate(halves, 1)


def branch_of(t, recv, w_own, others):
    first, second = ordered(t, w_own[...], out_other(others))
    w = jnp.concatenate([first, second], 0)
    rows = []
    for s in range(2):
        rows.append(mm(gather_ctx(recv, s).astype(F32).T.astype(BF), w))
    return jnp.concatenate(rows, 0)


def middle_body(
    at, x, part, part_other, recv, w_out_own, others, out_bias, gain, bias,
    w_qkv, b_qkv, w_up, b_up, w_down, w_out, cot, cs,
    stream, send, grads, parts, d_b_up, d_sum, act, slope,
):
    branch = part[...].astype(F32) + part_other[...].astype(F32)
    branch = branch + branch_of(at[1], recv, w_out_own, others)
    out = x[...] + branch + out_bias[0, 0:1] + out_bias[0, 1:2]
    stream[...] = out
    normed, _ = norm_rows(out)
    attn_in = (normed * gain[1, 0:1] + bias[1, 0:1]).astype(BF)
    mlp_in = (normed * gain[1, 1:2] + bias[1, 1:2]).astype(BF)
    send_qkv(send, attn_in, w_qkv, b_qkv, 1, cs)
    g_b = cot[...].astype(BF)
    d_ctx = mm(w_out[...], g_b, 1, 1)
    for s in range(2):
        for h in range(4):
            send[s * 4 + h, 3 * HEAD : 4 * HEAD, :] = d_ctx[
                h * HEAD : (h + 1) * HEAD, s * BLK : (s + 1) * BLK
            ].astype(BF)
    d_sum[...] = jnp.sum(cot[...], 0, keepdims=True)
    parts[0:256] = feed_forward(mlp_in, w_up, b_up, 1, w_down, act, slope).astype(BF)
    parts[256:512] = feed_back(
        g_b, act, slope, mlp_in, w_up, w_down, pack_up(grads, 0), pack_down(grads, 256), d_b_up
    ).astype(BF)


def norm_back(
    t, x, g, d_mlp_in, recv, row, w_own, others, cs, gain, bias, layer, d_qkv, d_b_qkv, d_norm
):
    normed, inv = norm_rows(x)
    attn_in = (normed * gain[layer, 0:1] + bias[layer, 0:1]).astype(BF)
    attn_t = attn_in.astype(F32).T.astype(BF)
    d_attn_t = None
    for e in range(3):
        halves = []
        for tt in range(2):
            blocks = []
            for h in range(4):
                pieces = []
                for s in range(2):
                    lo = row + e * HEAD
                    u = recv[s * 4 + h, tt, lo : lo + HEAD, :]
                    if e < 2:
                        u = turn_back(u.astype(F32), cs[s, 0], cs[s, 1]).astype(BF)
                    pieces.append(u)
                blocks.append(jnp.concatenate(pieces, 1))
            halves.append(jnp.concatenate(blocks, 0))
        first, second = ordered(t, w_own[e], others[e])
        term = mm(first, halves[0]) + mm(second, halves[1])
        d_attn_t = term if d_attn_t is None else d_attn_t + term
        own = jnp.where(t == 0, halves[0], halves[1])
        d_qkv(e, mm(attn_t, own, 1, 1))
        d_b_qkv[e : e + 1] = mm(jnp.ones((8, own.shape[1]), BF), own, 1, 1)[0:1]
    d_attn_in = d_attn_t.T
    d_norm[0:1] = jnp.sum(d_attn_in * normed, 0, keepdims=True)
    d_norm[1:2] = jnp.sum(d_mlp_in * normed, 0, keepdims=True)
    d_norm[2:3] = jnp.sum(d_attn_in, 0, keepdims=True)
    d_norm[3:4] = jnp.sum(d_mlp_in, 0, keepdims=True)
    d_normed = d_attn_in * gain[layer, 0:1] + d_mlp_in * gain[layer, 1:2]
    return g + inv * (
        d_normed
        - jnp.mean(d_normed, -1, keepdims=True)
        - normed * jnp.mean(d_normed * normed, -1, keepdims=True)
    )


def turn_point_body(
    at, stream, parts, parts_other, recv, w_out, w_qkv, others, out_bias,
    gain, bias, cot, cs, x, act, slope, w_up, w_down, w_out_first,
    block_out, g_out, send, grads, part, d_b_up, d_b_qkv, d_norm, d_sum,
):
    t = at[1]
    branch = parts[0:256].astype(F32) + parts_other[0:256].astype(F32)
    branch = branch + branch_of(t, recv, w_out, others)
    block_out[...] = stream[...] + branch + out_bias[1, 0:1] + out_bias[1, 1:2]
    d_mlp_in = parts[256:512].astype(F32) + parts_other[256:512].astype(F32)
    g = norm_back(
        t, stream[...], cot[...], d_mlp_in, recv, HEAD, w_qkv, others, cs, gain, bias, 1,
        pack_qkv(grads, 0), d_b_qkv, d_norm,
    )
    g_out[...] = g
    g_b = g.astype(BF)
    d_sum[...] = jnp.sum(g, 0, keepdims=True)
    d_ctx = mm(w_out_first[...], g_b, 1, 1)
    for s in range(2):
        for h in range(4):
            send[s * 4 + h] = d_ctx[h * HEAD : (h + 1) * HEAD, s * BLK : (s + 1) * BLK].astype(BF)
    pack_out(grads, 704, own_ctx(t, recv), cot[...].astype(BF))
    normed, _ = norm_rows(x[...])
    mlp_in = (normed * gain[0, 1:2] + bias[0, 1:2]).astype(BF)
    part[...] = feed_back(
        g_b, act, slope, mlp_in, w_up, w_down, pack_up(grads, 192), pack_down(grads, 448), d_b_up
    ).astype(BF)


def last_body(
    at, x, g, part, part_other, recv, recv_ctx, w_qkv, others, cs, gain, bias,
    d_b_up0, d_b_up1, d_b_qkv1, d_norm1, d_sum0, d_sum1,
    in_grad, grads, d_b_qkv0, d_norm0,
):
    d_mlp_in = part[...].astype(F32) + part_other[...].astype(F32)
    in_grad[...] = norm_back(
        at[1], x[...], g[...], d_mlp_in, recv, 0, w_qkv, others, cs, gain, bias, 0,
        pack_qkv(grads, 0), d_b_qkv0, d_norm0,
    )
    pack_out(grads, 192, own_ctx(at[1], recv_ctx), g[...].astype(BF))

    def lanes(ref, row, count):
        return [ref[row : row + 1, 256 * c : 256 * (c + 1)] for c in range(count)]

    def norms(ref):
        return [v for r in range(4) for v in lanes(ref, r, 2)]

    rows = [
        lanes(d_b_up0, 0, 4)
        + lanes(d_b_up1, 0, 4)
        + [v for e in range(3) for ref in (d_b_qkv0, d_b_qkv1) for v in lanes(ref, e, 1)],
        lanes(d_sum0, 0, 2) + lanes(d_sum1, 0, 2) + norms(d_norm0),
        norms(d_norm1),
    ]
    for p in range(8):
        have = rows[p] if p < len(rows) else []
        fill = [jnp.zeros((16 - len(have), 256), F32)]
        grads[p, 256:272, :] = jnp.concatenate(have + fill, 0).astype(BF)


def chunk_body(at, w_qkv, w_out, out):
    for layer in range(2):
        for e in range(3):
            out[layer, e] = w_qkv[layer, e, pl.ds(pl.multiple_of(at[2] * 64, 64), 64), :]
        rows = w_out[layer, pl.ds(pl.multiple_of(at[2] * 32, 32), 32), :]
        out[layer, 3, 0:32] = rows[:, 0:256]
        out[layer, 3, 32:64] = rows[:, 256:512]


def mix_body(got, early, out):
    total = got[0].astype(F32)
    for i in range(1, 8):
        total = total + got[i].astype(F32)
    for q in range(8):
        out[q, 0:96] = early[96 * q : 96 * (q + 1)]
        out[q, 96:128] = total[32 * q : 32 * (q + 1)].astype(BF)
        if q == 0:
            out[q, 128:144] = total[256:272].astype(BF)
        else:
            out[q, 128:144] = jnp.zeros((16, 256), BF)


def sum_body(got, out):
    total = got[0].astype(F32)
    for i in range(1, 8):
        total = total + got[i].astype(F32)
    out[...] = total.astype(BF)


def unpack_body(first, rest, g_qkv, g_out, g_up, g_down, g_b_up, g_b_qkv, g_sum, g_gain, g_bias):
    p = pl.program_id(0)

    def early(row):
        return rest[row // 96, row % 96 : row % 96 + 32].astype(F32)

    def late(row):
        return rest[row // 32, 96:128].astype(F32)

    for e in range(3):
        for k in range(2):
            g_qkv[0, e, 32 * k : 32 * (k + 1)] = late(64 * e + 32 * k)
            g_qkv[1, e, 32 * k : 32 * (k + 1)] = early(64 * e + 32 * k)
    for c in range(2):
        g_out[0, :, 256 * c : 256 * (c + 1)] = late(192 + 32 * c)
        g_out[1, :, 256 * c : 256 * (c + 1)] = early(704 + 32 * c)
    for c in range(4):
        cols = slice(256 * c, 256 * (c + 1))
        for k in range(2):
            g_up[0, 32 * k : 32 * (k + 1), cols] = early(192 + 64 * c + 32 * k)
        g_up[1, :, cols] = first[64 * c : 64 * (c + 1)].astype(F32)
    for c in range(2):
        cols = slice(256 * c, 256 * (c + 1))
        for k in range(4):
            g_down[0, 32 * k : 32 * (k + 1), cols] = early(448 + 128 * c + 32 * k)
        g_down[1, :, cols] = first[256 + 128 * c : 256 + 128 * (c + 1)].astype(F32)

    tiny = rest[0, 128:144].astype(F32)

    @pl.when(p == 0)
    def _():
        for layer in range(2):
            for c in range(4):
                r = 4 * layer + c
                g_b_up[layer : layer + 1, 256 * c : 256 * (c + 1)] = tiny[r : r + 1]
        for e in range(3):
            for layer in range(2):
                r = 8 + 2 * e + layer
                g_b_qkv[e, layer : layer + 1, :] = tiny[r : r + 1]

    def norms(layer, base):
        for which in range(2):
            for c in range(2):
                cols = slice(256 * c, 256 * (c + 1))
                r = base + 2 * which + c
                g_gain[layer, which : which + 1, cols] = tiny[r : r + 1]
                g_bias[layer, which : which + 1, cols] = tiny[r + 4 : r + 5]

    @pl.when(p == 1)
    def _():
        for layer in range(2):
            for c in range(2):
                r = 2 * layer + c
                for which in range(2):
                    g_sum[layer, which : which + 1, 256 * c : 256 * (c + 1)] = tiny[r : r + 1]
        norms(0, 4)

    @pl.when(p == 2)
    def _():
        norms(1, 0)


def unpack(first, rest):
    outs = [
        ((2, 3, 512, 256), pl.BlockSpec((2, 3, 64, 256), lambda p: (0, 0, p, 0))),
        ((2, 256, 512), pl.BlockSpec((2, 32, 512), lambda p: (0, p, 0))),
        ((2, 512, 1024), pl.BlockSpec((2, 64, 1024), lambda p: (0, p, 0))),
        ((2, 1024, 512), pl.BlockSpec((2, 128, 512), lambda p: (0, p, 0))),
        ((2, 1024), whole((2, 1024))),
        ((3, 2, 256), whole((3, 2, 256))),
        ((2, 2, 512), whole((2, 2, 512))),
        ((2, 2, 512), whole((2, 2, 512))),
        ((2, 2, 512), whole((2, 2, 512))),
    ]
    return pl.pallas_call(
        unpack_body,
        grid=(8,),
        out_shape=[jax.ShapeDtypeStruct(shape, F32) for shape, _ in outs],
        in_specs=[
            pl.BlockSpec((None, 512, 256), lambda p: (p, 0, 0)),
            pl.BlockSpec((None, 8, 144, 256), lambda p: (p, 0, 0, 0)),
        ],
        out_specs=[spec for _, spec in outs],
        compiler_params=pltpu.CompilerParams(vmem_limit_bytes=56 * 1024 * 1024),
        name="unpack",
    )(first, rest)


def swap(value):
    return lax.ppermute(value, "tensor", [(0, 1), (1, 0)])


def exchange(value, axes):
    return lax.all_to_all(value, axes, 0, 0)


def both(value):
    flat = value.reshape((16,) + value.shape[2:])
    return exchange(flat, ("context", "tensor")).reshape(value.shape)


def shards(
    tokens_in, cotangent, positions, w_qkv, b_qkv, w_out, w_up, b_up, w_down, out_bias, ln_gain, ln_bias
):
    rows, width = 256, 512
    x = tokens_in.reshape(rows, width)
    cot = cotangent.reshape(rows, width)
    wq = jnp.transpose(w_qkv, (0, 2, 1, 3))
    bq = jnp.transpose(b_qkv, (1, 0, 2))
    at = jnp.stack(
        [lax.axis_index("context"), lax.axis_index("tensor"), lax.axis_index("dp")]
    ).astype(jnp.int32)
    freqs = jnp.asarray(FREQS).reshape(HALF, 1)
    (chunk,) = call(chunk_body, [((2, 4, 64, 256), BF)], (at, wq, w_out), "chunk", smem_first=True)
    others = lax.all_gather(swap(chunk), "dp", axis=2, tiled=True)

    send, part, act, slope, cs = call(
        first_body,
        [
            ((8, 208, BLK), BF),
            ((rows, width), BF),
            ((rows, 1024), BF),
            ((rows, 1024), F32),
            ((2, 2, HALF, BLK), F32),
        ],
        (
            at, positions, freqs, x, ln_gain, ln_bias, Layer(wq, 0), bq, Layer(w_up, 0), b_up,
            Layer(w_down, 0),
        ),
        "norm_qkv_feed",
        smem_first=True,
    )
    part_other = swap(part)
    recv = exchange(send, "context")
    ctx_send, lse, ctx, start = call(
        attend_body,
        [((8, 2, HEAD, BLK), BF), ((1, 1024), F32), ((HEAD, 1024), F32), ((1, 1024), jnp.int32)],
        (recv,),
        "attend",
    )
    recv_ctx = both(ctx_send)
    stream, send, grads_a, parts, d_b_up1, d_sum1 = call(
        middle_body,
        [
            ((rows, width), F32),
            ((8, 256, BLK), BF),
            ((8, 512, 256), BF),
            ((2 * rows, width), BF),
            ((1, 1024), F32),
            ((1, width), F32),
        ],
        (
            at, x, part, part_other, recv_ctx, Layer(w_out, 0), Layer(others, 0), out_bias, ln_gain,
            ln_bias, Layer(wq, 1), bq, Layer(w_up, 1), b_up, Layer(w_down, 1), Layer(w_out, 1), cot, cs,
        ),
        "middle",
        scratch=[pltpu.VMEM((rows, 1024), BF), pltpu.VMEM((rows, 1024), F32)],
        smem_first=True,
    )
    sums_a = lax.psum_scatter(grads_a, "dp", scatter_dimension=0)
    sums_a = lax.psum(sums_a, "context")
    full_a = lax.all_gather(sums_a, "dp")
    parts_other = swap(parts)
    recv_both = exchange(send, "context")
    (both_send,) = call(
        attend_both_body,
        [((8, 2, 256, BLK), BF)],
        (recv_both, start),
        "attend_both",
        scratch=[pltpu.VMEM((HEAD, 1024), F32), pltpu.VMEM((HEAD, 1024), F32)],
    )
    recv_grad = both(both_send)
    block_out, g, send, grads_b, part_g, d_b_up0, d_b_qkv1, d_norm1, d_sum0 = call(
        turn_point_body,
        [
            ((rows, width), F32),
            ((rows, width), F32),
            ((8, HEAD, BLK), BF),
            ((8, 768, 256), BF),
            ((rows, width), BF),
            ((1, 1024), F32),
            ((3, 256), F32),
            ((4, width), F32),
            ((1, width), F32),
        ],
        (
            at, stream, parts, parts_other, recv_grad, Layer(w_out, 1), Layer(wq, 1), Layer(others, 1),
            out_bias, ln_gain, ln_bias, cot, cs, x, act, slope, Layer(w_up, 0), Layer(w_down, 0),
            Layer(w_out, 0),
        ),
        "turn_point",
        smem_first=True,
    )
    sums_b = lax.psum_scatter(grads_b, "dp", scatter_dimension=0)
    part_g_other = swap(part_g)
    recv_d = exchange(send, "context")
    (back_send,) = call(
        attend_back_body,
        [((8, 2, 192, BLK), BF)],
        (recv, recv_d, start, lse, ctx),
        "attend_back",
        scratch=[pltpu.VMEM((HEAD, 1024), F32), pltpu.VMEM((HEAD, 1024), F32)],
    )
    recv_grad0 = both(back_send)
    in_grad, grads_c, _, _ = call(
        last_body,
        [((rows, width), F32), ((8, 272, 256), BF), ((3, 256), F32), ((4, width), F32)],
        (
            at, x, g, part_g, part_g_other, recv_grad0, recv_ctx, Layer(wq, 0), Layer(others, 0), cs,
            ln_gain, ln_bias, d_b_up0, d_b_up1, d_b_qkv1, d_norm1, d_sum0, d_sum1,
        ),
        "last",
        smem_first=True,
    )
    (mixed,) = call(mix_body, [((8, 144, 256), BF)], (exchange(grads_c, "dp"), sums_b), "mix")
    (summed,) = call(sum_body, [((144, 256), BF)], (exchange(mixed, "context"),), "sum")
    summed = exchange(jnp.broadcast_to(summed[None], (8, 144, 256)), "context")
    full_bc = lax.all_gather(summed, "dp")
    g_qkv, g_out, g_up, g_down, g_b_up, g_b_qkv, g_sum, g_gain, g_bias = unpack(full_a, full_bc)
    return (
        block_out.reshape(tokens_in.shape),
        in_grad.reshape(tokens_in.shape),
        jnp.transpose(g_qkv, (0, 2, 1, 3)),
        jnp.transpose(g_b_qkv, (1, 0, 2)),
        g_out,
        g_up,
        g_b_up,
        g_down,
        g_sum,
        g_gain,
        g_bias,
    )


def solution(mesh):
    return jax.shard_map(
        shards,
        mesh=mesh,
        in_specs=(
            P("dp", "context", None),
            P("dp", "context", None),
            P("dp", "context"),
            P(None, None, None, "tensor"),
            P(None, None, "tensor"),
            P(None, "tensor", None),
            P(None, None, "tensor"),
            P(None, "tensor"),
            P(None, "tensor", None),
            P(),
            P(),
            P(),
        ),
        out_specs=(
            P("dp", "context", None),
            P("dp", "context", None),
            P(None, None, None, "tensor"),
            P(None, None, "tensor"),
            P(None, "tensor", None),
            P(None, None, "tensor"),
            P(None, "tensor"),
            P(None, "tensor", None),
            P(),
            P(),
            P(),
        ),
        check_vma=False,
    )
```

```python
from functools import partial

import numpy as np

import jax
import jax.numpy as jnp
from jax import lax
from jax.experimental import pallas as pl
from jax.experimental.pallas import tpu as pltpu
from jax.sharding import PartitionSpec as P

EPS = 1e-05
HALF = 8
HEAD = 64
BLK = 128
CHUNK = 256
NEG = -1e30
BF = jnp.bfloat16
F32 = jnp.float32

FREQS = (10000.0 ** (-np.arange(HALF, dtype=np.float64) * 2.0 / 16.0)).astype(np.float32)


def mm(a, b, ca=1, cb=0):
    return lax.dot_general(a, b, (((ca,), (cb,)), ((), ())), preferred_element_type=F32)


class After:
    def __init__(self, array):
        self.array = array

    def spec(self):
        return pl.BlockSpec(memory_space=pl.ANY)


class Layer:
    def __init__(self, array, index):
        self.array, self.index = array, index

    def spec(self):
        rest = self.array.shape[1:]
        place = (self.index,) + (0,) * len(rest)
        return pl.BlockSpec((None,) + rest, lambda i: place)


def whole(shape):
    return pl.BlockSpec(shape, lambda i: (0,) * len(shape))


def call(body, out_shape, args, name, scratch=(), smem_first=False):
    specs = [
        a.spec() if isinstance(a, (Layer, After)) else whole(a.shape) for a in args
    ]
    args = [a.array if isinstance(a, (Layer, After)) else a for a in args]
    if smem_first:
        specs[0] = pl.BlockSpec(memory_space=pltpu.SMEM)
    return pl.pallas_call(
        body,
        grid=(1,),
        out_shape=[jax.ShapeDtypeStruct(s, d) for s, d in out_shape],
        in_specs=specs,
        out_specs=[whole(s) for s, _ in out_shape],
        scratch_shapes=list(scratch),
        compiler_params=pltpu.CompilerParams(vmem_limit_bytes=56 * 1024 * 1024),
        name=name,
    )(*args)


def norm_rows(x):
    mean = jnp.mean(x, -1, keepdims=True)
    cen = x - mean
    inv = lax.rsqrt(jnp.mean(cen * cen, -1, keepdims=True) + EPS)
    return cen * inv, inv


def turn(t, cos, sin):
    a, b = t[:HALF], t[HALF : 2 * HALF]
    return jnp.concatenate([a * cos - b * sin, b * cos + a * sin, t[2 * HALF :]], 0)


def turn_back(u, cos, sin):
    a, b = u[:HALF], u[HALF : 2 * HALF]
    return jnp.concatenate([a * cos + b * sin, b * cos - a * sin, u[2 * HALF :]], 0)


def send_qkv(send, attn_in, w_qkv, b_qkv, layer, cs):
    for e in range(3):
        turned = (mm(attn_in, w_qkv[e]) + b_qkv[e, layer : layer + 1]).T
        for s in range(2):
            cos, sin = cs[s, 0], cs[s, 1]
            for h in range(4):
                j = s * 4 + h
                part = turned[h * HEAD : (h + 1) * HEAD, s * BLK : (s + 1) * BLK]
                if e < 2:
                    part = turn(part, cos, sin)
                if e == 0:
                    part = part * (HEAD**-0.5)
                send[j, e * HEAD : (e + 1) * HEAD, :] = part.astype(BF)


def feed_forward(mlp_in, w_up, b_up, layer, w_down, act, slope):
    width = w_up.shape[1]
    total = None
    for c in range(0, width, 256):
        cols = slice(c, c + 256)
        pre = mm(mlp_in, w_up[:, cols]) + b_up[layer : layer + 1, cols]
        cdf = 0.5 + 0.5 * lax.erf(pre * np.float32(0.7071067811865476))
        a = (pre * cdf).astype(BF)
        act[:, cols] = a
        slope[:, cols] = cdf + pre * (jnp.exp(-0.5 * pre * pre) * np.float32(0.3989422804014327))
        term = mm(a, w_down[cols, :])
        total = term if total is None else total + term
    return total


def feed_back(g_b, act, slope, mlp_in, w_up, w_down, d_up, d_down, d_b_up):
    width = w_up.shape[1]
    total = None
    mlp_t = mlp_in.astype(F32).T.astype(BF)
    for c in range(0, width, 256):
        cols = slice(c, c + 256)
        d_act = mm(g_b, w_down[cols, :], 1, 1)
        d_pre = d_act * slope[:, cols]
        d_pre_b = d_pre.astype(BF)
        d_b_up[:, cols] = jnp.sum(d_pre_b.astype(F32), 0, keepdims=True)
        d_up(c // 256, mm(mlp_t, d_pre_b))
        d_down(c, mm(act[:, cols].astype(F32).T.astype(BF), g_b))
        term = mm(d_pre_b, w_up[:, cols], 1, 1)
        total = term if total is None else total + term
    return total


def pack_up(out, row):
    def put(c, value):
        for p in range(8):
            out[p, row + 64 * c : row + 64 * (c + 1), :] = value[64 * p : 64 * (p + 1)].astype(BF)

    return put


def pack_down(out, row):
    def put(c, value):
        for half in range(2):
            for k in range(2):
                out[c // 128 + k, row + 128 * half : row + 128 * (half + 1), :] = value[
                    128 * k : 128 * (k + 1), 256 * half : 256 * (half + 1)
                ].astype(BF)

    return put


def pack_qkv(out, row):
    def put(e, value):
        for p in range(8):
            out[p, row + 64 * e : row + 64 * (e + 1), :] = value[64 * p : 64 * (p + 1)].astype(BF)

    return put


def own_ctx(t, recv):
    full = jnp.concatenate([gather_ctx(recv, s) for s in range(2)], 1)
    return jnp.where(t == 0, full[0:256], full[256:512])


def pack_out(out, row, ctx, upstream):
    value = mm(ctx, upstream)
    for p in range(8):
        for half in range(2):
            out[p, row + 32 * half : row + 32 * (half + 1), :] = value[
                32 * p : 32 * (p + 1), 256 * half : 256 * (half + 1)
            ].astype(BF)


def first_body(
    at, pos, freqs, x, gain, bias, w_qkv, b_qkv, w_up, b_up, w_down, w_out,
    send, pair, act, slope, cs, chunk,
):
    chunk_of(at, w_qkv, w_out, chunk)
    pair[256:512] = w_out[0]
    for s in range(2):
        p = pos[s : s + 1, :].astype(F32)
        angle = freqs[...] * p
        cs[s, 0] = jnp.cos(angle)
        cs[s, 1] = jnp.sin(angle)
    normed, _ = norm_rows(x[...])
    attn_in = (normed * gain[0, 0:1] + bias[0, 0:1]).astype(BF)
    mlp_in = (normed * gain[0, 1:2] + bias[0, 1:2]).astype(BF)
    send_qkv(send, attn_in, w_qkv.at[0], b_qkv, 0, cs)
    row = lax.broadcasted_iota(jnp.int32, (16, BLK), 0)
    token = at[0] * BLK + lax.broadcasted_iota(jnp.int32, (1, BLK), 1)
    for s in range(2):
        start = jnp.maximum(token - pos[s : s + 1, :], 0)
        high = (start // 8).astype(F32)
        low = (start % 8).astype(F32)
        block = jnp.where(row == 0, high, jnp.where(row == 1, low, 0.0)).astype(BF)
        for h in range(4):
            send[s * 4 + h, 3 * HEAD : 3 * HEAD + 16, :] = block
    pair[0:256] = feed_forward(mlp_in, w_up, b_up, 0, w_down, act, slope).astype(BF)


def load_rows(recv, lo, hi):
    return jnp.concatenate([recv[i, lo:hi, :] for i in range(8)], 1)


def starts_of(recv):
    rows = load_rows(recv, 3 * HEAD, 3 * HEAD + 16).astype(F32)
    return rows[0:1] * 8.0 + rows[1:2]


def visible_of(start, c, length):
    key = lax.broadcasted_iota(jnp.int32, (length, CHUNK), 0)
    query = lax.broadcasted_iota(jnp.int32, (length, CHUNK), 1) + c * CHUNK
    return (key <= query) & (key >= start[:, c * CHUNK : (c + 1) * CHUNK])


def attend_body(recv, send, lse, ctx, start_out):
    q = load_rows(recv, 0, HEAD)
    k_t = load_rows(recv, HEAD, 2 * HEAD)
    v_t = load_rows(recv, 2 * HEAD, 3 * HEAD)
    k = k_t.astype(F32).T.astype(BF)
    start = starts_of(recv).astype(jnp.int32)
    start_out[...] = start
    for c in range(4):
        cols = slice(c * CHUNK, (c + 1) * CHUNK)
        length = (c + 1) * CHUNK
        scores = mm(k[:length], q[:, cols])
        scores = jnp.where(visible_of(start, c, length), scores, NEG)
        peak = jnp.max(scores, 0, keepdims=True)
        shifted = jnp.exp(scores - peak)
        total = jnp.sum(shifted, 0, keepdims=True)
        lse[:, cols] = peak + jnp.log(total)
        out = mm(v_t[:, :length], shifted.astype(BF)) / total
        ctx[:, cols] = out
        for i in range(CHUNK // BLK):
            block = out[:, i * BLK : (i + 1) * BLK].astype(BF)
            for t in range(2):
                send[c * (CHUNK // BLK) + i, t] = block


def attend_both_body(recv, start, _, send, dk, dv):
    q = load_rows(recv, 0, HEAD)
    k_t = load_rows(recv, HEAD, 2 * HEAD)
    v_t = load_rows(recv, 2 * HEAD, 3 * HEAD)
    d_ctx = load_rows(recv, 3 * HEAD, 4 * HEAD)
    k = k_t.astype(F32).T.astype(BF)
    v = v_t.astype(F32).T.astype(BF)
    dk[...] = jnp.zeros_like(dk)
    dv[...] = jnp.zeros_like(dv)
    for c in range(4):
        cols = slice(c * CHUNK, (c + 1) * CHUNK)
        length = (c + 1) * CHUNK
        scores = mm(k[:length], q[:, cols])
        scores = jnp.where(visible_of(start[...], c, length), scores, NEG)
        peak = jnp.max(scores, 0, keepdims=True)
        shifted = jnp.exp(scores - peak)
        probs = shifted * (1.0 / jnp.sum(shifted, 0, keepdims=True))
        probs_b = probs.astype(BF)
        out = mm(v_t[:, :length], probs_b)
        dq = backward_chunk(q, k_t, v, d_ctx, probs, probs_b, out, cols, length, dk, dv)
        for i in range(CHUNK // BLK):
            b = c * (CHUNK // BLK) + i
            for t in range(2):
                send[b, t, 0:HEAD] = out[:, i * BLK : (i + 1) * BLK].astype(BF)
                send[b, t, HEAD : 2 * HEAD] = dq[:, i * BLK : (i + 1) * BLK].astype(BF)
    put_kv(send, dk, dv, 2 * HEAD)


def backward_chunk(q, k_t, v, d_ctx, probs, probs_b, out, cols, length, dk, dv):
    d_out = d_ctx[:, cols]
    d_probs = mm(v[:length], d_out)
    delta = jnp.sum(d_out.astype(F32) * out, 0, keepdims=True)
    d_scores = (probs * (d_probs - delta)).astype(BF)
    dk[:, :length] += mm(q[:, cols], d_scores, 1, 1)
    dv[:, :length] += mm(d_out, probs_b, 1, 1)
    return mm(k_t[:, :length], d_scores) * (HEAD**-0.5)


def put_kv(send, dk, dv, row):
    for b in range(8):
        for t in range(2):
            send[b, t, row : row + HEAD] = dk[:, b * BLK : (b + 1) * BLK].astype(BF)
            send[b, t, row + HEAD : row + 2 * HEAD] = dv[:, b * BLK : (b + 1) * BLK].astype(BF)


def attend_back_body(recv, recv_d, start, lse, ctx, _, send, dk, dv):
    ride = recv_d[0, 64:192].astype(F32)
    for i in range(1, 8):
        ride = ride + recv_d[i, 64:192].astype(F32)
    ride = ride.astype(BF)
    for b in range(8):
        for t in range(2):
            send[b, t, 192:320] = ride
    q = load_rows(recv, 0, HEAD)
    k_t = load_rows(recv, HEAD, 2 * HEAD)
    v_t = load_rows(recv, 2 * HEAD, 3 * HEAD)
    d_ctx = load_rows(recv_d, 0, HEAD)
    k = k_t.astype(F32).T.astype(BF)
    v = v_t.astype(F32).T.astype(BF)
    dk[...] = jnp.zeros_like(dk)
    dv[...] = jnp.zeros_like(dv)
    for c in range(4):
        cols = slice(c * CHUNK, (c + 1) * CHUNK)
        length = (c + 1) * CHUNK
        scores = mm(k[:length], q[:, cols])
        scores = jnp.where(visible_of(start[...], c, length), scores, NEG)
        probs = jnp.exp(scores - lse[:, cols])
        probs_b = probs.astype(BF)
        dq = backward_chunk(q, k_t, v, d_ctx, probs, probs_b, ctx[:, cols], cols, length, dk, dv)
        for i in range(CHUNK // BLK):
            for t in range(2):
                send[c * (CHUNK // BLK) + i, t, 0:HEAD] = dq[:, i * BLK : (i + 1) * BLK].astype(BF)
    put_kv(send, dk, dv, HEAD)


def gather_ctx(recv, s):
    return jnp.concatenate([recv[s * 4 + h, t, 0:HEAD, :] for t in range(2) for h in range(4)], 0)


def ordered(t, own, other):
    return jnp.where(t == 0, own, other), jnp.where(t == 0, other, own)


def out_other(others):
    halves = [
        jnp.concatenate([others[3, 64 * p + 32 * c : 64 * p + 32 * (c + 1), :] for p in range(8)], 0)
        for c in range(2)
    ]
    return jnp.concatenate(halves, 1)


def branch_of(t, recv, w_own, w_other):
    first, second = ordered(t, w_own, w_other)
    w = jnp.concatenate([first, second], 0)
    rows = []
    for s in range(2):
        rows.append(mm(gather_ctx(recv, s).astype(F32).T.astype(BF), w))
    return jnp.concatenate(rows, 0)


def middle_body(
    at, x, pair, pair_other, recv, w_out_own, out_bias, gain, bias,
    w_qkv, b_qkv, w_up, b_up, w_down, w_out, cot, cs,
    stream, send, grads, parts, d_b_up, d_sum, act, slope,
):
    branch = pair[0:256].astype(F32) + pair_other[0:256].astype(F32)
    branch = branch + branch_of(at[1], recv, w_out_own[...], pair_other[256:512])
    out = x[...] + branch + out_bias[0, 0:1] + out_bias[0, 1:2]
    stream[...] = out
    normed, _ = norm_rows(out)
    attn_in = (normed * gain[1, 0:1] + bias[1, 0:1]).astype(BF)
    mlp_in = (normed * gain[1, 1:2] + bias[1, 1:2]).astype(BF)
    send_qkv(send, attn_in, w_qkv, b_qkv, 1, cs)
    g_b = cot[...].astype(BF)
    d_ctx = mm(w_out[...], g_b, 1, 1)
    for s in range(2):
        for h in range(4):
            send[s * 4 + h, 3 * HEAD : 4 * HEAD, :] = d_ctx[
                h * HEAD : (h + 1) * HEAD, s * BLK : (s + 1) * BLK
            ].astype(BF)
    d_sum[...] = jnp.sum(cot[...], 0, keepdims=True)
    parts[0:256] = feed_forward(mlp_in, w_up, b_up, 1, w_down, act, slope).astype(BF)
    parts[256:512] = feed_back(
        g_b, act, slope, mlp_in, w_up, w_down, pack_up(grads, 0), pack_down(grads, 256), d_b_up
    ).astype(BF)


def norm_back(
    t, x, g, d_mlp_in, recv, row, w_own, others, cs, gain, bias, layer, d_qkv, d_b_qkv, d_norm
):
    normed, inv = norm_rows(x)
    attn_in = (normed * gain[layer, 0:1] + bias[layer, 0:1]).astype(BF)
    attn_t = attn_in.astype(F32).T.astype(BF)
    d_attn_t = None
    for e in range(3):
        halves = []
        for tt in range(2):
            blocks = []
            for h in range(4):
                pieces = []
                for s in range(2):
                    lo = row + e * HEAD
                    u = recv[s * 4 + h, tt, lo : lo + HEAD, :]
                    if e < 2:
                        u = turn_back(u.astype(F32), cs[s, 0], cs[s, 1]).astype(BF)
                    pieces.append(u)
                blocks.append(jnp.concatenate(pieces, 1))
            halves.append(jnp.concatenate(blocks, 0))
        first, second = ordered(t, w_own[e], others[e])
        term = mm(first, halves[0]) + mm(second, halves[1])
        d_attn_t = term if d_attn_t is None else d_attn_t + term
        own = jnp.where(t == 0, halves[0], halves[1])
        d_qkv(e, mm(attn_t, own, 1, 1))
        d_b_qkv[e : e + 1] = mm(jnp.ones((8, own.shape[1]), BF), own, 1, 1)[0:1]
    d_attn_in = d_attn_t.T
    d_norm[0:1] = jnp.sum(d_attn_in * normed, 0, keepdims=True)
    d_norm[1:2] = jnp.sum(d_mlp_in * normed, 0, keepdims=True)
    d_norm[2:3] = jnp.sum(d_attn_in, 0, keepdims=True)
    d_norm[3:4] = jnp.sum(d_mlp_in, 0, keepdims=True)
    d_normed = d_attn_in * gain[layer, 0:1] + d_mlp_in * gain[layer, 1:2]
    return g + inv * (
        d_normed
        - jnp.mean(d_normed, -1, keepdims=True)
        - normed * jnp.mean(d_normed * normed, -1, keepdims=True)
    )


def turn_point_body(
    at, stream, parts, parts_other, recv, w_out, w_qkv, others, out_bias,
    gain, bias, cot, cs, x, act, slope, w_up, w_down, w_out_first, recv_first, sums_a,
    block_out, g_out, send, grads, part, d_b_up, d_b_qkv, d_norm, d_sum,
):
    t = at[1]
    branch = parts[0:256].astype(F32) + parts_other[0:256].astype(F32)
    branch = branch + branch_of(t, recv, w_out[...], out_other(others))
    block_out[...] = stream[...] + branch + out_bias[1, 0:1] + out_bias[1, 1:2]
    d_mlp_in = parts[256:512].astype(F32) + parts_other[256:512].astype(F32)
    g = norm_back(
        t, stream[...], cot[...], d_mlp_in, recv, HEAD, w_qkv, others, cs, gain, bias, 1,
        pack_qkv(grads, 0), d_b_qkv, d_norm,
    )
    g_out[...] = g
    g_b = g.astype(BF)
    d_sum[...] = jnp.sum(g, 0, keepdims=True)
    d_ctx = mm(w_out_first[...], g_b, 1, 1)
    for s in range(2):
        for h in range(4):
            send[s * 4 + h, 0:HEAD] = d_ctx[
                h * HEAD : (h + 1) * HEAD, s * BLK : (s + 1) * BLK
            ].astype(BF)
    for q in range(8):
        for c in range(2):
            send[q, 64 + 64 * c : 128 + 64 * c] = sums_a[
                64 * q : 64 * (q + 1), BLK * c : BLK * (c + 1)
            ]
    pack_out(grads, 704, own_ctx(t, recv), cot[...].astype(BF))
    pack_out(grads, 768, own_ctx(t, recv_first), g_b)
    normed, _ = norm_rows(x[...])
    mlp_in = (normed * gain[0, 1:2] + bias[0, 1:2]).astype(BF)
    part[...] = feed_back(
        g_b, act, slope, mlp_in, w_up, w_down, pack_up(grads, 192), pack_down(grads, 448), d_b_up
    ).astype(BF)


def last_body(
    at, x, g, part, part_other, recv, w_qkv, others, cs, gain, bias,
    d_b_up0, d_b_up1, d_b_qkv1, d_norm1, d_sum0, d_sum1,
    in_grad, grads, sums_a, d_b_qkv0, d_norm0,
):
    d_mlp_in = part[...].astype(F32) + part_other[...].astype(F32)
    in_grad[...] = norm_back(
        at[1], x[...], g[...], d_mlp_in, recv, 0, w_qkv, others, cs, gain, bias, 0,
        pack_qkv(grads, 0), d_b_qkv0, d_norm0,
    )
    for q in range(8):
        both_planes = recv[q, :, 192:320]
        block = jnp.where(at[1] == 0, both_planes[0], both_planes[1])
        for c in range(2):
            sums_a[64 * q : 64 * (q + 1), BLK * c : BLK * (c + 1)] = block[64 * c : 64 * (c + 1)]

    def lanes(ref, row, count):
        return [ref[row : row + 1, 256 * c : 256 * (c + 1)] for c in range(count)]

    def norms(ref):
        return [v for r in range(4) for v in lanes(ref, r, 2)]

    rows = [
        lanes(d_b_up0, 0, 4)
        + lanes(d_b_up1, 0, 4)
        + [v for e in range(3) for ref in (d_b_qkv0, d_b_qkv1) for v in lanes(ref, e, 1)],
        lanes(d_sum0, 0, 2) + lanes(d_sum1, 0, 2) + norms(d_norm0),
        norms(d_norm1),
    ]
    for p in range(8):
        have = rows[p] if p < len(rows) else []
        fill = [jnp.zeros((16 - len(have), 256), F32)]
        grads[p, 192:208, :] = jnp.concatenate(have + fill, 0).astype(BF)


def chunk_of(at, w_qkv, w_out, out):
    for layer in range(2):
        for e in range(3):
            out[layer, e] = w_qkv[layer, e, pl.ds(pl.multiple_of(at[2] * 64, 64), 64), :]
        rows = w_out[layer, pl.ds(pl.multiple_of(at[2] * 32, 32), 32), :]
        out[layer, 3, 0:32] = rows[:, 0:256]
        out[layer, 3, 32:64] = rows[:, 256:512]


def mix_body(got, early, out):
    total = got[0].astype(F32)
    for i in range(1, 8):
        total = total + got[i].astype(F32)
    for q in range(8):
        mine = [early[104 * q : 104 * (q + 1)].astype(F32), total[24 * q : 24 * (q + 1)]]
        out[q, 0:128] = jnp.concatenate(mine, 0).astype(BF)
        out[q, 128:144] = total[192:208].astype(BF) if q == 0 else jnp.zeros((16, 256), BF)


def sum_body(got, out):
    total = got[0].astype(F32)
    for i in range(1, 8):
        total = total + got[i].astype(F32)
    out[...] = total.astype(BF)


def unpack_first_body(first, g_up, g_down):
    for c in range(4):
        g_up[0, :, 256 * c : 256 * (c + 1)] = first[64 * c : 64 * (c + 1)].astype(F32)
    for c in range(2):
        rows = first[256 + 128 * c : 256 + 128 * (c + 1)]
        g_down[0, :, 256 * c : 256 * (c + 1)] = rows.astype(F32)


def unpack_rest_body(rest, _, __, g_up, g_down, g_qkv, g_out, g_b_up, g_b_qkv, g_sum, g_gain, g_bias):
    p = pl.program_id(0)

    def early(row):
        return rest[row // 104, row % 104 : row % 104 + 8].astype(F32)

    def late(row):
        return rest[row // 24, 104 + row % 24 : 104 + row % 24 + 8].astype(F32)

    for k in range(0, 64, 8):
        for e in range(3):
            g_qkv[0, e, k : k + 8] = late(64 * e + k)
            g_qkv[1, e, k : k + 8] = early(64 * e + k)
        for c in range(4):
            g_up[0, k : k + 8, 256 * c : 256 * (c + 1)] = early(192 + 64 * c + k)
    for k in range(0, 32, 8):
        for c in range(2):
            g_out[0, k : k + 8, 256 * c : 256 * (c + 1)] = early(768 + 32 * c + k)
            g_out[1, k : k + 8, 256 * c : 256 * (c + 1)] = early(704 + 32 * c + k)
    for k in range(0, 128, 8):
        for c in range(2):
            g_down[0, k : k + 8, 256 * c : 256 * (c + 1)] = early(448 + 128 * c + k)

    tiny = rest[0, 128:144].astype(F32)

    @pl.when(p == 0)
    def _():
        for layer in range(2):
            for c in range(4):
                r = 4 * layer + c
                g_b_up[layer : layer + 1, 256 * c : 256 * (c + 1)] = tiny[r : r + 1]
        for e in range(3):
            for layer in range(2):
                r = 8 + 2 * e + layer
                g_b_qkv[e, layer : layer + 1, :] = tiny[r : r + 1]

    def norms(layer, base):
        for which in range(2):
            for c in range(2):
                cols = slice(256 * c, 256 * (c + 1))
                r = base + 2 * which + c
                g_gain[layer, which : which + 1, cols] = tiny[r : r + 1]
                g_bias[layer, which : which + 1, cols] = tiny[r + 4 : r + 5]

    @pl.when(p == 1)
    def _():
        for layer in range(2):
            for c in range(2):
                r = 2 * layer + c
                for which in range(2):
                    g_sum[layer, which : which + 1, 256 * c : 256 * (c + 1)] = tiny[r : r + 1]
        norms(0, 4)

    @pl.when(p == 2)
    def _():
        norms(1, 0)


UP = (2, 512, 1024)
DOWN = (2, 1024, 512)


def unpack(first, rest):
    def place(layer):
        return [
            pl.BlockSpec((1, 64, 1024), lambda p: (layer, p, 0)),
            pl.BlockSpec((1, 128, 512), lambda p: (layer, p, 0)),
        ]

    params = pltpu.CompilerParams(vmem_limit_bytes=56 * 1024 * 1024)
    g_up, g_down = pl.pallas_call(
        unpack_first_body,
        grid=(8,),
        out_shape=[jax.ShapeDtypeStruct(UP, F32), jax.ShapeDtypeStruct(DOWN, F32)],
        in_specs=[pl.BlockSpec((None, 512, 256), lambda p: (p, 0, 0))],
        out_specs=place(1),
        compiler_params=params,
        name="unpack_first",
    )(first)
    outs = [
        ((2, 3, 512, 256), pl.BlockSpec((2, 3, 64, 256), lambda p: (0, 0, p, 0))),
        ((2, 256, 512), pl.BlockSpec((2, 32, 512), lambda p: (0, p, 0))),
        ((2, 1024), whole((2, 1024))),
        ((3, 2, 256), whole((3, 2, 256))),
        ((2, 2, 512), whole((2, 2, 512))),
        ((2, 2, 512), whole((2, 2, 512))),
        ((2, 2, 512), whole((2, 2, 512))),
    ]
    return pl.pallas_call(
        unpack_rest_body,
        grid=(8,),
        out_shape=[jax.ShapeDtypeStruct(shape, F32) for shape in [UP, DOWN] + [o[0] for o in outs]],
        in_specs=[
            pl.BlockSpec((None, 8, 144, 256), lambda p: (p, 0, 0, 0)),
            pl.BlockSpec(memory_space=pl.ANY),
            pl.BlockSpec(memory_space=pl.ANY),
        ],
        out_specs=place(0) + [spec for _, spec in outs],
        input_output_aliases={1: 0, 2: 1},
        compiler_params=params,
        name="unpack_rest",
    )(rest, g_up, g_down)


def swap(value):
    return lax.ppermute(value, "tensor", [(0, 1), (1, 0)])


def exchange(value, axes):
    return lax.all_to_all(value, axes, 0, 0)


def both(value):
    flat = value.reshape((16,) + value.shape[2:])
    return exchange(flat, ("context", "tensor")).reshape(value.shape)


def shards(
    tokens_in, cotangent, positions, w_qkv, b_qkv, w_out, w_up, b_up, w_down, out_bias, ln_gain, ln_bias
):
    rows, width = 256, 512
    x = tokens_in.reshape(rows, width)
    cot = cotangent.reshape(rows, width)
    wq = jnp.transpose(w_qkv, (0, 2, 1, 3))
    bq = jnp.transpose(b_qkv, (1, 0, 2))
    at = jnp.stack(
        [lax.axis_index("context"), lax.axis_index("tensor"), lax.axis_index("dp")]
    ).astype(jnp.int32)
    freqs = jnp.asarray(FREQS).reshape(HALF, 1)
    send, pair, act, slope, cs, chunk = call(
        first_body,
        [
            ((8, 208, BLK), BF),
            ((2 * rows, width), BF),
            ((rows, 1024), BF),
            ((rows, 1024), F32),
            ((2, 2, HALF, BLK), F32),
            ((2, 4, 64, 256), BF),
        ],
        (
            at, positions, freqs, x, ln_gain, ln_bias, wq, bq, Layer(w_up, 0), b_up,
            Layer(w_down, 0), w_out,
        ),
        "norm_qkv_feed",
        smem_first=True,
    )
    pair_other = swap(pair)
    others = lax.all_gather(swap(chunk), "dp", axis=2, tiled=True)
    recv = exchange(send, "context")
    ctx_send, lse, ctx, start = call(
        attend_body,
        [((8, 2, HEAD, BLK), BF), ((1, 1024), F32), ((HEAD, 1024), F32), ((1, 1024), jnp.int32)],
        (recv,),
        "attend",
    )
    recv_ctx = both(ctx_send)
    stream, send, grads_a, parts, d_b_up1, d_sum1 = call(
        middle_body,
        [
            ((rows, width), F32),
            ((8, 256, BLK), BF),
            ((8, 512, 256), BF),
            ((2 * rows, width), BF),
            ((1, 1024), F32),
            ((1, width), F32),
        ],
        (
            at, x, pair, pair_other, recv_ctx, Layer(w_out, 0), out_bias, ln_gain, ln_bias,
            Layer(wq, 1), bq, Layer(w_up, 1), b_up, Layer(w_down, 1), Layer(w_out, 1), cot, cs,
        ),
        "middle",
        scratch=[pltpu.VMEM((rows, 1024), BF), pltpu.VMEM((rows, 1024), F32)],
        smem_first=True,
    )
    sums_a = lax.psum_scatter(grads_a, "dp", scatter_dimension=0)
    parts_other = swap(parts)
    recv_both = exchange(send, "context")
    (both_send,) = call(
        attend_both_body,
        [((8, 2, 256, BLK), BF)],
        (recv_both, start, After(parts_other)),
        "attend_both",
        scratch=[pltpu.VMEM((HEAD, 1024), F32), pltpu.VMEM((HEAD, 1024), F32)],
    )
    recv_grad = both(both_send)
    block_out, g, send, grads_b, part_g, d_b_up0, d_b_qkv1, d_norm1, d_sum0 = call(
        turn_point_body,
        [
            ((rows, width), F32),
            ((rows, width), F32),
            ((8, 192, BLK), BF),
            ((8, 832, 256), BF),
            ((rows, width), BF),
            ((1, 1024), F32),
            ((3, 256), F32),
            ((4, width), F32),
            ((1, width), F32),
        ],
        (
            at, stream, parts, parts_other, recv_grad, Layer(w_out, 1), Layer(wq, 1), Layer(others, 1),
            out_bias, ln_gain, ln_bias, cot, cs, x, act, slope, Layer(w_up, 0), Layer(w_down, 0),
            Layer(w_out, 0), recv_ctx, sums_a,
        ),
        "turn_point",
        smem_first=True,
    )
    sums_b = lax.psum_scatter(grads_b, "dp", scatter_dimension=0)
    part_g_other = swap(part_g)
    recv_d = exchange(send, "context")
    (back_send,) = call(
        attend_back_body,
        [((8, 2, 320, BLK), BF)],
        (recv, recv_d, start, lse, ctx, After(part_g_other)),
        "attend_back",
        scratch=[pltpu.VMEM((HEAD, 1024), F32), pltpu.VMEM((HEAD, 1024), F32)],
    )
    recv_grad0 = both(back_send)
    in_grad, grads_c, sums_a, _, _ = call(
        last_body,
        [
            ((rows, width), F32),
            ((8, 208, 256), BF),
            ((512, 256), BF),
            ((3, 256), F32),
            ((4, width), F32),
        ],
        (
            at, x, g, part_g, part_g_other, recv_grad0, Layer(wq, 0), Layer(others, 0), cs,
            ln_gain, ln_bias, d_b_up0, d_b_up1, d_b_qkv1, d_norm1, d_sum0, d_sum1,
        ),
        "last",
        smem_first=True,
    )
    full_a = lax.all_gather(sums_a, "dp")
    (mixed,) = call(mix_body, [((8, 144, 256), BF)], (exchange(grads_c, "dp"), sums_b), "mix")
    (summed,) = call(sum_body, [((144, 256), BF)], (exchange(mixed, "context"),), "sum")
    summed = exchange(jnp.broadcast_to(summed[None], (8, 144, 256)), "context")
    full_bc = lax.all_gather(summed, "dp")
    g_up, g_down, g_qkv, g_out, g_b_up, g_b_qkv, g_sum, g_gain, g_bias = unpack(full_a, full_bc)
    return (
        block_out.reshape(tokens_in.shape),
        in_grad.reshape(tokens_in.shape),
        jnp.transpose(g_qkv, (0, 2, 1, 3)),
        jnp.transpose(g_b_qkv, (1, 0, 2)),
        g_out,
        g_up,
        g_b_up,
        g_down,
        g_sum,
        g_gain,
        g_bias,
    )


def solution(mesh):
    return jax.shard_map(
        shards,
        mesh=mesh,
        in_specs=(
            P("dp", "context", None),
            P("dp", "context", None),
            P("dp", "context"),
            P(None, None, None, "tensor"),
            P(None, None, "tensor"),
            P(None, "tensor", None),
            P(None, None, "tensor"),
            P(None, "tensor"),
            P(None, "tensor", None),
            P(),
            P(),
            P(),
        ),
        out_specs=(
            P("dp", "context", None),
            P("dp", "context", None),
            P(None, None, None, "tensor"),
            P(None, None, "tensor"),
            P(None, "tensor", None),
            P(None, None, "tensor"),
            P(None, "tensor"),
            P(None, "tensor", None),
            P(),
            P(),
            P(),
        ),
        check_vma=False,
    )
```

```python
from functools import partial

import numpy as np

import jax
import jax.numpy as jnp
from jax import lax
from jax.experimental import pallas as pl
from jax.experimental.pallas import tpu as pltpu
from jax.sharding import PartitionSpec as P

EPS = 1e-05
HALF = 8
HEAD = 64
BLK = 128
CHUNK = 256
NEG = -1e30
BF = jnp.bfloat16
F32 = jnp.float32

FREQS = (10000.0 ** (-np.arange(HALF, dtype=np.float64) * 2.0 / 16.0)).astype(np.float32)


def mm(a, b, ca=1, cb=0):
    return lax.dot_general(a, b, (((ca,), (cb,)), ((), ())), preferred_element_type=F32)


class After:
    def __init__(self, array):
        self.array = array

    def spec(self):
        return pl.BlockSpec(memory_space=pl.ANY)


class Rows:
    def __init__(self, array, rows, at=0):
        self.array, self.rows, self.at = array, rows, at

    def spec(self):
        shape = self.array.shape
        place = (0,) * (len(shape) - 2) + (self.at, 0)
        return pl.BlockSpec(shape[:-2] + (self.rows, shape[-1]), lambda i: place)


class Layer:
    def __init__(self, array, index):
        self.array, self.index = array, index

    def spec(self):
        rest = self.array.shape[1:]
        place = (self.index,) + (0,) * len(rest)
        return pl.BlockSpec((None,) + rest, lambda i: place)


def whole(shape):
    return pl.BlockSpec(shape, lambda i: (0,) * len(shape))


def call(body, out_shape, args, name, scratch=(), smem_first=False):
    specs = [
        a.spec() if isinstance(a, (Layer, Rows, After)) else whole(a.shape) for a in args
    ]
    args = [a.array if isinstance(a, (Layer, Rows, After)) else a for a in args]
    if smem_first:
        specs[0] = pl.BlockSpec(memory_space=pltpu.SMEM)
    return pl.pallas_call(
        body,
        grid=(1,),
        out_shape=[jax.ShapeDtypeStruct(s, d) for s, d in out_shape],
        in_specs=specs,
        out_specs=[whole(s) for s, _ in out_shape],
        scratch_shapes=list(scratch),
        compiler_params=pltpu.CompilerParams(vmem_limit_bytes=56 * 1024 * 1024),
        name=name,
    )(*args)


def norm_rows(x):
    mean = jnp.mean(x, -1, keepdims=True)
    cen = x - mean
    inv = lax.rsqrt(jnp.mean(cen * cen, -1, keepdims=True) + EPS)
    return cen * inv, inv


def turn(t, cos, sin):
    a, b = t[:HALF], t[HALF : 2 * HALF]
    return jnp.concatenate([a * cos - b * sin, b * cos + a * sin, t[2 * HALF :]], 0)


def turn_back(u, cos, sin):
    a, b = u[:HALF], u[HALF : 2 * HALF]
    return jnp.concatenate([a * cos + b * sin, b * cos - a * sin, u[2 * HALF :]], 0)


def send_qkv(send, attn_in, w_qkv, b_qkv, layer, cs):
    for e in range(3):
        turned = (mm(attn_in, w_qkv[e]) + b_qkv[e, layer : layer + 1]).T
        for s in range(2):
            cos, sin = cs[s, 0], cs[s, 1]
            for h in range(4):
                j = s * 4 + h
                part = turned[h * HEAD : (h + 1) * HEAD, s * BLK : (s + 1) * BLK]
                if e < 2:
                    part = turn(part, cos, sin)
                if e == 0:
                    part = part * (HEAD**-0.5)
                send[j, e * HEAD : (e + 1) * HEAD, :] = part.astype(BF)


def feed_forward(mlp_in, w_up, b_up, layer, w_down, act, slope):
    width = w_up.shape[1]
    total = None
    for c in range(0, width, 256):
        cols = slice(c, c + 256)
        pre = mm(mlp_in, w_up[:, cols]) + b_up[layer : layer + 1, cols]
        cdf = 0.5 + 0.5 * lax.erf(pre * np.float32(0.7071067811865476))
        a = (pre * cdf).astype(BF)
        act[:, cols] = a
        slope[:, cols] = cdf + pre * (jnp.exp(-0.5 * pre * pre) * np.float32(0.3989422804014327))
        term = mm(a, w_down[cols, :])
        total = term if total is None else total + term
    return total


def feed_back(g_b, act, slope, mlp_in, w_up, w_down, d_up, d_down, d_b_up):
    width = w_up.shape[1]
    total = None
    mlp_t = mlp_in.astype(F32).T.astype(BF)
    for c in range(0, width, 256):
        cols = slice(c, c + 256)
        d_act = mm(g_b, w_down[cols, :], 1, 1)
        d_pre = d_act * slope[:, cols]
        d_pre_b = d_pre.astype(BF)
        d_b_up[:, cols] = jnp.sum(d_pre_b.astype(F32), 0, keepdims=True)
        d_up(c // 256, mm(mlp_t, d_pre_b))
        d_down(c, mm(act[:, cols].astype(F32).T.astype(BF), g_b))
        term = mm(d_pre_b, w_up[:, cols], 1, 1)
        total = term if total is None else total + term
    return total


def pack_up(out, row):
    def put(c, value):
        for p in range(8):
            out[p, row + 64 * c : row + 64 * (c + 1), :] = value[64 * p : 64 * (p + 1)].astype(BF)

    return put


def pack_down(out, row):
    def put(c, value):
        for half in range(2):
            for k in range(2):
                out[c // 128 + k, row + 128 * half : row + 128 * (half + 1), :] = value[
                    128 * k : 128 * (k + 1), 256 * half : 256 * (half + 1)
                ].astype(BF)

    return put


def pack_qkv(out, row):
    def put(e, value):
        for p in range(8):
            out[p, row + 64 * e : row + 64 * (e + 1), :] = value[64 * p : 64 * (p + 1)].astype(BF)

    return put


def own_ctx(t, recv):
    full = jnp.concatenate([gather_ctx(recv, s) for s in range(2)], 1)
    return jnp.where(t == 0, full[0:256], full[256:512])


def pack_out(out, row, ctx, upstream):
    value = mm(ctx, upstream)
    for p in range(8):
        for half in range(2):
            out[p, row + 32 * half : row + 32 * (half + 1), :] = value[
                32 * p : 32 * (p + 1), 256 * half : 256 * (half + 1)
            ].astype(BF)


def first_body(
    at, pos, freqs, x, gain, bias, w_qkv, b_qkv, w_up, b_up, w_down, w_out,
    send, pair, act, slope, cs,
):
    pair[256:512] = w_out[...]
    for s in range(2):
        p = pos[s : s + 1, :].astype(F32)
        angle = freqs[...] * p
        cs[s, 0] = jnp.cos(angle)
        cs[s, 1] = jnp.sin(angle)
    normed, _ = norm_rows(x[...])
    attn_in = (normed * gain[0, 0:1] + bias[0, 0:1]).astype(BF)
    mlp_in = (normed * gain[0, 1:2] + bias[0, 1:2]).astype(BF)
    send_qkv(send, attn_in, w_qkv, b_qkv, 0, cs)
    row = lax.broadcasted_iota(jnp.int32, (16, BLK), 0)
    token = at[0] * BLK + lax.broadcasted_iota(jnp.int32, (1, BLK), 1)
    for s in range(2):
        start = jnp.maximum(token - pos[s : s + 1, :], 0)
        high = (start // 8).astype(F32)
        low = (start % 8).astype(F32)
        block = jnp.where(row == 0, high, jnp.where(row == 1, low, 0.0)).astype(BF)
        for h in range(4):
            send[s * 4 + h, 3 * HEAD : 3 * HEAD + 16, :] = block
    pair[0:256] = feed_forward(mlp_in, w_up, b_up, 0, w_down, act, slope).astype(BF)


def load_rows(recv, lo, hi):
    return jnp.concatenate([recv[i, lo:hi, :] for i in range(8)], 1)


def starts_of(recv):
    rows = load_rows(recv, 3 * HEAD, 3 * HEAD + 16).astype(F32)
    return rows[0:1] * 8.0 + rows[1:2]


def visible_of(start, c, length):
    key = lax.broadcasted_iota(jnp.int32, (length, CHUNK), 0)
    query = lax.broadcasted_iota(jnp.int32, (length, CHUNK), 1) + c * CHUNK
    return (key <= query) & (key >= start[:, c * CHUNK : (c + 1) * CHUNK])


def attend_body(at, recv, w_qkv, w_out, send, lse, ctx, start_out):
    for layer in range(2):
        piece = jnp.where(at[2] // 2 == 3, w_out[layer], w_qkv[layer, 0])
        for b in range(8):
            for t in range(2):
                for half in range(2):
                    row = 64 + 64 * layer + 32 * half
                    send[b, t, row : row + 32] = piece[:, BLK * half : BLK * (half + 1)]
    q = load_rows(recv, 0, HEAD)
    k_t = load_rows(recv, HEAD, 2 * HEAD)
    v_t = load_rows(recv, 2 * HEAD, 3 * HEAD)
    k = k_t.astype(F32).T.astype(BF)
    start = starts_of(recv).astype(jnp.int32)
    start_out[...] = start
    for c in range(4):
        cols = slice(c * CHUNK, (c + 1) * CHUNK)
        length = (c + 1) * CHUNK
        scores = mm(k[:length], q[:, cols])
        scores = jnp.where(visible_of(start, c, length), scores, NEG)
        peak = jnp.max(scores, 0, keepdims=True)
        shifted = jnp.exp(scores - peak)
        total = jnp.sum(shifted, 0, keepdims=True)
        lse[:, cols] = peak + jnp.log(total)
        out = mm(v_t[:, :length], shifted.astype(BF)) / total
        ctx[:, cols] = out
        for i in range(CHUNK // BLK):
            block = out[:, i * BLK : (i + 1) * BLK].astype(BF)
            for t in range(2):
                send[c * (CHUNK // BLK) + i, t, 0:HEAD] = block


def attend_both_body(at, recv, start, pieces, _, send, piece, dk, dv):
    for b in range(8):
        piece[b] = jnp.where(at[1] == 0, pieces[b, 1], pieces[b, 0])
    q = load_rows(recv, 0, HEAD)
    k_t = load_rows(recv, HEAD, 2 * HEAD)
    v_t = load_rows(recv, 2 * HEAD, 3 * HEAD)
    d_ctx = load_rows(recv, 3 * HEAD, 4 * HEAD)
    k = k_t.astype(F32).T.astype(BF)
    v = v_t.astype(F32).T.astype(BF)
    dk[...] = jnp.zeros_like(dk)
    dv[...] = jnp.zeros_like(dv)
    for c in range(4):
        cols = slice(c * CHUNK, (c + 1) * CHUNK)
        length = (c + 1) * CHUNK
        scores = mm(k[:length], q[:, cols])
        scores = jnp.where(visible_of(start[...], c, length), scores, NEG)
        peak = jnp.max(scores, 0, keepdims=True)
        shifted = jnp.exp(scores - peak)
        probs = shifted * (1.0 / jnp.sum(shifted, 0, keepdims=True))
        probs_b = probs.astype(BF)
        out = mm(v_t[:, :length], probs_b)
        dq = backward_chunk(q, k_t, v, d_ctx, probs, probs_b, out, cols, length, dk, dv)
        for i in range(CHUNK // BLK):
            b = c * (CHUNK // BLK) + i
            for t in range(2):
                send[b, t, 0:HEAD] = out[:, i * BLK : (i + 1) * BLK].astype(BF)
                send[b, t, HEAD : 2 * HEAD] = dq[:, i * BLK : (i + 1) * BLK].astype(BF)
    put_kv(send, dk, dv, 2 * HEAD)


def backward_chunk(q, k_t, v, d_ctx, probs, probs_b, out, cols, length, dk, dv):
    d_out = d_ctx[:, cols]
    d_probs = mm(v[:length], d_out)
    delta = jnp.sum(d_out.astype(F32) * out, 0, keepdims=True)
    d_scores = (probs * (d_probs - delta)).astype(BF)
    dk[:, :length] += mm(q[:, cols], d_scores, 1, 1)
    dv[:, :length] += mm(d_out, probs_b, 1, 1)
    return mm(k_t[:, :length], d_scores) * (HEAD**-0.5)


def put_kv(send, dk, dv, row):
    for b in range(8):
        for t in range(2):
            send[b, t, row : row + HEAD] = dk[:, b * BLK : (b + 1) * BLK].astype(BF)
            send[b, t, row + HEAD : row + 2 * HEAD] = dv[:, b * BLK : (b + 1) * BLK].astype(BF)


def attend_back_body(recv, recv_d, start, lse, ctx, _, send, dk, dv):
    ride = recv_d[0, 64:192].astype(F32)
    for i in range(1, 8):
        ride = ride + recv_d[i, 64:192].astype(F32)
    ride = ride.astype(BF)
    for b in range(8):
        for t in range(2):
            send[b, t, 192:320] = ride
    q = load_rows(recv, 0, HEAD)
    k_t = load_rows(recv, HEAD, 2 * HEAD)
    v_t = load_rows(recv, 2 * HEAD, 3 * HEAD)
    d_ctx = load_rows(recv_d, 0, HEAD)
    k = k_t.astype(F32).T.astype(BF)
    v = v_t.astype(F32).T.astype(BF)
    dk[...] = jnp.zeros_like(dk)
    dv[...] = jnp.zeros_like(dv)
    for c in range(4):
        cols = slice(c * CHUNK, (c + 1) * CHUNK)
        length = (c + 1) * CHUNK
        scores = mm(k[:length], q[:, cols])
        scores = jnp.where(visible_of(start[...], c, length), scores, NEG)
        probs = jnp.exp(scores - lse[:, cols])
        probs_b = probs.astype(BF)
        dq = backward_chunk(q, k_t, v, d_ctx, probs, probs_b, ctx[:, cols], cols, length, dk, dv)
        for i in range(CHUNK // BLK):
            for t in range(2):
                send[c * (CHUNK // BLK) + i, t, 0:HEAD] = dq[:, i * BLK : (i + 1) * BLK].astype(BF)
    put_kv(send, dk, dv, HEAD)


def gather_ctx(recv, s):
    return jnp.concatenate([recv[s * 4 + h, t, 0:HEAD, :] for t in range(2) for h in range(4)], 0)


def ordered(t, own, other):
    return jnp.where(t == 0, own, other), jnp.where(t == 0, other, own)


def other_matrix(others, m):
    rows = []
    for d in (2 * m, 2 * m + 1):
        for c in range(8):
            rows.append(jnp.concatenate([others[d, c, 0:32, :], others[d, c, 32:64, :]], 1))
    return jnp.concatenate(rows, 0)


def out_other(others):
    stacked = other_matrix(others, 3)
    return jnp.concatenate([stacked[0:256], stacked[256:512]], 1)


def branch_of(t, recv, w_own, w_other):
    first, second = ordered(t, w_own, w_other)
    w = jnp.concatenate([first, second], 0)
    rows = []
    for s in range(2):
        rows.append(mm(gather_ctx(recv, s).astype(F32).T.astype(BF), w))
    return jnp.concatenate(rows, 0)


def middle_body(
    at, x, pair, pair_other, recv, w_out_own, out_bias, gain, bias,
    w_qkv, b_qkv, w_up, b_up, w_down, w_out, cot, cs,
    stream, send, grads, parts, d_b_up, d_sum, act, slope,
):
    branch = pair[0:256].astype(F32) + pair_other[0:256].astype(F32)
    branch = branch + branch_of(at[1], recv, w_out_own[...], pair_other[256:512])
    out = x[...] + branch + out_bias[0, 0:1] + out_bias[0, 1:2]
    stream[...] = out
    normed, _ = norm_rows(out)
    attn_in = (normed * gain[1, 0:1] + bias[1, 0:1]).astype(BF)
    mlp_in = (normed * gain[1, 1:2] + bias[1, 1:2]).astype(BF)
    send_qkv(send, attn_in, w_qkv, b_qkv, 1, cs)
    g_b = cot[...].astype(BF)
    d_ctx = mm(w_out[...], g_b, 1, 1)
    for s in range(2):
        for h in range(4):
            send[s * 4 + h, 3 * HEAD : 4 * HEAD, :] = d_ctx[
                h * HEAD : (h + 1) * HEAD, s * BLK : (s + 1) * BLK
            ].astype(BF)
    d_sum[...] = jnp.sum(cot[...], 0, keepdims=True)
    parts[0:256] = feed_forward(mlp_in, w_up, b_up, 1, w_down, act, slope).astype(BF)
    parts[256:512] = feed_back(
        g_b, act, slope, mlp_in, w_up, w_down, pack_up(grads, 0), pack_down(grads, 256), d_b_up
    ).astype(BF)


def norm_back(
    t, x, g, d_mlp_in, recv, row, w_own, others, cs, gain, bias, layer, d_qkv, d_b_qkv, d_norm
):
    normed, inv = norm_rows(x)
    attn_in = (normed * gain[layer, 0:1] + bias[layer, 0:1]).astype(BF)
    attn_t = attn_in.astype(F32).T.astype(BF)
    d_attn_t = None
    for e in range(3):
        halves = []
        for tt in range(2):
            blocks = []
            for h in range(4):
                pieces = []
                for s in range(2):
                    lo = row + e * HEAD
                    u = recv[s * 4 + h, tt, lo : lo + HEAD, :]
                    if e < 2:
                        u = turn_back(u.astype(F32), cs[s, 0], cs[s, 1]).astype(BF)
                    pieces.append(u)
                blocks.append(jnp.concatenate(pieces, 1))
            halves.append(jnp.concatenate(blocks, 0))
        first, second = ordered(t, w_own[e], other_matrix(others, e))
        term = mm(first, halves[0]) + mm(second, halves[1])
        d_attn_t = term if d_attn_t is None else d_attn_t + term
        own = jnp.where(t == 0, halves[0], halves[1])
        d_qkv(e, mm(attn_t, own, 1, 1))
        d_b_qkv[e : e + 1] = mm(jnp.ones((8, own.shape[1]), BF), own, 1, 1)[0:1]
    d_attn_in = d_attn_t.T
    d_norm[0:1] = jnp.sum(d_attn_in * normed, 0, keepdims=True)
    d_norm[1:2] = jnp.sum(d_mlp_in * normed, 0, keepdims=True)
    d_norm[2:3] = jnp.sum(d_attn_in, 0, keepdims=True)
    d_norm[3:4] = jnp.sum(d_mlp_in, 0, keepdims=True)
    d_normed = d_attn_in * gain[layer, 0:1] + d_mlp_in * gain[layer, 1:2]
    return g + inv * (
        d_normed
        - jnp.mean(d_normed, -1, keepdims=True)
        - normed * jnp.mean(d_normed * normed, -1, keepdims=True)
    )


def turn_point_body(
    at, stream, parts, parts_other, recv, w_out, w_qkv, others, out_bias,
    gain, bias, cot, cs, x, act, slope, w_up, w_down, w_out_first, recv_first, sums_a,
    block_out, g_out, send, grads, part, d_b_up, d_b_qkv, d_norm, d_sum,
):
    t = at[1]
    branch = parts[0:256].astype(F32) + parts_other[0:256].astype(F32)
    branch = branch + branch_of(t, recv, w_out[...], out_other(others))
    block_out[...] = stream[...] + branch + out_bias[1, 0:1] + out_bias[1, 1:2]
    d_mlp_in = parts[256:512].astype(F32) + parts_other[256:512].astype(F32)
    g = norm_back(
        t, stream[...], cot[...], d_mlp_in, recv, HEAD, w_qkv, others, cs, gain, bias, 1,
        pack_qkv(grads, 0), d_b_qkv, d_norm,
    )
    g_out[...] = g
    g_b = g.astype(BF)
    d_sum[...] = jnp.sum(g, 0, keepdims=True)
    d_ctx = mm(w_out_first[...], g_b, 1, 1)
    for s in range(2):
        for h in range(4):
            send[s * 4 + h, 0:HEAD] = d_ctx[
                h * HEAD : (h + 1) * HEAD, s * BLK : (s + 1) * BLK
            ].astype(BF)
    for q in range(8):
        for c in range(2):
            send[q, 64 + 64 * c : 128 + 64 * c] = sums_a[
                64 * q : 64 * (q + 1), BLK * c : BLK * (c + 1)
            ]
    pack_out(grads, 704, own_ctx(t, recv), cot[...].astype(BF))
    pack_out(grads, 768, own_ctx(t, recv_first), g_b)
    normed, _ = norm_rows(x[...])
    mlp_in = (normed * gain[0, 1:2] + bias[0, 1:2]).astype(BF)
    part[...] = feed_back(
        g_b, act, slope, mlp_in, w_up, w_down, pack_up(grads, 192), pack_down(grads, 448), d_b_up
    ).astype(BF)


def last_body(
    at, x, g, part, part_other, recv, w_qkv, others, cs, gain, bias,
    d_b_up0, d_b_up1, d_b_qkv1, d_norm1, d_sum0, d_sum1, sums_b,
    in_grad, grads, sums_a, d_b_qkv0, d_norm0,
):
    d_mlp_in = part[...].astype(F32) + part_other[...].astype(F32)
    in_grad[...] = norm_back(
        at[1], x[...], g[...], d_mlp_in, recv, 0, w_qkv, others, cs, gain, bias, 0,
        pack_qkv(grads, 0), d_b_qkv0, d_norm0,
    )
    for q in range(8):
        both_planes = recv[q, :, 192:320]
        block = jnp.where(at[1] == 0, both_planes[0], both_planes[1])
        for c in range(2):
            sums_a[64 * q : 64 * (q + 1), BLK * c : BLK * (c + 1)] = block[64 * c : 64 * (c + 1)]

    def lanes(ref, row, count):
        return [ref[row : row + 1, 256 * c : 256 * (c + 1)] for c in range(count)]

    def norms(ref):
        return [v for r in range(4) for v in lanes(ref, r, 2)]

    rows = [
        lanes(d_b_up0, 0, 4)
        + lanes(d_b_up1, 0, 4)
        + [v for e in range(3) for ref in (d_b_qkv0, d_b_qkv1) for v in lanes(ref, e, 1)],
        lanes(d_sum0, 0, 2) + lanes(d_sum1, 0, 2) + norms(d_norm0),
        norms(d_norm1),
    ]
    for p in range(8):
        have = rows[p] if p < len(rows) else []
        fill = [jnp.zeros((16 - len(have), 256), F32)]
        grads[p, 192:208, :] = jnp.concatenate(have + fill, 0).astype(BF)
        rows_b = sums_b[104 * p : 104 * (p + 1)].astype(F32)
        grads[p, 208:320, :] = jnp.concatenate([rows_b, jnp.zeros((8, 256), F32)], 0).astype(BF)


def sum_of(got):
    total = got[0].astype(F32)
    for i in range(1, 8):
        total = total + got[i].astype(F32)
    return total.astype(BF)


def sum_both_body(got, late, early):
    total = sum_of(got)
    for q in range(8):
        late[q] = total[0:208]
        early[q] = total[208:320]


def sum_body(got, late):
    total = sum_of(got)
    for q in range(8):
        late[q] = total


def unpack_first_body(first, g_up, g_down):
    for c in range(4):
        g_up[0, :, 256 * c : 256 * (c + 1)] = first[64 * c : 64 * (c + 1)].astype(F32)
    for c in range(2):
        rows = first[256 + 128 * c : 256 + 128 * (c + 1)]
        g_down[0, :, 256 * c : 256 * (c + 1)] = rows.astype(F32)


def unpack_rest_body(
    rest, last, _, __, g_up, g_down, g_qkv, g_out, g_b_up, g_b_qkv, g_sum, g_gain, g_bias
):
    p = pl.program_id(0)
    for e in range(3):
        g_qkv[0, e] = last[64 * e : 64 * (e + 1)].astype(F32)
    for q in range(8):
        block = rest[q, 0:104].astype(F32)
        for i in range(13):
            row = 104 * q + 8 * i
            value = block[8 * i : 8 * (i + 1)]
            if row < 192:
                g_qkv[1, row // 64, row % 64 : row % 64 + 8] = value
            elif row < 448:
                c, r = divmod(row - 192, 64)
                g_up[0, r : r + 8, 256 * c : 256 * (c + 1)] = value
            elif row < 704:
                c, r = divmod(row - 448, 128)
                g_down[0, r : r + 8, 256 * c : 256 * (c + 1)] = value
            else:
                c, r = divmod((row - 704) % 64, 32)
                g_out[1 - (row - 704) // 64, r : r + 8, 256 * c : 256 * (c + 1)] = value

    tiny = last[192:208].astype(F32)

    @pl.when(p == 0)
    def _():
        for layer in range(2):
            for c in range(4):
                r = 4 * layer + c
                g_b_up[layer : layer + 1, 256 * c : 256 * (c + 1)] = tiny[r : r + 1]
        for e in range(3):
            for layer in range(2):
                r = 8 + 2 * e + layer
                g_b_qkv[e, layer : layer + 1, :] = tiny[r : r + 1]

    def norms(layer, base):
        for which in range(2):
            for c in range(2):
                cols = slice(256 * c, 256 * (c + 1))
                r = base + 2 * which + c
                g_gain[layer, which : which + 1, cols] = tiny[r : r + 1]
                g_bias[layer, which : which + 1, cols] = tiny[r + 4 : r + 5]

    @pl.when(p == 1)
    def _():
        for layer in range(2):
            for c in range(2):
                r = 2 * layer + c
                for which in range(2):
                    g_sum[layer, which : which + 1, 256 * c : 256 * (c + 1)] = tiny[r : r + 1]
        norms(0, 4)

    @pl.when(p == 2)
    def _():
        norms(1, 0)


UP = (2, 512, 1024)
DOWN = (2, 1024, 512)


def unpack(first, rest, last):
    def place(layer):
        return [
            pl.BlockSpec((1, 64, 1024), lambda p: (layer, p, 0)),
            pl.BlockSpec((1, 128, 512), lambda p: (layer, p, 0)),
        ]

    params = pltpu.CompilerParams(vmem_limit_bytes=56 * 1024 * 1024)
    g_up, g_down = pl.pallas_call(
        unpack_first_body,
        grid=(8,),
        out_shape=[jax.ShapeDtypeStruct(UP, F32), jax.ShapeDtypeStruct(DOWN, F32)],
        in_specs=[pl.BlockSpec((None, 512, 256), lambda p: (p, 0, 0))],
        out_specs=place(1),
        compiler_params=params,
        name="unpack_first",
    )(first)
    outs = [
        ((2, 3, 512, 256), pl.BlockSpec((2, 3, 64, 256), lambda p: (0, 0, p, 0))),
        ((2, 256, 512), pl.BlockSpec((2, 32, 512), lambda p: (0, p, 0))),
        ((2, 1024), whole((2, 1024))),
        ((3, 2, 256), whole((3, 2, 256))),
        ((2, 2, 512), whole((2, 2, 512))),
        ((2, 2, 512), whole((2, 2, 512))),
        ((2, 2, 512), whole((2, 2, 512))),
    ]
    return pl.pallas_call(
        unpack_rest_body,
        grid=(8,),
        out_shape=[jax.ShapeDtypeStruct(shape, F32) for shape in [UP, DOWN] + [o[0] for o in outs]],
        in_specs=[
            pl.BlockSpec((None, 8, 112, 256), lambda p: (p, 0, 0, 0)),
            pl.BlockSpec((None, 208, 256), lambda p: (p, 0, 0)),
            pl.BlockSpec(memory_space=pl.ANY),
            pl.BlockSpec(memory_space=pl.ANY),
        ],
        out_specs=place(0) + [spec for _, spec in outs],
        input_output_aliases={2: 0, 3: 1},
        compiler_params=params,
        name="unpack_rest",
    )(rest, last, g_up, g_down)


def swap(value):
    return lax.ppermute(value, "tensor", [(0, 1), (1, 0)])


def exchange(value, axes):
    return lax.all_to_all(value, axes, 0, 0)


def both(value):
    flat = value.reshape((16,) + value.shape[2:])
    return exchange(flat, ("context", "tensor")).reshape(value.shape)


def attend(at, recv, wq, w_out):
    outs = [((8, 2, 192, BLK), BF), ((1, 1024), F32), ((HEAD, 1024), F32), ((1, 1024), jnp.int32)]

    def all_of(shape):
        return pl.BlockSpec(shape, lambda i, at: (0,) * len(shape))

    return pl.pallas_call(
        attend_body,
        out_shape=[jax.ShapeDtypeStruct(s, d) for s, d in outs],
        grid_spec=pltpu.PrefetchScalarGridSpec(
            num_scalar_prefetch=1,
            grid=(1,),
            in_specs=[
                all_of(recv.shape),
                pl.BlockSpec(
                    (2, 1, 32, 256),
                    lambda i, at: (0, jnp.minimum(at[2] // 2, 2), (at[2] % 2) * 8 + at[0], 0),
                ),
                pl.BlockSpec((2, 32, 256), lambda i, at: (0, at[0], at[2] % 2)),
            ],
            out_specs=[all_of(s) for s, _ in outs],
        ),
        compiler_params=pltpu.CompilerParams(vmem_limit_bytes=56 * 1024 * 1024),
        name="attend",
    )(at, recv, wq, w_out)


def shards(
    tokens_in, cotangent, positions, w_qkv, b_qkv, w_out, w_up, b_up, w_down, out_bias, ln_gain, ln_bias
):
    rows, width = 256, 512
    x = tokens_in.reshape(rows, width)
    cot = cotangent.reshape(rows, width)
    wq = jnp.transpose(w_qkv, (0, 2, 1, 3))
    bq = jnp.transpose(b_qkv, (1, 0, 2))
    at = jnp.stack(
        [lax.axis_index("context"), lax.axis_index("tensor"), lax.axis_index("dp")]
    ).astype(jnp.int32)
    freqs = jnp.asarray(FREQS).reshape(HALF, 1)
    send, pair, act, slope, cs = call(
        first_body,
        [
            ((8, 208, BLK), BF),
            ((2 * rows, width), BF),
            ((rows, 1024), BF),
            ((rows, 1024), F32),
            ((2, 2, HALF, BLK), F32),
        ],
        (
            at, positions, freqs, x, ln_gain, ln_bias, Layer(wq, 0), bq, Layer(w_up, 0), b_up,
            Layer(w_down, 0), Layer(w_out, 0),
        ),
        "norm_qkv_feed",
        smem_first=True,
    )
    pair_other = swap(pair)
    recv = exchange(send, "context")
    ctx_send, lse, ctx, start = attend(at, recv, wq, w_out)
    recv_ctx = both(ctx_send)
    piece = lax.dynamic_index_in_dim(recv_ctx, 1 - at[1], 1, keepdims=False)[:, 128:192]
    others1 = lax.all_gather(piece, "dp")
    stream, send, grads_a, parts, d_b_up1, d_sum1 = call(
        middle_body,
        [
            ((rows, width), F32),
            ((8, 256, BLK), BF),
            ((8, 512, 256), BF),
            ((2 * rows, width), BF),
            ((1, 1024), F32),
            ((1, width), F32),
        ],
        (
            at, x, pair, pair_other, Rows(recv_ctx, HEAD), Layer(w_out, 0), out_bias, ln_gain, ln_bias,
            Layer(wq, 1), bq, Layer(w_up, 1), b_up, Layer(w_down, 1), Layer(w_out, 1), cot, cs,
        ),
        "middle",
        scratch=[pltpu.VMEM((rows, 1024), BF), pltpu.VMEM((rows, 1024), F32)],
        smem_first=True,
    )
    sums_a = lax.psum_scatter(grads_a, "dp", scatter_dimension=0)
    parts_other = swap(parts)
    recv_both = exchange(send, "context")
    both_send, piece = call(
        attend_both_body,
        [((8, 2, 256, BLK), BF), ((8, HEAD, BLK), BF)],
        (at, recv_both, start, Rows(recv_ctx, HEAD, 1), After(parts_other)),
        "attend_both",
        scratch=[pltpu.VMEM((HEAD, 1024), F32), pltpu.VMEM((HEAD, 1024), F32)],
        smem_first=True,
    )
    others0 = lax.all_gather(piece, "dp")
    recv_grad = both(both_send)
    block_out, g, send, grads_b, part_g, d_b_up0, d_b_qkv1, d_norm1, d_sum0 = call(
        turn_point_body,
        [
            ((rows, width), F32),
            ((rows, width), F32),
            ((8, 192, BLK), BF),
            ((8, 832, 256), BF),
            ((rows, width), BF),
            ((1, 1024), F32),
            ((3, 256), F32),
            ((4, width), F32),
            ((1, width), F32),
        ],
        (
            at, stream, parts, parts_other, recv_grad, Layer(w_out, 1), Layer(wq, 1), others1,
            out_bias, ln_gain, ln_bias, cot, cs, x, act, slope, Layer(w_up, 0), Layer(w_down, 0),
            Layer(w_out, 0), Rows(recv_ctx, HEAD), sums_a,
        ),
        "turn_point",
        smem_first=True,
    )
    sums_b = lax.psum_scatter(grads_b, "dp", scatter_dimension=0)
    part_g_other = swap(part_g)
    recv_d = exchange(send, "context")
    (back_send,) = call(
        attend_back_body,
        [((8, 2, 320, BLK), BF)],
        (recv, recv_d, start, lse, ctx, After(part_g_other)),
        "attend_back",
        scratch=[pltpu.VMEM((HEAD, 1024), F32), pltpu.VMEM((HEAD, 1024), F32)],
    )
    recv_grad0 = both(back_send)
    in_grad, grads_c, sums_a, _, _ = call(
        last_body,
        [
            ((rows, width), F32),
            ((8, 320, 256), BF),
            ((512, 256), BF),
            ((3, 256), F32),
            ((4, width), F32),
        ],
        (
            at, x, g, part_g, part_g_other, recv_grad0, Layer(wq, 0), others0, cs,
            ln_gain, ln_bias, d_b_up0, d_b_up1, d_b_qkv1, d_norm1, d_sum0, d_sum1, sums_b,
        ),
        "last",
        smem_first=True,
    )
    full_a = lax.all_gather(sums_a, "dp")
    late, early = call(
        sum_both_body,
        [((8, 208, 256), BF), ((8, 112, 256), BF)],
        (exchange(grads_c, "context"),),
        "sum_both",
    )
    full_b = lax.all_gather(exchange(early, "context"), "dp")
    (late,) = call(sum_body, [((8, 208, 256), BF)], (exchange(late, "dp"),), "sum")
    full_c = exchange(late, "context")
    g_up, g_down, g_qkv, g_out, g_b_up, g_b_qkv, g_sum, g_gain, g_bias = unpack(full_a, full_b, full_c)
    return (
        block_out.reshape(tokens_in.shape),
        in_grad.reshape(tokens_in.shape),
        jnp.transpose(g_qkv, (0, 2, 1, 3)),
        jnp.transpose(g_b_qkv, (1, 0, 2)),
        g_out,
        g_up,
        g_b_up,
        g_down,
        g_sum,
        g_gain,
        g_bias,
    )


def solution(mesh):
    return jax.shard_map(
        shards,
        mesh=mesh,
        in_specs=(
            P("dp", "context", None),
            P("dp", "context", None),
            P("dp", "context"),
            P(None, None, None, "tensor"),
            P(None, None, "tensor"),
            P(None, "tensor", None),
            P(None, None, "tensor"),
            P(None, "tensor"),
            P(None, "tensor", None),
            P(),
            P(),
            P(),
        ),
        out_specs=(
            P("dp", "context", None),
            P("dp", "context", None),
            P(None, None, None, "tensor"),
            P(None, None, "tensor"),
            P(None, "tensor", None),
            P(None, None, "tensor"),
            P(None, "tensor"),
            P(None, "tensor", None),
            P(),
            P(),
            P(),
        ),
        check_vma=False,
    )
```

```python
from functools import partial

import numpy as np

import jax
import jax.numpy as jnp
from jax import lax
from jax.experimental import pallas as pl
from jax.experimental.pallas import tpu as pltpu
from jax.sharding import PartitionSpec as P

EPS = 1e-05
HALF = 8
HEAD = 64
BLK = 128
CHUNK = 256
NEG = -1e30
BF = jnp.bfloat16
F32 = jnp.float32

FREQS = (10000.0 ** (-np.arange(HALF, dtype=np.float64) * 2.0 / 16.0)).astype(np.float32)


def mm(a, b, ca=1, cb=0):
    return lax.dot_general(a, b, (((ca,), (cb,)), ((), ())), preferred_element_type=F32)


class After:
    def __init__(self, array):
        self.array = array

    def spec(self):
        return pl.BlockSpec(memory_space=pl.ANY)


class Rows:
    def __init__(self, array, rows, at=0):
        self.array, self.rows, self.at = array, rows, at

    def spec(self):
        shape = self.array.shape
        place = (0,) * (len(shape) - 2) + (self.at, 0)
        return pl.BlockSpec(shape[:-2] + (self.rows, shape[-1]), lambda i: place)


class Lead:
    def __init__(self, array, count, at):
        self.array, self.count, self.at = array, count, at

    def spec(self):
        rest = self.array.shape[1:]
        place = (self.at,) + (0,) * len(rest)
        return pl.BlockSpec((self.count,) + rest, lambda i: place)


class Layer:
    def __init__(self, array, index):
        self.array, self.index = array, index

    def spec(self):
        rest = self.array.shape[1:]
        place = (self.index,) + (0,) * len(rest)
        return pl.BlockSpec((None,) + rest, lambda i: place)


def whole(shape):
    return pl.BlockSpec(shape, lambda i: (0,) * len(shape))


def call(body, out_shape, args, name, scratch=(), smem_first=False):
    specs = [
        a.spec() if isinstance(a, (Layer, Lead, Rows, After)) else whole(a.shape) for a in args
    ]
    args = [a.array if isinstance(a, (Layer, Lead, Rows, After)) else a for a in args]
    if smem_first:
        specs[0] = pl.BlockSpec(memory_space=pltpu.SMEM)
    return pl.pallas_call(
        body,
        grid=(1,),
        out_shape=[jax.ShapeDtypeStruct(s, d) for s, d in out_shape],
        in_specs=specs,
        out_specs=[whole(s) for s, _ in out_shape],
        scratch_shapes=list(scratch),
        compiler_params=pltpu.CompilerParams(vmem_limit_bytes=56 * 1024 * 1024),
        name=name,
    )(*args)


def norm_rows(x):
    mean = jnp.mean(x, -1, keepdims=True)
    cen = x - mean
    inv = lax.rsqrt(jnp.mean(cen * cen, -1, keepdims=True) + EPS)
    return cen * inv, inv


def turn(t, cos, sin):
    a, b = t[:HALF], t[HALF : 2 * HALF]
    return jnp.concatenate([a * cos - b * sin, b * cos + a * sin, t[2 * HALF :]], 0)


def turn_back(u, cos, sin):
    a, b = u[:HALF], u[HALF : 2 * HALF]
    return jnp.concatenate([a * cos + b * sin, b * cos - a * sin, u[2 * HALF :]], 0)


def send_qkv(send, attn_in, w_qkv, b_qkv, layer, cs):
    for e in range(3):
        turned = (mm(attn_in, w_qkv[e]) + b_qkv[e, layer : layer + 1]).T
        for s in range(2):
            cos, sin = cs[s, 0], cs[s, 1]
            for h in range(4):
                j = s * 4 + h
                part = turned[h * HEAD : (h + 1) * HEAD, s * BLK : (s + 1) * BLK]
                if e < 2:
                    part = turn(part, cos, sin)
                if e == 0:
                    part = part * (HEAD**-0.5)
                send[j, e * HEAD : (e + 1) * HEAD, :] = part.astype(BF)


def feed_forward(mlp_in, w_up, b_up, layer, w_down, act, slope):
    width = w_up.shape[1]
    total = None
    for c in range(0, width, 256):
        cols = slice(c, c + 256)
        pre = mm(mlp_in, w_up[:, cols]) + b_up[layer : layer + 1, cols]
        cdf = 0.5 + 0.5 * lax.erf(pre * np.float32(0.7071067811865476))
        a = (pre * cdf).astype(BF)
        act[:, cols] = a
        slope[:, cols] = cdf + pre * (jnp.exp(-0.5 * pre * pre) * np.float32(0.3989422804014327))
        term = mm(a, w_down[cols, :])
        total = term if total is None else total + term
    return total


def feed_back(g_b, act, slope, mlp_in, w_up, w_down, d_up, d_down, d_b_up):
    width = w_up.shape[1]
    total = None
    mlp_t = mlp_in.astype(F32).T.astype(BF)
    for c in range(0, width, 256):
        cols = slice(c, c + 256)
        d_act = mm(g_b, w_down[cols, :], 1, 1)
        d_pre = d_act * slope[:, cols]
        d_pre_b = d_pre.astype(BF)
        d_b_up[:, cols] = jnp.sum(d_pre_b.astype(F32), 0, keepdims=True)
        d_up(c // 256, mm(mlp_t, d_pre_b))
        d_down(c, mm(act[:, cols].astype(F32).T.astype(BF), g_b))
        term = mm(d_pre_b, w_up[:, cols], 1, 1)
        total = term if total is None else total + term
    return total


def pack_up(out, row):
    def put(c, value):
        for p in range(8):
            out[p, row + 64 * c : row + 64 * (c + 1), :] = value[64 * p : 64 * (p + 1)].astype(BF)

    return put


def pack_down(out, row):
    def put(c, value):
        for half in range(2):
            for k in range(2):
                out[c // 128 + k, row + 128 * half : row + 128 * (half + 1), :] = value[
                    128 * k : 128 * (k + 1), 256 * half : 256 * (half + 1)
                ].astype(BF)

    return put


def pack_qkv(out, row, d_b_qkv):
    def put(e, attn_t, own):
        d_b_qkv[e : e + 1] = mm(jnp.ones((8, own.shape[1]), BF), own, 1, 1)[0:1]
        value = mm(attn_t, own, 1, 1)
        for p in range(8):
            out[p, row + 64 * e : row + 64 * (e + 1), :] = value[64 * p : 64 * (p + 1)].astype(BF)

    return put


def own_ctx(t, recv):
    full = jnp.concatenate([gather_ctx(recv, s) for s in range(2)], 1)
    return jnp.where(t == 0, full[0:256], full[256:512])


def pack_out(out, row, ctx, upstream):
    value = mm(ctx, upstream)
    for p in range(8):
        for half in range(2):
            out[p, row + 32 * half : row + 32 * (half + 1), :] = value[
                32 * p : 32 * (p + 1), 256 * half : 256 * (half + 1)
            ].astype(BF)


def first_body(
    at, pos, freqs, x, gain, bias, w_qkv, b_qkv, w_up, b_up, w_down, w_out,
    send, pair, act, slope, cs,
):
    pair[256:512] = w_out[...]
    for s in range(2):
        p = pos[s : s + 1, :].astype(F32)
        angle = freqs[...] * p
        cs[s, 0] = jnp.cos(angle)
        cs[s, 1] = jnp.sin(angle)
    normed, _ = norm_rows(x[...])
    attn_in = (normed * gain[0, 0:1] + bias[0, 0:1]).astype(BF)
    mlp_in = (normed * gain[0, 1:2] + bias[0, 1:2]).astype(BF)
    send_qkv(send, attn_in, w_qkv, b_qkv, 0, cs)
    row = lax.broadcasted_iota(jnp.int32, (16, BLK), 0)
    token = at[0] * BLK + lax.broadcasted_iota(jnp.int32, (1, BLK), 1)
    for s in range(2):
        start = jnp.maximum(token - pos[s : s + 1, :], 0)
        high = (start // 8).astype(F32)
        low = (start % 8).astype(F32)
        block = jnp.where(row == 0, high, jnp.where(row == 1, low, 0.0)).astype(BF)
        for h in range(4):
            send[s * 4 + h, 3 * HEAD : 3 * HEAD + 16, :] = block
    pair[0:256] = feed_forward(mlp_in, w_up, b_up, 0, w_down, act, slope).astype(BF)


def load_rows(recv, lo, hi):
    return jnp.concatenate([recv[i, lo:hi, :] for i in range(8)], 1)


def starts_of(recv):
    rows = load_rows(recv, 3 * HEAD, 3 * HEAD + 16).astype(F32)
    return rows[0:1] * 8.0 + rows[1:2]


def visible_of(start, c, length):
    key = lax.broadcasted_iota(jnp.int32, (length, CHUNK), 0)
    query = lax.broadcasted_iota(jnp.int32, (length, CHUNK), 1) + c * CHUNK
    return (key <= query) & (key >= start[:, c * CHUNK : (c + 1) * CHUNK])


def attend_body(at, recv, w_qkv, w_out, _, send, lse, ctx, start_out):
    for layer in range(2):
        piece = jnp.where(at[2] // 2 == 3, w_out[layer], w_qkv[layer, 0])
        for b in range(8):
            for t in range(2):
                for half in range(2):
                    row = 64 + 64 * layer + 32 * half
                    send[b, t, row : row + 32] = piece[:, BLK * half : BLK * (half + 1)]
    q = load_rows(recv, 0, HEAD)
    k_t = load_rows(recv, HEAD, 2 * HEAD)
    v_t = load_rows(recv, 2 * HEAD, 3 * HEAD)
    k = k_t.astype(F32).T.astype(BF)
    start = starts_of(recv).astype(jnp.int32)
    start_out[...] = start
    for c in range(4):
        cols = slice(c * CHUNK, (c + 1) * CHUNK)
        length = (c + 1) * CHUNK
        scores = mm(k[:length], q[:, cols])
        scores = jnp.where(visible_of(start, c, length), scores, NEG)
        peak = jnp.max(scores, 0, keepdims=True)
        shifted = jnp.exp(scores - peak)
        total = jnp.sum(shifted, 0, keepdims=True)
        lse[:, cols] = peak + jnp.log(total)
        out = mm(v_t[:, :length], shifted.astype(BF)) / total
        ctx[:, cols] = out
        for i in range(CHUNK // BLK):
            block = out[:, i * BLK : (i + 1) * BLK].astype(BF)
            for t in range(2):
                send[c * (CHUNK // BLK) + i, t, 0:HEAD] = block


def attend_both_body(at, recv, start, pieces, _, send, piece, dk, dv):
    for b in range(8):
        piece[b] = jnp.where(at[1] == 0, pieces[b, 1], pieces[b, 0])
    q = load_rows(recv, 0, HEAD)
    k_t = load_rows(recv, HEAD, 2 * HEAD)
    v_t = load_rows(recv, 2 * HEAD, 3 * HEAD)
    d_ctx = load_rows(recv, 3 * HEAD, 4 * HEAD)
    k = k_t.astype(F32).T.astype(BF)
    v = v_t.astype(F32).T.astype(BF)
    dk[...] = jnp.zeros_like(dk)
    dv[...] = jnp.zeros_like(dv)
    for c in range(4):
        cols = slice(c * CHUNK, (c + 1) * CHUNK)
        length = (c + 1) * CHUNK
        scores = mm(k[:length], q[:, cols])
        scores = jnp.where(visible_of(start[...], c, length), scores, NEG)
        peak = jnp.max(scores, 0, keepdims=True)
        shifted = jnp.exp(scores - peak)
        probs = shifted * (1.0 / jnp.sum(shifted, 0, keepdims=True))
        probs_b = probs.astype(BF)
        out = mm(v_t[:, :length], probs_b)
        dq = backward_chunk(q, k_t, v, d_ctx, probs, probs_b, out, cols, length, dk, dv)
        for i in range(CHUNK // BLK):
            b = c * (CHUNK // BLK) + i
            for t in range(2):
                send[b, t, 0:HEAD] = out[:, i * BLK : (i + 1) * BLK].astype(BF)
                send[b, t, HEAD : 2 * HEAD] = dq[:, i * BLK : (i + 1) * BLK].astype(BF)
    put_kv(send, dk, dv, 2 * HEAD)


def backward_chunk(q, k_t, v, d_ctx, probs, probs_b, out, cols, length, dk, dv):
    d_out = d_ctx[:, cols]
    d_probs = mm(v[:length], d_out)
    delta = jnp.sum(d_out.astype(F32) * out, 0, keepdims=True)
    d_scores = (probs * (d_probs - delta)).astype(BF)
    dk[:, :length] += mm(q[:, cols], d_scores, 1, 1)
    dv[:, :length] += mm(d_out, probs_b, 1, 1)
    return mm(k_t[:, :length], d_scores) * (HEAD**-0.5)


def put_kv(send, dk, dv, row):
    for b in range(8):
        for t in range(2):
            send[b, t, row : row + HEAD] = dk[:, b * BLK : (b + 1) * BLK].astype(BF)
            send[b, t, row + HEAD : row + 2 * HEAD] = dv[:, b * BLK : (b + 1) * BLK].astype(BF)


def attend_back_body(recv, recv_d, start, lse, ctx, send, dk, dv):
    ride = recv_d[0, 64:192].astype(F32)
    for i in range(1, 8):
        ride = ride + recv_d[i, 64:192].astype(F32)
    ride = ride.astype(BF)
    for b in range(8):
        for t in range(2):
            send[b, t, 192:320] = ride
    q = load_rows(recv, 0, HEAD)
    k_t = load_rows(recv, HEAD, 2 * HEAD)
    v_t = load_rows(recv, 2 * HEAD, 3 * HEAD)
    d_ctx = load_rows(recv_d, 0, HEAD)
    k = k_t.astype(F32).T.astype(BF)
    v = v_t.astype(F32).T.astype(BF)
    dk[...] = jnp.zeros_like(dk)
    dv[...] = jnp.zeros_like(dv)
    for c in range(4):
        cols = slice(c * CHUNK, (c + 1) * CHUNK)
        length = (c + 1) * CHUNK
        scores = mm(k[:length], q[:, cols])
        scores = jnp.where(visible_of(start[...], c, length), scores, NEG)
        probs = jnp.exp(scores - lse[:, cols])
        probs_b = probs.astype(BF)
        dq = backward_chunk(q, k_t, v, d_ctx, probs, probs_b, ctx[:, cols], cols, length, dk, dv)
        for i in range(CHUNK // BLK):
            for t in range(2):
                send[c * (CHUNK // BLK) + i, t, 0:HEAD] = dq[:, i * BLK : (i + 1) * BLK].astype(BF)
    put_kv(send, dk, dv, HEAD)


def gather_ctx(recv, s):
    return jnp.concatenate([recv[s * 4 + h, t, 0:HEAD, :] for t in range(2) for h in range(4)], 0)


def ordered(t, own, other):
    return jnp.where(t == 0, own, other), jnp.where(t == 0, other, own)


def other_matrix(others, m):
    rows = []
    for d in (2 * m, 2 * m + 1):
        for c in range(8):
            rows.append(jnp.concatenate([others[d, c, 0:32, :], others[d, c, 32:64, :]], 1))
    return jnp.concatenate(rows, 0)


def out_other(others):
    stacked = other_matrix(others, 0)
    return jnp.concatenate([stacked[0:256], stacked[256:512]], 1)


def branch_of(t, recv, w_own, w_other):
    first, second = ordered(t, w_own, w_other)
    w = jnp.concatenate([first, second], 0)
    rows = []
    for s in range(2):
        rows.append(mm(gather_ctx(recv, s).astype(F32).T.astype(BF), w))
    return jnp.concatenate(rows, 0)


def middle_body(
    at, x, pair, pair_other, recv, w_out_own, out_bias, gain, bias,
    w_qkv, b_qkv, w_up, b_up, w_down, w_out, cot, cs,
    stream, send, grads, parts, d_b_up, d_sum, act, slope,
):
    branch = pair[0:256].astype(F32) + pair_other[0:256].astype(F32)
    branch = branch + branch_of(at[1], recv, w_out_own[...], pair_other[256:512])
    out = x[...] + branch + out_bias[0, 0:1] + out_bias[0, 1:2]
    stream[...] = out
    normed, _ = norm_rows(out)
    attn_in = (normed * gain[1, 0:1] + bias[1, 0:1]).astype(BF)
    mlp_in = (normed * gain[1, 1:2] + bias[1, 1:2]).astype(BF)
    send_qkv(send, attn_in, w_qkv, b_qkv, 1, cs)
    g_b = cot[...].astype(BF)
    d_ctx = mm(w_out[...], g_b, 1, 1)
    for s in range(2):
        for h in range(4):
            send[s * 4 + h, 3 * HEAD : 4 * HEAD, :] = d_ctx[
                h * HEAD : (h + 1) * HEAD, s * BLK : (s + 1) * BLK
            ].astype(BF)
    d_sum[...] = jnp.sum(cot[...], 0, keepdims=True)
    parts[0:256] = feed_forward(mlp_in, w_up, b_up, 1, w_down, act, slope).astype(BF)
    parts[256:512] = feed_back(
        g_b, act, slope, mlp_in, w_up, w_down, pack_up(grads, 0), pack_down(grads, 256), d_b_up
    ).astype(BF)


def norm_back(
    t, x, g, d_mlp_in, recv, row, w_own, others, cs, gain, bias, layer, d_qkv, d_norm
):
    normed, inv = norm_rows(x)
    attn_in = (normed * gain[layer, 0:1] + bias[layer, 0:1]).astype(BF)
    attn_t = attn_in.astype(F32).T.astype(BF)
    d_attn_t = None
    for e in range(3):
        halves = []
        for tt in range(2):
            blocks = []
            for h in range(4):
                pieces = []
                for s in range(2):
                    lo = row + e * HEAD
                    u = recv[s * 4 + h, tt, lo : lo + HEAD, :]
                    if e < 2:
                        u = turn_back(u.astype(F32), cs[s, 0], cs[s, 1]).astype(BF)
                    pieces.append(u)
                blocks.append(jnp.concatenate(pieces, 1))
            halves.append(jnp.concatenate(blocks, 0))
        first, second = ordered(t, w_own[e], other_matrix(others, e))
        term = mm(first, halves[0]) + mm(second, halves[1])
        d_attn_t = term if d_attn_t is None else d_attn_t + term
        d_qkv(e, attn_t, jnp.where(t == 0, halves[0], halves[1]))
    d_attn_in = d_attn_t.T
    d_norm[0:1] = jnp.sum(d_attn_in * normed, 0, keepdims=True)
    d_norm[1:2] = jnp.sum(d_mlp_in * normed, 0, keepdims=True)
    d_norm[2:3] = jnp.sum(d_attn_in, 0, keepdims=True)
    d_norm[3:4] = jnp.sum(d_mlp_in, 0, keepdims=True)
    d_normed = d_attn_in * gain[layer, 0:1] + d_mlp_in * gain[layer, 1:2]
    return g + inv * (
        d_normed
        - jnp.mean(d_normed, -1, keepdims=True)
        - normed * jnp.mean(d_normed * normed, -1, keepdims=True)
    )


def turn_point_body(
    at, stream, parts, parts_other, recv, w_qkv, others, gain, bias, cot, cs, w_out_first, sums_a,
    g_out, send, d_qkv, d_norm, d_sum,
):
    def keep(e, _, own):
        d_qkv[e] = own

    d_mlp_in = parts[...].astype(F32) + parts_other[...].astype(F32)
    g = norm_back(
        at[1], stream[...], cot[...], d_mlp_in, recv, HEAD, w_qkv, others, cs, gain, bias, 1,
        keep, d_norm,
    )
    g_out[...] = g
    d_sum[...] = jnp.sum(g, 0, keepdims=True)
    d_ctx = mm(w_out_first[...], g.astype(BF), 1, 1)
    for s in range(2):
        for h in range(4):
            send[s * 4 + h, 0:HEAD] = d_ctx[
                h * HEAD : (h + 1) * HEAD, s * BLK : (s + 1) * BLK
            ].astype(BF)
    for q in range(8):
        for c in range(2):
            send[q, 64 + 64 * c : 128 + 64 * c] = sums_a[
                64 * q : 64 * (q + 1), BLK * c : BLK * (c + 1)
            ]


def weights_body(
    at, stream, parts, parts_other, recv, w_out, others, out_bias, gain, bias, cot, x, g, d_qkv,
    act, slope, w_up, w_down, recv_first,
    block_out, grads, part, d_b_up, d_b_qkv,
):
    t = at[1]
    g_b = g[...].astype(BF)
    normed, _ = norm_rows(x[...])
    mlp_in = (normed * gain[0, 1:2] + bias[0, 1:2]).astype(BF)
    part[...] = feed_back(
        g_b, act, slope, mlp_in, w_up, w_down, pack_up(grads, 192), pack_down(grads, 448), d_b_up
    ).astype(BF)
    branch = parts[...].astype(F32) + parts_other[...].astype(F32)
    branch = branch + branch_of(t, recv, w_out[...], out_other(others))
    block_out[...] = stream[...] + branch + out_bias[1, 0:1] + out_bias[1, 1:2]
    normed, _ = norm_rows(stream[...])
    attn_t = (normed * gain[1, 0:1] + bias[1, 0:1]).T.astype(BF)
    put = pack_qkv(grads, 0, d_b_qkv)
    for e in range(3):
        put(e, attn_t, d_qkv[e])
    pack_out(grads, 704, own_ctx(t, recv), cot[...].astype(BF))
    pack_out(grads, 768, own_ctx(t, recv_first), g_b)


def last_body(
    at, x, g, part, part_other, recv, w_qkv, others, cs, gain, bias,
    d_b_up0, d_b_up1, d_b_qkv1, d_norm1, d_sum0, d_sum1,
    in_grad, grads, sums_a, d_b_qkv0, d_norm0,
):
    d_mlp_in = part[...].astype(F32) + part_other[...].astype(F32)
    in_grad[...] = norm_back(
        at[1], x[...], g[...], d_mlp_in, recv, 0, w_qkv, others, cs, gain, bias, 0,
        pack_qkv(grads, 0, d_b_qkv0), d_norm0,
    )
    for q in range(8):
        both_planes = recv[q, :, 192:320]
        block = jnp.where(at[1] == 0, both_planes[0], both_planes[1])
        for c in range(2):
            sums_a[64 * q : 64 * (q + 1), BLK * c : BLK * (c + 1)] = block[64 * c : 64 * (c + 1)]

    def lanes(ref, row, count):
        return [ref[row : row + 1, 256 * c : 256 * (c + 1)] for c in range(count)]

    def norms(ref):
        return [v for r in range(4) for v in lanes(ref, r, 2)]

    rows = [
        lanes(d_b_up0, 0, 4)
        + lanes(d_b_up1, 0, 4)
        + [v for e in range(3) for ref in (d_b_qkv0, d_b_qkv1) for v in lanes(ref, e, 1)],
        lanes(d_sum0, 0, 2) + lanes(d_sum1, 0, 2) + norms(d_norm0),
        norms(d_norm1),
    ]
    for p in range(8):
        have = rows[p] if p < len(rows) else []
        fill = [jnp.zeros((16 - len(have), 256), F32)]
        grads[p, 192:208, :] = jnp.concatenate(have + fill, 0).astype(BF)


def sum_of(got):
    total = got[0].astype(F32)
    for i in range(1, 8):
        total = total + got[i].astype(F32)
    return total.astype(BF)


def mix_body(got, early, first, out, first_out):
    total = sum_of(got).astype(F32)
    for q in range(8):
        mine = [early[104 * q : 104 * (q + 1)].astype(F32), total[24 * q : 24 * (q + 1)]]
        out[q, 0:128] = jnp.concatenate(mine, 0).astype(BF)
        out[q, 128:144] = total[192:208].astype(BF) if q == 0 else jnp.zeros((16, 256), BF)
    first_out[...] = first[...]


def sum_body(got, out):
    total = sum_of(got)
    for q in range(8):
        out[q] = total


def unpack_first_body(first, g_up, g_down):
    for c in range(4):
        g_up[0, :, 256 * c : 256 * (c + 1)] = first[64 * c : 64 * (c + 1)].astype(F32)
    for c in range(2):
        rows = first[256 + 128 * c : 256 + 128 * (c + 1)]
        g_down[0, :, 256 * c : 256 * (c + 1)] = rows.astype(F32)


def unpack_rest_body(
    rest, _, __, g_up, g_down, g_qkv, g_out, g_b_up, g_b_qkv, g_sum, g_gain, g_bias
):
    p = pl.program_id(0)
    for q in range(8):
        block = rest[q, 0:128].astype(F32)
        for i in range(3):
            row = 24 * q + 8 * i
            g_qkv[0, row // 64, row % 64 : row % 64 + 8] = block[104 + 8 * i : 112 + 8 * i]
        for i in range(13):
            row = 104 * q + 8 * i
            value = block[8 * i : 8 * (i + 1)]
            if row < 192:
                g_qkv[1, row // 64, row % 64 : row % 64 + 8] = value
            elif row < 448:
                c, r = divmod(row - 192, 64)
                g_up[0, r : r + 8, 256 * c : 256 * (c + 1)] = value
            elif row < 704:
                c, r = divmod(row - 448, 128)
                g_down[0, r : r + 8, 256 * c : 256 * (c + 1)] = value
            else:
                c, r = divmod((row - 704) % 64, 32)
                g_out[1 - (row - 704) // 64, r : r + 8, 256 * c : 256 * (c + 1)] = value

    tiny = rest[0, 128:144].astype(F32)

    @pl.when(p == 0)
    def _():
        for layer in range(2):
            for c in range(4):
                r = 4 * layer + c
                g_b_up[layer : layer + 1, 256 * c : 256 * (c + 1)] = tiny[r : r + 1]
        for e in range(3):
            for layer in range(2):
                r = 8 + 2 * e + layer
                g_b_qkv[e, layer : layer + 1, :] = tiny[r : r + 1]

    def norms(layer, base):
        for which in range(2):
            for c in range(2):
                cols = slice(256 * c, 256 * (c + 1))
                r = base + 2 * which + c
                g_gain[layer, which : which + 1, cols] = tiny[r : r + 1]
                g_bias[layer, which : which + 1, cols] = tiny[r + 4 : r + 5]

    @pl.when(p == 1)
    def _():
        for layer in range(2):
            for c in range(2):
                r = 2 * layer + c
                for which in range(2):
                    g_sum[layer, which : which + 1, 256 * c : 256 * (c + 1)] = tiny[r : r + 1]
        norms(0, 4)

    @pl.when(p == 2)
    def _():
        norms(1, 0)


UP = (2, 512, 1024)
DOWN = (2, 1024, 512)


def unpack(first, rest):
    def place(layer):
        return [
            pl.BlockSpec((1, 64, 1024), lambda p: (layer, p, 0)),
            pl.BlockSpec((1, 128, 512), lambda p: (layer, p, 0)),
        ]

    params = pltpu.CompilerParams(vmem_limit_bytes=56 * 1024 * 1024)
    g_up, g_down = pl.pallas_call(
        unpack_first_body,
        grid=(8,),
        out_shape=[jax.ShapeDtypeStruct(UP, F32), jax.ShapeDtypeStruct(DOWN, F32)],
        in_specs=[pl.BlockSpec((None, 512, 256), lambda p: (p, 0, 0))],
        out_specs=place(1),
        compiler_params=params,
        name="unpack_first",
    )(first)
    outs = [
        ((2, 3, 512, 256), pl.BlockSpec((2, 3, 64, 256), lambda p: (0, 0, p, 0))),
        ((2, 256, 512), pl.BlockSpec((2, 32, 512), lambda p: (0, p, 0))),
        ((2, 1024), whole((2, 1024))),
        ((3, 2, 256), whole((3, 2, 256))),
        ((2, 2, 512), whole((2, 2, 512))),
        ((2, 2, 512), whole((2, 2, 512))),
        ((2, 2, 512), whole((2, 2, 512))),
    ]
    return pl.pallas_call(
        unpack_rest_body,
        grid=(8,),
        out_shape=[jax.ShapeDtypeStruct(shape, F32) for shape in [UP, DOWN] + [o[0] for o in outs]],
        in_specs=[
            pl.BlockSpec((None, 8, 144, 256), lambda p: (p, 0, 0, 0)),
            pl.BlockSpec(memory_space=pl.ANY),
            pl.BlockSpec(memory_space=pl.ANY),
        ],
        out_specs=place(0) + [spec for _, spec in outs],
        input_output_aliases={1: 0, 2: 1},
        compiler_params=params,
        name="unpack_rest",
    )(rest, g_up, g_down)


def swap(value):
    return lax.ppermute(value, "tensor", [(0, 1), (1, 0)])


def exchange(value, axes):
    return lax.all_to_all(value, axes, 0, 0)


def both(value):
    flat = value.reshape((16,) + value.shape[2:])
    return exchange(flat, ("context", "tensor")).reshape(value.shape)


def attend(at, recv, wq, w_out, after):
    outs = [((8, 2, 192, BLK), BF), ((1, 1024), F32), ((HEAD, 1024), F32), ((1, 1024), jnp.int32)]

    def all_of(shape):
        return pl.BlockSpec(shape, lambda i, at: (0,) * len(shape))

    return pl.pallas_call(
        attend_body,
        out_shape=[jax.ShapeDtypeStruct(s, d) for s, d in outs],
        grid_spec=pltpu.PrefetchScalarGridSpec(
            num_scalar_prefetch=1,
            grid=(1,),
            in_specs=[
                all_of(recv.shape),
                pl.BlockSpec(
                    (2, 1, 32, 256),
                    lambda i, at: (0, jnp.minimum(at[2] // 2, 2), (at[2] % 2) * 8 + at[0], 0),
                ),
                pl.BlockSpec((2, 32, 256), lambda i, at: (0, at[0], at[2] % 2)),
                pl.BlockSpec(memory_space=pl.ANY),
            ],
            out_specs=[all_of(s) for s, _ in outs],
        ),
        compiler_params=pltpu.CompilerParams(vmem_limit_bytes=56 * 1024 * 1024),
        name="attend",
    )(at, recv, wq, w_out, after)


def shards(
    tokens_in, cotangent, positions, w_qkv, b_qkv, w_out, w_up, b_up, w_down, out_bias, ln_gain, ln_bias
):
    rows, width = 256, 512
    x = tokens_in.reshape(rows, width)
    cot = cotangent.reshape(rows, width)
    wq = jnp.transpose(w_qkv, (0, 2, 1, 3))
    bq = jnp.transpose(b_qkv, (1, 0, 2))
    at = jnp.stack(
        [lax.axis_index("context"), lax.axis_index("tensor"), lax.axis_index("dp")]
    ).astype(jnp.int32)
    freqs = jnp.asarray(FREQS).reshape(HALF, 1)
    send, pair, act, slope, cs = call(
        first_body,
        [
            ((8, 208, BLK), BF),
            ((2 * rows, width), BF),
            ((rows, 1024), BF),
            ((rows, 1024), F32),
            ((2, 2, HALF, BLK), F32),
        ],
        (
            at, positions, freqs, x, ln_gain, ln_bias, Layer(wq, 0), bq, Layer(w_up, 0), b_up,
            Layer(w_down, 0), Layer(w_out, 0),
        ),
        "norm_qkv_feed",
        smem_first=True,
    )
    pair_other = swap(pair)
    recv = exchange(send, "context")
    ctx_send, lse, ctx, start = attend(at, recv, wq, w_out, pair_other)
    recv_ctx = both(ctx_send)
    piece = lax.dynamic_index_in_dim(recv_ctx, 1 - at[1], 1, keepdims=False)[:, 128:192]
    others1 = lax.all_gather(piece, "dp")
    stream, send, grads_a, parts, d_b_up1, d_sum1 = call(
        middle_body,
        [
            ((rows, width), F32),
            ((8, 256, BLK), BF),
            ((8, 512, 256), BF),
            ((2 * rows, width), BF),
            ((1, 1024), F32),
            ((1, width), F32),
        ],
        (
            at, x, pair, pair_other, Rows(recv_ctx, HEAD), Layer(w_out, 0), out_bias, ln_gain, ln_bias,
            Layer(wq, 1), bq, Layer(w_up, 1), b_up, Layer(w_down, 1), Layer(w_out, 1), cot, cs,
        ),
        "middle",
        scratch=[pltpu.VMEM((rows, 1024), BF), pltpu.VMEM((rows, 1024), F32)],
        smem_first=True,
    )
    sums_a = lax.psum_scatter(grads_a, "dp", scatter_dimension=0)
    parts_other = swap(parts)
    recv_both = exchange(send, "context")
    both_send, piece = call(
        attend_both_body,
        [((8, 2, 256, BLK), BF), ((8, HEAD, BLK), BF)],
        (at, recv_both, start, Rows(recv_ctx, HEAD, 1), After(parts_other)),
        "attend_both",
        scratch=[pltpu.VMEM((HEAD, 1024), F32), pltpu.VMEM((HEAD, 1024), F32)],
        smem_first=True,
    )
    others0 = lax.all_gather(piece, "dp")
    recv_grad = both(both_send)
    g, send, d_qkv, d_norm1, d_sum0 = call(
        turn_point_body,
        [
            ((rows, width), F32),
            ((8, 192, BLK), BF),
            ((3, 256, rows), BF),
            ((4, width), F32),
            ((1, width), F32),
        ],
        (
            at, stream, Rows(parts, rows, 1), Rows(parts_other, rows, 1), recv_grad, Layer(wq, 1),
            others1, ln_gain, ln_bias, cot, cs, Layer(w_out, 0), sums_a,
        ),
        "turn_point",
        smem_first=True,
    )
    recv_d = exchange(send, "context")
    block_out, grads_b, part_g, d_b_up0, d_b_qkv1 = call(
        weights_body,
        [
            ((rows, width), F32),
            ((8, 832, 256), BF),
            ((rows, width), BF),
            ((1, 1024), F32),
            ((3, 256), F32),
        ],
        (
            at, stream, Rows(parts, rows), Rows(parts_other, rows), Rows(recv_grad, HEAD),
            Layer(w_out, 1), Lead(others1, 2, 3), out_bias, ln_gain, ln_bias, cot, x, g, d_qkv, act,
            slope, Layer(w_up, 0), Layer(w_down, 0), Rows(recv_ctx, HEAD),
        ),
        "weights",
        smem_first=True,
    )
    sums_b = lax.psum_scatter(grads_b, "dp", scatter_dimension=0)
    part_g_other = swap(part_g)
    (back_send,) = call(
        attend_back_body,
        [((8, 2, 320, BLK), BF)],
        (recv, recv_d, start, lse, ctx),
        "attend_back",
        scratch=[pltpu.VMEM((HEAD, 1024), F32), pltpu.VMEM((HEAD, 1024), F32)],
    )
    recv_grad0 = both(back_send)
    in_grad, grads_c, sums_a, _, _ = call(
        last_body,
        [
            ((rows, width), F32),
            ((8, 208, 256), BF),
            ((512, 256), BF),
            ((3, 256), F32),
            ((4, width), F32),
        ],
        (
            at, x, g, part_g, part_g_other, recv_grad0, Layer(wq, 0), others0, cs,
            ln_gain, ln_bias, d_b_up0, d_b_up1, d_b_qkv1, d_norm1, d_sum0, d_sum1,
        ),
        "last",
        smem_first=True,
    )
    mixed, sums_a = call(
        mix_body,
        [((8, 144, 256), BF), ((512, 256), BF)],
        (exchange(grads_c, "dp"), sums_b, sums_a),
        "mix",
    )
    full_a = lax.all_gather(sums_a, "dp")
    (summed,) = call(sum_body, [((8, 144, 256), BF)], (exchange(mixed, "context"),), "sum")
    full_b = lax.all_gather(exchange(summed, "context"), "dp")
    g_up, g_down, g_qkv, g_out, g_b_up, g_b_qkv, g_sum, g_gain, g_bias = unpack(full_a, full_b)
    return (
        block_out.reshape(tokens_in.shape),
        in_grad.reshape(tokens_in.shape),
        jnp.transpose(g_qkv, (0, 2, 1, 3)),
        jnp.transpose(g_b_qkv, (1, 0, 2)),
        g_out,
        g_up,
        g_b_up,
        g_down,
        g_sum,
        g_gain,
        g_bias,
    )


def solution(mesh):
    return jax.shard_map(
        shards,
        mesh=mesh,
        in_specs=(
            P("dp", "context", None),
            P("dp", "context", None),
            P("dp", "context"),
            P(None, None, None, "tensor"),
            P(None, None, "tensor"),
            P(None, "tensor", None),
            P(None, None, "tensor"),
            P(None, "tensor"),
            P(None, "tensor", None),
            P(),
            P(),
            P(),
        ),
        out_specs=(
            P("dp", "context", None),
            P("dp", "context", None),
            P(None, None, None, "tensor"),
            P(None, None, "tensor"),
            P(None, "tensor", None),
            P(None, None, "tensor"),
            P(None, "tensor"),
            P(None, "tensor", None),
            P(),
            P(),
            P(),
        ),
        check_vma=False,
    )
```

```python
from functools import partial

import numpy as np

import jax
import jax.numpy as jnp
from jax import lax
from jax.experimental import pallas as pl
from jax.experimental.pallas import tpu as pltpu
from jax.sharding import PartitionSpec as P

EPS = 1e-05
HALF = 8
HEAD = 64
BLK = 128
CHUNK = 256
NEG = -1e30
BF = jnp.bfloat16
F32 = jnp.float32

FREQS = (10000.0 ** (-np.arange(HALF, dtype=np.float64) * 2.0 / 16.0)).astype(np.float32)


def mm(a, b, ca=1, cb=0):
    return lax.dot_general(a, b, (((ca,), (cb,)), ((), ())), preferred_element_type=F32)


class After:
    def __init__(self, array):
        self.array = array

    def spec(self):
        return pl.BlockSpec(memory_space=pl.ANY)


class Layer:
    def __init__(self, array, index):
        self.array, self.index = array, index

    def spec(self):
        rest = self.array.shape[1:]
        place = (self.index,) + (0,) * len(rest)
        return pl.BlockSpec((None,) + rest, lambda i: place)


def whole(shape):
    return pl.BlockSpec(shape, lambda i: (0,) * len(shape))


def call(body, out_shape, args, name, scratch=(), smem_first=False):
    specs = [
        a.spec() if isinstance(a, (Layer, After)) else whole(a.shape) for a in args
    ]
    args = [a.array if isinstance(a, (Layer, After)) else a for a in args]
    if smem_first:
        specs[0] = pl.BlockSpec(memory_space=pltpu.SMEM)
    return pl.pallas_call(
        body,
        grid=(1,),
        out_shape=[jax.ShapeDtypeStruct(s, d) for s, d in out_shape],
        in_specs=specs,
        out_specs=[whole(s) for s, _ in out_shape],
        scratch_shapes=list(scratch),
        compiler_params=pltpu.CompilerParams(vmem_limit_bytes=63 * 1024 * 1024),
        name=name,
    )(*args)


def norm_rows(x):
    mean = jnp.mean(x, -1, keepdims=True)
    cen = x - mean
    inv = lax.rsqrt(jnp.mean(cen * cen, -1, keepdims=True) + EPS)
    return cen * inv, inv


def turn(t, cos, sin):
    a, b = t[:HALF], t[HALF : 2 * HALF]
    return jnp.concatenate([a * cos - b * sin, b * cos + a * sin, t[2 * HALF :]], 0)


def turn_back(u, cos, sin):
    a, b = u[:HALF], u[HALF : 2 * HALF]
    return jnp.concatenate([a * cos + b * sin, b * cos - a * sin, u[2 * HALF :]], 0)


def send_qkv(send, attn_in, w_qkv, b_qkv, layer, cs):
    for e in range(3):
        turned = (mm(attn_in, w_qkv[e]) + b_qkv[e, layer : layer + 1]).T
        for s in range(2):
            cos, sin = cs[s, 0], cs[s, 1]
            for h in range(4):
                j = s * 4 + h
                part = turned[h * HEAD : (h + 1) * HEAD, s * BLK : (s + 1) * BLK]
                if e < 2:
                    part = turn(part, cos, sin)
                if e == 0:
                    part = part * (HEAD**-0.5)
                send[j, e * HEAD : (e + 1) * HEAD, :] = part.astype(BF)


def feed_forward(mlp_in, w_up, b_up, layer, w_down, act, slope):
    width = w_up.shape[1]
    total = None
    for c in range(0, width, 256):
        cols = slice(c, c + 256)
        pre = mm(mlp_in, w_up[:, cols]) + b_up[layer : layer + 1, cols]
        cdf = 0.5 + 0.5 * lax.erf(pre * np.float32(0.7071067811865476))
        a = (pre * cdf).astype(BF)
        act[:, cols] = a
        slope[:, cols] = cdf + pre * (jnp.exp(-0.5 * pre * pre) * np.float32(0.3989422804014327))
        term = mm(a, w_down[cols, :])
        total = term if total is None else total + term
    return total


def feed_back(g_b, act, slope, mlp_in, w_up, w_down, d_up, d_down, d_b_up):
    width = w_up.shape[1]
    total = None
    mlp_t = mlp_in.astype(F32).T.astype(BF)
    for c in range(0, width, 256):
        cols = slice(c, c + 256)
        d_act = mm(g_b, w_down[cols, :], 1, 1)
        d_pre = d_act * slope[:, cols]
        d_pre_b = d_pre.astype(BF)
        d_b_up[:, cols] = jnp.sum(d_pre_b.astype(F32), 0, keepdims=True)
        d_up(c // 256, mm(mlp_t, d_pre_b))
        d_down(c, mm(act[:, cols].astype(F32).T.astype(BF), g_b))
        term = mm(d_pre_b, w_up[:, cols], 1, 1)
        total = term if total is None else total + term
    return total


def pack_up(out, row):
    def put(c, value):
        for p in range(8):
            out[p, row + 64 * c : row + 64 * (c + 1), :] = value[64 * p : 64 * (p + 1)].astype(BF)

    return put


def pack_down(out, row):
    def put(c, value):
        for half in range(2):
            for k in range(2):
                out[c // 128 + k, row + 128 * half : row + 128 * (half + 1), :] = value[
                    128 * k : 128 * (k + 1), 256 * half : 256 * (half + 1)
                ].astype(BF)

    return put


def pack_qkv(out, row):
    def put(e, value):
        for p in range(8):
            out[p, row + 64 * e : row + 64 * (e + 1), :] = value[64 * p : 64 * (p + 1)].astype(BF)

    return put


def own_ctx(t, recv):
    full = jnp.concatenate([gather_ctx(recv, s) for s in range(2)], 1)
    return jnp.where(t == 0, full[0:256], full[256:512])


def pack_out(out, row, ctx, upstream):
    value = mm(ctx, upstream)
    for p in range(8):
        for half in range(2):
            out[p, row + 32 * half : row + 32 * (half + 1), :] = value[
                32 * p : 32 * (p + 1), 256 * half : 256 * (half + 1)
            ].astype(BF)


def first_body(
    at, pos, freqs, x, gain, bias, w_qkv, b_qkv, w_up, b_up, w_down, w_out,
    send, pair, act, slope, cs,
):
    pair[256:512] = w_out[...]
    for s in range(2):
        p = pos[s : s + 1, :].astype(F32)
        angle = freqs[...] * p
        cs[s, 0] = jnp.cos(angle)
        cs[s, 1] = jnp.sin(angle)
    normed, _ = norm_rows(x[...])
    attn_in = (normed * gain[0, 0:1] + bias[0, 0:1]).astype(BF)
    mlp_in = (normed * gain[0, 1:2] + bias[0, 1:2]).astype(BF)
    send_qkv(send, attn_in, w_qkv, b_qkv, 0, cs)
    row = lax.broadcasted_iota(jnp.int32, (16, BLK), 0)
    token = at[0] * BLK + lax.broadcasted_iota(jnp.int32, (1, BLK), 1)
    for s in range(2):
        start = jnp.maximum(token - pos[s : s + 1, :], 0)
        high = (start // 8).astype(F32)
        low = (start % 8).astype(F32)
        block = jnp.where(row == 0, high, jnp.where(row == 1, low, 0.0)).astype(BF)
        for h in range(4):
            send[s * 4 + h, 3 * HEAD : 3 * HEAD + 16, :] = block
    pair[0:256] = feed_forward(mlp_in, w_up, b_up, 0, w_down, act, slope).astype(BF)


def load_rows(recv, lo, hi):
    return jnp.concatenate([recv[i, lo:hi, :] for i in range(8)], 1)


def starts_of(recv):
    rows = load_rows(recv, 3 * HEAD, 3 * HEAD + 16).astype(F32)
    return rows[0:1] * 8.0 + rows[1:2]


def visible_of(start, c, length):
    key = lax.broadcasted_iota(jnp.int32, (length, CHUNK), 0)
    query = lax.broadcasted_iota(jnp.int32, (length, CHUNK), 1) + c * CHUNK
    return (key <= query) & (key >= start[:, c * CHUNK : (c + 1) * CHUNK])


def attend_body(recv, send, lse, ctx, start_out):
    q = load_rows(recv, 0, HEAD)
    k_t = load_rows(recv, HEAD, 2 * HEAD)
    v_t = load_rows(recv, 2 * HEAD, 3 * HEAD)
    k = k_t.astype(F32).T.astype(BF)
    start = starts_of(recv).astype(jnp.int32)
    start_out[...] = start
    for c in range(4):
        cols = slice(c * CHUNK, (c + 1) * CHUNK)
        length = (c + 1) * CHUNK
        scores = mm(k[:length], q[:, cols])
        scores = jnp.where(visible_of(start, c, length), scores, NEG)
        peak = jnp.max(scores, 0, keepdims=True)
        shifted = jnp.exp(scores - peak)
        total = jnp.sum(shifted, 0, keepdims=True)
        lse[:, cols] = peak + jnp.log(total)
        out = mm(v_t[:, :length], shifted.astype(BF)) / total
        ctx[:, cols] = out
        for i in range(CHUNK // BLK):
            block = out[:, i * BLK : (i + 1) * BLK].astype(BF)
            for t in range(2):
                send[c * (CHUNK // BLK) + i, t] = block


def attend_both_body(recv, start, _, send, dk, dv):
    q = load_rows(recv, 0, HEAD)
    k_t = load_rows(recv, HEAD, 2 * HEAD)
    v_t = load_rows(recv, 2 * HEAD, 3 * HEAD)
    d_ctx = load_rows(recv, 3 * HEAD, 4 * HEAD)
    k = k_t.astype(F32).T.astype(BF)
    v = v_t.astype(F32).T.astype(BF)
    dk[...] = jnp.zeros_like(dk)
    dv[...] = jnp.zeros_like(dv)
    for c in range(4):
        cols = slice(c * CHUNK, (c + 1) * CHUNK)
        length = (c + 1) * CHUNK
        scores = mm(k[:length], q[:, cols])
        scores = jnp.where(visible_of(start[...], c, length), scores, NEG)
        peak = jnp.max(scores, 0, keepdims=True)
        shifted = jnp.exp(scores - peak)
        probs = shifted * (1.0 / jnp.sum(shifted, 0, keepdims=True))
        probs_b = probs.astype(BF)
        out = mm(v_t[:, :length], probs_b)
        dq = backward_chunk(q, k_t, v, d_ctx, probs, probs_b, out, cols, length, dk, dv)
        for i in range(CHUNK // BLK):
            b = c * (CHUNK // BLK) + i
            for t in range(2):
                send[b, t, 0:HEAD] = out[:, i * BLK : (i + 1) * BLK].astype(BF)
                send[b, t, HEAD : 2 * HEAD] = dq[:, i * BLK : (i + 1) * BLK].astype(BF)
    put_kv(send, dk, dv, 2 * HEAD)


def backward_chunk(q, k_t, v, d_ctx, probs, probs_b, out, cols, length, dk, dv):
    d_out = d_ctx[:, cols]
    d_probs = mm(v[:length], d_out)
    delta = jnp.sum(d_out.astype(F32) * out, 0, keepdims=True)
    d_scores = (probs * (d_probs - delta)).astype(BF)
    dk[:, :length] += mm(q[:, cols], d_scores, 1, 1)
    dv[:, :length] += mm(d_out, probs_b, 1, 1)
    return mm(k_t[:, :length], d_scores) * (HEAD**-0.5)


def put_kv(send, dk, dv, row):
    for b in range(8):
        for t in range(2):
            send[b, t, row : row + HEAD] = dk[:, b * BLK : (b + 1) * BLK].astype(BF)
            send[b, t, row + HEAD : row + 2 * HEAD] = dv[:, b * BLK : (b + 1) * BLK].astype(BF)


def attend_back_body(recv, recv_d, start, lse, ctx, _, send, dk, dv):
    ride = recv_d[0, 64:192].astype(F32)
    for i in range(1, 8):
        ride = ride + recv_d[i, 64:192].astype(F32)
    ride = ride.astype(BF)
    for b in range(8):
        for t in range(2):
            send[b, t, 192:320] = ride
    q = load_rows(recv, 0, HEAD)
    k_t = load_rows(recv, HEAD, 2 * HEAD)
    v_t = load_rows(recv, 2 * HEAD, 3 * HEAD)
    d_ctx = load_rows(recv_d, 0, HEAD)
    k = k_t.astype(F32).T.astype(BF)
    v = v_t.astype(F32).T.astype(BF)
    dk[...] = jnp.zeros_like(dk)
    dv[...] = jnp.zeros_like(dv)
    for c in range(4):
        cols = slice(c * CHUNK, (c + 1) * CHUNK)
        length = (c + 1) * CHUNK
        scores = mm(k[:length], q[:, cols])
        scores = jnp.where(visible_of(start[...], c, length), scores, NEG)
        probs = jnp.exp(scores - lse[:, cols])
        probs_b = probs.astype(BF)
        dq = backward_chunk(q, k_t, v, d_ctx, probs, probs_b, ctx[:, cols], cols, length, dk, dv)
        for i in range(CHUNK // BLK):
            for t in range(2):
                send[c * (CHUNK // BLK) + i, t, 0:HEAD] = dq[:, i * BLK : (i + 1) * BLK].astype(BF)
    put_kv(send, dk, dv, HEAD)


def gather_ctx(recv, s):
    return jnp.concatenate([recv[s * 4 + h, t, 0:HEAD, :] for t in range(2) for h in range(4)], 0)


def ordered(t, own, other):
    return jnp.where(t == 0, own, other), jnp.where(t == 0, other, own)


def out_other(others):
    halves = [
        jnp.concatenate([others[3, 64 * p + 32 * c : 64 * p + 32 * (c + 1), :] for p in range(8)], 0)
        for c in range(2)
    ]
    return jnp.concatenate(halves, 1)


def branch_of(t, recv, w_own, w_other):
    first, second = ordered(t, w_own, w_other)
    w = jnp.concatenate([first, second], 0)
    rows = []
    for s in range(2):
        rows.append(mm(gather_ctx(recv, s).astype(F32).T.astype(BF), w))
    return jnp.concatenate(rows, 0)


def middle_body(
    at, x, pair, pair_other, recv, w_out_own, out_bias, gain, bias,
    w_qkv, b_qkv, w_up, b_up, w_down, w_out, cot, cs,
    stream, send, grads, parts, d_b_up, d_sum, act, slope,
):
    branch = pair[0:256].astype(F32) + pair_other[0:256].astype(F32)
    branch = branch + branch_of(at[1], recv, w_out_own[...], pair_other[256:512])
    out = x[...] + branch + out_bias[0, 0:1] + out_bias[0, 1:2]
    stream[...] = out
    normed, _ = norm_rows(out)
    attn_in = (normed * gain[1, 0:1] + bias[1, 0:1]).astype(BF)
    mlp_in = (normed * gain[1, 1:2] + bias[1, 1:2]).astype(BF)
    send_qkv(send, attn_in, w_qkv, b_qkv, 1, cs)
    g_b = cot[...].astype(BF)
    d_ctx = mm(w_out[...], g_b, 1, 1)
    for s in range(2):
        for h in range(4):
            send[s * 4 + h, 3 * HEAD : 4 * HEAD, :] = d_ctx[
                h * HEAD : (h + 1) * HEAD, s * BLK : (s + 1) * BLK
            ].astype(BF)
    d_sum[...] = jnp.sum(cot[...], 0, keepdims=True)
    parts[0:256] = feed_forward(mlp_in, w_up, b_up, 1, w_down, act, slope).astype(BF)
    parts[256:512] = feed_back(
        g_b, act, slope, mlp_in, w_up, w_down, pack_up(grads, 0), pack_down(grads, 256), d_b_up
    ).astype(BF)


def norm_back(
    t, x, g, d_mlp_in, recv, row, w_own, others, cs, gain, bias, layer, d_qkv, d_b_qkv, d_norm
):
    normed, inv = norm_rows(x)
    attn_in = (normed * gain[layer, 0:1] + bias[layer, 0:1]).astype(BF)
    attn_t = attn_in.astype(F32).T.astype(BF)
    d_attn_t = None
    for e in range(3):
        halves = []
        for tt in range(2):
            blocks = []
            for h in range(4):
                pieces = []
                for s in range(2):
                    lo = row + e * HEAD
                    u = recv[s * 4 + h, tt, lo : lo + HEAD, :]
                    if e < 2:
                        u = turn_back(u.astype(F32), cs[s, 0], cs[s, 1]).astype(BF)
                    pieces.append(u)
                blocks.append(jnp.concatenate(pieces, 1))
            halves.append(jnp.concatenate(blocks, 0))
        first, second = ordered(t, w_own[e], others[e])
        term = mm(first, halves[0]) + mm(second, halves[1])
        d_attn_t = term if d_attn_t is None else d_attn_t + term
        own = jnp.where(t == 0, halves[0], halves[1])
        d_qkv(e, mm(attn_t, own, 1, 1))
        d_b_qkv[e : e + 1] = mm(jnp.ones((8, own.shape[1]), BF), own, 1, 1)[0:1]
    d_attn_in = d_attn_t.T
    d_norm[0:1] = jnp.sum(d_attn_in * normed, 0, keepdims=True)
    d_norm[1:2] = jnp.sum(d_mlp_in * normed, 0, keepdims=True)
    d_norm[2:3] = jnp.sum(d_attn_in, 0, keepdims=True)
    d_norm[3:4] = jnp.sum(d_mlp_in, 0, keepdims=True)
    d_normed = d_attn_in * gain[layer, 0:1] + d_mlp_in * gain[layer, 1:2]
    return g + inv * (
        d_normed
        - jnp.mean(d_normed, -1, keepdims=True)
        - normed * jnp.mean(d_normed * normed, -1, keepdims=True)
    )


def turn_point_body(
    at, stream, parts, parts_other, recv, w_out, w_qkv, others, out_bias,
    gain, bias, cot, cs, x, act, slope, w_up, w_down, w_out_first, recv_first, sums_a,
    block_out, g_out, send, grads, part, d_b_up, d_b_qkv, d_norm, d_sum,
):
    t = at[1]
    branch = parts[0:256].astype(F32) + parts_other[0:256].astype(F32)
    branch = branch + branch_of(t, recv, w_out[...], out_other(others))
    block_out[...] = stream[...] + branch + out_bias[1, 0:1] + out_bias[1, 1:2]
    d_mlp_in = parts[256:512].astype(F32) + parts_other[256:512].astype(F32)
    g = norm_back(
        t, stream[...], cot[...], d_mlp_in, recv, HEAD, w_qkv, others, cs, gain, bias, 1,
        pack_qkv(grads, 0), d_b_qkv, d_norm,
    )
    g_out[...] = g
    g_b = g.astype(BF)
    d_sum[...] = jnp.sum(g, 0, keepdims=True)
    d_ctx = mm(w_out_first[...], g_b, 1, 1)
    for s in range(2):
        for h in range(4):
            send[s * 4 + h, 0:HEAD] = d_ctx[
                h * HEAD : (h + 1) * HEAD, s * BLK : (s + 1) * BLK
            ].astype(BF)
    for q in range(8):
        for c in range(2):
            send[q, 64 + 64 * c : 128 + 64 * c] = sums_a[
                64 * q : 64 * (q + 1), BLK * c : BLK * (c + 1)
            ]
    pack_out(grads, 704, own_ctx(t, recv), cot[...].astype(BF))
    pack_out(grads, 768, own_ctx(t, recv_first), g_b)
    normed, _ = norm_rows(x[...])
    mlp_in = (normed * gain[0, 1:2] + bias[0, 1:2]).astype(BF)
    part[...] = feed_back(
        g_b, act, slope, mlp_in, w_up, w_down, pack_up(grads, 192), pack_down(grads, 448), d_b_up
    ).astype(BF)


def last_body(
    at, x, g, part, part_other, recv, w_qkv, others, cs, gain, bias,
    d_b_up0, d_b_up1, d_b_qkv1, d_norm1, d_sum0, d_sum1,
    in_grad, grads, sums_a, d_b_qkv0, d_norm0,
):
    d_mlp_in = part[...].astype(F32) + part_other[...].astype(F32)
    in_grad[...] = norm_back(
        at[1], x[...], g[...], d_mlp_in, recv, 0, w_qkv, others, cs, gain, bias, 0,
        pack_qkv(grads, 0), d_b_qkv0, d_norm0,
    )
    for q in range(8):
        both_planes = recv[q, :, 192:320]
        block = jnp.where(at[1] == 0, both_planes[0], both_planes[1])
        for c in range(2):
            sums_a[64 * q : 64 * (q + 1), BLK * c : BLK * (c + 1)] = block[64 * c : 64 * (c + 1)]

    def lanes(ref, row, count):
        return [ref[row : row + 1, 256 * c : 256 * (c + 1)] for c in range(count)]

    def norms(ref):
        return [v for r in range(4) for v in lanes(ref, r, 2)]

    rows = [
        lanes(d_b_up0, 0, 4)
        + lanes(d_b_up1, 0, 4)
        + [v for e in range(3) for ref in (d_b_qkv0, d_b_qkv1) for v in lanes(ref, e, 1)],
        lanes(d_sum0, 0, 2) + lanes(d_sum1, 0, 2) + norms(d_norm0),
        norms(d_norm1),
    ]
    for p in range(8):
        have = rows[p] if p < len(rows) else []
        fill = [jnp.zeros((16 - len(have), 256), F32)]
        grads[p, 192:208, :] = jnp.concatenate(have + fill, 0).astype(BF)


def chunk_body(at, w_qkv, w_out, out):
    for layer in range(2):
        for e in range(3):
            out[layer, e] = w_qkv[layer, e]
        out[layer, 3, 0:32] = w_out[layer, :, 0:256]
        out[layer, 3, 32:64] = w_out[layer, :, 256:512]


def chunk_of(at, wq, w_out):
    return pl.pallas_call(
        chunk_body,
        out_shape=jax.ShapeDtypeStruct((2, 4, 64, 256), BF),
        grid_spec=pltpu.PrefetchScalarGridSpec(
            num_scalar_prefetch=1,
            grid=(1,),
            in_specs=[
                pl.BlockSpec((2, 3, 64, 256), lambda i, at: (0, 0, at[2], 0)),
                pl.BlockSpec((2, 32, 512), lambda i, at: (0, at[2], 0)),
            ],
            out_specs=pl.BlockSpec((2, 4, 64, 256), lambda i, at: (0, 0, 0, 0)),
        ),
        compiler_params=pltpu.CompilerParams(vmem_limit_bytes=63 * 1024 * 1024),
        name="chunk",
    )(at, wq, w_out)


def hand_on_body(value, _, out):
    out[...] = value[...]


def mix_body(got, early, first, out, first_out):
    total = got[0].astype(F32)
    for i in range(1, 8):
        total = total + got[i].astype(F32)
    for q in range(8):
        mine = [early[104 * q : 104 * (q + 1)].astype(F32), total[24 * q : 24 * (q + 1)]]
        out[q, 0:128] = jnp.concatenate(mine, 0).astype(BF)
        out[q, 128:144] = total[192:208].astype(BF) if q == 0 else jnp.zeros((16, 256), BF)
    first_out[...] = first[...]


def sum_body(got, out):
    total = got[0].astype(F32)
    for i in range(1, 8):
        total = total + got[i].astype(F32)
    for q in range(8):
        out[q] = total.astype(BF)


def unpack_first_body(first, g_up, g_down):
    for k in range(2):
        for c in range(4):
            cols = slice(256 * c, 256 * (c + 1))
            g_up[0, 64 * k : 64 * (k + 1), cols] = first[k, 64 * c : 64 * (c + 1)].astype(F32)
        for c in range(2):
            rows = first[k, 256 + 128 * c : 256 + 128 * (c + 1)]
            cols = slice(256 * c, 256 * (c + 1))
            g_down[0, 128 * k : 128 * (k + 1), cols] = rows.astype(F32)


def unpack_rest_body(rest, _, __, g_up, g_down, g_qkv, g_out, g_b_up, g_b_qkv, g_sum, g_gain, g_bias):
    p = pl.program_id(0)
    for k in range(2):
        for q in range(8):
            block = rest[k, q, 0:128].astype(F32)
            for i in range(16):
                value = block[8 * i : 8 * (i + 1)]
                row = 104 * q + 8 * i
                if i >= 13:
                    row = 24 * q + 8 * (i - 13)
                    r = 64 * k + row % 64
                    g_qkv[0, row // 64, r : r + 8] = value
                elif row < 192:
                    r = 64 * k + row % 64
                    g_qkv[1, row // 64, r : r + 8] = value
                elif row < 448:
                    c, r = divmod(row - 192, 64)
                    r += 64 * k
                    g_up[0, r : r + 8, 256 * c : 256 * (c + 1)] = value
                elif row < 704:
                    c, r = divmod(row - 448, 128)
                    r += 128 * k
                    g_down[0, r : r + 8, 256 * c : 256 * (c + 1)] = value
                else:
                    c, r = divmod((row - 704) % 64, 32)
                    r += 32 * k
                    g_out[1 - (row - 704) // 64, r : r + 8, 256 * c : 256 * (c + 1)] = value

    tiny = [rest[k, 0, 128:144].astype(F32) for k in range(2)]

    @pl.when(p == 0)
    def _():
        for layer in range(2):
            for c in range(4):
                r = 4 * layer + c
                g_b_up[layer : layer + 1, 256 * c : 256 * (c + 1)] = tiny[0][r : r + 1]
        for e in range(3):
            for layer in range(2):
                r = 8 + 2 * e + layer
                g_b_qkv[e, layer : layer + 1, :] = tiny[0][r : r + 1]
        for layer in range(2):
            for c in range(2):
                r = 2 * layer + c
                for which in range(2):
                    g_sum[layer, which : which + 1, 256 * c : 256 * (c + 1)] = tiny[1][r : r + 1]

    def norms(layer, rows, base):
        for which in range(2):
            for c in range(2):
                cols = slice(256 * c, 256 * (c + 1))
                r = base + 2 * which + c
                g_gain[layer, which : which + 1, cols] = rows[r : r + 1]
                g_bias[layer, which : which + 1, cols] = rows[r + 4 : r + 5]

    @pl.when(p == 0)
    def _():
        norms(0, tiny[1], 4)

    @pl.when(p == 1)
    def _():
        norms(1, tiny[0], 0)


UP = (2, 512, 1024)
DOWN = (2, 1024, 512)


def unpack(first, rest):
    def place(layer):
        return [
            pl.BlockSpec((1, 128, 1024), lambda p: (layer, p, 0)),
            pl.BlockSpec((1, 256, 512), lambda p: (layer, p, 0)),
        ]

    params = pltpu.CompilerParams(vmem_limit_bytes=63 * 1024 * 1024)
    g_up, g_down = pl.pallas_call(
        unpack_first_body,
        grid=(4,),
        out_shape=[jax.ShapeDtypeStruct(UP, F32), jax.ShapeDtypeStruct(DOWN, F32)],
        in_specs=[pl.BlockSpec((2, 512, 256), lambda p: (p, 0, 0))],
        out_specs=place(1),
        compiler_params=params,
        name="unpack_first",
    )(first)
    outs = [
        ((2, 3, 512, 256), pl.BlockSpec((2, 3, 128, 256), lambda p: (0, 0, p, 0))),
        ((2, 256, 512), pl.BlockSpec((2, 64, 512), lambda p: (0, p, 0))),
        ((2, 1024), whole((2, 1024))),
        ((3, 2, 256), whole((3, 2, 256))),
        ((2, 2, 512), whole((2, 2, 512))),
        ((2, 2, 512), whole((2, 2, 512))),
        ((2, 2, 512), whole((2, 2, 512))),
    ]
    return pl.pallas_call(
        unpack_rest_body,
        grid=(4,),
        out_shape=[jax.ShapeDtypeStruct(shape, F32) for shape in [UP, DOWN] + [o[0] for o in outs]],
        in_specs=[
            pl.BlockSpec((2, 8, 144, 256), lambda p: (p, 0, 0, 0)),
            pl.BlockSpec(memory_space=pl.ANY),
            pl.BlockSpec(memory_space=pl.ANY),
        ],
        out_specs=place(0) + [spec for _, spec in outs],
        input_output_aliases={1: 0, 2: 1},
        compiler_params=params,
        name="unpack_rest",
    )(rest, g_up, g_down)


def swap(value):
    return lax.ppermute(value, "tensor", [(0, 1), (1, 0)])


def exchange(value, axes):
    return lax.all_to_all(value, axes, 0, 0)


def both(value):
    flat = value.reshape((16,) + value.shape[2:])
    return exchange(flat, ("context", "tensor")).reshape(value.shape)


def shards(
    tokens_in, cotangent, positions, w_qkv, b_qkv, w_out, w_up, b_up, w_down, out_bias, ln_gain, ln_bias
):
    rows, width = 256, 512
    x = tokens_in.reshape(rows, width)
    cot = cotangent.reshape(rows, width)
    wq = jnp.transpose(w_qkv, (0, 2, 1, 3))
    bq = jnp.transpose(b_qkv, (1, 0, 2))
    at = jnp.stack(
        [lax.axis_index("context"), lax.axis_index("tensor"), lax.axis_index("dp")]
    ).astype(jnp.int32)
    freqs = jnp.asarray(FREQS).reshape(HALF, 1)
    chunk = swap(chunk_of(at, wq, w_out))
    send, pair, act, slope, cs = call(
        first_body,
        [
            ((8, 208, BLK), BF),
            ((2 * rows, width), BF),
            ((rows, 1024), BF),
            ((rows, 1024), F32),
            ((2, 2, HALF, BLK), F32),
        ],
        (
            at, positions, freqs, x, ln_gain, ln_bias, Layer(wq, 0), bq, Layer(w_up, 0), b_up,
            Layer(w_down, 0), Layer(w_out, 0),
        ),
        "norm_qkv_feed",
        smem_first=True,
    )
    pair_other = swap(pair)
    (chunk,) = call(hand_on_body, [(chunk.shape, BF)], (chunk, After(send)), "hand_on")
    others = lax.all_gather(chunk, "dp", axis=2, tiled=True)
    recv = exchange(send, "context")
    ctx_send, lse, ctx, start = call(
        attend_body,
        [((8, 2, HEAD, BLK), BF), ((1, 1024), F32), ((HEAD, 1024), F32), ((1, 1024), jnp.int32)],
        (recv,),
        "attend",
    )
    recv_ctx = both(ctx_send)
    stream, send, grads_a, parts, d_b_up1, d_sum1 = call(
        middle_body,
        [
            ((rows, width), F32),
            ((8, 256, BLK), BF),
            ((8, 512, 256), BF),
            ((2 * rows, width), BF),
            ((1, 1024), F32),
            ((1, width), F32),
        ],
        (
            at, x, pair, pair_other, recv_ctx, Layer(w_out, 0), out_bias, ln_gain, ln_bias,
            Layer(wq, 1), bq, Layer(w_up, 1), b_up, Layer(w_down, 1), Layer(w_out, 1), cot, cs,
        ),
        "middle",
        scratch=[pltpu.VMEM((rows, 1024), BF), pltpu.VMEM((rows, 1024), F32)],
        smem_first=True,
    )
    sums_a = lax.psum_scatter(grads_a, "dp", scatter_dimension=0)
    parts_other = swap(parts)
    recv_both = exchange(send, "context")
    (both_send,) = call(
        attend_both_body,
        [((8, 2, 256, BLK), BF)],
        (recv_both, start, After(parts_other)),
        "attend_both",
        scratch=[pltpu.VMEM((HEAD, 1024), F32), pltpu.VMEM((HEAD, 1024), F32)],
    )
    recv_grad = both(both_send)
    block_out, g, send, grads_b, part_g, d_b_up0, d_b_qkv1, d_norm1, d_sum0 = call(
        turn_point_body,
        [
            ((rows, width), F32),
            ((rows, width), F32),
            ((8, 192, BLK), BF),
            ((8, 832, 256), BF),
            ((rows, width), BF),
            ((1, 1024), F32),
            ((3, 256), F32),
            ((4, width), F32),
            ((1, width), F32),
        ],
        (
            at, stream, parts, parts_other, recv_grad, Layer(w_out, 1), Layer(wq, 1), Layer(others, 1),
            out_bias, ln_gain, ln_bias, cot, cs, x, act, slope, Layer(w_up, 0), Layer(w_down, 0),
            Layer(w_out, 0), recv_ctx, sums_a,
        ),
        "turn_point",
        smem_first=True,
    )
    sums_b = lax.psum_scatter(grads_b, "dp", scatter_dimension=0)
    part_g_other = swap(part_g)
    recv_d = exchange(send, "context")
    (back_send,) = call(
        attend_back_body,
        [((8, 2, 320, BLK), BF)],
        (recv, recv_d, start, lse, ctx, After(part_g_other)),
        "attend_back",
        scratch=[pltpu.VMEM((HEAD, 1024), F32), pltpu.VMEM((HEAD, 1024), F32)],
    )
    recv_grad0 = both(back_send)
    in_grad, grads_c, sums_a, _, _ = call(
        last_body,
        [
            ((rows, width), F32),
            ((8, 208, 256), BF),
            ((512, 256), BF),
            ((3, 256), F32),
            ((4, width), F32),
        ],
        (
            at, x, g, part_g, part_g_other, recv_grad0, Layer(wq, 0), Layer(others, 0), cs,
            ln_gain, ln_bias, d_b_up0, d_b_up1, d_b_qkv1, d_norm1, d_sum0, d_sum1,
        ),
        "last",
        smem_first=True,
    )
    mixed, sums_a = call(
        mix_body,
        [((8, 144, 256), BF), ((512, 256), BF)],
        (exchange(grads_c, "dp"), sums_b, sums_a),
        "mix",
    )
    full_a = lax.all_gather(sums_a, "dp")
    (summed,) = call(sum_body, [((8, 144, 256), BF)], (exchange(mixed, "context"),), "sum")
    full_bc = lax.all_gather(exchange(summed, "context"), "dp")
    g_up, g_down, g_qkv, g_out, g_b_up, g_b_qkv, g_sum, g_gain, g_bias = unpack(full_a, full_bc)
    return (
        block_out.reshape(tokens_in.shape),
        in_grad.reshape(tokens_in.shape),
        jnp.transpose(g_qkv, (0, 2, 1, 3)),
        jnp.transpose(g_b_qkv, (1, 0, 2)),
        g_out,
        g_up,
        g_b_up,
        g_down,
        g_sum,
        g_gain,
        g_bias,
    )


def solution(mesh):
    return jax.shard_map(
        shards,
        mesh=mesh,
        in_specs=(
            P("dp", "context", None),
            P("dp", "context", None),
            P("dp", "context"),
            P(None, None, None, "tensor"),
            P(None, None, "tensor"),
            P(None, "tensor", None),
            P(None, None, "tensor"),
            P(None, "tensor"),
            P(None, "tensor", None),
            P(),
            P(),
            P(),
        ),
        out_specs=(
            P("dp", "context", None),
            P("dp", "context", None),
            P(None, None, None, "tensor"),
            P(None, None, "tensor"),
            P(None, "tensor", None),
            P(None, None, "tensor"),
            P(None, "tensor"),
            P(None, "tensor", None),
            P(),
            P(),
            P(),
        ),
        check_vma=False,
    )
```

```python
from functools import partial

import numpy as np

import jax
import jax.numpy as jnp
from jax import lax
from jax.experimental import pallas as pl
from jax.experimental.pallas import tpu as pltpu
from jax.sharding import PartitionSpec as P

EPS = 1e-05
HALF = 8
HEAD = 64
BLK = 128
CHUNK = 256
NEG = -1e30
BF = jnp.bfloat16
F32 = jnp.float32

FREQS = (10000.0 ** (-np.arange(HALF, dtype=np.float64) * 2.0 / 16.0)).astype(np.float32)


def mm(a, b, ca=1, cb=0):
    return lax.dot_general(a, b, (((ca,), (cb,)), ((), ())), preferred_element_type=F32)


class After:
    def __init__(self, array):
        self.array = array

    def spec(self):
        return pl.BlockSpec(memory_space=pl.ANY)


class Layer:
    def __init__(self, array, index):
        self.array, self.index = array, index

    def spec(self):
        rest = self.array.shape[1:]
        place = (self.index,) + (0,) * len(rest)
        return pl.BlockSpec((None,) + rest, lambda i: place)


def whole(shape):
    return pl.BlockSpec(shape, lambda i: (0,) * len(shape))


class Fetch:
    def __init__(self, array, layer=None, rows=None, at=0):
        self.array, self.layer, self.rows, self.at = array, layer, rows, at
        shape = array.shape if layer is None else array.shape[1:]
        self.shape = shape if rows is None else shape[:-2] + (rows, shape[-1])

    def spec(self):
        return pl.BlockSpec(memory_space=pl.ANY)

    def source(self, ref):
        if self.layer is not None:
            ref = ref.at[self.layer]
        if self.rows is not None:
            place = (slice(None),) * (len(self.shape) - 2) + (pl.ds(self.at * self.rows, self.rows),)
            ref = ref.at[place]
        return ref


class Lazy:
    def __init__(self, ref, copy):
        self.ref, self.copy, self.shape = ref, copy, ref.shape

    def __getitem__(self, index):
        if self.copy is not None:
            self.copy.wait()
            self.copy = None
        return self.ref[index]


class Store:
    def __init__(self, shape, dtype):
        self.shape, self.dtype = shape, dtype


class Out:
    def __init__(self, ref, target, sems, copies):
        self.ref, self.target, self.sems, self.copies, self.done = ref, target, sems, copies, False

    def __setitem__(self, index, value):
        self.ref[index] = value

    def __getitem__(self, index):
        return self.ref[index]

    def flush(self, *place):
        source, target = self.ref, self.target
        if place:
            source, target = source.at[place], target.at[place]
        copy = pltpu.make_async_copy(source, target, self.sems.at[len(self.copies)])
        copy.start()
        self.copies.append(copy)
        self.done = True


FLUSHES = 40


def flush(ref, *place):
    if isinstance(ref, Out):
        ref.flush(*place)


def call(body, out_shape, args, name, scratch=(), smem_first=False):
    own = (Layer, After, Fetch)
    specs = [a.spec() if isinstance(a, own) else whole(a.shape) for a in args]
    fetched = [i for i, a in enumerate(args) if isinstance(a, Fetch)]
    stored = [i for i, o in enumerate(out_shape) if isinstance(o, Store)]
    plans = list(args)
    arrays = [a.array if isinstance(a, own) else a for a in args]
    shapes = [(o.shape, o.dtype) if isinstance(o, Store) else o for o in out_shape]
    if smem_first:
        specs[0] = pl.BlockSpec(memory_space=pltpu.SMEM)
    buffers = [pltpu.VMEM(plans[i].shape, arrays[i].dtype) for i in fetched]
    buffers += [pltpu.VMEM(*shapes[i]) for i in stored]
    sems = []
    if fetched:
        sems.append(pltpu.SemaphoreType.DMA((len(fetched),)))
    if stored:
        sems.append(pltpu.SemaphoreType.DMA((FLUSHES,)))
    n_in, n_out, n_scratch = len(args), len(out_shape), len(scratch)

    def run(*refs):
        ins, outs = list(refs[:n_in]), list(refs[n_in : n_in + n_out])
        rest = list(refs[n_in + n_out :])
        mine, rest = rest[:n_scratch], rest[n_scratch:]
        for k, i in enumerate(fetched):
            copy = pltpu.make_async_copy(
                plans[i].source(ins[i]), rest[k], rest[len(buffers)].at[k]
            )
            copy.start()
            ins[i] = Lazy(rest[k], copy)
        copies = []
        for k, i in enumerate(stored):
            outs[i] = Out(rest[len(fetched) + k], outs[i], rest[-1], copies)
        body(*ins, *outs, *mine)
        for i in fetched:
            if ins[i].copy is not None:
                ins[i].copy.wait()
        for i in stored:
            if not outs[i].done:
                outs[i].flush()
        for copy in copies:
            copy.wait()

    return pl.pallas_call(
        run,
        grid=(1,),
        out_shape=[jax.ShapeDtypeStruct(s, d) for s, d in shapes],
        in_specs=specs,
        out_specs=[
            pl.BlockSpec(memory_space=pl.ANY) if isinstance(o, Store) else whole(o[0])
            for o in out_shape
        ],
        scratch_shapes=list(scratch) + buffers + sems,
        compiler_params=pltpu.CompilerParams(vmem_limit_bytes=63 * 1024 * 1024),
        name=name,
    )(*arrays)


def norm_rows(x):
    mean = jnp.mean(x, -1, keepdims=True)
    cen = x - mean
    inv = lax.rsqrt(jnp.mean(cen * cen, -1, keepdims=True) + EPS)
    return cen * inv, inv


def turn(t, cos, sin):
    a, b = t[:HALF], t[HALF : 2 * HALF]
    return jnp.concatenate([a * cos - b * sin, b * cos + a * sin, t[2 * HALF :]], 0)


def turn_back(u, cos, sin):
    a, b = u[:HALF], u[HALF : 2 * HALF]
    return jnp.concatenate([a * cos + b * sin, b * cos - a * sin, u[2 * HALF :]], 0)


def send_qkv(send, attn_in, w_qkv, b_qkv, layer, cs):
    for e in range(3):
        turned = (mm(attn_in, w_qkv[e]) + b_qkv[e, layer : layer + 1]).T
        for s in range(2):
            cos, sin = cs[s, 0], cs[s, 1]
            for h in range(4):
                j = s * 4 + h
                part = turned[h * HEAD : (h + 1) * HEAD, s * BLK : (s + 1) * BLK]
                if e < 2:
                    part = turn(part, cos, sin)
                if e == 0:
                    part = part * (HEAD**-0.5)
                send[j, e * HEAD : (e + 1) * HEAD, :] = part.astype(BF)


def feed_forward(mlp_in, w_up, b_up, layer, w_down, act, slope):
    width = w_up.shape[1]
    total = None
    for c in range(0, width, 256):
        cols = slice(c, c + 256)
        pre = mm(mlp_in, w_up[:, cols]) + b_up[layer : layer + 1, cols]
        cdf = 0.5 + 0.5 * lax.erf(pre * np.float32(0.7071067811865476))
        a = (pre * cdf).astype(BF)
        act[:, cols] = a
        tail = pre * (jnp.exp(-0.5 * pre * pre) * np.float32(0.3989422804014327))
        slope[:, cols] = (cdf + tail).astype(BF)
        flush(act, slice(None), cols)
        flush(slope, slice(None), cols)
        term = mm(a, w_down[cols, :])
        total = term if total is None else total + term
    return total


def feed_back(g_b, act, slope, mlp_in, w_up, w_down, d_up, d_down, d_b_up):
    width = w_up.shape[1]
    total = None
    mlp_t = mlp_in.astype(F32).T.astype(BF)
    for c in range(0, width, 256):
        cols = slice(c, c + 256)
        d_act = mm(g_b, w_down[cols, :], 1, 1)
        d_pre = d_act * slope[:, cols].astype(F32)
        d_pre_b = d_pre.astype(BF)
        d_b_up[:, cols] = jnp.sum(d_pre_b.astype(F32), 0, keepdims=True)
        d_up(c // 256, mm(mlp_t, d_pre_b))
        d_down(c, mm(act[:, cols].astype(F32).T.astype(BF), g_b))
        term = mm(d_pre_b, w_up[:, cols], 1, 1)
        total = term if total is None else total + term
    return total


def pack_up(out, row):
    def put(c, value):
        for p in range(8):
            out[p, row + 64 * c : row + 64 * (c + 1), :] = value[64 * p : 64 * (p + 1)].astype(BF)
        flush(out, slice(None), slice(row + 64 * c, row + 64 * (c + 1)))

    return put


def pack_down(out, row):
    def put(c, value):
        for half in range(2):
            for k in range(2):
                out[c // 128 + k, row + 128 * half : row + 128 * (half + 1), :] = value[
                    128 * k : 128 * (k + 1), 256 * half : 256 * (half + 1)
                ].astype(BF)
        flush(out, slice(c // 128, c // 128 + 2), slice(row, row + 256))

    return put


def pack_qkv(out, row):
    def put(e, value):
        for p in range(8):
            out[p, row + 64 * e : row + 64 * (e + 1), :] = value[64 * p : 64 * (p + 1)].astype(BF)
        flush(out, slice(None), slice(row + 64 * e, row + 64 * (e + 1)))

    return put


def own_ctx(t, recv):
    full = jnp.concatenate([gather_ctx(recv, s) for s in range(2)], 1)
    return jnp.where(t == 0, full[0:256], full[256:512])


def pack_out(out, row, ctx, upstream):
    value = mm(ctx, upstream)
    for p in range(8):
        for half in range(2):
            out[p, row + 32 * half : row + 32 * (half + 1), :] = value[
                32 * p : 32 * (p + 1), 256 * half : 256 * (half + 1)
            ].astype(BF)
    flush(out, slice(None), slice(row, row + 64))


def first_body(
    at, pos, freqs, x, gain, bias, w_qkv, b_qkv, w_up, b_up, w_down, w_out,
    send, pair, act, slope, cs,
):

    for s in range(2):
        p = pos[s : s + 1, :].astype(F32)
        angle = freqs[...] * p
        cs[s, 0] = jnp.cos(angle)
        cs[s, 1] = jnp.sin(angle)
    normed, _ = norm_rows(x[...])
    attn_in = (normed * gain[0, 0:1] + bias[0, 0:1]).astype(BF)
    mlp_in = (normed * gain[0, 1:2] + bias[0, 1:2]).astype(BF)
    send_qkv(send, attn_in, w_qkv, b_qkv, 0, cs)
    row = lax.broadcasted_iota(jnp.int32, (16, BLK), 0)
    token = at[0] * BLK + lax.broadcasted_iota(jnp.int32, (1, BLK), 1)
    for s in range(2):
        start = jnp.maximum(token - pos[s : s + 1, :], 0)
        high = (start // 8).astype(F32)
        low = (start % 8).astype(F32)
        block = jnp.where(row == 0, high, jnp.where(row == 1, low, 0.0)).astype(BF)
        for h in range(4):
            send[s * 4 + h, 3 * HEAD : 3 * HEAD + 16, :] = block
    flush(send)
    pair[256:512] = w_out[...]
    pair[0:256] = feed_forward(mlp_in, w_up, b_up, 0, w_down, act, slope).astype(BF)


def load_rows(recv, lo, hi):
    return jnp.concatenate([recv[i, lo:hi, :] for i in range(8)], 1)


def starts_of(recv):
    rows = load_rows(recv, 3 * HEAD, 3 * HEAD + 16).astype(F32)
    return rows[0:1] * 8.0 + rows[1:2]


def visible_of(start, c, length):
    key = lax.broadcasted_iota(jnp.int32, (length, CHUNK), 0)
    query = lax.broadcasted_iota(jnp.int32, (length, CHUNK), 1) + c * CHUNK
    return (key <= query) & (key >= start[:, c * CHUNK : (c + 1) * CHUNK])


def attend_body(recv, send, lse, ctx, start_out):
    q = load_rows(recv, 0, HEAD)
    k_t = load_rows(recv, HEAD, 2 * HEAD)
    v_t = load_rows(recv, 2 * HEAD, 3 * HEAD)
    k = k_t.astype(F32).T.astype(BF)
    start = starts_of(recv).astype(jnp.int32)
    start_out[...] = start
    for c in range(4):
        cols = slice(c * CHUNK, (c + 1) * CHUNK)
        length = (c + 1) * CHUNK
        scores = mm(k[:length], q[:, cols])
        scores = jnp.where(visible_of(start, c, length), scores, NEG)
        peak = jnp.max(scores, 0, keepdims=True)
        shifted = jnp.exp(scores - peak)
        total = jnp.sum(shifted, 0, keepdims=True)
        lse[:, cols] = peak + jnp.log(total)
        out = mm(v_t[:, :length], shifted.astype(BF)) / total
        ctx[:, cols] = out
        for i in range(CHUNK // BLK):
            block = out[:, i * BLK : (i + 1) * BLK].astype(BF)
            for t in range(2):
                send[c * (CHUNK // BLK) + i, t] = block


def attend_both_body(recv, start, _, send, dk, dv):
    q = load_rows(recv, 0, HEAD)
    k_t = load_rows(recv, HEAD, 2 * HEAD)
    v_t = load_rows(recv, 2 * HEAD, 3 * HEAD)
    d_ctx = load_rows(recv, 3 * HEAD, 4 * HEAD)
    k = k_t.astype(F32).T.astype(BF)
    v = v_t.astype(F32).T.astype(BF)
    dk[...] = jnp.zeros_like(dk)
    dv[...] = jnp.zeros_like(dv)
    for c in range(4):
        cols = slice(c * CHUNK, (c + 1) * CHUNK)
        length = (c + 1) * CHUNK
        scores = mm(k[:length], q[:, cols])
        scores = jnp.where(visible_of(start[...], c, length), scores, NEG)
        peak = jnp.max(scores, 0, keepdims=True)
        shifted = jnp.exp(scores - peak)
        probs = shifted * (1.0 / jnp.sum(shifted, 0, keepdims=True))
        probs_b = probs.astype(BF)
        out = mm(v_t[:, :length], probs_b)
        dq = backward_chunk(q, k_t, v, d_ctx, probs, probs_b, out, cols, length, dk, dv)
        for i in range(CHUNK // BLK):
            b = c * (CHUNK // BLK) + i
            for t in range(2):
                send[b, t, 0:HEAD] = out[:, i * BLK : (i + 1) * BLK].astype(BF)
                send[b, t, HEAD : 2 * HEAD] = dq[:, i * BLK : (i + 1) * BLK].astype(BF)
    put_kv(send, dk, dv, 2 * HEAD)


def backward_chunk(q, k_t, v, d_ctx, probs, probs_b, out, cols, length, dk, dv):
    d_out = d_ctx[:, cols]
    d_probs = mm(v[:length], d_out)
    delta = jnp.sum(d_out.astype(F32) * out, 0, keepdims=True)
    d_scores = (probs * (d_probs - delta)).astype(BF)
    dk[:, :length] += mm(q[:, cols], d_scores, 1, 1)
    dv[:, :length] += mm(d_out, probs_b, 1, 1)
    return mm(k_t[:, :length], d_scores) * (HEAD**-0.5)


def put_kv(send, dk, dv, row):
    for b in range(8):
        for t in range(2):
            send[b, t, row : row + HEAD] = dk[:, b * BLK : (b + 1) * BLK].astype(BF)
            send[b, t, row + HEAD : row + 2 * HEAD] = dv[:, b * BLK : (b + 1) * BLK].astype(BF)


def attend_back_body(recv, recv_d, start, lse, ctx, _, send, dk, dv):
    ride = recv_d[0, 64:192].astype(F32)
    for i in range(1, 8):
        ride = ride + recv_d[i, 64:192].astype(F32)
    ride = ride.astype(BF)
    for b in range(8):
        for t in range(2):
            send[b, t, 192:320] = ride
    q = load_rows(recv, 0, HEAD)
    k_t = load_rows(recv, HEAD, 2 * HEAD)
    v_t = load_rows(recv, 2 * HEAD, 3 * HEAD)
    d_ctx = load_rows(recv_d, 0, HEAD)
    k = k_t.astype(F32).T.astype(BF)
    v = v_t.astype(F32).T.astype(BF)
    dk[...] = jnp.zeros_like(dk)
    dv[...] = jnp.zeros_like(dv)
    for c in range(4):
        cols = slice(c * CHUNK, (c + 1) * CHUNK)
        length = (c + 1) * CHUNK
        scores = mm(k[:length], q[:, cols])
        scores = jnp.where(visible_of(start[...], c, length), scores, NEG)
        probs = jnp.exp(scores - lse[:, cols])
        probs_b = probs.astype(BF)
        dq = backward_chunk(q, k_t, v, d_ctx, probs, probs_b, ctx[:, cols], cols, length, dk, dv)
        for i in range(CHUNK // BLK):
            for t in range(2):
                send[c * (CHUNK // BLK) + i, t, 0:HEAD] = dq[:, i * BLK : (i + 1) * BLK].astype(BF)
    put_kv(send, dk, dv, HEAD)


def gather_ctx(recv, s):
    return jnp.concatenate([recv[s * 4 + h, t, 0:HEAD, :] for t in range(2) for h in range(4)], 0)


def ordered(t, own, other):
    return jnp.where(t == 0, own, other), jnp.where(t == 0, other, own)


def out_other(others):
    halves = [
        jnp.concatenate([others[3, 64 * p + 32 * c : 64 * p + 32 * (c + 1), :] for p in range(8)], 0)
        for c in range(2)
    ]
    return jnp.concatenate(halves, 1)


def branch_of(t, recv, w_own, w_other):
    first, second = ordered(t, w_own, w_other)
    w = jnp.concatenate([first, second], 0)
    rows = []
    for s in range(2):
        rows.append(mm(gather_ctx(recv, s).astype(F32).T.astype(BF), w))
    return jnp.concatenate(rows, 0)


def middle_body(
    at, x, pair, pair_other, recv, w_out_own, out_bias, gain, bias,
    w_qkv, b_qkv, w_up, b_up, w_down, w_out, cot, cs,
    stream, send, grads, parts, d_b_up, d_sum, act, slope,
):
    branch = pair[0:256].astype(F32) + pair_other[0:256].astype(F32)
    branch = branch + branch_of(at[1], recv, w_out_own[...], pair_other[256:512])
    out = x[...] + branch + out_bias[0, 0:1] + out_bias[0, 1:2]
    stream[...] = out
    flush(stream)
    normed, _ = norm_rows(out)
    attn_in = (normed * gain[1, 0:1] + bias[1, 0:1]).astype(BF)
    mlp_in = (normed * gain[1, 1:2] + bias[1, 1:2]).astype(BF)
    send_qkv(send, attn_in, w_qkv, b_qkv, 1, cs)
    g_b = cot[...].astype(BF)
    d_ctx = mm(w_out[...], g_b, 1, 1)
    for s in range(2):
        for h in range(4):
            send[s * 4 + h, 3 * HEAD : 4 * HEAD, :] = d_ctx[
                h * HEAD : (h + 1) * HEAD, s * BLK : (s + 1) * BLK
            ].astype(BF)
    flush(send)
    d_sum[...] = jnp.sum(cot[...], 0, keepdims=True)
    parts[0:256] = feed_forward(mlp_in, w_up, b_up, 1, w_down, act, slope).astype(BF)
    parts[256:512] = feed_back(
        g_b, act, slope, mlp_in, w_up, w_down, pack_up(grads, 0), pack_down(grads, 256), d_b_up
    ).astype(BF)


def norm_back(
    t, x, g, d_mlp_in, recv, row, w_own, others, cs, gain, bias, layer, d_qkv, d_b_qkv, d_norm
):
    normed, inv = norm_rows(x)
    attn_in = (normed * gain[layer, 0:1] + bias[layer, 0:1]).astype(BF)
    attn_t = attn_in.astype(F32).T.astype(BF)
    d_attn_t = None
    for e in range(3):
        halves = []
        for tt in range(2):
            blocks = []
            for h in range(4):
                pieces = []
                for s in range(2):
                    lo = row + e * HEAD
                    u = recv[s * 4 + h, tt, lo : lo + HEAD, :]
                    if e < 2:
                        u = turn_back(u.astype(F32), cs[s, 0], cs[s, 1]).astype(BF)
                    pieces.append(u)
                blocks.append(jnp.concatenate(pieces, 1))
            halves.append(jnp.concatenate(blocks, 0))
        first, second = ordered(t, w_own[e], others[e])
        term = mm(first, halves[0]) + mm(second, halves[1])
        d_attn_t = term if d_attn_t is None else d_attn_t + term
        own = jnp.where(t == 0, halves[0], halves[1])
        d_qkv(e, mm(attn_t, own, 1, 1))
        d_b_qkv[e : e + 1] = mm(jnp.ones((8, own.shape[1]), BF), own, 1, 1)[0:1]
    d_attn_in = d_attn_t.T
    d_norm[0:1] = jnp.sum(d_attn_in * normed, 0, keepdims=True)
    d_norm[1:2] = jnp.sum(d_mlp_in * normed, 0, keepdims=True)
    d_norm[2:3] = jnp.sum(d_attn_in, 0, keepdims=True)
    d_norm[3:4] = jnp.sum(d_mlp_in, 0, keepdims=True)
    d_normed = d_attn_in * gain[layer, 0:1] + d_mlp_in * gain[layer, 1:2]
    return g + inv * (
        d_normed
        - jnp.mean(d_normed, -1, keepdims=True)
        - normed * jnp.mean(d_normed * normed, -1, keepdims=True)
    )


def turn_point_body(
    at, stream, parts, parts_other, recv, w_out, w_qkv, others, out_bias,
    gain, bias, cot, cs, x, act, slope, w_up, w_down, w_out_first, recv_first, sums_a,
    block_out, g_out, send, grads, part, d_b_up, d_b_qkv, d_norm, d_sum,
):
    t = at[1]
    branch = parts[0:256].astype(F32) + parts_other[0:256].astype(F32)
    branch = branch + branch_of(t, recv, w_out[...], out_other(others))
    block_out[...] = stream[...] + branch + out_bias[1, 0:1] + out_bias[1, 1:2]
    flush(block_out)
    d_mlp_in = parts[256:512].astype(F32) + parts_other[256:512].astype(F32)
    g = norm_back(
        t, stream[...], cot[...], d_mlp_in, recv, HEAD, w_qkv, others, cs, gain, bias, 1,
        pack_qkv(grads, 0), d_b_qkv, d_norm,
    )
    g_out[...] = g
    flush(g_out)
    g_b = g.astype(BF)
    d_sum[...] = jnp.sum(g, 0, keepdims=True)
    d_ctx = mm(w_out_first[...], g_b, 1, 1)
    for s in range(2):
        for h in range(4):
            send[s * 4 + h, 0:HEAD] = d_ctx[
                h * HEAD : (h + 1) * HEAD, s * BLK : (s + 1) * BLK
            ].astype(BF)
    for q in range(8):
        for c in range(2):
            send[q, 64 + 64 * c : 128 + 64 * c] = sums_a[
                64 * q : 64 * (q + 1), BLK * c : BLK * (c + 1)
            ]
    flush(send)
    pack_out(grads, 704, own_ctx(t, recv), cot[...].astype(BF))
    pack_out(grads, 768, own_ctx(t, recv_first), g_b)
    normed, _ = norm_rows(x[...])
    mlp_in = (normed * gain[0, 1:2] + bias[0, 1:2]).astype(BF)
    part[...] = feed_back(
        g_b, act, slope, mlp_in, w_up, w_down, pack_up(grads, 192), pack_down(grads, 448), d_b_up
    ).astype(BF)


def last_body(
    at, x, g, part, part_other, recv, w_qkv, others, cs, gain, bias,
    d_b_up0, d_b_up1, d_b_qkv1, d_norm1, d_sum0, d_sum1,
    in_grad, grads, sums_a, d_b_qkv0, d_norm0,
):
    d_mlp_in = part[...].astype(F32) + part_other[...].astype(F32)
    in_grad[...] = norm_back(
        at[1], x[...], g[...], d_mlp_in, recv, 0, w_qkv, others, cs, gain, bias, 0,
        pack_qkv(grads, 0), d_b_qkv0, d_norm0,
    )
    for q in range(8):
        both_planes = recv[q, :, 192:320]
        block = jnp.where(at[1] == 0, both_planes[0], both_planes[1])
        for c in range(2):
            sums_a[64 * q : 64 * (q + 1), BLK * c : BLK * (c + 1)] = block[64 * c : 64 * (c + 1)]

    def lanes(ref, row, count):
        return [ref[row : row + 1, 256 * c : 256 * (c + 1)] for c in range(count)]

    def norms(ref):
        return [v for r in range(4) for v in lanes(ref, r, 2)]

    rows = [
        lanes(d_b_up0, 0, 4)
        + lanes(d_b_up1, 0, 4)
        + [v for e in range(3) for ref in (d_b_qkv0, d_b_qkv1) for v in lanes(ref, e, 1)],
        lanes(d_sum0, 0, 2) + lanes(d_sum1, 0, 2) + norms(d_norm0),
        norms(d_norm1),
    ]
    for p in range(8):
        have = rows[p] if p < len(rows) else []
        fill = [jnp.zeros((16 - len(have), 256), F32)]
        grads[p, 192:208, :] = jnp.concatenate(have + fill, 0).astype(BF)
    flush(grads, slice(None), slice(192, 208))


def chunk_body(at, w_qkv, w_out, out):
    for layer in range(2):
        for e in range(3):
            out[layer, e] = w_qkv[layer, e]
        out[layer, 3, 0:32] = w_out[layer, :, 0:256]
        out[layer, 3, 32:64] = w_out[layer, :, 256:512]


def chunk_of(at, wq, w_out):
    return pl.pallas_call(
        chunk_body,
        out_shape=jax.ShapeDtypeStruct((2, 4, 64, 256), BF),
        grid_spec=pltpu.PrefetchScalarGridSpec(
            num_scalar_prefetch=1,
            grid=(1,),
            in_specs=[
                pl.BlockSpec((2, 3, 64, 256), lambda i, at: (0, 0, at[2], 0)),
                pl.BlockSpec((2, 32, 512), lambda i, at: (0, at[2], 0)),
            ],
            out_specs=pl.BlockSpec((2, 4, 64, 256), lambda i, at: (0, 0, 0, 0)),
        ),
        compiler_params=pltpu.CompilerParams(vmem_limit_bytes=63 * 1024 * 1024),
        name="chunk",
    )(at, wq, w_out)


def mix_body(got, early, first, out, first_out):
    total = got[0].astype(F32)
    for i in range(1, 8):
        total = total + got[i].astype(F32)
    for q in range(8):
        mine = [early[104 * q : 104 * (q + 1)].astype(F32), total[24 * q : 24 * (q + 1)]]
        out[q, 0:128] = jnp.concatenate(mine, 0).astype(BF)
        out[q, 128:144] = total[192:208].astype(BF) if q == 0 else jnp.zeros((16, 256), BF)
    first_out[...] = first[...]


def sum_body(got, out):
    total = got[0].astype(F32)
    for i in range(1, 8):
        total = total + got[i].astype(F32)
    for q in range(8):
        out[q] = total.astype(BF)


def unpack_first_body(first, g_up, g_down):
    for k in range(2):
        for c in range(4):
            cols = slice(256 * c, 256 * (c + 1))
            g_up[0, 64 * k : 64 * (k + 1), cols] = first[k, 64 * c : 64 * (c + 1)].astype(F32)
        for c in range(2):
            rows = first[k, 256 + 128 * c : 256 + 128 * (c + 1)]
            cols = slice(256 * c, 256 * (c + 1))
            g_down[0, 128 * k : 128 * (k + 1), cols] = rows.astype(F32)


def unpack_rest_body(rest, _, __, g_up, g_down, g_qkv, g_out, g_b_up, g_b_qkv, g_sum, g_gain, g_bias):
    p = pl.program_id(0)
    for k in range(2):
        for q in range(8):
            block = rest[k, q, 0:128].astype(F32)
            for i in range(16):
                value = block[8 * i : 8 * (i + 1)]
                row = 104 * q + 8 * i
                if i >= 13:
                    row = 24 * q + 8 * (i - 13)
                    r = 64 * k + row % 64
                    g_qkv[0, row // 64, r : r + 8] = value
                elif row < 192:
                    r = 64 * k + row % 64
                    g_qkv[1, row // 64, r : r + 8] = value
                elif row < 448:
                    c, r = divmod(row - 192, 64)
                    r += 64 * k
                    g_up[0, r : r + 8, 256 * c : 256 * (c + 1)] = value
                elif row < 704:
                    c, r = divmod(row - 448, 128)
                    r += 128 * k
                    g_down[0, r : r + 8, 256 * c : 256 * (c + 1)] = value
                else:
                    c, r = divmod((row - 704) % 64, 32)
                    r += 32 * k
                    g_out[1 - (row - 704) // 64, r : r + 8, 256 * c : 256 * (c + 1)] = value

    tiny = [rest[k, 0, 128:144].astype(F32) for k in range(2)]

    @pl.when(p == 0)
    def _():
        for layer in range(2):
            for c in range(4):
                r = 4 * layer + c
                g_b_up[layer : layer + 1, 256 * c : 256 * (c + 1)] = tiny[0][r : r + 1]
        for e in range(3):
            for layer in range(2):
                r = 8 + 2 * e + layer
                g_b_qkv[e, layer : layer + 1, :] = tiny[0][r : r + 1]
        for layer in range(2):
            for c in range(2):
                r = 2 * layer + c
                for which in range(2):
                    g_sum[layer, which : which + 1, 256 * c : 256 * (c + 1)] = tiny[1][r : r + 1]

    def norms(layer, rows, base):
        for which in range(2):
            for c in range(2):
                cols = slice(256 * c, 256 * (c + 1))
                r = base + 2 * which + c
                g_gain[layer, which : which + 1, cols] = rows[r : r + 1]
                g_bias[layer, which : which + 1, cols] = rows[r + 4 : r + 5]

    @pl.when(p == 0)
    def _():
        norms(0, tiny[1], 4)

    @pl.when(p == 1)
    def _():
        norms(1, tiny[0], 0)


UP = (2, 512, 1024)
DOWN = (2, 1024, 512)


def unpack(first, rest):
    def place(layer):
        return [
            pl.BlockSpec((1, 128, 1024), lambda p: (layer, p, 0)),
            pl.BlockSpec((1, 256, 512), lambda p: (layer, p, 0)),
        ]

    params = pltpu.CompilerParams(vmem_limit_bytes=63 * 1024 * 1024)
    g_up, g_down = pl.pallas_call(
        unpack_first_body,
        grid=(4,),
        out_shape=[jax.ShapeDtypeStruct(UP, F32), jax.ShapeDtypeStruct(DOWN, F32)],
        in_specs=[pl.BlockSpec((2, 512, 256), lambda p: (p, 0, 0))],
        out_specs=place(1),
        compiler_params=params,
        name="unpack_first",
    )(first)
    outs = [
        ((2, 3, 512, 256), pl.BlockSpec((2, 3, 128, 256), lambda p: (0, 0, p, 0))),
        ((2, 256, 512), pl.BlockSpec((2, 64, 512), lambda p: (0, p, 0))),
        ((2, 1024), whole((2, 1024))),
        ((3, 2, 256), whole((3, 2, 256))),
        ((2, 2, 512), whole((2, 2, 512))),
        ((2, 2, 512), whole((2, 2, 512))),
        ((2, 2, 512), whole((2, 2, 512))),
    ]
    return pl.pallas_call(
        unpack_rest_body,
        grid=(4,),
        out_shape=[jax.ShapeDtypeStruct(shape, F32) for shape in [UP, DOWN] + [o[0] for o in outs]],
        in_specs=[
            pl.BlockSpec((2, 8, 144, 256), lambda p: (p, 0, 0, 0)),
            pl.BlockSpec(memory_space=pl.ANY),
            pl.BlockSpec(memory_space=pl.ANY),
        ],
        out_specs=place(0) + [spec for _, spec in outs],
        input_output_aliases={1: 0, 2: 1},
        compiler_params=params,
        name="unpack_rest",
    )(rest, g_up, g_down)


def swap(value):
    return lax.ppermute(value, "tensor", [(0, 1), (1, 0)])


def exchange(value, axes):
    return lax.all_to_all(value, axes, 0, 0)


def both(value):
    flat = value.reshape((16,) + value.shape[2:])
    return exchange(flat, ("context", "tensor")).reshape(value.shape)


def shards(
    tokens_in, cotangent, positions, w_qkv, b_qkv, w_out, w_up, b_up, w_down, out_bias, ln_gain, ln_bias
):
    rows, width = 256, 512
    x = tokens_in.reshape(rows, width)
    cot = cotangent.reshape(rows, width)
    wq = jnp.transpose(w_qkv, (0, 2, 1, 3))
    bq = jnp.transpose(b_qkv, (1, 0, 2))
    at = jnp.stack(
        [lax.axis_index("context"), lax.axis_index("tensor"), lax.axis_index("dp")]
    ).astype(jnp.int32)
    freqs = jnp.asarray(FREQS).reshape(HALF, 1)
    chunk = swap(chunk_of(at, wq, w_out))
    send, pair, act, slope, cs = call(
        first_body,
        [
            Store((8, 208, BLK), BF),
            Store((2 * rows, width), BF),
            Store((rows, 1024), BF),
            Store((rows, 1024), BF),
            ((2, 2, HALF, BLK), F32),
        ],
        (
            at, positions, freqs, Fetch(x), ln_gain, ln_bias, Fetch(wq, 0), bq, Fetch(w_up, 0), b_up,
            Fetch(w_down, 0), Fetch(w_out, 0),
        ),
        "norm_qkv_feed",
        smem_first=True,
    )
    pair_other = swap(pair)
    mark = send[0, 0, 0]
    chunk = jnp.where(mark == mark, chunk, 0)
    others = lax.all_gather(chunk, "dp", axis=2, tiled=True)
    recv = exchange(send, "context")
    ctx_send, lse, ctx, start = call(
        attend_body,
        [((8, 2, HEAD, BLK), BF), ((1, 1024), F32), ((HEAD, 1024), F32), ((1, 1024), jnp.int32)],
        (recv,),
        "attend",
    )
    recv_ctx = both(ctx_send)
    stream, send, grads_a, parts, d_b_up1, d_sum1 = call(
        middle_body,
        [
            Store((rows, width), F32),
            Store((8, 256, BLK), BF),
            Store((8, 512, 256), BF),
            Store((2 * rows, width), BF),
            ((1, 1024), F32),
            ((1, width), F32),
        ],
        (
            at, Fetch(x), Fetch(pair), Fetch(pair_other), Fetch(recv_ctx), Fetch(w_out, 0), out_bias,
            ln_gain, ln_bias, Fetch(wq, 1), bq, Fetch(w_up, 1), b_up, Fetch(w_down, 1),
            Fetch(w_out, 1), Fetch(cot), cs,
        ),
        "middle",
        scratch=[pltpu.VMEM((rows, 1024), BF), pltpu.VMEM((rows, 1024), BF)],
        smem_first=True,
    )
    sums_a = lax.psum_scatter(grads_a, "dp", scatter_dimension=0)
    parts_other = swap(parts)
    recv_both = exchange(send, "context")
    (both_send,) = call(
        attend_both_body,
        [((8, 2, 256, BLK), BF)],
        (recv_both, start, After(parts_other)),
        "attend_both",
        scratch=[pltpu.VMEM((HEAD, 1024), F32), pltpu.VMEM((HEAD, 1024), F32)],
    )
    recv_grad = both(both_send)
    block_out, g, send, grads_b, part_g, d_b_up0, d_b_qkv1, d_norm1, d_sum0 = call(
        turn_point_body,
        [
            Store((rows, width), F32),
            Store((rows, width), F32),
            Store((8, 192, BLK), BF),
            Store((8, 832, 256), BF),
            Store((rows, width), BF),
            ((1, 1024), F32),
            ((3, 256), F32),
            ((4, width), F32),
            ((1, width), F32),
        ],
        (
            at, Fetch(stream), Fetch(parts), Fetch(parts_other), Fetch(recv_grad), Fetch(w_out, 1),
            Fetch(wq, 1), Fetch(others, 1), out_bias, ln_gain, ln_bias, Fetch(cot), cs, Fetch(x),
            Fetch(act), Fetch(slope), Fetch(w_up, 0), Fetch(w_down, 0), Fetch(w_out, 0),
            Fetch(recv_ctx), Fetch(sums_a),
        ),
        "turn_point",
        smem_first=True,
    )
    sums_b = lax.psum_scatter(grads_b, "dp", scatter_dimension=0)
    part_g_other = swap(part_g)
    recv_d = exchange(send, "context")
    (back_send,) = call(
        attend_back_body,
        [((8, 2, 320, BLK), BF)],
        (recv, recv_d, start, lse, ctx, After(part_g_other)),
        "attend_back",
        scratch=[pltpu.VMEM((HEAD, 1024), F32), pltpu.VMEM((HEAD, 1024), F32)],
    )
    recv_grad0 = both(back_send)
    in_grad, grads_c, sums_a, _, _ = call(
        last_body,
        [
            Store((rows, width), F32),
            Store((8, 208, 256), BF),
            Store((512, 256), BF),
            ((3, 256), F32),
            ((4, width), F32),
        ],
        (
            at, Fetch(x), Fetch(g), Fetch(part_g), Fetch(part_g_other), Fetch(recv_grad0), Fetch(wq, 0),
            Fetch(others, 0), cs,
            ln_gain, ln_bias, d_b_up0, d_b_up1, d_b_qkv1, d_norm1, d_sum0, d_sum1,
        ),
        "last",
        smem_first=True,
    )
    mixed, sums_a = call(
        mix_body,
        [((8, 144, 256), BF), ((512, 256), BF)],
        (exchange(grads_c, "dp"), sums_b, sums_a),
        "mix",
    )
    full_a = lax.all_gather(sums_a, "dp")
    (summed,) = call(sum_body, [((8, 144, 256), BF)], (exchange(mixed, "context"),), "sum")
    full_bc = lax.all_gather(exchange(summed, "context"), "dp")
    g_up, g_down, g_qkv, g_out, g_b_up, g_b_qkv, g_sum, g_gain, g_bias = unpack(full_a, full_bc)
    return (
        block_out.reshape(tokens_in.shape),
        in_grad.reshape(tokens_in.shape),
        jnp.transpose(g_qkv, (0, 2, 1, 3)),
        jnp.transpose(g_b_qkv, (1, 0, 2)),
        g_out,
        g_up,
        g_b_up,
        g_down,
        g_sum,
        g_gain,
        g_bias,
    )


def solution(mesh):
    return jax.shard_map(
        shards,
        mesh=mesh,
        in_specs=(
            P("dp", "context", None),
            P("dp", "context", None),
            P("dp", "context"),
            P(None, None, None, "tensor"),
            P(None, None, "tensor"),
            P(None, "tensor", None),
            P(None, None, "tensor"),
            P(None, "tensor"),
            P(None, "tensor", None),
            P(),
            P(),
            P(),
        ),
        out_specs=(
            P("dp", "context", None),
            P("dp", "context", None),
            P(None, None, None, "tensor"),
            P(None, None, "tensor"),
            P(None, "tensor", None),
            P(None, None, "tensor"),
            P(None, "tensor"),
            P(None, "tensor", None),
            P(),
            P(),
            P(),
        ),
        check_vma=False,
    )
```

```python
from functools import partial

import numpy as np

import jax
import jax.numpy as jnp
from jax import lax
from jax.experimental import pallas as pl
from jax.experimental.pallas import tpu as pltpu
from jax.sharding import PartitionSpec as P

EPS = 1e-05
HALF = 8
HEAD = 64
BLK = 128
CHUNK = 256
NEG = -1e30
BF = jnp.bfloat16
F32 = jnp.float32

FREQS = (10000.0 ** (-np.arange(HALF, dtype=np.float64) * 2.0 / 16.0)).astype(np.float32)


def mm(a, b, ca=1, cb=0):
    return lax.dot_general(a, b, (((ca,), (cb,)), ((), ())), preferred_element_type=F32)


class After:
    def __init__(self, array):
        self.array = array

    def spec(self):
        return pl.BlockSpec(memory_space=pl.ANY)


class Layer:
    def __init__(self, array, index):
        self.array, self.index = array, index

    def spec(self):
        rest = self.array.shape[1:]
        place = (self.index,) + (0,) * len(rest)
        return pl.BlockSpec((None,) + rest, lambda i: place)


def whole(shape):
    return pl.BlockSpec(shape, lambda i: (0,) * len(shape))


class Fetch:
    def __init__(self, array, layer=None, rows=None, at=0):
        self.array, self.layer, self.rows, self.at = array, layer, rows, at
        shape = array.shape if layer is None else array.shape[1:]
        self.shape = shape if rows is None else shape[:-2] + (rows, shape[-1])

    def spec(self):
        return pl.BlockSpec(memory_space=pl.ANY)

    def source(self, ref):
        if self.layer is not None:
            ref = ref.at[self.layer]
        if self.rows is not None:
            place = (slice(None),) * (len(self.shape) - 2) + (pl.ds(self.at * self.rows, self.rows),)
            ref = ref.at[place]
        return ref


class Lazy:
    def __init__(self, ref, copy):
        self.ref, self.copy, self.shape = ref, copy, ref.shape

    def __getitem__(self, index):
        if self.copy is not None:
            self.copy.wait()
            self.copy = None
        return self.ref[index]


class Store:
    def __init__(self, shape, dtype):
        self.shape, self.dtype = shape, dtype


class Out:
    def __init__(self, ref, target, sems, copies):
        self.ref, self.target, self.sems, self.copies, self.done = ref, target, sems, copies, False

    def __setitem__(self, index, value):
        self.ref[index] = value

    def __getitem__(self, index):
        return self.ref[index]

    def flush(self, *place):
        source, target = self.ref, self.target
        if place:
            source, target = source.at[place], target.at[place]
        copy = pltpu.make_async_copy(source, target, self.sems.at[len(self.copies)])
        copy.start()
        self.copies.append(copy)
        self.done = True


FLUSHES = 40


def flush(ref, *place):
    if isinstance(ref, Out):
        ref.flush(*place)


def call(body, out_shape, args, name, scratch=(), smem_first=False):
    own = (Layer, After, Fetch)
    specs = [a.spec() if isinstance(a, own) else whole(a.shape) for a in args]
    fetched = [i for i, a in enumerate(args) if isinstance(a, Fetch)]
    stored = [i for i, o in enumerate(out_shape) if isinstance(o, Store)]
    plans = list(args)
    arrays = [a.array if isinstance(a, own) else a for a in args]
    shapes = [(o.shape, o.dtype) if isinstance(o, Store) else o for o in out_shape]
    if smem_first:
        specs[0] = pl.BlockSpec(memory_space=pltpu.SMEM)
    buffers = [pltpu.VMEM(plans[i].shape, arrays[i].dtype) for i in fetched]
    buffers += [pltpu.VMEM(*shapes[i]) for i in stored]
    sems = []
    if fetched:
        sems.append(pltpu.SemaphoreType.DMA((len(fetched),)))
    if stored:
        sems.append(pltpu.SemaphoreType.DMA((FLUSHES,)))
    n_in, n_out, n_scratch = len(args), len(out_shape), len(scratch)

    def run(*refs):
        ins, outs = list(refs[:n_in]), list(refs[n_in : n_in + n_out])
        rest = list(refs[n_in + n_out :])
        mine, rest = rest[:n_scratch], rest[n_scratch:]
        for k, i in enumerate(fetched):
            copy = pltpu.make_async_copy(
                plans[i].source(ins[i]), rest[k], rest[len(buffers)].at[k]
            )
            copy.start()
            ins[i] = Lazy(rest[k], copy)
        copies = []
        for k, i in enumerate(stored):
            outs[i] = Out(rest[len(fetched) + k], outs[i], rest[-1], copies)
        body(*ins, *outs, *mine)
        for i in fetched:
            if ins[i].copy is not None:
                ins[i].copy.wait()
        for i in stored:
            if not outs[i].done:
                outs[i].flush()
        for copy in copies:
            copy.wait()

    return pl.pallas_call(
        run,
        grid=(1,),
        out_shape=[jax.ShapeDtypeStruct(s, d) for s, d in shapes],
        in_specs=specs,
        out_specs=[
            pl.BlockSpec(memory_space=pl.ANY) if isinstance(o, Store) else whole(o[0])
            for o in out_shape
        ],
        scratch_shapes=list(scratch) + buffers + sems,
        compiler_params=pltpu.CompilerParams(vmem_limit_bytes=32 * 1024 * 1024),
        name=name,
    )(*arrays)


def norm_rows(x):
    mean = jnp.mean(x, -1, keepdims=True)
    cen = x - mean
    inv = lax.rsqrt(jnp.mean(cen * cen, -1, keepdims=True) + EPS)
    return cen * inv, inv


def turn(t, cos, sin):
    a, b = t[:HALF], t[HALF : 2 * HALF]
    return jnp.concatenate([a * cos - b * sin, b * cos + a * sin, t[2 * HALF :]], 0)


def turn_back(u, cos, sin):
    a, b = u[:HALF], u[HALF : 2 * HALF]
    return jnp.concatenate([a * cos + b * sin, b * cos - a * sin, u[2 * HALF :]], 0)


def send_qkv(send, attn_in, w_qkv, b_qkv, layer, cs):
    for e in range(3):
        turned = (mm(attn_in, w_qkv[e]) + b_qkv[e, layer : layer + 1]).T
        for s in range(2):
            cos, sin = cs[s, 0], cs[s, 1]
            for h in range(4):
                j = s * 4 + h
                part = turned[h * HEAD : (h + 1) * HEAD, s * BLK : (s + 1) * BLK]
                if e < 2:
                    part = turn(part, cos, sin)
                if e == 0:
                    part = part * (HEAD**-0.5)
                send[j, e * HEAD : (e + 1) * HEAD, :] = part.astype(BF)


def feed_forward(mlp_in, w_up, b_up, layer, w_down, act, slope):
    width = w_up.shape[1]
    total = None
    for c in range(0, width, 256):
        cols = slice(c, c + 256)
        pre = mm(mlp_in, w_up[:, cols]) + b_up[layer : layer + 1, cols]
        cdf = 0.5 + 0.5 * lax.erf(pre * np.float32(0.7071067811865476))
        a = (pre * cdf).astype(BF)
        act[:, cols] = a
        tail = pre * (jnp.exp(-0.5 * pre * pre) * np.float32(0.3989422804014327))
        slope[:, cols] = (cdf + tail).astype(BF)
        flush(act, slice(None), cols)
        flush(slope, slice(None), cols)
        term = mm(a, w_down[cols, :])
        total = term if total is None else total + term
    return total


def feed_back(g_b, act, slope, mlp_in, w_up, w_down, d_up, d_down, d_b_up):
    width = w_up.shape[1]
    total = None
    mlp_t = mlp_in.astype(F32).T.astype(BF)
    for c in range(0, width, 256):
        cols = slice(c, c + 256)
        d_act = mm(g_b, w_down[cols, :], 1, 1)
        d_pre = d_act * slope[:, cols].astype(F32)
        d_pre_b = d_pre.astype(BF)
        d_b_up[:, cols] = jnp.sum(d_pre_b.astype(F32), 0, keepdims=True)
        d_up(c // 256, mm(mlp_t, d_pre_b))
        d_down(c, mm(act[:, cols].astype(F32).T.astype(BF), g_b))
        term = mm(d_pre_b, w_up[:, cols], 1, 1)
        total = term if total is None else total + term
    return total


def pack_up(out, row):
    def put(c, value):
        for p in range(8):
            out[p, row + 64 * c : row + 64 * (c + 1), :] = value[64 * p : 64 * (p + 1)].astype(BF)
        flush(out, slice(None), slice(row + 64 * c, row + 64 * (c + 1)))

    return put


def pack_down(out, row):
    def put(c, value):
        for half in range(2):
            for k in range(2):
                out[c // 128 + k, row + 128 * half : row + 128 * (half + 1), :] = value[
                    128 * k : 128 * (k + 1), 256 * half : 256 * (half + 1)
                ].astype(BF)
        flush(out, slice(c // 128, c // 128 + 2), slice(row, row + 256))

    return put


def pack_qkv(out, row):
    def put(e, value):
        for p in range(8):
            out[p, row + 64 * e : row + 64 * (e + 1), :] = value[64 * p : 64 * (p + 1)].astype(BF)
        flush(out, slice(None), slice(row + 64 * e, row + 64 * (e + 1)))

    return put


def own_ctx(t, recv):
    full = jnp.concatenate([gather_ctx(recv, s) for s in range(2)], 1)
    return jnp.where(t == 0, full[0:256], full[256:512])


def pack_out(out, row, ctx, upstream):
    value = mm(ctx, upstream)
    for p in range(8):
        for half in range(2):
            out[p, row + 32 * half : row + 32 * (half + 1), :] = value[
                32 * p : 32 * (p + 1), 256 * half : 256 * (half + 1)
            ].astype(BF)
    flush(out, slice(None), slice(row, row + 64))


def first_body(
    at, pos, freqs, x, gain, bias, w_qkv, b_qkv, w_up, b_up, w_down, w_out,
    send, pair, act, slope, cs,
):

    for s in range(2):
        p = pos[s : s + 1, :].astype(F32)
        angle = freqs[...] * p
        cs[s, 0] = jnp.cos(angle)
        cs[s, 1] = jnp.sin(angle)
    normed, _ = norm_rows(x[...])
    attn_in = (normed * gain[0, 0:1] + bias[0, 0:1]).astype(BF)
    mlp_in = (normed * gain[0, 1:2] + bias[0, 1:2]).astype(BF)
    send_qkv(send, attn_in, w_qkv, b_qkv, 0, cs)
    row = lax.broadcasted_iota(jnp.int32, (16, BLK), 0)
    token = at[0] * BLK + lax.broadcasted_iota(jnp.int32, (1, BLK), 1)
    for s in range(2):
        start = jnp.maximum(token - pos[s : s + 1, :], 0)
        high = (start // 8).astype(F32)
        low = (start % 8).astype(F32)
        block = jnp.where(row == 0, high, jnp.where(row == 1, low, 0.0)).astype(BF)
        for h in range(4):
            send[s * 4 + h, 3 * HEAD : 3 * HEAD + 16, :] = block
    flush(send)
    pair[256:512] = w_out[...]
    pair[0:256] = feed_forward(mlp_in, w_up, b_up, 0, w_down, act, slope).astype(BF)


def load_rows(recv, lo, hi):
    return jnp.concatenate([recv[i, lo:hi, :] for i in range(8)], 1)


def starts_of(recv):
    rows = load_rows(recv, 3 * HEAD, 3 * HEAD + 16).astype(F32)
    return rows[0:1] * 8.0 + rows[1:2]


def visible_of(start, c, length):
    key = lax.broadcasted_iota(jnp.int32, (length, CHUNK), 0)
    query = lax.broadcasted_iota(jnp.int32, (length, CHUNK), 1) + c * CHUNK
    return (key <= query) & (key >= start[:, c * CHUNK : (c + 1) * CHUNK])


def attend_body(recv, send, lse, ctx, start_out):
    q = load_rows(recv, 0, HEAD)
    k_t = load_rows(recv, HEAD, 2 * HEAD)
    v_t = load_rows(recv, 2 * HEAD, 3 * HEAD)
    k = k_t.astype(F32).T.astype(BF)
    start = starts_of(recv).astype(jnp.int32)
    start_out[...] = start
    for c in range(4):
        cols = slice(c * CHUNK, (c + 1) * CHUNK)
        length = (c + 1) * CHUNK
        scores = mm(k[:length], q[:, cols])
        scores = jnp.where(visible_of(start, c, length), scores, NEG)
        peak = jnp.max(scores, 0, keepdims=True)
        shifted = jnp.exp(scores - peak)
        total = jnp.sum(shifted, 0, keepdims=True)
        lse[:, cols] = peak + jnp.log(total)
        out = mm(v_t[:, :length], shifted.astype(BF)) / total
        ctx[:, cols] = out
        for i in range(CHUNK // BLK):
            block = out[:, i * BLK : (i + 1) * BLK].astype(BF)
            for t in range(2):
                send[c * (CHUNK // BLK) + i, t] = block


def attend_both_body(recv, start, _, send, dk, dv):
    q = load_rows(recv, 0, HEAD)
    k_t = load_rows(recv, HEAD, 2 * HEAD)
    v_t = load_rows(recv, 2 * HEAD, 3 * HEAD)
    d_ctx = load_rows(recv, 3 * HEAD, 4 * HEAD)
    k = k_t.astype(F32).T.astype(BF)
    v = v_t.astype(F32).T.astype(BF)
    dk[...] = jnp.zeros_like(dk)
    dv[...] = jnp.zeros_like(dv)
    for c in range(4):
        cols = slice(c * CHUNK, (c + 1) * CHUNK)
        length = (c + 1) * CHUNK
        scores = mm(k[:length], q[:, cols])
        scores = jnp.where(visible_of(start[...], c, length), scores, NEG)
        peak = jnp.max(scores, 0, keepdims=True)
        shifted = jnp.exp(scores - peak)
        probs = shifted * (1.0 / jnp.sum(shifted, 0, keepdims=True))
        probs_b = probs.astype(BF)
        out = mm(v_t[:, :length], probs_b)
        dq = backward_chunk(q, k_t, v, d_ctx, probs, probs_b, out, cols, length, dk, dv)
        for i in range(CHUNK // BLK):
            b = c * (CHUNK // BLK) + i
            for t in range(2):
                send[b, t, 0:HEAD] = out[:, i * BLK : (i + 1) * BLK].astype(BF)
                send[b, t, HEAD : 2 * HEAD] = dq[:, i * BLK : (i + 1) * BLK].astype(BF)
    put_kv(send, dk, dv, 2 * HEAD)


def backward_chunk(q, k_t, v, d_ctx, probs, probs_b, out, cols, length, dk, dv):
    d_out = d_ctx[:, cols]
    d_probs = mm(v[:length], d_out)
    delta = jnp.sum(d_out.astype(F32) * out, 0, keepdims=True)
    d_scores = (probs * (d_probs - delta)).astype(BF)
    dk[:, :length] += mm(q[:, cols], d_scores, 1, 1)
    dv[:, :length] += mm(d_out, probs_b, 1, 1)
    return mm(k_t[:, :length], d_scores) * (HEAD**-0.5)


def put_kv(send, dk, dv, row):
    for b in range(8):
        for t in range(2):
            send[b, t, row : row + HEAD] = dk[:, b * BLK : (b + 1) * BLK].astype(BF)
            send[b, t, row + HEAD : row + 2 * HEAD] = dv[:, b * BLK : (b + 1) * BLK].astype(BF)


def attend_back_body(recv, recv_d, start, lse, ctx, _, send, dk, dv):
    ride = recv_d[0, 64:192].astype(F32)
    for i in range(1, 8):
        ride = ride + recv_d[i, 64:192].astype(F32)
    ride = ride.astype(BF)
    for b in range(8):
        for t in range(2):
            send[b, t, 192:320] = ride
    q = load_rows(recv, 0, HEAD)
    k_t = load_rows(recv, HEAD, 2 * HEAD)
    v_t = load_rows(recv, 2 * HEAD, 3 * HEAD)
    d_ctx = load_rows(recv_d, 0, HEAD)
    k = k_t.astype(F32).T.astype(BF)
    v = v_t.astype(F32).T.astype(BF)
    dk[...] = jnp.zeros_like(dk)
    dv[...] = jnp.zeros_like(dv)
    for c in range(4):
        cols = slice(c * CHUNK, (c + 1) * CHUNK)
        length = (c + 1) * CHUNK
        scores = mm(k[:length], q[:, cols])
        scores = jnp.where(visible_of(start[...], c, length), scores, NEG)
        probs = jnp.exp(scores - lse[:, cols])
        probs_b = probs.astype(BF)
        dq = backward_chunk(q, k_t, v, d_ctx, probs, probs_b, ctx[:, cols], cols, length, dk, dv)
        for i in range(CHUNK // BLK):
            for t in range(2):
                send[c * (CHUNK // BLK) + i, t, 0:HEAD] = dq[:, i * BLK : (i + 1) * BLK].astype(BF)
    put_kv(send, dk, dv, HEAD)


def gather_ctx(recv, s):
    return jnp.concatenate([recv[s * 4 + h, t, 0:HEAD, :] for t in range(2) for h in range(4)], 0)


def ordered(t, own, other):
    return jnp.where(t == 0, own, other), jnp.where(t == 0, other, own)


def out_other(others):
    halves = [
        jnp.concatenate([others[3, 64 * p + 32 * c : 64 * p + 32 * (c + 1), :] for p in range(8)], 0)
        for c in range(2)
    ]
    return jnp.concatenate(halves, 1)


def branch_of(t, recv, w_own, w_other):
    first, second = ordered(t, w_own, w_other)
    w = jnp.concatenate([first, second], 0)
    rows = []
    for s in range(2):
        rows.append(mm(gather_ctx(recv, s).astype(F32).T.astype(BF), w))
    return jnp.concatenate(rows, 0)


def middle_body(
    at, x, pair, pair_other, recv, w_out_own, out_bias, gain, bias,
    w_qkv, b_qkv, w_up, b_up, w_down, w_out, cot, cs,
    stream, send, grads, parts, d_b_up, d_sum, act, slope,
):
    branch = pair[0:256].astype(F32) + pair_other[0:256].astype(F32)
    branch = branch + branch_of(at[1], recv, w_out_own[...], pair_other[256:512])
    out = x[...] + branch + out_bias[0, 0:1] + out_bias[0, 1:2]
    stream[...] = out
    flush(stream)
    normed, _ = norm_rows(out)
    attn_in = (normed * gain[1, 0:1] + bias[1, 0:1]).astype(BF)
    mlp_in = (normed * gain[1, 1:2] + bias[1, 1:2]).astype(BF)
    send_qkv(send, attn_in, w_qkv, b_qkv, 1, cs)
    g_b = cot[...].astype(BF)
    d_ctx = mm(w_out[...], g_b, 1, 1)
    for s in range(2):
        for h in range(4):
            send[s * 4 + h, 3 * HEAD : 4 * HEAD, :] = d_ctx[
                h * HEAD : (h + 1) * HEAD, s * BLK : (s + 1) * BLK
            ].astype(BF)
    flush(send)
    d_sum[...] = jnp.sum(cot[...], 0, keepdims=True)
    parts[0:256] = feed_forward(mlp_in, w_up, b_up, 1, w_down, act, slope).astype(BF)
    parts[256:512] = feed_back(
        g_b, act, slope, mlp_in, w_up, w_down, pack_up(grads, 0), pack_down(grads, 256), d_b_up
    ).astype(BF)


def norm_back(
    t, x, g, d_mlp_in, recv, row, w_own, others, cs, gain, bias, layer, d_qkv, d_b_qkv, d_norm
):
    normed, inv = norm_rows(x)
    attn_in = (normed * gain[layer, 0:1] + bias[layer, 0:1]).astype(BF)
    attn_t = attn_in.astype(F32).T.astype(BF)
    d_attn_t = None
    for e in range(3):
        halves = []
        for tt in range(2):
            blocks = []
            for h in range(4):
                pieces = []
                for s in range(2):
                    lo = row + e * HEAD
                    u = recv[s * 4 + h, tt, lo : lo + HEAD, :]
                    if e < 2:
                        u = turn_back(u.astype(F32), cs[s, 0], cs[s, 1]).astype(BF)
                    pieces.append(u)
                blocks.append(jnp.concatenate(pieces, 1))
            halves.append(jnp.concatenate(blocks, 0))
        first, second = ordered(t, w_own[e], others[e])
        term = mm(first, halves[0]) + mm(second, halves[1])
        d_attn_t = term if d_attn_t is None else d_attn_t + term
        own = jnp.where(t == 0, halves[0], halves[1])
        d_qkv(e, mm(attn_t, own, 1, 1))
        d_b_qkv[e : e + 1] = mm(jnp.ones((8, own.shape[1]), BF), own, 1, 1)[0:1]
    d_attn_in = d_attn_t.T
    d_norm[0:1] = jnp.sum(d_attn_in * normed, 0, keepdims=True)
    d_norm[1:2] = jnp.sum(d_mlp_in * normed, 0, keepdims=True)
    d_norm[2:3] = jnp.sum(d_attn_in, 0, keepdims=True)
    d_norm[3:4] = jnp.sum(d_mlp_in, 0, keepdims=True)
    d_normed = d_attn_in * gain[layer, 0:1] + d_mlp_in * gain[layer, 1:2]
    return g + inv * (
        d_normed
        - jnp.mean(d_normed, -1, keepdims=True)
        - normed * jnp.mean(d_normed * normed, -1, keepdims=True)
    )


def turn_point_body(
    at, stream, parts, parts_other, recv, w_out, w_qkv, others, out_bias,
    gain, bias, cot, cs, x, act, slope, w_up, w_down, w_out_first, recv_first, sums_a,
    block_out, g_out, send, grads, part, d_b_up, d_b_qkv, d_norm, d_sum,
):
    t = at[1]
    branch = parts[0:256].astype(F32) + parts_other[0:256].astype(F32)
    branch = branch + branch_of(t, recv, w_out[...], out_other(others))
    block_out[...] = stream[...] + branch + out_bias[1, 0:1] + out_bias[1, 1:2]
    flush(block_out)
    d_mlp_in = parts[256:512].astype(F32) + parts_other[256:512].astype(F32)
    g = norm_back(
        t, stream[...], cot[...], d_mlp_in, recv, HEAD, w_qkv, others, cs, gain, bias, 1,
        pack_qkv(grads, 0), d_b_qkv, d_norm,
    )
    g_out[...] = g
    flush(g_out)
    g_b = g.astype(BF)
    d_sum[...] = jnp.sum(g, 0, keepdims=True)
    d_ctx = mm(w_out_first[...], g_b, 1, 1)
    for s in range(2):
        for h in range(4):
            send[s * 4 + h, 0:HEAD] = d_ctx[
                h * HEAD : (h + 1) * HEAD, s * BLK : (s + 1) * BLK
            ].astype(BF)
    for q in range(8):
        for c in range(2):
            send[q, 64 + 64 * c : 128 + 64 * c] = sums_a[
                64 * q : 64 * (q + 1), BLK * c : BLK * (c + 1)
            ]
    flush(send)
    pack_out(grads, 704, own_ctx(t, recv), cot[...].astype(BF))
    pack_out(grads, 768, own_ctx(t, recv_first), g_b)
    normed, _ = norm_rows(x[...])
    mlp_in = (normed * gain[0, 1:2] + bias[0, 1:2]).astype(BF)
    part[...] = feed_back(
        g_b, act, slope, mlp_in, w_up, w_down, pack_up(grads, 192), pack_down(grads, 448), d_b_up
    ).astype(BF)


def last_body(
    at, x, g, part, part_other, recv, w_qkv, others, cs, gain, bias,
    d_b_up0, d_b_up1, d_b_qkv1, d_norm1, d_sum0, d_sum1,
    in_grad, grads, sums_a, d_b_qkv0, d_norm0,
):
    d_mlp_in = part[...].astype(F32) + part_other[...].astype(F32)
    in_grad[...] = norm_back(
        at[1], x[...], g[...], d_mlp_in, recv, 0, w_qkv, others, cs, gain, bias, 0,
        pack_qkv(grads, 0), d_b_qkv0, d_norm0,
    )
    for q in range(8):
        both_planes = recv[q, :, 192:320]
        block = jnp.where(at[1] == 0, both_planes[0], both_planes[1])
        for c in range(2):
            sums_a[64 * q : 64 * (q + 1), BLK * c : BLK * (c + 1)] = block[64 * c : 64 * (c + 1)]

    def lanes(ref, row, count):
        return [ref[row : row + 1, 256 * c : 256 * (c + 1)] for c in range(count)]

    def norms(ref):
        return [v for r in range(4) for v in lanes(ref, r, 2)]

    rows = [
        lanes(d_b_up0, 0, 4)
        + lanes(d_b_up1, 0, 4)
        + [v for e in range(3) for ref in (d_b_qkv0, d_b_qkv1) for v in lanes(ref, e, 1)],
        lanes(d_sum0, 0, 2) + lanes(d_sum1, 0, 2) + norms(d_norm0),
        norms(d_norm1),
    ]
    for p in range(8):
        have = rows[p] if p < len(rows) else []
        fill = [jnp.zeros((16 - len(have), 256), F32)]
        grads[p, 192:208, :] = jnp.concatenate(have + fill, 0).astype(BF)
    flush(grads, slice(None), slice(192, 208))


def chunk_body(at, w_qkv, w_out, out):
    for layer in range(2):
        for e in range(3):
            out[layer, e] = w_qkv[layer, e]
        out[layer, 3, 0:32] = w_out[layer, :, 0:256]
        out[layer, 3, 32:64] = w_out[layer, :, 256:512]


def chunk_of(at, wq, w_out):
    return pl.pallas_call(
        chunk_body,
        out_shape=jax.ShapeDtypeStruct((2, 4, 64, 256), BF),
        grid_spec=pltpu.PrefetchScalarGridSpec(
            num_scalar_prefetch=1,
            grid=(1,),
            in_specs=[
                pl.BlockSpec((2, 3, 64, 256), lambda i, at: (0, 0, at[2], 0)),
                pl.BlockSpec((2, 32, 512), lambda i, at: (0, at[2], 0)),
            ],
            out_specs=pl.BlockSpec((2, 4, 64, 256), lambda i, at: (0, 0, 0, 0)),
        ),
        compiler_params=pltpu.CompilerParams(vmem_limit_bytes=32 * 1024 * 1024),
        name="chunk",
    )(at, wq, w_out)


def mix_body(got, early, first, out, first_out):
    total = got[0].astype(F32)
    for i in range(1, 8):
        total = total + got[i].astype(F32)
    for q in range(8):
        mine = [early[104 * q : 104 * (q + 1)].astype(F32), total[24 * q : 24 * (q + 1)]]
        out[q, 0:128] = jnp.concatenate(mine, 0).astype(BF)
        out[q, 128:144] = total[192:208].astype(BF) if q == 0 else jnp.zeros((16, 256), BF)
    first_out[...] = first[...]


def sum_body(got, out):
    total = got[0].astype(F32)
    for i in range(1, 8):
        total = total + got[i].astype(F32)
    for q in range(8):
        out[q] = total.astype(BF)


def unpack_first_body(first, g_up, g_down):
    for k in range(2):
        for c in range(4):
            cols = slice(256 * c, 256 * (c + 1))
            g_up[0, 64 * k : 64 * (k + 1), cols] = first[k, 64 * c : 64 * (c + 1)].astype(F32)
        for c in range(2):
            rows = first[k, 256 + 128 * c : 256 + 128 * (c + 1)]
            cols = slice(256 * c, 256 * (c + 1))
            g_down[0, 128 * k : 128 * (k + 1), cols] = rows.astype(F32)


def unpack_rest_body(rest, _, __, g_up, g_down, g_qkv, g_out, g_b_up, g_b_qkv, g_sum, g_gain, g_bias):
    p = pl.program_id(0)
    for k in range(2):
        for q in range(8):
            block = rest[k, q, 0:128].astype(F32)
            for i in range(16):
                value = block[8 * i : 8 * (i + 1)]
                row = 104 * q + 8 * i
                if i >= 13:
                    row = 24 * q + 8 * (i - 13)
                    r = 64 * k + row % 64
                    g_qkv[0, row // 64, r : r + 8] = value
                elif row < 192:
                    r = 64 * k + row % 64
                    g_qkv[1, row // 64, r : r + 8] = value
                elif row < 448:
                    c, r = divmod(row - 192, 64)
                    r += 64 * k
                    g_up[0, r : r + 8, 256 * c : 256 * (c + 1)] = value
                elif row < 704:
                    c, r = divmod(row - 448, 128)
                    r += 128 * k
                    g_down[0, r : r + 8, 256 * c : 256 * (c + 1)] = value
                else:
                    c, r = divmod((row - 704) % 64, 32)
                    r += 32 * k
                    g_out[1 - (row - 704) // 64, r : r + 8, 256 * c : 256 * (c + 1)] = value

    tiny = [rest[k, 0, 128:144].astype(F32) for k in range(2)]

    @pl.when(p == 0)
    def _():
        for layer in range(2):
            for c in range(4):
                r = 4 * layer + c
                g_b_up[layer : layer + 1, 256 * c : 256 * (c + 1)] = tiny[0][r : r + 1]
        for e in range(3):
            for layer in range(2):
                r = 8 + 2 * e + layer
                g_b_qkv[e, layer : layer + 1, :] = tiny[0][r : r + 1]
        for layer in range(2):
            for c in range(2):
                r = 2 * layer + c
                for which in range(2):
                    g_sum[layer, which : which + 1, 256 * c : 256 * (c + 1)] = tiny[1][r : r + 1]

    def norms(layer, rows, base):
        for which in range(2):
            for c in range(2):
                cols = slice(256 * c, 256 * (c + 1))
                r = base + 2 * which + c
                g_gain[layer, which : which + 1, cols] = rows[r : r + 1]
                g_bias[layer, which : which + 1, cols] = rows[r + 4 : r + 5]

    @pl.when(p == 0)
    def _():
        norms(0, tiny[1], 4)

    @pl.when(p == 1)
    def _():
        norms(1, tiny[0], 0)


UP = (2, 512, 1024)
DOWN = (2, 1024, 512)


def unpack(first, rest):
    def place(layer):
        return [
            pl.BlockSpec((1, 128, 1024), lambda p: (layer, p, 0)),
            pl.BlockSpec((1, 256, 512), lambda p: (layer, p, 0)),
        ]

    params = pltpu.CompilerParams(vmem_limit_bytes=32 * 1024 * 1024)
    g_up, g_down = pl.pallas_call(
        unpack_first_body,
        grid=(4,),
        out_shape=[jax.ShapeDtypeStruct(UP, F32), jax.ShapeDtypeStruct(DOWN, F32)],
        in_specs=[pl.BlockSpec((2, 512, 256), lambda p: (p, 0, 0))],
        out_specs=place(1),
        compiler_params=params,
        name="unpack_first",
    )(first)
    outs = [
        ((2, 3, 512, 256), pl.BlockSpec((2, 3, 128, 256), lambda p: (0, 0, p, 0))),
        ((2, 256, 512), pl.BlockSpec((2, 64, 512), lambda p: (0, p, 0))),
        ((2, 1024), whole((2, 1024))),
        ((3, 2, 256), whole((3, 2, 256))),
        ((2, 2, 512), whole((2, 2, 512))),
        ((2, 2, 512), whole((2, 2, 512))),
        ((2, 2, 512), whole((2, 2, 512))),
    ]
    return pl.pallas_call(
        unpack_rest_body,
        grid=(4,),
        out_shape=[jax.ShapeDtypeStruct(shape, F32) for shape in [UP, DOWN] + [o[0] for o in outs]],
        in_specs=[
            pl.BlockSpec((2, 8, 144, 256), lambda p: (p, 0, 0, 0)),
            pl.BlockSpec(memory_space=pl.ANY),
            pl.BlockSpec(memory_space=pl.ANY),
        ],
        out_specs=place(0) + [spec for _, spec in outs],
        input_output_aliases={1: 0, 2: 1},
        compiler_params=params,
        name="unpack_rest",
    )(rest, g_up, g_down)


def swap(value):
    return lax.ppermute(value, "tensor", [(0, 1), (1, 0)])


def exchange(value, axes):
    return lax.all_to_all(value, axes, 0, 0)


def both(value):
    flat = value.reshape((16,) + value.shape[2:])
    return exchange(flat, ("context", "tensor")).reshape(value.shape)


def shards(
    tokens_in, cotangent, positions, w_qkv, b_qkv, w_out, w_up, b_up, w_down, out_bias, ln_gain, ln_bias
):
    rows, width = 256, 512
    x = tokens_in.reshape(rows, width)
    cot = cotangent.reshape(rows, width)
    wq = jnp.transpose(w_qkv, (0, 2, 1, 3))
    bq = jnp.transpose(b_qkv, (1, 0, 2))
    at = jnp.stack(
        [lax.axis_index("context"), lax.axis_index("tensor"), lax.axis_index("dp")]
    ).astype(jnp.int32)
    freqs = jnp.asarray(FREQS).reshape(HALF, 1)
    chunk = swap(chunk_of(at, wq, w_out))
    send, pair, act, slope, cs = call(
        first_body,
        [
            Store((8, 208, BLK), BF),
            Store((2 * rows, width), BF),
            Store((rows, 1024), BF),
            Store((rows, 1024), BF),
            ((2, 2, HALF, BLK), F32),
        ],
        (
            at, positions, freqs, Fetch(x), ln_gain, ln_bias, Fetch(wq, 0), bq, Fetch(w_up, 0), b_up,
            Fetch(w_down, 0), Fetch(w_out, 0),
        ),
        "norm_qkv_feed",
        smem_first=True,
    )
    pair_other = swap(pair)
    mark = send[0, 0, 0]
    chunk = jnp.where(mark == mark, chunk, 0)
    others = lax.all_gather(chunk, "dp", axis=2, tiled=True)
    recv = exchange(send, "context")
    ctx_send, lse, ctx, start = call(
        attend_body,
        [((8, 2, HEAD, BLK), BF), ((1, 1024), F32), ((HEAD, 1024), F32), ((1, 1024), jnp.int32)],
        (recv,),
        "attend",
    )
    recv_ctx = both(ctx_send)
    stream, send, grads_a, parts, d_b_up1, d_sum1 = call(
        middle_body,
        [
            Store((rows, width), F32),
            Store((8, 256, BLK), BF),
            Store((8, 512, 256), BF),
            Store((2 * rows, width), BF),
            ((1, 1024), F32),
            ((1, width), F32),
        ],
        (
            at, Fetch(x), Fetch(pair), Fetch(pair_other), Fetch(recv_ctx), Fetch(w_out, 0), out_bias,
            ln_gain, ln_bias, Fetch(wq, 1), bq, Fetch(w_up, 1), b_up, Fetch(w_down, 1),
            Fetch(w_out, 1), Fetch(cot), cs,
        ),
        "middle",
        scratch=[pltpu.VMEM((rows, 1024), BF), pltpu.VMEM((rows, 1024), BF)],
        smem_first=True,
    )
    sums_a = lax.psum_scatter(grads_a, "dp", scatter_dimension=0)
    parts_other = swap(parts)
    recv_both = exchange(send, "context")
    (both_send,) = call(
        attend_both_body,
        [((8, 2, 256, BLK), BF)],
        (recv_both, start, After(parts_other)),
        "attend_both",
        scratch=[pltpu.VMEM((HEAD, 1024), F32), pltpu.VMEM((HEAD, 1024), F32)],
    )
    recv_grad = both(both_send)
    block_out, g, send, grads_b, part_g, d_b_up0, d_b_qkv1, d_norm1, d_sum0 = call(
        turn_point_body,
        [
            Store((rows, width), F32),
            Store((rows, width), F32),
            Store((8, 192, BLK), BF),
            Store((8, 832, 256), BF),
            Store((rows, width), BF),
            ((1, 1024), F32),
            ((3, 256), F32),
            ((4, width), F32),
            ((1, width), F32),
        ],
        (
            at, Fetch(stream), Fetch(parts), Fetch(parts_other), Fetch(recv_grad), Fetch(w_out, 1),
            Fetch(wq, 1), Fetch(others, 1), out_bias, ln_gain, ln_bias, Fetch(cot), cs, Fetch(x),
            Fetch(act), Fetch(slope), Fetch(w_up, 0), Fetch(w_down, 0), Fetch(w_out, 0),
            Fetch(recv_ctx), Fetch(sums_a),
        ),
        "turn_point",
        smem_first=True,
    )
    sums_b = lax.psum_scatter(grads_b, "dp", scatter_dimension=0)
    part_g_other = swap(part_g)
    recv_d = exchange(send, "context")
    (back_send,) = call(
        attend_back_body,
        [((8, 2, 320, BLK), BF)],
        (recv, recv_d, start, lse, ctx, After(part_g_other)),
        "attend_back",
        scratch=[pltpu.VMEM((HEAD, 1024), F32), pltpu.VMEM((HEAD, 1024), F32)],
    )
    recv_grad0 = both(back_send)
    in_grad, grads_c, sums_a, _, _ = call(
        last_body,
        [
            Store((rows, width), F32),
            Store((8, 208, 256), BF),
            Store((512, 256), BF),
            ((3, 256), F32),
            ((4, width), F32),
        ],
        (
            at, Fetch(x), Fetch(g), Fetch(part_g), Fetch(part_g_other), Fetch(recv_grad0), Fetch(wq, 0),
            Fetch(others, 0), cs,
            ln_gain, ln_bias, d_b_up0, d_b_up1, d_b_qkv1, d_norm1, d_sum0, d_sum1,
        ),
        "last",
        smem_first=True,
    )
    mixed, sums_a = call(
        mix_body,
        [((8, 144, 256), BF), ((512, 256), BF)],
        (exchange(grads_c, "dp"), sums_b, sums_a),
        "mix",
    )
    full_a = lax.all_gather(sums_a, "dp")
    (summed,) = call(sum_body, [((8, 144, 256), BF)], (exchange(mixed, "context"),), "sum")
    full_bc = lax.all_gather(exchange(summed, "context"), "dp")
    g_up, g_down, g_qkv, g_out, g_b_up, g_b_qkv, g_sum, g_gain, g_bias = unpack(full_a, full_bc)
    return (
        block_out.reshape(tokens_in.shape),
        in_grad.reshape(tokens_in.shape),
        jnp.transpose(g_qkv, (0, 2, 1, 3)),
        jnp.transpose(g_b_qkv, (1, 0, 2)),
        g_out,
        g_up,
        g_b_up,
        g_down,
        g_sum,
        g_gain,
        g_bias,
    )


def solution(mesh):
    return jax.shard_map(
        shards,
        mesh=mesh,
        in_specs=(
            P("dp", "context", None),
            P("dp", "context", None),
            P("dp", "context"),
            P(None, None, None, "tensor"),
            P(None, None, "tensor"),
            P(None, "tensor", None),
            P(None, None, "tensor"),
            P(None, "tensor"),
            P(None, "tensor", None),
            P(),
            P(),
            P(),
        ),
        out_specs=(
            P("dp", "context", None),
            P("dp", "context", None),
            P(None, None, None, "tensor"),
            P(None, None, "tensor"),
            P(None, "tensor", None),
            P(None, None, "tensor"),
            P(None, "tensor"),
            P(None, "tensor", None),
            P(),
            P(),
            P(),
        ),
        check_vma=False,
    )
```

```python
from functools import partial

import numpy as np

import jax
import jax.numpy as jnp
from jax import lax
from jax.experimental import pallas as pl
from jax.experimental.pallas import tpu as pltpu
from jax.sharding import PartitionSpec as P

EPS = 1e-05
HALF = 8
HEAD = 64
BLK = 128
CHUNK = 256
NEG = -1e30
BF = jnp.bfloat16
F32 = jnp.float32

FREQS = (10000.0 ** (-np.arange(HALF, dtype=np.float64) * 2.0 / 16.0)).astype(np.float32)


def mm(a, b, ca=1, cb=0):
    return lax.dot_general(a, b, (((ca,), (cb,)), ((), ())), preferred_element_type=F32)


class After:
    def __init__(self, array):
        self.array = array

    def spec(self):
        return pl.BlockSpec(memory_space=pl.ANY)


class Layer:
    def __init__(self, array, index):
        self.array, self.index = far(array), index

    def spec(self):
        rest = self.array.shape[1:]
        place = (self.index,) + (0,) * len(rest)
        return pl.BlockSpec((None,) + rest, lambda i: place)


class Far:
    def __init__(self, array):
        self.array = far(array)

    def spec(self):
        return whole(self.array.shape)


Kept = type(pltpu.HBM((8, 128), F32))


def far(array):
    return pltpu.with_memory_space_constraint(array, pltpu.HBM)


def whole(shape):
    return pl.BlockSpec(shape, lambda i: (0,) * len(shape))


def call(body, out_shape, args, name, scratch=(), smem_first=False):
    specs = [
        a.spec() if isinstance(a, (Layer, Far, After)) else whole(a.shape) for a in args
    ]
    args = [a.array if isinstance(a, (Layer, Far, After)) else a for a in args]
    if smem_first:
        specs[0] = pl.BlockSpec(memory_space=pltpu.SMEM)
    return pl.pallas_call(
        body,
        grid=(1,),
        out_shape=[o if isinstance(o, Kept) else jax.ShapeDtypeStruct(*o) for o in out_shape],
        in_specs=specs,
        out_specs=[whole(o.shape if isinstance(o, Kept) else o[0]) for o in out_shape],
        scratch_shapes=list(scratch),
        compiler_params=pltpu.CompilerParams(vmem_limit_bytes=40 * 1024 * 1024),
        name=name,
    )(*args)


def norm_rows(x):
    mean = jnp.mean(x, -1, keepdims=True)
    cen = x - mean
    inv = lax.rsqrt(jnp.mean(cen * cen, -1, keepdims=True) + EPS)
    return cen * inv, inv


def turn(t, cos, sin):
    a, b = t[:HALF], t[HALF : 2 * HALF]
    return jnp.concatenate([a * cos - b * sin, b * cos + a * sin, t[2 * HALF :]], 0)


def turn_back(u, cos, sin):
    a, b = u[:HALF], u[HALF : 2 * HALF]
    return jnp.concatenate([a * cos + b * sin, b * cos - a * sin, u[2 * HALF :]], 0)


def send_qkv(send, attn_in, w_qkv, b_qkv, layer, cs):
    for e in range(3):
        turned = (mm(attn_in, w_qkv[e]) + b_qkv[e, layer : layer + 1]).T
        for s in range(2):
            cos, sin = cs[s, 0], cs[s, 1]
            for h in range(4):
                j = s * 4 + h
                part = turned[h * HEAD : (h + 1) * HEAD, s * BLK : (s + 1) * BLK]
                if e < 2:
                    part = turn(part, cos, sin)
                if e == 0:
                    part = part * (HEAD**-0.5)
                send[j, e * HEAD : (e + 1) * HEAD, :] = part.astype(BF)


def feed_forward(mlp_in, w_up, b_up, layer, w_down, act, slope):
    width = w_up.shape[1]
    total = None
    for c in range(0, width, 256):
        cols = slice(c, c + 256)
        pre = mm(mlp_in, w_up[:, cols]) + b_up[layer : layer + 1, cols]
        cdf = 0.5 + 0.5 * lax.erf(pre * np.float32(0.7071067811865476))
        a = (pre * cdf).astype(BF)
        act[:, cols] = a
        tail = pre * (jnp.exp(-0.5 * pre * pre) * np.float32(0.3989422804014327))
        slope[:, cols] = (cdf + tail).astype(BF)
        term = mm(a, w_down[cols, :])
        total = term if total is None else total + term
    return total


def feed_back(g_b, act, slope, mlp_in, w_up, w_down, d_up, d_down, d_b_up):
    width = w_up.shape[1]
    total = None
    mlp_t = mlp_in.astype(F32).T.astype(BF)
    for c in range(0, width, 256):
        cols = slice(c, c + 256)
        d_act = mm(g_b, w_down[cols, :], 1, 1)
        d_pre = d_act * slope[:, cols].astype(F32)
        d_pre_b = d_pre.astype(BF)
        d_b_up[:, cols] = jnp.sum(d_pre_b.astype(F32), 0, keepdims=True)
        d_up(c // 256, mm(mlp_t, d_pre_b))
        d_down(c, mm(act[:, cols].astype(F32).T.astype(BF), g_b))
        term = mm(d_pre_b, w_up[:, cols], 1, 1)
        total = term if total is None else total + term
    return total


def pack_up(out, row):
    def put(c, value):
        for p in range(8):
            out[p, row + 64 * c : row + 64 * (c + 1), :] = value[64 * p : 64 * (p + 1)].astype(BF)

    return put


def pack_down(out, row):
    def put(c, value):
        for half in range(2):
            for k in range(2):
                out[c // 128 + k, row + 128 * half : row + 128 * (half + 1), :] = value[
                    128 * k : 128 * (k + 1), 256 * half : 256 * (half + 1)
                ].astype(BF)

    return put


def pack_qkv(out, row):
    def put(e, value):
        for p in range(8):
            out[p, row + 64 * e : row + 64 * (e + 1), :] = value[64 * p : 64 * (p + 1)].astype(BF)

    return put


def own_ctx(t, recv):
    full = jnp.concatenate([gather_ctx(recv, s) for s in range(2)], 1)
    return jnp.where(t == 0, full[0:256], full[256:512])


def pack_out(out, row, ctx, upstream):
    value = mm(ctx, upstream)
    for p in range(8):
        for half in range(2):
            out[p, row + 32 * half : row + 32 * (half + 1), :] = value[
                32 * p : 32 * (p + 1), 256 * half : 256 * (half + 1)
            ].astype(BF)


def first_body(
    at, pos, freqs, x, gain, bias, w_qkv, b_qkv, w_up, b_up, w_down, w_out,
    send, pair, act, slope, cs,
):
    pair[256:512] = w_out[...]
    for s in range(2):
        p = pos[s : s + 1, :].astype(F32)
        angle = freqs[...] * p
        cs[s, 0] = jnp.cos(angle)
        cs[s, 1] = jnp.sin(angle)
    normed, _ = norm_rows(x[...])
    attn_in = (normed * gain[0, 0:1] + bias[0, 0:1]).astype(BF)
    mlp_in = (normed * gain[0, 1:2] + bias[0, 1:2]).astype(BF)
    send_qkv(send, attn_in, w_qkv, b_qkv, 0, cs)
    row = lax.broadcasted_iota(jnp.int32, (16, BLK), 0)
    token = at[0] * BLK + lax.broadcasted_iota(jnp.int32, (1, BLK), 1)
    for s in range(2):
        start = jnp.maximum(token - pos[s : s + 1, :], 0)
        high = (start // 8).astype(F32)
        low = (start % 8).astype(F32)
        block = jnp.where(row == 0, high, jnp.where(row == 1, low, 0.0)).astype(BF)
        for h in range(4):
            send[s * 4 + h, 3 * HEAD : 3 * HEAD + 16, :] = block
    pair[0:256] = feed_forward(mlp_in, w_up, b_up, 0, w_down, act, slope).astype(BF)


def load_rows(recv, lo, hi):
    return jnp.concatenate([recv[i, lo:hi, :] for i in range(8)], 1)


def starts_of(recv):
    rows = load_rows(recv, 3 * HEAD, 3 * HEAD + 16).astype(F32)
    return rows[0:1] * 8.0 + rows[1:2]


def visible_of(start, c, length):
    key = lax.broadcasted_iota(jnp.int32, (length, CHUNK), 0)
    query = lax.broadcasted_iota(jnp.int32, (length, CHUNK), 1) + c * CHUNK
    return (key <= query) & (key >= start[:, c * CHUNK : (c + 1) * CHUNK])


def attend_body(recv, send, lse, ctx, start_out):
    q = load_rows(recv, 0, HEAD)
    k_t = load_rows(recv, HEAD, 2 * HEAD)
    v_t = load_rows(recv, 2 * HEAD, 3 * HEAD)
    k = k_t.astype(F32).T.astype(BF)
    start = starts_of(recv).astype(jnp.int32)
    start_out[...] = start
    for c in range(4):
        cols = slice(c * CHUNK, (c + 1) * CHUNK)
        length = (c + 1) * CHUNK
        scores = mm(k[:length], q[:, cols])
        scores = jnp.where(visible_of(start, c, length), scores, NEG)
        peak = jnp.max(scores, 0, keepdims=True)
        shifted = jnp.exp(scores - peak)
        total = jnp.sum(shifted, 0, keepdims=True)
        lse[:, cols] = peak + jnp.log(total)
        out = mm(v_t[:, :length], shifted.astype(BF)) / total
        ctx[:, cols] = out
        for i in range(CHUNK // BLK):
            block = out[:, i * BLK : (i + 1) * BLK].astype(BF)
            for t in range(2):
                send[c * (CHUNK // BLK) + i, t] = block


def attend_both_body(recv, start, _, send, dk, dv):
    q = load_rows(recv, 0, HEAD)
    k_t = load_rows(recv, HEAD, 2 * HEAD)
    v_t = load_rows(recv, 2 * HEAD, 3 * HEAD)
    d_ctx = load_rows(recv, 3 * HEAD, 4 * HEAD)
    k = k_t.astype(F32).T.astype(BF)
    v = v_t.astype(F32).T.astype(BF)
    dk[...] = jnp.zeros_like(dk)
    dv[...] = jnp.zeros_like(dv)
    for c in range(4):
        cols = slice(c * CHUNK, (c + 1) * CHUNK)
        length = (c + 1) * CHUNK
        scores = mm(k[:length], q[:, cols])
        scores = jnp.where(visible_of(start[...], c, length), scores, NEG)
        peak = jnp.max(scores, 0, keepdims=True)
        shifted = jnp.exp(scores - peak)
        probs = shifted * (1.0 / jnp.sum(shifted, 0, keepdims=True))
        probs_b = probs.astype(BF)
        out = mm(v_t[:, :length], probs_b)
        dq = backward_chunk(q, k_t, v, d_ctx, probs, probs_b, out, cols, length, dk, dv)
        for i in range(CHUNK // BLK):
            b = c * (CHUNK // BLK) + i
            for t in range(2):
                send[b, t, 0:HEAD] = out[:, i * BLK : (i + 1) * BLK].astype(BF)
                send[b, t, HEAD : 2 * HEAD] = dq[:, i * BLK : (i + 1) * BLK].astype(BF)
    put_kv(send, dk, dv, 2 * HEAD)


def backward_chunk(q, k_t, v, d_ctx, probs, probs_b, out, cols, length, dk, dv):
    d_out = d_ctx[:, cols]
    d_probs = mm(v[:length], d_out)
    delta = jnp.sum(d_out.astype(F32) * out, 0, keepdims=True)
    d_scores = (probs * (d_probs - delta)).astype(BF)
    dk[:, :length] += mm(q[:, cols], d_scores, 1, 1)
    dv[:, :length] += mm(d_out, probs_b, 1, 1)
    return mm(k_t[:, :length], d_scores) * (HEAD**-0.5)


def put_kv(send, dk, dv, row):
    for b in range(8):
        for t in range(2):
            send[b, t, row : row + HEAD] = dk[:, b * BLK : (b + 1) * BLK].astype(BF)
            send[b, t, row + HEAD : row + 2 * HEAD] = dv[:, b * BLK : (b + 1) * BLK].astype(BF)


def attend_back_body(recv, recv_d, start, lse, ctx, _, send, dk, dv):
    ride = recv_d[0, 64:192].astype(F32)
    for i in range(1, 8):
        ride = ride + recv_d[i, 64:192].astype(F32)
    ride = ride.astype(BF)
    for b in range(8):
        for t in range(2):
            send[b, t, 192:320] = ride
    q = load_rows(recv, 0, HEAD)
    k_t = load_rows(recv, HEAD, 2 * HEAD)
    v_t = load_rows(recv, 2 * HEAD, 3 * HEAD)
    d_ctx = load_rows(recv_d, 0, HEAD)
    k = k_t.astype(F32).T.astype(BF)
    v = v_t.astype(F32).T.astype(BF)
    dk[...] = jnp.zeros_like(dk)
    dv[...] = jnp.zeros_like(dv)
    for c in range(4):
        cols = slice(c * CHUNK, (c + 1) * CHUNK)
        length = (c + 1) * CHUNK
        scores = mm(k[:length], q[:, cols])
        scores = jnp.where(visible_of(start[...], c, length), scores, NEG)
        probs = jnp.exp(scores - lse[:, cols])
        probs_b = probs.astype(BF)
        dq = backward_chunk(q, k_t, v, d_ctx, probs, probs_b, ctx[:, cols], cols, length, dk, dv)
        for i in range(CHUNK // BLK):
            for t in range(2):
                send[c * (CHUNK // BLK) + i, t, 0:HEAD] = dq[:, i * BLK : (i + 1) * BLK].astype(BF)
    put_kv(send, dk, dv, HEAD)


def gather_ctx(recv, s):
    return jnp.concatenate([recv[s * 4 + h, t, 0:HEAD, :] for t in range(2) for h in range(4)], 0)


def ordered(t, own, other):
    return jnp.where(t == 0, own, other), jnp.where(t == 0, other, own)


def out_other(others):
    halves = [
        jnp.concatenate([others[3, 64 * p + 32 * c : 64 * p + 32 * (c + 1), :] for p in range(8)], 0)
        for c in range(2)
    ]
    return jnp.concatenate(halves, 1)


def branch_of(t, recv, w_own, w_other):
    first, second = ordered(t, w_own, w_other)
    w = jnp.concatenate([first, second], 0)
    rows = []
    for s in range(2):
        rows.append(mm(gather_ctx(recv, s).astype(F32).T.astype(BF), w))
    return jnp.concatenate(rows, 0)


def middle_body(
    at, x, pair, pair_other, recv, w_out_own, out_bias, gain, bias,
    w_qkv, b_qkv, w_up, b_up, w_down, w_out, cot, cs,
    stream, send, grads, parts, d_b_up, d_sum, act, slope,
):
    branch = pair[0:256].astype(F32) + pair_other[0:256].astype(F32)
    branch = branch + branch_of(at[1], recv, w_out_own[...], pair_other[256:512])
    out = x[...] + branch + out_bias[0, 0:1] + out_bias[0, 1:2]
    stream[...] = out
    normed, _ = norm_rows(out)
    attn_in = (normed * gain[1, 0:1] + bias[1, 0:1]).astype(BF)
    mlp_in = (normed * gain[1, 1:2] + bias[1, 1:2]).astype(BF)
    send_qkv(send, attn_in, w_qkv, b_qkv, 1, cs)
    g_b = cot[...].astype(BF)
    d_ctx = mm(w_out[...], g_b, 1, 1)
    for s in range(2):
        for h in range(4):
            send[s * 4 + h, 3 * HEAD : 4 * HEAD, :] = d_ctx[
                h * HEAD : (h + 1) * HEAD, s * BLK : (s + 1) * BLK
            ].astype(BF)
    d_sum[...] = jnp.sum(cot[...], 0, keepdims=True)
    parts[0:256] = feed_forward(mlp_in, w_up, b_up, 1, w_down, act, slope).astype(BF)
    parts[256:512] = feed_back(
        g_b, act, slope, mlp_in, w_up, w_down, pack_up(grads, 0), pack_down(grads, 256), d_b_up
    ).astype(BF)


def norm_back(
    t, x, g, d_mlp_in, recv, row, w_own, others, cs, gain, bias, layer, d_qkv, d_b_qkv, d_norm
):
    normed, inv = norm_rows(x)
    attn_in = (normed * gain[layer, 0:1] + bias[layer, 0:1]).astype(BF)
    attn_t = attn_in.astype(F32).T.astype(BF)
    d_attn_t = None
    for e in range(3):
        halves = []
        for tt in range(2):
            blocks = []
            for h in range(4):
                pieces = []
                for s in range(2):
                    lo = row + e * HEAD
                    u = recv[s * 4 + h, tt, lo : lo + HEAD, :]
                    if e < 2:
                        u = turn_back(u.astype(F32), cs[s, 0], cs[s, 1]).astype(BF)
                    pieces.append(u)
                blocks.append(jnp.concatenate(pieces, 1))
            halves.append(jnp.concatenate(blocks, 0))
        first, second = ordered(t, w_own[e], others[e])
        term = mm(first, halves[0]) + mm(second, halves[1])
        d_attn_t = term if d_attn_t is None else d_attn_t + term
        own = jnp.where(t == 0, halves[0], halves[1])
        d_qkv(e, mm(attn_t, own, 1, 1))
        d_b_qkv[e : e + 1] = mm(jnp.ones((8, own.shape[1]), BF), own, 1, 1)[0:1]
    d_attn_in = d_attn_t.T
    d_norm[0:1] = jnp.sum(d_attn_in * normed, 0, keepdims=True)
    d_norm[1:2] = jnp.sum(d_mlp_in * normed, 0, keepdims=True)
    d_norm[2:3] = jnp.sum(d_attn_in, 0, keepdims=True)
    d_norm[3:4] = jnp.sum(d_mlp_in, 0, keepdims=True)
    d_normed = d_attn_in * gain[layer, 0:1] + d_mlp_in * gain[layer, 1:2]
    return g + inv * (
        d_normed
        - jnp.mean(d_normed, -1, keepdims=True)
        - normed * jnp.mean(d_normed * normed, -1, keepdims=True)
    )


def turn_point_body(
    at, stream, parts, parts_other, recv, w_out, w_qkv, others, out_bias,
    gain, bias, cot, cs, x, act, slope, w_up, w_down, w_out_first, recv_first, sums_a,
    block_out, g_out, send, grads, part, d_b_up, d_b_qkv, d_norm, d_sum,
):
    t = at[1]
    branch = parts[0:256].astype(F32) + parts_other[0:256].astype(F32)
    branch = branch + branch_of(t, recv, w_out[...], out_other(others))
    block_out[...] = stream[...] + branch + out_bias[1, 0:1] + out_bias[1, 1:2]
    d_mlp_in = parts[256:512].astype(F32) + parts_other[256:512].astype(F32)
    g = norm_back(
        t, stream[...], cot[...], d_mlp_in, recv, HEAD, w_qkv, others, cs, gain, bias, 1,
        pack_qkv(grads, 0), d_b_qkv, d_norm,
    )
    g_out[...] = g
    g_b = g.astype(BF)
    d_sum[...] = jnp.sum(g, 0, keepdims=True)
    d_ctx = mm(w_out_first[...], g_b, 1, 1)
    for s in range(2):
        for h in range(4):
            send[s * 4 + h, 0:HEAD] = d_ctx[
                h * HEAD : (h + 1) * HEAD, s * BLK : (s + 1) * BLK
            ].astype(BF)
    for q in range(8):
        for c in range(2):
            send[q, 64 + 64 * c : 128 + 64 * c] = sums_a[
                64 * q : 64 * (q + 1), BLK * c : BLK * (c + 1)
            ]
    pack_out(grads, 704, own_ctx(t, recv), cot[...].astype(BF))
    pack_out(grads, 768, own_ctx(t, recv_first), g_b)
    normed, _ = norm_rows(x[...])
    mlp_in = (normed * gain[0, 1:2] + bias[0, 1:2]).astype(BF)
    part[...] = feed_back(
        g_b, act, slope, mlp_in, w_up, w_down, pack_up(grads, 192), pack_down(grads, 448), d_b_up
    ).astype(BF)


def last_body(
    at, x, g, part, part_other, recv, w_qkv, others, cs, gain, bias,
    d_b_up0, d_b_up1, d_b_qkv1, d_norm1, d_sum0, d_sum1,
    in_grad, grads, sums_a, d_b_qkv0, d_norm0,
):
    d_mlp_in = part[...].astype(F32) + part_other[...].astype(F32)
    in_grad[...] = norm_back(
        at[1], x[...], g[...], d_mlp_in, recv, 0, w_qkv, others, cs, gain, bias, 0,
        pack_qkv(grads, 0), d_b_qkv0, d_norm0,
    )
    for q in range(8):
        both_planes = recv[q, :, 192:320]
        block = jnp.where(at[1] == 0, both_planes[0], both_planes[1])
        for c in range(2):
            sums_a[64 * q : 64 * (q + 1), BLK * c : BLK * (c + 1)] = block[64 * c : 64 * (c + 1)]

    def lanes(ref, row, count):
        return [ref[row : row + 1, 256 * c : 256 * (c + 1)] for c in range(count)]

    def norms(ref):
        return [v for r in range(4) for v in lanes(ref, r, 2)]

    rows = [
        lanes(d_b_up0, 0, 4)
        + lanes(d_b_up1, 0, 4)
        + [v for e in range(3) for ref in (d_b_qkv0, d_b_qkv1) for v in lanes(ref, e, 1)],
        lanes(d_sum0, 0, 2) + lanes(d_sum1, 0, 2) + norms(d_norm0),
        norms(d_norm1),
    ]
    for p in range(8):
        have = rows[p] if p < len(rows) else []
        fill = [jnp.zeros((16 - len(have), 256), F32)]
        grads[p, 192:208, :] = jnp.concatenate(have + fill, 0).astype(BF)


def chunk_body(at, w_qkv, w_out, out):
    for layer in range(2):
        for e in range(3):
            out[layer, e] = w_qkv[layer, e]
        out[layer, 3, 0:32] = w_out[layer, :, 0:256]
        out[layer, 3, 32:64] = w_out[layer, :, 256:512]


def chunk_of(at, wq, w_out):
    return pl.pallas_call(
        chunk_body,
        out_shape=jax.ShapeDtypeStruct((2, 4, 64, 256), BF),
        grid_spec=pltpu.PrefetchScalarGridSpec(
            num_scalar_prefetch=1,
            grid=(1,),
            in_specs=[
                pl.BlockSpec((2, 3, 64, 256), lambda i, at: (0, 0, at[2], 0)),
                pl.BlockSpec((2, 32, 512), lambda i, at: (0, at[2], 0)),
            ],
            out_specs=pl.BlockSpec((2, 4, 64, 256), lambda i, at: (0, 0, 0, 0)),
        ),
        compiler_params=pltpu.CompilerParams(vmem_limit_bytes=40 * 1024 * 1024),
        name="chunk",
    )(at, far(wq), far(w_out))


def mix_body(got, early, first, out, first_out):
    total = got[0].astype(F32)
    for i in range(1, 8):
        total = total + got[i].astype(F32)
    for q in range(8):
        mine = [early[104 * q : 104 * (q + 1)].astype(F32), total[24 * q : 24 * (q + 1)]]
        out[q, 0:128] = jnp.concatenate(mine, 0).astype(BF)
        out[q, 128:144] = total[192:208].astype(BF) if q == 0 else jnp.zeros((16, 256), BF)
    first_out[...] = first[...]


def sum_body(got, out):
    total = got[0].astype(F32)
    for i in range(1, 8):
        total = total + got[i].astype(F32)
    for q in range(8):
        out[q] = total.astype(BF)


def unpack_first_body(first, g_up, g_down):
    for k in range(2):
        for c in range(4):
            cols = slice(256 * c, 256 * (c + 1))
            g_up[0, 64 * k : 64 * (k + 1), cols] = first[k, 64 * c : 64 * (c + 1)].astype(F32)
        for c in range(2):
            rows = first[k, 256 + 128 * c : 256 + 128 * (c + 1)]
            cols = slice(256 * c, 256 * (c + 1))
            g_down[0, 128 * k : 128 * (k + 1), cols] = rows.astype(F32)


def unpack_rest_body(rest, _, __, g_up, g_down, g_qkv, g_out, g_b_up, g_b_qkv, g_sum, g_gain, g_bias):
    p = pl.program_id(0)
    for k in range(2):
        for q in range(8):
            block = rest[k, q, 0:128].astype(F32)
            for i in range(16):
                value = block[8 * i : 8 * (i + 1)]
                row = 104 * q + 8 * i
                if i >= 13:
                    row = 24 * q + 8 * (i - 13)
                    r = 64 * k + row % 64
                    g_qkv[0, row // 64, r : r + 8] = value
                elif row < 192:
                    r = 64 * k + row % 64
                    g_qkv[1, row // 64, r : r + 8] = value
                elif row < 448:
                    c, r = divmod(row - 192, 64)
                    r += 64 * k
                    g_up[0, r : r + 8, 256 * c : 256 * (c + 1)] = value
                elif row < 704:
                    c, r = divmod(row - 448, 128)
                    r += 128 * k
                    g_down[0, r : r + 8, 256 * c : 256 * (c + 1)] = value
                else:
                    c, r = divmod((row - 704) % 64, 32)
                    r += 32 * k
                    g_out[1 - (row - 704) // 64, r : r + 8, 256 * c : 256 * (c + 1)] = value

    tiny = [rest[k, 0, 128:144].astype(F32) for k in range(2)]

    @pl.when(p == 0)
    def _():
        for layer in range(2):
            for c in range(4):
                r = 4 * layer + c
                g_b_up[layer : layer + 1, 256 * c : 256 * (c + 1)] = tiny[0][r : r + 1]
        for e in range(3):
            for layer in range(2):
                r = 8 + 2 * e + layer
                g_b_qkv[e, layer : layer + 1, :] = tiny[0][r : r + 1]
        for layer in range(2):
            for c in range(2):
                r = 2 * layer + c
                for which in range(2):
                    g_sum[layer, which : which + 1, 256 * c : 256 * (c + 1)] = tiny[1][r : r + 1]

    def norms(layer, rows, base):
        for which in range(2):
            for c in range(2):
                cols = slice(256 * c, 256 * (c + 1))
                r = base + 2 * which + c
                g_gain[layer, which : which + 1, cols] = rows[r : r + 1]
                g_bias[layer, which : which + 1, cols] = rows[r + 4 : r + 5]

    @pl.when(p == 0)
    def _():
        norms(0, tiny[1], 4)

    @pl.when(p == 1)
    def _():
        norms(1, tiny[0], 0)


UP = (2, 512, 1024)
DOWN = (2, 1024, 512)


def unpack(first, rest):
    def place(layer):
        return [
            pl.BlockSpec((1, 128, 1024), lambda p: (layer, p, 0)),
            pl.BlockSpec((1, 256, 512), lambda p: (layer, p, 0)),
        ]

    params = pltpu.CompilerParams(vmem_limit_bytes=40 * 1024 * 1024)
    g_up, g_down = pl.pallas_call(
        unpack_first_body,
        grid=(4,),
        out_shape=[pltpu.HBM(UP, F32), pltpu.HBM(DOWN, F32)],
        in_specs=[pl.BlockSpec((2, 512, 256), lambda p: (p, 0, 0))],
        out_specs=place(1),
        compiler_params=params,
        name="unpack_first",
    )(far(first))
    outs = [
        ((2, 3, 512, 256), pl.BlockSpec((2, 3, 128, 256), lambda p: (0, 0, p, 0))),
        ((2, 256, 512), pl.BlockSpec((2, 64, 512), lambda p: (0, p, 0))),
        ((2, 1024), whole((2, 1024))),
        ((3, 2, 256), whole((3, 2, 256))),
        ((2, 2, 512), whole((2, 2, 512))),
        ((2, 2, 512), whole((2, 2, 512))),
        ((2, 2, 512), whole((2, 2, 512))),
    ]
    return pl.pallas_call(
        unpack_rest_body,
        grid=(4,),
        out_shape=[pltpu.HBM(shape, F32) for shape in [UP, DOWN] + [o[0] for o in outs]],
        in_specs=[
            pl.BlockSpec((2, 8, 144, 256), lambda p: (p, 0, 0, 0)),
            pl.BlockSpec(memory_space=pl.ANY),
            pl.BlockSpec(memory_space=pl.ANY),
        ],
        out_specs=place(0) + [spec for _, spec in outs],
        input_output_aliases={1: 0, 2: 1},
        compiler_params=params,
        name="unpack_rest",
    )(far(rest), far(g_up), far(g_down))


def swap(value):
    return lax.ppermute(value, "tensor", [(0, 1), (1, 0)])


def exchange(value, axes):
    return lax.all_to_all(value, axes, 0, 0)


def both(value):
    flat = value.reshape((16,) + value.shape[2:])
    return exchange(flat, ("context", "tensor")).reshape(value.shape)


def shards(
    tokens_in, cotangent, positions, w_qkv, b_qkv, w_out, w_up, b_up, w_down, out_bias, ln_gain, ln_bias
):
    rows, width = 256, 512
    x = tokens_in.reshape(rows, width)
    cot = cotangent.reshape(rows, width)
    wq = jnp.transpose(w_qkv, (0, 2, 1, 3))
    bq = jnp.transpose(b_qkv, (1, 0, 2))
    at = jnp.stack(
        [lax.axis_index("context"), lax.axis_index("tensor"), lax.axis_index("dp")]
    ).astype(jnp.int32)
    freqs = jnp.asarray(FREQS).reshape(HALF, 1)
    chunk = swap(chunk_of(at, wq, w_out))
    send, pair, act, slope, cs = call(
        first_body,
        [
            ((8, 208, BLK), BF),
            ((2 * rows, width), BF),
            pltpu.HBM((rows, 1024), BF),
            pltpu.HBM((rows, 1024), BF),
            ((2, 2, HALF, BLK), F32),
        ],
        (
            at, positions, freqs, Far(x), ln_gain, ln_bias, Layer(wq, 0), bq, Layer(w_up, 0), b_up,
            Layer(w_down, 0), Layer(w_out, 0),
        ),
        "norm_qkv_feed",
        smem_first=True,
    )
    pair_other = swap(pair)
    mark = send[0, 0, 0]
    chunk = jnp.where(mark == mark, chunk, 0)
    others = lax.all_gather(chunk, "dp", axis=2, tiled=True)
    recv = exchange(send, "context")
    ctx_send, lse, ctx, start = call(
        attend_body,
        [((8, 2, HEAD, BLK), BF), ((1, 1024), F32), ((HEAD, 1024), F32), ((1, 1024), jnp.int32)],
        (recv,),
        "attend",
    )
    recv_ctx = both(ctx_send)
    stream, send, grads_a, parts, d_b_up1, d_sum1 = call(
        middle_body,
        [
            pltpu.HBM((rows, width), F32),
            ((8, 256, BLK), BF),
            pltpu.HBM((8, 512, 256), BF),
            ((2 * rows, width), BF),
            ((1, 1024), F32),
            ((1, width), F32),
        ],
        (
            at, Far(x), pair, pair_other, recv_ctx, Layer(w_out, 0), out_bias, ln_gain, ln_bias,
            Layer(wq, 1), bq, Layer(w_up, 1), b_up, Layer(w_down, 1), Layer(w_out, 1), Far(cot), cs,
        ),
        "middle",
        scratch=[pltpu.VMEM((rows, 1024), BF), pltpu.VMEM((rows, 1024), BF)],
        smem_first=True,
    )
    sums_a = lax.psum_scatter(grads_a, "dp", scatter_dimension=0)
    parts_other = swap(parts)
    recv_both = exchange(send, "context")
    (both_send,) = call(
        attend_both_body,
        [((8, 2, 256, BLK), BF)],
        (recv_both, start, After(parts_other)),
        "attend_both",
        scratch=[pltpu.VMEM((HEAD, 1024), F32), pltpu.VMEM((HEAD, 1024), F32)],
    )
    recv_grad = both(both_send)
    block_out, g, send, grads_b, part_g, d_b_up0, d_b_qkv1, d_norm1, d_sum0 = call(
        turn_point_body,
        [
            pltpu.HBM((rows, width), F32),
            pltpu.HBM((rows, width), F32),
            ((8, 192, BLK), BF),
            pltpu.HBM((8, 832, 256), BF),
            ((rows, width), BF),
            ((1, 1024), F32),
            ((3, 256), F32),
            ((4, width), F32),
            ((1, width), F32),
        ],
        (
            at, Far(stream), parts, parts_other, recv_grad, Layer(w_out, 1), Layer(wq, 1),
            Layer(others, 1), out_bias, ln_gain, ln_bias, Far(cot), cs, Far(x), Far(act), Far(slope),
            Layer(w_up, 0), Layer(w_down, 0), Layer(w_out, 0), recv_ctx, Far(sums_a),
        ),
        "turn_point",
        smem_first=True,
    )
    sums_b = lax.psum_scatter(grads_b, "dp", scatter_dimension=0)
    part_g_other = swap(part_g)
    recv_d = exchange(send, "context")
    (back_send,) = call(
        attend_back_body,
        [((8, 2, 320, BLK), BF)],
        (recv, recv_d, start, lse, ctx, After(part_g_other)),
        "attend_back",
        scratch=[pltpu.VMEM((HEAD, 1024), F32), pltpu.VMEM((HEAD, 1024), F32)],
    )
    recv_grad0 = both(back_send)
    in_grad, grads_c, sums_a, _, _ = call(
        last_body,
        [
            pltpu.HBM((rows, width), F32),
            ((8, 208, 256), BF),
            pltpu.HBM((512, 256), BF),
            ((3, 256), F32),
            ((4, width), F32),
        ],
        (
            at, Far(x), Far(g), part_g, part_g_other, recv_grad0, Layer(wq, 0), Layer(others, 0), cs,
            ln_gain, ln_bias, d_b_up0, d_b_up1, d_b_qkv1, d_norm1, d_sum0, d_sum1,
        ),
        "last",
        smem_first=True,
    )
    mixed, sums_a = call(
        mix_body,
        [((8, 144, 256), BF), pltpu.HBM((512, 256), BF)],
        (exchange(grads_c, "dp"), Far(sums_b), Far(sums_a)),
        "mix",
    )
    full_a = lax.all_gather(sums_a, "dp")
    (summed,) = call(sum_body, [((8, 144, 256), BF)], (exchange(mixed, "context"),), "sum")
    full_bc = lax.all_gather(exchange(summed, "context"), "dp")
    g_up, g_down, g_qkv, g_out, g_b_up, g_b_qkv, g_sum, g_gain, g_bias = unpack(full_a, full_bc)
    return (
        block_out.reshape(tokens_in.shape),
        in_grad.reshape(tokens_in.shape),
        jnp.transpose(g_qkv, (0, 2, 1, 3)),
        jnp.transpose(g_b_qkv, (1, 0, 2)),
        g_out,
        g_up,
        g_b_up,
        g_down,
        g_sum,
        g_gain,
        g_bias,
    )


def solution(mesh):
    return jax.shard_map(
        shards,
        mesh=mesh,
        in_specs=(
            P("dp", "context", None),
            P("dp", "context", None),
            P("dp", "context"),
            P(None, None, None, "tensor"),
            P(None, None, "tensor"),
            P(None, "tensor", None),
            P(None, None, "tensor"),
            P(None, "tensor"),
            P(None, "tensor", None),
            P(),
            P(),
            P(),
        ),
        out_specs=(
            P("dp", "context", None),
            P("dp", "context", None),
            P(None, None, None, "tensor"),
            P(None, None, "tensor"),
            P(None, "tensor", None),
            P(None, None, "tensor"),
            P(None, "tensor"),
            P(None, "tensor", None),
            P(),
            P(),
            P(),
        ),
        check_vma=False,
    )
```

```python
from functools import partial

import numpy as np

import jax
import jax.numpy as jnp
from jax import lax
from jax.experimental import pallas as pl
from jax.experimental.pallas import tpu as pltpu
from jax.sharding import PartitionSpec as P

EPS = 1e-05
HALF = 8
HEAD = 64
BLK = 128
CHUNK = 256
NEG = -1e30
BF = jnp.bfloat16
F32 = jnp.float32

FREQS = (10000.0 ** (-np.arange(HALF, dtype=np.float64) * 2.0 / 16.0)).astype(np.float32)


def mm(a, b, ca=1, cb=0):
    return lax.dot_general(a, b, (((ca,), (cb,)), ((), ())), preferred_element_type=F32)


class After:
    def __init__(self, array):
        self.array = array

    def spec(self):
        return pl.BlockSpec(memory_space=pl.ANY)


class Layer:
    def __init__(self, array, index):
        self.array, self.index = far(array), index

    def spec(self):
        rest = self.array.shape[1:]
        place = (self.index,) + (0,) * len(rest)
        return pl.BlockSpec((None,) + rest, lambda i: place)


class Far:
    def __init__(self, array):
        self.array = far(array)

    def spec(self):
        return whole(self.array.shape)


Kept = type(pltpu.HBM((8, 128), F32))


def far(array):
    return pltpu.with_memory_space_constraint(array, pltpu.HBM)


def whole(shape):
    return pl.BlockSpec(shape, lambda i: (0,) * len(shape))


def call(body, out_shape, args, name, scratch=(), smem_first=False):
    specs = [
        a.spec() if isinstance(a, (Layer, Far, After)) else whole(a.shape) for a in args
    ]
    args = [a.array if isinstance(a, (Layer, Far, After)) else a for a in args]
    if smem_first:
        specs[0] = pl.BlockSpec(memory_space=pltpu.SMEM)
    return pl.pallas_call(
        body,
        grid=(1,),
        out_shape=[o if isinstance(o, Kept) else jax.ShapeDtypeStruct(*o) for o in out_shape],
        in_specs=specs,
        out_specs=[whole(o.shape if isinstance(o, Kept) else o[0]) for o in out_shape],
        scratch_shapes=list(scratch),
        compiler_params=pltpu.CompilerParams(vmem_limit_bytes=40 * 1024 * 1024),
        name=name,
    )(*args)


def norm_rows(x):
    mean = jnp.mean(x, -1, keepdims=True)
    cen = x - mean
    inv = lax.rsqrt(jnp.mean(cen * cen, -1, keepdims=True) + EPS)
    return cen * inv, inv


def turn(t, cos, sin):
    a, b = t[:HALF], t[HALF : 2 * HALF]
    return jnp.concatenate([a * cos - b * sin, b * cos + a * sin, t[2 * HALF :]], 0)


def turn_back(u, cos, sin):
    a, b = u[:HALF], u[HALF : 2 * HALF]
    return jnp.concatenate([a * cos + b * sin, b * cos - a * sin, u[2 * HALF :]], 0)


def send_qkv(send, attn_in, w_qkv, b_qkv, layer, cs):
    for e in range(3):
        turned = (mm(attn_in, w_qkv[e]) + b_qkv[e, layer : layer + 1]).T
        for s in range(2):
            cos, sin = cs[s, 0], cs[s, 1]
            for h in range(4):
                j = s * 4 + h
                part = turned[h * HEAD : (h + 1) * HEAD, s * BLK : (s + 1) * BLK]
                if e < 2:
                    part = turn(part, cos, sin)
                if e == 0:
                    part = part * (HEAD**-0.5)
                send[j, e * HEAD : (e + 1) * HEAD, :] = part.astype(BF)


def feed_forward(mlp_in, w_up, b_up, layer, w_down, act, slope):
    width = w_up.shape[1]
    total = None
    for c in range(0, width, 256):
        cols = slice(c, c + 256)
        pre = mm(mlp_in, w_up[:, cols]) + b_up[layer : layer + 1, cols]
        cdf = 0.5 + 0.5 * lax.erf(pre * np.float32(0.7071067811865476))
        a = (pre * cdf).astype(BF)
        act[:, cols] = a
        tail = pre * (jnp.exp(-0.5 * pre * pre) * np.float32(0.3989422804014327))
        slope[:, cols] = (cdf + tail).astype(BF)
        term = mm(a, w_down[cols, :])
        total = term if total is None else total + term
    return total


def feed_back(g_b, act, slope, mlp_in, w_up, w_down, d_up, d_down, d_b_up):
    width = w_up.shape[1]
    total = None
    mlp_t = mlp_in.T
    for c in range(0, width, 256):
        cols = slice(c, c + 256)
        d_act = mm(g_b, w_down[cols, :], 1, 1)
        d_pre = d_act * slope[:, cols].astype(F32)
        d_pre_b = d_pre.astype(BF)
        d_b_up[:, cols] = jnp.sum(d_pre_b.astype(F32), 0, keepdims=True)
        d_up(c // 256, mm(mlp_t, d_pre_b))
        d_down(c, mm(act[:, cols].T, g_b))
        term = mm(d_pre_b, w_up[:, cols], 1, 1)
        total = term if total is None else total + term
    return total


def pack_up(out, row):
    def put(c, value):
        for p in range(8):
            out[p, row + 64 * c : row + 64 * (c + 1), :] = value[64 * p : 64 * (p + 1)].astype(BF)

    return put


def pack_down(out, row):
    def put(c, value):
        for half in range(2):
            for k in range(2):
                out[c // 128 + k, row + 128 * half : row + 128 * (half + 1), :] = value[
                    128 * k : 128 * (k + 1), 256 * half : 256 * (half + 1)
                ].astype(BF)

    return put


def pack_qkv(out, row):
    def put(e, value):
        for p in range(8):
            out[p, row + 64 * e : row + 64 * (e + 1), :] = value[64 * p : 64 * (p + 1)].astype(BF)

    return put


def own_ctx(t, recv):
    full = jnp.concatenate([gather_ctx(recv, s) for s in range(2)], 1)
    return jnp.where(t == 0, full[0:256], full[256:512])


def pack_out(out, row, ctx, upstream):
    value = mm(ctx, upstream)
    for p in range(8):
        for half in range(2):
            out[p, row + 32 * half : row + 32 * (half + 1), :] = value[
                32 * p : 32 * (p + 1), 256 * half : 256 * (half + 1)
            ].astype(BF)


def first_body(
    at, pos, freqs, x, gain, bias, w_qkv, b_qkv, w_up, b_up, w_down, w_out,
    send, pair, act, slope, cs,
):
    pair[256:512] = w_out[...]
    for s in range(2):
        p = pos[s : s + 1, :].astype(F32)
        angle = freqs[...] * p
        cs[s, 0] = jnp.cos(angle)
        cs[s, 1] = jnp.sin(angle)
    normed, _ = norm_rows(x[...])
    attn_in = (normed * gain[0, 0:1] + bias[0, 0:1]).astype(BF)
    mlp_in = (normed * gain[0, 1:2] + bias[0, 1:2]).astype(BF)
    send_qkv(send, attn_in, w_qkv, b_qkv, 0, cs)
    row = lax.broadcasted_iota(jnp.int32, (16, BLK), 0)
    token = at[0] * BLK + lax.broadcasted_iota(jnp.int32, (1, BLK), 1)
    for s in range(2):
        start = jnp.maximum(token - pos[s : s + 1, :], 0)
        high = (start // 8).astype(F32)
        low = (start % 8).astype(F32)
        block = jnp.where(row == 0, high, jnp.where(row == 1, low, 0.0)).astype(BF)
        for h in range(4):
            send[s * 4 + h, 3 * HEAD : 3 * HEAD + 16, :] = block
    pair[0:256] = feed_forward(mlp_in, w_up, b_up, 0, w_down, act, slope).astype(BF)


def load_rows(recv, lo, hi):
    return jnp.concatenate([recv[i, lo:hi, :] for i in range(8)], 1)


def starts_of(recv):
    rows = load_rows(recv, 3 * HEAD, 3 * HEAD + 16).astype(F32)
    return rows[0:1] * 8.0 + rows[1:2]


def visible_of(start, c, length):
    key = lax.broadcasted_iota(jnp.int32, (length, CHUNK), 0)
    query = lax.broadcasted_iota(jnp.int32, (length, CHUNK), 1) + c * CHUNK
    return (key <= query) & (key >= start[:, c * CHUNK : (c + 1) * CHUNK])


def attend_body(recv, send, lse, ctx, start_out):
    q = load_rows(recv, 0, HEAD)
    k_t = load_rows(recv, HEAD, 2 * HEAD)
    v_t = load_rows(recv, 2 * HEAD, 3 * HEAD)
    k = k_t.T
    start = starts_of(recv).astype(jnp.int32)
    start_out[...] = start
    for c in range(4):
        cols = slice(c * CHUNK, (c + 1) * CHUNK)
        length = (c + 1) * CHUNK
        scores = mm(k[:length], q[:, cols])
        scores = jnp.where(visible_of(start, c, length), scores, NEG)
        peak = jnp.max(scores, 0, keepdims=True)
        shifted = jnp.exp(scores - peak)
        total = jnp.sum(shifted, 0, keepdims=True)
        lse[:, cols] = peak + jnp.log(total)
        out = mm(v_t[:, :length], shifted.astype(BF)) / total
        ctx[:, cols] = out
        for i in range(CHUNK // BLK):
            block = out[:, i * BLK : (i + 1) * BLK].astype(BF)
            for t in range(2):
                send[c * (CHUNK // BLK) + i, t] = block


def attend_both_body(recv, start, _, send, dk, dv):
    q = load_rows(recv, 0, HEAD)
    k_t = load_rows(recv, HEAD, 2 * HEAD)
    v_t = load_rows(recv, 2 * HEAD, 3 * HEAD)
    d_ctx = load_rows(recv, 3 * HEAD, 4 * HEAD)
    k = k_t.T
    v = v_t.T
    dk[...] = jnp.zeros_like(dk)
    dv[...] = jnp.zeros_like(dv)
    for c in range(4):
        cols = slice(c * CHUNK, (c + 1) * CHUNK)
        length = (c + 1) * CHUNK
        scores = mm(k[:length], q[:, cols])
        scores = jnp.where(visible_of(start[...], c, length), scores, NEG)
        peak = jnp.max(scores, 0, keepdims=True)
        shifted = jnp.exp(scores - peak)
        probs = shifted * (1.0 / jnp.sum(shifted, 0, keepdims=True))
        probs_b = probs.astype(BF)
        out = mm(v_t[:, :length], probs_b)
        dq = backward_chunk(q, k_t, v, d_ctx, probs, probs_b, out, cols, length, dk, dv)
        for i in range(CHUNK // BLK):
            b = c * (CHUNK // BLK) + i
            for t in range(2):
                send[b, t, 0:HEAD] = out[:, i * BLK : (i + 1) * BLK].astype(BF)
                send[b, t, HEAD : 2 * HEAD] = dq[:, i * BLK : (i + 1) * BLK].astype(BF)
    put_kv(send, dk, dv, 2 * HEAD)


def backward_chunk(q, k_t, v, d_ctx, probs, probs_b, out, cols, length, dk, dv):
    d_out = d_ctx[:, cols]
    d_probs = mm(v[:length], d_out)
    delta = jnp.sum(d_out.astype(F32) * out, 0, keepdims=True)
    d_scores = (probs * (d_probs - delta)).astype(BF)
    dk[:, :length] += mm(q[:, cols], d_scores, 1, 1)
    dv[:, :length] += mm(d_out, probs_b, 1, 1)
    return mm(k_t[:, :length], d_scores) * (HEAD**-0.5)


def put_kv(send, dk, dv, row):
    for b in range(8):
        for t in range(2):
            send[b, t, row : row + HEAD] = dk[:, b * BLK : (b + 1) * BLK].astype(BF)
            send[b, t, row + HEAD : row + 2 * HEAD] = dv[:, b * BLK : (b + 1) * BLK].astype(BF)


def attend_back_body(recv, recv_d, start, lse, ctx, _, send, dk, dv):
    ride = recv_d[0, 64:192].astype(F32)
    for i in range(1, 8):
        ride = ride + recv_d[i, 64:192].astype(F32)
    ride = ride.astype(BF)
    for b in range(8):
        for t in range(2):
            send[b, t, 192:320] = ride
    q = load_rows(recv, 0, HEAD)
    k_t = load_rows(recv, HEAD, 2 * HEAD)
    v_t = load_rows(recv, 2 * HEAD, 3 * HEAD)
    d_ctx = load_rows(recv_d, 0, HEAD)
    k = k_t.T
    v = v_t.T
    dk[...] = jnp.zeros_like(dk)
    dv[...] = jnp.zeros_like(dv)
    for c in range(4):
        cols = slice(c * CHUNK, (c + 1) * CHUNK)
        length = (c + 1) * CHUNK
        scores = mm(k[:length], q[:, cols])
        scores = jnp.where(visible_of(start[...], c, length), scores, NEG)
        probs = jnp.exp(scores - lse[:, cols])
        probs_b = probs.astype(BF)
        dq = backward_chunk(q, k_t, v, d_ctx, probs, probs_b, ctx[:, cols], cols, length, dk, dv)
        for i in range(CHUNK // BLK):
            for t in range(2):
                send[c * (CHUNK // BLK) + i, t, 0:HEAD] = dq[:, i * BLK : (i + 1) * BLK].astype(BF)
    put_kv(send, dk, dv, HEAD)


def gather_ctx(recv, s):
    return jnp.concatenate([recv[s * 4 + h, t, 0:HEAD, :] for t in range(2) for h in range(4)], 0)


def ordered(t, own, other):
    return jnp.where(t == 0, own, other), jnp.where(t == 0, other, own)


def out_other(others):
    halves = [
        jnp.concatenate([others[3, 64 * p + 32 * c : 64 * p + 32 * (c + 1), :] for p in range(8)], 0)
        for c in range(2)
    ]
    return jnp.concatenate(halves, 1)


def branch_of(t, recv, w_own, w_other):
    first, second = ordered(t, w_own, w_other)
    w = jnp.concatenate([first, second], 0)
    rows = []
    for s in range(2):
        rows.append(mm(gather_ctx(recv, s).T, w))
    return jnp.concatenate(rows, 0)


def middle_body(
    at, x, pair, pair_other, recv, w_out_own, out_bias, gain, bias,
    w_qkv, b_qkv, w_up, b_up, w_down, w_out, cot, cs,
    stream, send, grads, parts, d_b_up, d_sum, act, slope,
):
    branch = pair[0:256].astype(F32) + pair_other[0:256].astype(F32)
    branch = branch + branch_of(at[1], recv, w_out_own[...], pair_other[256:512])
    out = x[...] + branch + out_bias[0, 0:1] + out_bias[0, 1:2]
    stream[...] = out
    normed, _ = norm_rows(out)
    attn_in = (normed * gain[1, 0:1] + bias[1, 0:1]).astype(BF)
    mlp_in = (normed * gain[1, 1:2] + bias[1, 1:2]).astype(BF)
    send_qkv(send, attn_in, w_qkv, b_qkv, 1, cs)
    g_b = cot[...].astype(BF)
    d_ctx = mm(w_out[...], g_b, 1, 1)
    for s in range(2):
        for h in range(4):
            send[s * 4 + h, 3 * HEAD : 4 * HEAD, :] = d_ctx[
                h * HEAD : (h + 1) * HEAD, s * BLK : (s + 1) * BLK
            ].astype(BF)
    d_sum[...] = jnp.sum(cot[...], 0, keepdims=True)
    parts[0:256] = feed_forward(mlp_in, w_up, b_up, 1, w_down, act, slope).astype(BF)
    parts[256:512] = feed_back(
        g_b, act, slope, mlp_in, w_up, w_down, pack_up(grads, 0), pack_down(grads, 256), d_b_up
    ).astype(BF)


def norm_back(
    t, x, g, d_mlp_in, recv, row, w_own, others, cs, gain, bias, layer, d_qkv, d_b_qkv, d_norm
):
    normed, inv = norm_rows(x)
    attn_in = (normed * gain[layer, 0:1] + bias[layer, 0:1]).astype(BF)
    attn_t = attn_in.T
    d_attn_t = None
    for e in range(3):
        halves = []
        for tt in range(2):
            blocks = []
            for h in range(4):
                pieces = []
                for s in range(2):
                    lo = row + e * HEAD
                    u = recv[s * 4 + h, tt, lo : lo + HEAD, :]
                    if e < 2:
                        u = turn_back(u.astype(F32), cs[s, 0], cs[s, 1]).astype(BF)
                    pieces.append(u)
                blocks.append(jnp.concatenate(pieces, 1))
            halves.append(jnp.concatenate(blocks, 0))
        first, second = ordered(t, w_own[e], others[e])
        term = mm(first, halves[0]) + mm(second, halves[1])
        d_attn_t = term if d_attn_t is None else d_attn_t + term
        own = jnp.where(t == 0, halves[0], halves[1])
        d_qkv(e, mm(attn_t, own, 1, 1))
        d_b_qkv[e : e + 1] = mm(jnp.ones((8, own.shape[1]), BF), own, 1, 1)[0:1]
    d_attn_in = d_attn_t.T
    d_norm[0:1] = jnp.sum(d_attn_in * normed, 0, keepdims=True)
    d_norm[1:2] = jnp.sum(d_mlp_in * normed, 0, keepdims=True)
    d_norm[2:3] = jnp.sum(d_attn_in, 0, keepdims=True)
    d_norm[3:4] = jnp.sum(d_mlp_in, 0, keepdims=True)
    d_normed = d_attn_in * gain[layer, 0:1] + d_mlp_in * gain[layer, 1:2]
    return g + inv * (
        d_normed
        - jnp.mean(d_normed, -1, keepdims=True)
        - normed * jnp.mean(d_normed * normed, -1, keepdims=True)
    )


def turn_point_body(
    at, stream, parts, parts_other, recv, w_out, w_qkv, others, out_bias,
    gain, bias, cot, cs, x, act, slope, w_up, w_down, w_out_first, recv_first, sums_a,
    block_out, g_out, send, grads, part, d_b_up, d_b_qkv, d_norm, d_sum,
):
    t = at[1]
    branch = parts[0:256].astype(F32) + parts_other[0:256].astype(F32)
    branch = branch + branch_of(t, recv, w_out[...], out_other(others))
    block_out[...] = stream[...] + branch + out_bias[1, 0:1] + out_bias[1, 1:2]
    d_mlp_in = parts[256:512].astype(F32) + parts_other[256:512].astype(F32)
    g = norm_back(
        t, stream[...], cot[...], d_mlp_in, recv, HEAD, w_qkv, others, cs, gain, bias, 1,
        pack_qkv(grads, 0), d_b_qkv, d_norm,
    )
    g_out[...] = g
    g_b = g.astype(BF)
    d_sum[...] = jnp.sum(g, 0, keepdims=True)
    d_ctx = mm(w_out_first[...], g_b, 1, 1)
    for s in range(2):
        for h in range(4):
            send[s * 4 + h, 0:HEAD] = d_ctx[
                h * HEAD : (h + 1) * HEAD, s * BLK : (s + 1) * BLK
            ].astype(BF)
    for q in range(8):
        for c in range(2):
            send[q, 64 + 64 * c : 128 + 64 * c] = sums_a[
                64 * q : 64 * (q + 1), BLK * c : BLK * (c + 1)
            ]
    pack_out(grads, 704, own_ctx(t, recv), cot[...].astype(BF))
    pack_out(grads, 768, own_ctx(t, recv_first), g_b)
    normed, _ = norm_rows(x[...])
    mlp_in = (normed * gain[0, 1:2] + bias[0, 1:2]).astype(BF)
    part[...] = feed_back(
        g_b, act, slope, mlp_in, w_up, w_down, pack_up(grads, 192), pack_down(grads, 448), d_b_up
    ).astype(BF)


def last_body(
    at, x, g, part, part_other, recv, w_qkv, others, cs, gain, bias,
    d_b_up0, d_b_up1, d_b_qkv1, d_norm1, d_sum0, d_sum1,
    in_grad, grads, sums_a, d_b_qkv0, d_norm0,
):
    d_mlp_in = part[...].astype(F32) + part_other[...].astype(F32)
    in_grad[...] = norm_back(
        at[1], x[...], g[...], d_mlp_in, recv, 0, w_qkv, others, cs, gain, bias, 0,
        pack_qkv(grads, 0), d_b_qkv0, d_norm0,
    )
    for q in range(8):
        both_planes = recv[q, :, 192:320]
        block = jnp.where(at[1] == 0, both_planes[0], both_planes[1])
        for c in range(2):
            sums_a[64 * q : 64 * (q + 1), BLK * c : BLK * (c + 1)] = block[64 * c : 64 * (c + 1)]

    def lanes(ref, row, count):
        return [ref[row : row + 1, 256 * c : 256 * (c + 1)] for c in range(count)]

    def norms(ref):
        return [v for r in range(4) for v in lanes(ref, r, 2)]

    rows = [
        lanes(d_b_up0, 0, 4)
        + lanes(d_b_up1, 0, 4)
        + [v for e in range(3) for ref in (d_b_qkv0, d_b_qkv1) for v in lanes(ref, e, 1)],
        lanes(d_sum0, 0, 2) + lanes(d_sum1, 0, 2) + norms(d_norm0),
        norms(d_norm1),
    ]
    for p in range(8):
        have = rows[p] if p < len(rows) else []
        fill = [jnp.zeros((16 - len(have), 256), F32)]
        grads[p, 192:208, :] = jnp.concatenate(have + fill, 0).astype(BF)


def chunk_body(at, w_qkv, w_out, out):
    for layer in range(2):
        for e in range(3):
            out[layer, e] = w_qkv[layer, e]
        out[layer, 3, 0:32] = w_out[layer, :, 0:256]
        out[layer, 3, 32:64] = w_out[layer, :, 256:512]


def chunk_of(at, wq, w_out):
    return pl.pallas_call(
        chunk_body,
        out_shape=jax.ShapeDtypeStruct((2, 4, 64, 256), BF),
        grid_spec=pltpu.PrefetchScalarGridSpec(
            num_scalar_prefetch=1,
            grid=(1,),
            in_specs=[
                pl.BlockSpec((2, 3, 64, 256), lambda i, at: (0, 0, at[2], 0)),
                pl.BlockSpec((2, 32, 512), lambda i, at: (0, at[2], 0)),
            ],
            out_specs=pl.BlockSpec((2, 4, 64, 256), lambda i, at: (0, 0, 0, 0)),
        ),
        compiler_params=pltpu.CompilerParams(vmem_limit_bytes=40 * 1024 * 1024),
        name="chunk",
    )(at, far(wq), far(w_out))


def hand_on_body(value, _, out):
    out[...] = value[...]


def mix_body(got, early, first, out, first_out):
    total = got[0].astype(F32)
    for i in range(1, 8):
        total = total + got[i].astype(F32)
    for q in range(8):
        tiny = total[192 + 8 * q : 200 + 8 * q] if q < 2 else jnp.zeros((8, 256), F32)
        mine = [early[104 * q : 104 * (q + 1)].astype(F32), total[24 * q : 24 * (q + 1)], tiny]
        out[q] = jnp.concatenate(mine, 0).astype(BF)
    first_out[...] = first[...]


def sum_body(got, out):
    total = got[0].astype(F32)
    for i in range(1, 8):
        total = total + got[i].astype(F32)
    for q in range(8):
        out[q] = total.astype(BF)


def unpack_first_body(first, g_up, g_down):
    for k in range(2):
        for c in range(4):
            cols = slice(256 * c, 256 * (c + 1))
            g_up[0, 64 * k : 64 * (k + 1), cols] = first[k, 64 * c : 64 * (c + 1)].astype(F32)
        for c in range(2):
            rows = first[k, 256 + 128 * c : 256 + 128 * (c + 1)]
            cols = slice(256 * c, 256 * (c + 1))
            g_down[0, 128 * k : 128 * (k + 1), cols] = rows.astype(F32)


def unpack_rest_body(rest, _, __, g_up, g_down, g_qkv, g_out, g_b_up, g_b_qkv, g_sum, g_gain, g_bias):
    p = pl.program_id(0)
    for k in range(2):
        for q in range(8):
            block = rest[k, q].astype(F32)
            for i in range(16):
                value = block[8 * i : 8 * (i + 1)]
                row = 104 * q + 8 * i
                if i >= 13:
                    row = 24 * q + 8 * (i - 13)
                    r = 64 * k + row % 64
                    g_qkv[0, row // 64, r : r + 8] = value
                elif row < 192:
                    r = 64 * k + row % 64
                    g_qkv[1, row // 64, r : r + 8] = value
                elif row < 448:
                    c, r = divmod(row - 192, 64)
                    r += 64 * k
                    g_up[0, r : r + 8, 256 * c : 256 * (c + 1)] = value
                elif row < 704:
                    c, r = divmod(row - 448, 128)
                    r += 128 * k
                    g_down[0, r : r + 8, 256 * c : 256 * (c + 1)] = value
                else:
                    c, r = divmod((row - 704) % 64, 32)
                    r += 32 * k
                    g_out[1 - (row - 704) // 64, r : r + 8, 256 * c : 256 * (c + 1)] = value

    tiny = [jnp.concatenate([rest[k, q].astype(F32)[128:136] for q in range(2)], 0) for k in range(2)]

    @pl.when(p == 0)
    def _():
        for layer in range(2):
            for c in range(4):
                r = 4 * layer + c
                g_b_up[layer : layer + 1, 256 * c : 256 * (c + 1)] = tiny[0][r : r + 1]
        for e in range(3):
            for layer in range(2):
                r = 8 + 2 * e + layer
                g_b_qkv[e, layer : layer + 1, :] = tiny[0][r : r + 1]
        for layer in range(2):
            for c in range(2):
                r = 2 * layer + c
                for which in range(2):
                    g_sum[layer, which : which + 1, 256 * c : 256 * (c + 1)] = tiny[1][r : r + 1]

    def norms(layer, rows, base):
        for which in range(2):
            for c in range(2):
                cols = slice(256 * c, 256 * (c + 1))
                r = base + 2 * which + c
                g_gain[layer, which : which + 1, cols] = rows[r : r + 1]
                g_bias[layer, which : which + 1, cols] = rows[r + 4 : r + 5]

    @pl.when(p == 0)
    def _():
        norms(0, tiny[1], 4)

    @pl.when(p == 1)
    def _():
        norms(1, tiny[0], 0)


UP = (2, 512, 1024)
DOWN = (2, 1024, 512)


def unpack(first, rest):
    def place(layer):
        return [
            pl.BlockSpec((1, 128, 1024), lambda p: (layer, p, 0)),
            pl.BlockSpec((1, 256, 512), lambda p: (layer, p, 0)),
        ]

    params = pltpu.CompilerParams(vmem_limit_bytes=40 * 1024 * 1024)
    g_up, g_down = pl.pallas_call(
        unpack_first_body,
        grid=(4,),
        out_shape=[pltpu.HBM(UP, F32), pltpu.HBM(DOWN, F32)],
        in_specs=[pl.BlockSpec((2, 512, 256), lambda p: (p, 0, 0))],
        out_specs=place(1),
        compiler_params=params,
        name="unpack_first",
    )(far(first))
    outs = [
        ((2, 3, 512, 256), pl.BlockSpec((2, 3, 128, 256), lambda p: (0, 0, p, 0))),
        ((2, 256, 512), pl.BlockSpec((2, 64, 512), lambda p: (0, p, 0))),
        ((2, 1024), whole((2, 1024))),
        ((3, 2, 256), whole((3, 2, 256))),
        ((2, 2, 512), whole((2, 2, 512))),
        ((2, 2, 512), whole((2, 2, 512))),
        ((2, 2, 512), whole((2, 2, 512))),
    ]
    return pl.pallas_call(
        unpack_rest_body,
        grid=(4,),
        out_shape=[pltpu.HBM(shape, F32) for shape in [UP, DOWN] + [o[0] for o in outs]],
        in_specs=[
            pl.BlockSpec((2, 8, 136, 256), lambda p: (p, 0, 0, 0)),
            pl.BlockSpec(memory_space=pl.ANY),
            pl.BlockSpec(memory_space=pl.ANY),
        ],
        out_specs=place(0) + [spec for _, spec in outs],
        input_output_aliases={1: 0, 2: 1},
        compiler_params=params,
        name="unpack_rest",
    )(far(rest), far(g_up), far(g_down))


def swap(value):
    return lax.ppermute(value, "tensor", [(0, 1), (1, 0)])


def exchange(value, axes):
    return lax.all_to_all(value, axes, 0, 0)


def both(value):
    flat = value.reshape((16,) + value.shape[2:])
    return exchange(flat, ("context", "tensor")).reshape(value.shape)


def shards(
    tokens_in, cotangent, positions, w_qkv, b_qkv, w_out, w_up, b_up, w_down, out_bias, ln_gain, ln_bias
):
    rows, width = 256, 512
    x = tokens_in.reshape(rows, width)
    cot = cotangent.reshape(rows, width)
    wq = jnp.transpose(w_qkv, (0, 2, 1, 3))
    bq = jnp.transpose(b_qkv, (1, 0, 2))
    at = jnp.stack(
        [lax.axis_index("context"), lax.axis_index("tensor"), lax.axis_index("dp")]
    ).astype(jnp.int32)
    freqs = jnp.asarray(FREQS).reshape(HALF, 1)
    chunk = swap(chunk_of(at, wq, w_out))
    send, pair, act, slope, cs = call(
        first_body,
        [
            pltpu.VMEM((8, 208, BLK), BF),
            ((2 * rows, width), BF),
            pltpu.HBM((rows, 1024), BF),
            pltpu.HBM((rows, 1024), BF),
            ((2, 2, HALF, BLK), F32),
        ],
        (
            at, positions, freqs, Far(x), ln_gain, ln_bias, Layer(wq, 0), bq, Layer(w_up, 0), b_up,
            Layer(w_down, 0), Layer(w_out, 0),
        ),
        "norm_qkv_feed",
        smem_first=True,
    )
    pair_other = swap(pair)
    (chunk,) = call(
        hand_on_body, [pltpu.HBM(chunk.shape, BF)], (chunk, After(send)), "hand_on"
    )
    others = lax.all_gather(chunk, "dp", axis=2, tiled=True)
    recv = exchange(send, "context")
    ctx_send, lse, ctx, start = call(
        attend_body,
        [((8, 2, HEAD, BLK), BF), ((1, 1024), F32), pltpu.HBM((HEAD, 1024), F32), ((1, 1024), jnp.int32)],
        (recv,),
        "attend",
    )
    recv_ctx = both(ctx_send)
    stream, send, grads_a, parts, d_b_up1, d_sum1 = call(
        middle_body,
        [
            pltpu.HBM((rows, width), F32),
            ((8, 256, BLK), BF),
            pltpu.HBM((8, 512, 256), BF),
            ((2 * rows, width), BF),
            ((1, 1024), F32),
            ((1, width), F32),
        ],
        (
            at, Far(x), pair, pair_other, recv_ctx, Layer(w_out, 0), out_bias, ln_gain, ln_bias,
            Layer(wq, 1), bq, Layer(w_up, 1), b_up, Layer(w_down, 1), Layer(w_out, 1), Far(cot), cs,
        ),
        "middle",
        scratch=[pltpu.VMEM((rows, 1024), BF), pltpu.VMEM((rows, 1024), BF)],
        smem_first=True,
    )
    sums_a = lax.psum_scatter(grads_a, "dp", scatter_dimension=0)
    parts_other = swap(parts)
    recv_both = exchange(send, "context")
    (both_send,) = call(
        attend_both_body,
        [((8, 2, 256, BLK), BF)],
        (recv_both, start, After(parts_other)),
        "attend_both",
        scratch=[pltpu.VMEM((HEAD, 1024), F32), pltpu.VMEM((HEAD, 1024), F32)],
    )
    recv_grad = both(both_send)
    block_out, g, send, grads_b, part_g, d_b_up0, d_b_qkv1, d_norm1, d_sum0 = call(
        turn_point_body,
        [
            pltpu.HBM((rows, width), F32),
            pltpu.HBM((rows, width), F32),
            pltpu.VMEM((8, 192, BLK), BF),
            pltpu.HBM((8, 832, 256), BF),
            ((rows, width), BF),
            ((1, 1024), F32),
            ((3, 256), F32),
            ((4, width), F32),
            ((1, width), F32),
        ],
        (
            at, Far(stream), parts, parts_other, recv_grad, Layer(w_out, 1), Layer(wq, 1),
            Layer(others, 1), out_bias, ln_gain, ln_bias, Far(cot), cs, Far(x), Far(act), Far(slope),
            Layer(w_up, 0), Layer(w_down, 0), Layer(w_out, 0), recv_ctx, Far(sums_a),
        ),
        "turn_point",
        smem_first=True,
    )
    sums_b = lax.psum_scatter(grads_b, "dp", scatter_dimension=0)
    part_g_other = swap(part_g)
    recv_d = exchange(send, "context")
    (back_send,) = call(
        attend_back_body,
        [((8, 2, 320, BLK), BF)],
        (recv, recv_d, start, lse, ctx, After(part_g_other)),
        "attend_back",
        scratch=[pltpu.VMEM((HEAD, 1024), F32), pltpu.VMEM((HEAD, 1024), F32)],
    )
    recv_grad0 = both(back_send)
    in_grad, grads_c, sums_a, _, _ = call(
        last_body,
        [
            pltpu.HBM((rows, width), F32),
            ((8, 208, 256), BF),
            pltpu.HBM((512, 256), BF),
            ((3, 256), F32),
            ((4, width), F32),
        ],
        (
            at, Far(x), Far(g), part_g, part_g_other, recv_grad0, Layer(wq, 0), Layer(others, 0), cs,
            ln_gain, ln_bias, d_b_up0, d_b_up1, d_b_qkv1, d_norm1, d_sum0, d_sum1,
        ),
        "last",
        smem_first=True,
    )
    mixed, sums_a = call(
        mix_body,
        [((8, 136, 256), BF), pltpu.HBM((512, 256), BF)],
        (exchange(grads_c, "dp"), Far(sums_b), Far(sums_a)),
        "mix",
    )
    full_a = lax.all_gather(sums_a, "dp")
    (summed,) = call(sum_body, [((8, 136, 256), BF)], (exchange(mixed, "context"),), "sum")
    full_bc = lax.all_gather(exchange(summed, "context"), "dp")
    g_up, g_down, g_qkv, g_out, g_b_up, g_b_qkv, g_sum, g_gain, g_bias = unpack(full_a, full_bc)
    return (
        block_out.reshape(tokens_in.shape),
        in_grad.reshape(tokens_in.shape),
        jnp.transpose(g_qkv, (0, 2, 1, 3)),
        jnp.transpose(g_b_qkv, (1, 0, 2)),
        g_out,
        g_up,
        g_b_up,
        g_down,
        g_sum,
        g_gain,
        g_bias,
    )


def solution(mesh):
    return jax.shard_map(
        shards,
        mesh=mesh,
        in_specs=(
            P("dp", "context", None),
            P("dp", "context", None),
            P("dp", "context"),
            P(None, None, None, "tensor"),
            P(None, None, "tensor"),
            P(None, "tensor", None),
            P(None, None, "tensor"),
            P(None, "tensor"),
            P(None, "tensor", None),
            P(),
            P(),
            P(),
        ),
        out_specs=(
            P("dp", "context", None),
            P("dp", "context", None),
            P(None, None, None, "tensor"),
            P(None, None, "tensor"),
            P(None, "tensor", None),
            P(None, None, "tensor"),
            P(None, "tensor"),
            P(None, "tensor", None),
            P(),
            P(),
            P(),
        ),
        check_vma=False,
    )
```

```python
from functools import partial

import numpy as np

import jax
import jax.numpy as jnp
from jax import lax
from jax.experimental import pallas as pl
from jax.experimental.pallas import tpu as pltpu
from jax.sharding import PartitionSpec as P

EPS = 1e-05
HALF = 8
HEAD = 64
BLK = 128
CHUNK = 256
NEG = -1e30
BF = jnp.bfloat16
F32 = jnp.float32

FREQS = (10000.0 ** (-np.arange(HALF, dtype=np.float64) * 2.0 / 16.0)).astype(np.float32)


def mm(a, b, ca=1, cb=0):
    return lax.dot_general(a, b, (((ca,), (cb,)), ((), ())), preferred_element_type=F32)


class After:
    def __init__(self, array):
        self.array = array

    def spec(self):
        return pl.BlockSpec(memory_space=pl.ANY)


class Layer:
    def __init__(self, array, index):
        self.array, self.index = far(array), index

    def spec(self):
        rest = self.array.shape[1:]
        place = (self.index,) + (0,) * len(rest)
        return pl.BlockSpec((None,) + rest, lambda i: place)


class Quarter:
    def __init__(self, array, at):
        self.array, self.at = far(array), at

    def spec(self):
        rest = self.array.shape[1:]
        place = (self.at,) + (0,) * len(rest)
        return pl.BlockSpec((4,) + rest, lambda i: place)


class Raw:
    def __init__(self, array):
        self.array = far(array)

    def spec(self):
        return pl.BlockSpec(memory_space=pltpu.HBM)


class Far:
    def __init__(self, array):
        self.array = far(array)

    def spec(self):
        return whole(self.array.shape)


Kept = type(pltpu.HBM((8, 128), F32))


def far(array):
    return pltpu.with_memory_space_constraint(array, pltpu.HBM)


def whole(shape):
    return pl.BlockSpec(shape, lambda i: (0,) * len(shape))


def call(body, out_shape, args, name, scratch=(), smem_first=False):
    specs = [
        a.spec() if isinstance(a, (Layer, Quarter, Raw, Far, After)) else whole(a.shape) for a in args
    ]
    args = [a.array if isinstance(a, (Layer, Quarter, Raw, Far, After)) else a for a in args]
    if smem_first:
        specs[0] = pl.BlockSpec(memory_space=pltpu.SMEM)
    return pl.pallas_call(
        body,
        grid=(1,),
        out_shape=[o if isinstance(o, Kept) else jax.ShapeDtypeStruct(*o) for o in out_shape],
        in_specs=specs,
        out_specs=[whole(o.shape if isinstance(o, Kept) else o[0]) for o in out_shape],
        scratch_shapes=list(scratch),
        compiler_params=pltpu.CompilerParams(vmem_limit_bytes=40 * 1024 * 1024),
        name=name,
    )(*args)


def norm_rows(x):
    mean = jnp.mean(x, -1, keepdims=True)
    cen = x - mean
    inv = lax.rsqrt(jnp.mean(cen * cen, -1, keepdims=True) + EPS)
    return cen * inv, inv


def turn(t, cos, sin):
    a, b = t[:HALF], t[HALF : 2 * HALF]
    return jnp.concatenate([a * cos - b * sin, b * cos + a * sin, t[2 * HALF :]], 0)


def turn_back(u, cos, sin):
    a, b = u[:HALF], u[HALF : 2 * HALF]
    return jnp.concatenate([a * cos + b * sin, b * cos - a * sin, u[2 * HALF :]], 0)


def send_qkv(send, attn_in, w_qkv, b_qkv, layer, cs, plane=None):
    for e in range(3):
        turned = (mm(attn_in, w_qkv[e]) + b_qkv[e, layer : layer + 1]).T
        for s in range(2):
            cos, sin = cs[s, 0], cs[s, 1]
            for h in range(4):
                j = s * 4 + h
                part = turned[h * HEAD : (h + 1) * HEAD, s * BLK : (s + 1) * BLK]
                if e < 2:
                    part = turn(part, cos, sin)
                if e == 0:
                    part = part * (HEAD**-0.5)
                rows = slice(e * HEAD, (e + 1) * HEAD)
                if plane is None:
                    send[j, rows, :] = part.astype(BF)
                else:
                    send[j, plane, rows, :] = part.astype(BF)


def feed_forward(mlp_in, w_up, b_up, layer, w_down, act, slope):
    width = w_up.shape[1]
    total = None
    for c in range(0, width, 256):
        cols = slice(c, c + 256)
        pre = mm(mlp_in, w_up[:, cols]) + b_up[layer : layer + 1, cols]
        cdf = 0.5 + 0.5 * lax.erf(pre * np.float32(0.7071067811865476))
        a = (pre * cdf).astype(BF)
        act[:, cols] = a
        tail = pre * (jnp.exp(-0.5 * pre * pre) * np.float32(0.3989422804014327))
        slope[:, cols] = (cdf + tail).astype(BF)
        term = mm(a, w_down[cols, :])
        total = term if total is None else total + term
    return total


def feed_back(g_b, act, slope, mlp_in, w_up, w_down, d_up, d_down, d_b_up):
    width = w_up.shape[1]
    total = None
    mlp_t = mlp_in.T
    for c in range(0, width, 256):
        cols = slice(c, c + 256)
        d_act = mm(g_b, w_down[cols, :], 1, 1)
        d_pre = d_act * slope[:, cols].astype(F32)
        d_pre_b = d_pre.astype(BF)
        d_b_up[:, cols] = jnp.sum(d_pre_b.astype(F32), 0, keepdims=True)
        d_up(c // 256, mm(mlp_t, d_pre_b))
        d_down(c, mm(act[:, cols].T, g_b))
        term = mm(d_pre_b, w_up[:, cols], 1, 1)
        total = term if total is None else total + term
    return total


def pack_up(out, row):
    def put(c, value):
        for p in range(8):
            out[p, row + 64 * c : row + 64 * (c + 1), :] = value[64 * p : 64 * (p + 1)].astype(BF)

    return put


def pack_down(out, row):
    def put(c, value):
        for half in range(2):
            for k in range(2):
                out[c // 128 + k, row + 128 * half : row + 128 * (half + 1), :] = value[
                    128 * k : 128 * (k + 1), 256 * half : 256 * (half + 1)
                ].astype(BF)

    return put


def pack_qkv(out, row):
    def put(e, value):
        for p in range(8):
            out[p, row + 64 * e : row + 64 * (e + 1), :] = value[64 * p : 64 * (p + 1)].astype(BF)

    return put


def own_ctx(t, recv):
    full = jnp.concatenate([gather_ctx(recv, s) for s in range(2)], 1)
    return jnp.where(t == 0, full[0:256], full[256:512])


def pack_out(out, row, ctx, upstream):
    value = mm(ctx, upstream)
    for p in range(8):
        for half in range(2):
            out[p, row + 32 * half : row + 32 * (half + 1), :] = value[
                32 * p : 32 * (p + 1), 256 * half : 256 * (half + 1)
            ].astype(BF)


def first_body(
    at, pos, freqs, x, gain, bias, w_qkv, b_qkv, w_up, b_up, w_down, w_out, all_qkv, all_out,
    send, pair, act, slope, cs, piece_a, piece_b, sems,
):
    matrix, part_of = at[2], at[0]
    rows_a = pl.ds(pl.multiple_of(part_of * 64, 64), 64)
    rows_b = pl.ds(pl.multiple_of(part_of % 4 * 64, 64), 64)
    cols_b = pl.ds(pl.multiple_of(part_of // 4 * 256, 256), 256)
    copies = [
        pltpu.make_async_copy(
            all_qkv.at[matrix // 4, jnp.minimum(matrix % 4, 2), rows_a], piece_a, sems.at[0]
        ),
        pltpu.make_async_copy(all_out.at[matrix // 4, rows_b, cols_b], piece_b, sems.at[1]),
    ]
    for copy in copies:
        copy.start()
    pair[256:512] = w_out[...]
    for s in range(2):
        p = pos[s : s + 1, :].astype(F32)
        angle = freqs[...] * p
        cs[s, 0] = jnp.cos(angle)
        cs[s, 1] = jnp.sin(angle)
    normed, _ = norm_rows(x[...])
    attn_in = (normed * gain[0, 0:1] + bias[0, 0:1]).astype(BF)
    mlp_in = (normed * gain[0, 1:2] + bias[0, 1:2]).astype(BF)
    send_qkv(send, attn_in, w_qkv, b_qkv, 0, cs, at[1])
    for copy in copies:
        copy.wait()
    piece = jnp.where(matrix % 4 == 3, piece_b[...], piece_a[...])
    for j in range(8):
        send[j, 1 - at[1], 0:64, :] = piece[:, 0:BLK]
        send[j, 1 - at[1], 64:128, :] = piece[:, BLK : 2 * BLK]
        send[j, 1 - at[1], 128:208, :] = jnp.zeros((80, BLK), BF)
    row = lax.broadcasted_iota(jnp.int32, (16, BLK), 0)
    token = at[0] * BLK + lax.broadcasted_iota(jnp.int32, (1, BLK), 1)
    for s in range(2):
        start = jnp.maximum(token - pos[s : s + 1, :], 0)
        high = (start // 8).astype(F32)
        low = (start % 8).astype(F32)
        block = jnp.where(row == 0, high, jnp.where(row == 1, low, 0.0)).astype(BF)
        for h in range(4):
            send[s * 4 + h, at[1], 3 * HEAD : 3 * HEAD + 16, :] = block
    pair[0:256] = feed_forward(mlp_in, w_up, b_up, 0, w_down, act, slope).astype(BF)


def load_rows(recv, lo, hi, plane=None):
    if plane is not None:
        return jnp.concatenate([recv[i, plane, lo:hi, :] for i in range(8)], 1)
    return jnp.concatenate([recv[i, lo:hi, :] for i in range(8)], 1)


def starts_of(recv, plane):
    rows = load_rows(recv, 3 * HEAD, 3 * HEAD + 16, plane).astype(F32)
    return rows[0:1] * 8.0 + rows[1:2]


def visible_of(start, c, length):
    key = lax.broadcasted_iota(jnp.int32, (length, CHUNK), 0)
    query = lax.broadcasted_iota(jnp.int32, (length, CHUNK), 1) + c * CHUNK
    return (key <= query) & (key >= start[:, c * CHUNK : (c + 1) * CHUNK])


def attend_body(at, recv, send, lse, ctx, start_out, pieces):
    for b in range(8):
        pieces[b] = recv[b, 1 - at[1], 0 : 2 * HEAD, :]
    q = load_rows(recv, 0, HEAD, at[1])
    k_t = load_rows(recv, HEAD, 2 * HEAD, at[1])
    v_t = load_rows(recv, 2 * HEAD, 3 * HEAD, at[1])
    k = k_t.T
    start = starts_of(recv, at[1]).astype(jnp.int32)
    start_out[...] = start
    for c in range(4):
        cols = slice(c * CHUNK, (c + 1) * CHUNK)
        length = (c + 1) * CHUNK
        scores = mm(k[:length], q[:, cols])
        scores = jnp.where(visible_of(start, c, length), scores, NEG)
        peak = jnp.max(scores, 0, keepdims=True)
        shifted = jnp.exp(scores - peak)
        total = jnp.sum(shifted, 0, keepdims=True)
        lse[:, cols] = peak + jnp.log(total)
        out = mm(v_t[:, :length], shifted.astype(BF)) / total
        ctx[:, cols] = out
        for i in range(CHUNK // BLK):
            block = out[:, i * BLK : (i + 1) * BLK].astype(BF)
            for t in range(2):
                send[c * (CHUNK // BLK) + i, t] = block


def attend_both_body(recv, start, _, send, dk, dv):
    q = load_rows(recv, 0, HEAD)
    k_t = load_rows(recv, HEAD, 2 * HEAD)
    v_t = load_rows(recv, 2 * HEAD, 3 * HEAD)
    d_ctx = load_rows(recv, 3 * HEAD, 4 * HEAD)
    k = k_t.T
    v = v_t.T
    dk[...] = jnp.zeros_like(dk)
    dv[...] = jnp.zeros_like(dv)
    for c in range(4):
        cols = slice(c * CHUNK, (c + 1) * CHUNK)
        length = (c + 1) * CHUNK
        scores = mm(k[:length], q[:, cols])
        scores = jnp.where(visible_of(start[...], c, length), scores, NEG)
        peak = jnp.max(scores, 0, keepdims=True)
        shifted = jnp.exp(scores - peak)
        probs = shifted * (1.0 / jnp.sum(shifted, 0, keepdims=True))
        probs_b = probs.astype(BF)
        out = mm(v_t[:, :length], probs_b)
        dq = backward_chunk(q, k_t, v, d_ctx, probs, probs_b, out, cols, length, dk, dv)
        for i in range(CHUNK // BLK):
            b = c * (CHUNK // BLK) + i
            for t in range(2):
                send[b, t, 0:HEAD] = out[:, i * BLK : (i + 1) * BLK].astype(BF)
                send[b, t, HEAD : 2 * HEAD] = dq[:, i * BLK : (i + 1) * BLK].astype(BF)
    put_kv(send, dk, dv, 2 * HEAD)


def backward_chunk(q, k_t, v, d_ctx, probs, probs_b, out, cols, length, dk, dv):
    d_out = d_ctx[:, cols]
    d_probs = mm(v[:length], d_out)
    delta = jnp.sum(d_out.astype(F32) * out, 0, keepdims=True)
    d_scores = (probs * (d_probs - delta)).astype(BF)
    dk[:, :length] += mm(q[:, cols], d_scores, 1, 1)
    dv[:, :length] += mm(d_out, probs_b, 1, 1)
    return mm(k_t[:, :length], d_scores) * (HEAD**-0.5)


def put_kv(send, dk, dv, row):
    for b in range(8):
        for t in range(2):
            send[b, t, row : row + HEAD] = dk[:, b * BLK : (b + 1) * BLK].astype(BF)
            send[b, t, row + HEAD : row + 2 * HEAD] = dv[:, b * BLK : (b + 1) * BLK].astype(BF)


def attend_back_body(at, recv, recv_d, start, lse, ctx, _, send, dk, dv):
    ride = recv_d[0, 64:192].astype(F32)
    for i in range(1, 8):
        ride = ride + recv_d[i, 64:192].astype(F32)
    ride = ride.astype(BF)
    for b in range(8):
        for t in range(2):
            send[b, t, 192:320] = ride
    q = load_rows(recv, 0, HEAD, at[1])
    k_t = load_rows(recv, HEAD, 2 * HEAD, at[1])
    v_t = load_rows(recv, 2 * HEAD, 3 * HEAD, at[1])
    d_ctx = load_rows(recv_d, 0, HEAD)
    k = k_t.T
    v = v_t.T
    dk[...] = jnp.zeros_like(dk)
    dv[...] = jnp.zeros_like(dv)
    for c in range(4):
        cols = slice(c * CHUNK, (c + 1) * CHUNK)
        length = (c + 1) * CHUNK
        scores = mm(k[:length], q[:, cols])
        scores = jnp.where(visible_of(start[...], c, length), scores, NEG)
        probs = jnp.exp(scores - lse[:, cols])
        probs_b = probs.astype(BF)
        dq = backward_chunk(q, k_t, v, d_ctx, probs, probs_b, ctx[:, cols], cols, length, dk, dv)
        for i in range(CHUNK // BLK):
            for t in range(2):
                send[c * (CHUNK // BLK) + i, t, 0:HEAD] = dq[:, i * BLK : (i + 1) * BLK].astype(BF)
    put_kv(send, dk, dv, HEAD)


def gather_ctx(recv, s):
    return jnp.concatenate([recv[s * 4 + h, t, 0:HEAD, :] for t in range(2) for h in range(4)], 0)


def ordered(t, own, other):
    return jnp.where(t == 0, own, other), jnp.where(t == 0, other, own)


def other_matrix(others, m):
    rows = [
        jnp.concatenate([others[m, c, 0:64, :], others[m, c, 64:128, :]], 1) for c in range(8)
    ]
    return jnp.concatenate(rows, 0)


def out_other(others):
    stacked = other_matrix(others, 3)
    return jnp.concatenate([stacked[0:256], stacked[256:512]], 1)


def branch_of(t, recv, w_own, w_other):
    first, second = ordered(t, w_own, w_other)
    w = jnp.concatenate([first, second], 0)
    rows = []
    for s in range(2):
        rows.append(mm(gather_ctx(recv, s).T, w))
    return jnp.concatenate(rows, 0)


def middle_body(
    at, x, pair, pair_other, recv, w_out_own, out_bias, gain, bias,
    w_qkv, b_qkv, w_up, b_up, w_down, w_out, cot, cs,
    stream, send, grads, parts, d_b_up, d_sum, act, slope,
):
    branch = pair[0:256].astype(F32) + pair_other[0:256].astype(F32)
    branch = branch + branch_of(at[1], recv, w_out_own[...], pair_other[256:512])
    out = x[...] + branch + out_bias[0, 0:1] + out_bias[0, 1:2]
    stream[...] = out
    normed, _ = norm_rows(out)
    attn_in = (normed * gain[1, 0:1] + bias[1, 0:1]).astype(BF)
    mlp_in = (normed * gain[1, 1:2] + bias[1, 1:2]).astype(BF)
    send_qkv(send, attn_in, w_qkv, b_qkv, 1, cs)
    g_b = cot[...].astype(BF)
    d_ctx = mm(w_out[...], g_b, 1, 1)
    for s in range(2):
        for h in range(4):
            send[s * 4 + h, 3 * HEAD : 4 * HEAD, :] = d_ctx[
                h * HEAD : (h + 1) * HEAD, s * BLK : (s + 1) * BLK
            ].astype(BF)
    d_sum[...] = jnp.sum(cot[...], 0, keepdims=True)
    parts[0:256] = feed_forward(mlp_in, w_up, b_up, 1, w_down, act, slope).astype(BF)
    parts[256:512] = feed_back(
        g_b, act, slope, mlp_in, w_up, w_down, pack_up(grads, 0), pack_down(grads, 256), d_b_up
    ).astype(BF)


def norm_back(
    t, x, g, d_mlp_in, recv, row, w_own, others, cs, gain, bias, layer, d_qkv, d_b_qkv, d_norm
):
    normed, inv = norm_rows(x)
    attn_in = (normed * gain[layer, 0:1] + bias[layer, 0:1]).astype(BF)
    attn_t = attn_in.T
    d_attn_t = None
    for e in range(3):
        halves = []
        for tt in range(2):
            blocks = []
            for h in range(4):
                pieces = []
                for s in range(2):
                    lo = row + e * HEAD
                    u = recv[s * 4 + h, tt, lo : lo + HEAD, :]
                    if e < 2:
                        u = turn_back(u.astype(F32), cs[s, 0], cs[s, 1]).astype(BF)
                    pieces.append(u)
                blocks.append(jnp.concatenate(pieces, 1))
            halves.append(jnp.concatenate(blocks, 0))
        first, second = ordered(t, w_own[e], other_matrix(others, e))
        term = mm(first, halves[0]) + mm(second, halves[1])
        d_attn_t = term if d_attn_t is None else d_attn_t + term
        own = jnp.where(t == 0, halves[0], halves[1])
        d_qkv(e, mm(attn_t, own, 1, 1))
        d_b_qkv[e : e + 1] = mm(jnp.ones((8, own.shape[1]), BF), own, 1, 1)[0:1]
    d_attn_in = d_attn_t.T
    d_norm[0:1] = jnp.sum(d_attn_in * normed, 0, keepdims=True)
    d_norm[1:2] = jnp.sum(d_mlp_in * normed, 0, keepdims=True)
    d_norm[2:3] = jnp.sum(d_attn_in, 0, keepdims=True)
    d_norm[3:4] = jnp.sum(d_mlp_in, 0, keepdims=True)
    d_normed = d_attn_in * gain[layer, 0:1] + d_mlp_in * gain[layer, 1:2]
    return g + inv * (
        d_normed
        - jnp.mean(d_normed, -1, keepdims=True)
        - normed * jnp.mean(d_normed * normed, -1, keepdims=True)
    )


def turn_point_body(
    at, stream, parts, parts_other, recv, w_out, w_qkv, others, out_bias,
    gain, bias, cot, cs, x, act, slope, w_up, w_down, w_out_first, recv_first, sums_a,
    block_out, g_out, send, grads, part, d_b_up, d_b_qkv, d_norm, d_sum,
):
    t = at[1]
    branch = parts[0:256].astype(F32) + parts_other[0:256].astype(F32)
    branch = branch + branch_of(t, recv, w_out[...], out_other(others))
    block_out[...] = stream[...] + branch + out_bias[1, 0:1] + out_bias[1, 1:2]
    d_mlp_in = parts[256:512].astype(F32) + parts_other[256:512].astype(F32)
    g = norm_back(
        t, stream[...], cot[...], d_mlp_in, recv, HEAD, w_qkv, others, cs, gain, bias, 1,
        pack_qkv(grads, 0), d_b_qkv, d_norm,
    )
    g_out[...] = g
    g_b = g.astype(BF)
    d_sum[...] = jnp.sum(g, 0, keepdims=True)
    d_ctx = mm(w_out_first[...], g_b, 1, 1)
    for s in range(2):
        for h in range(4):
            send[s * 4 + h, 0:HEAD] = d_ctx[
                h * HEAD : (h + 1) * HEAD, s * BLK : (s + 1) * BLK
            ].astype(BF)
    for q in range(8):
        for c in range(2):
            send[q, 64 + 64 * c : 128 + 64 * c] = sums_a[
                64 * q : 64 * (q + 1), BLK * c : BLK * (c + 1)
            ]
    pack_out(grads, 704, own_ctx(t, recv), cot[...].astype(BF))
    pack_out(grads, 768, own_ctx(t, recv_first), g_b)
    normed, _ = norm_rows(x[...])
    mlp_in = (normed * gain[0, 1:2] + bias[0, 1:2]).astype(BF)
    part[...] = feed_back(
        g_b, act, slope, mlp_in, w_up, w_down, pack_up(grads, 192), pack_down(grads, 448), d_b_up
    ).astype(BF)


def last_body(
    at, x, g, part, part_other, recv, w_qkv, others, cs, gain, bias,
    d_b_up0, d_b_up1, d_b_qkv1, d_norm1, d_sum0, d_sum1,
    in_grad, grads, sums_a, d_b_qkv0, d_norm0,
):
    d_mlp_in = part[...].astype(F32) + part_other[...].astype(F32)
    in_grad[...] = norm_back(
        at[1], x[...], g[...], d_mlp_in, recv, 0, w_qkv, others, cs, gain, bias, 0,
        pack_qkv(grads, 0), d_b_qkv0, d_norm0,
    )
    for q in range(8):
        both_planes = recv[q, :, 192:320]
        block = jnp.where(at[1] == 0, both_planes[0], both_planes[1])
        for c in range(2):
            sums_a[64 * q : 64 * (q + 1), BLK * c : BLK * (c + 1)] = block[64 * c : 64 * (c + 1)]

    def lanes(ref, row, count):
        return [ref[row : row + 1, 256 * c : 256 * (c + 1)] for c in range(count)]

    def norms(ref):
        return [v for r in range(4) for v in lanes(ref, r, 2)]

    rows = [
        lanes(d_b_up0, 0, 4)
        + lanes(d_b_up1, 0, 4)
        + [v for e in range(3) for ref in (d_b_qkv0, d_b_qkv1) for v in lanes(ref, e, 1)],
        lanes(d_sum0, 0, 2) + lanes(d_sum1, 0, 2) + norms(d_norm0),
        norms(d_norm1),
    ]
    for p in range(8):
        have = rows[p] if p < len(rows) else []
        fill = [jnp.zeros((16 - len(have), 256), F32)]
        grads[p, 192:208, :] = jnp.concatenate(have + fill, 0).astype(BF)


def mix_body(got, early, first, out, first_out):
    total = got[0].astype(F32)
    for i in range(1, 8):
        total = total + got[i].astype(F32)
    for q in range(8):
        tiny = total[192 + 8 * q : 200 + 8 * q] if q < 2 else jnp.zeros((8, 256), F32)
        mine = [early[104 * q : 104 * (q + 1)].astype(F32), total[24 * q : 24 * (q + 1)], tiny]
        out[q] = jnp.concatenate(mine, 0).astype(BF)
    first_out[...] = first[...]


def sum_body(got, out):
    total = got[0].astype(F32)
    for i in range(1, 8):
        total = total + got[i].astype(F32)
    for q in range(8):
        out[q] = total.astype(BF)


def unpack_first_body(first, g_up, g_down):
    for k in range(2):
        for c in range(4):
            cols = slice(256 * c, 256 * (c + 1))
            g_up[0, 64 * k : 64 * (k + 1), cols] = first[k, 64 * c : 64 * (c + 1)].astype(F32)
        for c in range(2):
            rows = first[k, 256 + 128 * c : 256 + 128 * (c + 1)]
            cols = slice(256 * c, 256 * (c + 1))
            g_down[0, 128 * k : 128 * (k + 1), cols] = rows.astype(F32)


def unpack_rest_body(rest, _, __, g_up, g_down, g_qkv, g_out, g_b_up, g_b_qkv, g_sum, g_gain, g_bias):
    p = pl.program_id(0)
    for k in range(2):
        for q in range(8):
            block = rest[k, q].astype(F32)
            for i in range(16):
                value = block[8 * i : 8 * (i + 1)]
                row = 104 * q + 8 * i
                if i >= 13:
                    row = 24 * q + 8 * (i - 13)
                    r = 64 * k + row % 64
                    g_qkv[0, row // 64, r : r + 8] = value
                elif row < 192:
                    r = 64 * k + row % 64
                    g_qkv[1, row // 64, r : r + 8] = value
                elif row < 448:
                    c, r = divmod(row - 192, 64)
                    r += 64 * k
                    g_up[0, r : r + 8, 256 * c : 256 * (c + 1)] = value
                elif row < 704:
                    c, r = divmod(row - 448, 128)
                    r += 128 * k
                    g_down[0, r : r + 8, 256 * c : 256 * (c + 1)] = value
                else:
                    c, r = divmod((row - 704) % 64, 32)
                    r += 32 * k
                    g_out[1 - (row - 704) // 64, r : r + 8, 256 * c : 256 * (c + 1)] = value

    tiny = [jnp.concatenate([rest[k, q].astype(F32)[128:136] for q in range(2)], 0) for k in range(2)]

    @pl.when(p == 0)
    def _():
        for layer in range(2):
            for c in range(4):
                r = 4 * layer + c
                g_b_up[layer : layer + 1, 256 * c : 256 * (c + 1)] = tiny[0][r : r + 1]
        for e in range(3):
            for layer in range(2):
                r = 8 + 2 * e + layer
                g_b_qkv[e, layer : layer + 1, :] = tiny[0][r : r + 1]
        for layer in range(2):
            for c in range(2):
                r = 2 * layer + c
                for which in range(2):
                    g_sum[layer, which : which + 1, 256 * c : 256 * (c + 1)] = tiny[1][r : r + 1]

    def norms(layer, rows, base):
        for which in range(2):
            for c in range(2):
                cols = slice(256 * c, 256 * (c + 1))
                r = base + 2 * which + c
                g_gain[layer, which : which + 1, cols] = rows[r : r + 1]
                g_bias[layer, which : which + 1, cols] = rows[r + 4 : r + 5]

    @pl.when(p == 0)
    def _():
        norms(0, tiny[1], 4)

    @pl.when(p == 1)
    def _():
        norms(1, tiny[0], 0)


UP = (2, 512, 1024)
DOWN = (2, 1024, 512)


def unpack(first, rest):
    def place(layer):
        return [
            pl.BlockSpec((1, 128, 1024), lambda p: (layer, p, 0)),
            pl.BlockSpec((1, 256, 512), lambda p: (layer, p, 0)),
        ]

    params = pltpu.CompilerParams(vmem_limit_bytes=40 * 1024 * 1024)
    g_up, g_down = pl.pallas_call(
        unpack_first_body,
        grid=(4,),
        out_shape=[pltpu.HBM(UP, F32), pltpu.HBM(DOWN, F32)],
        in_specs=[pl.BlockSpec((2, 512, 256), lambda p: (p, 0, 0))],
        out_specs=place(1),
        compiler_params=params,
        name="unpack_first",
    )(far(first))
    outs = [
        ((2, 3, 512, 256), pl.BlockSpec((2, 3, 128, 256), lambda p: (0, 0, p, 0))),
        ((2, 256, 512), pl.BlockSpec((2, 64, 512), lambda p: (0, p, 0))),
        ((2, 1024), whole((2, 1024))),
        ((3, 2, 256), whole((3, 2, 256))),
        ((2, 2, 512), whole((2, 2, 512))),
        ((2, 2, 512), whole((2, 2, 512))),
        ((2, 2, 512), whole((2, 2, 512))),
    ]
    return pl.pallas_call(
        unpack_rest_body,
        grid=(4,),
        out_shape=[pltpu.HBM(shape, F32) for shape in [UP, DOWN] + [o[0] for o in outs]],
        in_specs=[
            pl.BlockSpec((2, 8, 136, 256), lambda p: (p, 0, 0, 0)),
            pl.BlockSpec(memory_space=pl.ANY),
            pl.BlockSpec(memory_space=pl.ANY),
        ],
        out_specs=place(0) + [spec for _, spec in outs],
        input_output_aliases={1: 0, 2: 1},
        compiler_params=params,
        name="unpack_rest",
    )(far(rest), far(g_up), far(g_down))


def swap(value):
    return lax.ppermute(value, "tensor", [(0, 1), (1, 0)])


def exchange(value, axes):
    return lax.all_to_all(value, axes, 0, 0)


def both(value):
    flat = value.reshape((16,) + value.shape[2:])
    return exchange(flat, ("context", "tensor")).reshape(value.shape)


def shards(
    tokens_in, cotangent, positions, w_qkv, b_qkv, w_out, w_up, b_up, w_down, out_bias, ln_gain, ln_bias
):
    rows, width = 256, 512
    x = tokens_in.reshape(rows, width)
    cot = cotangent.reshape(rows, width)
    wq = jnp.transpose(w_qkv, (0, 2, 1, 3))
    bq = jnp.transpose(b_qkv, (1, 0, 2))
    at = jnp.stack(
        [lax.axis_index("context"), lax.axis_index("tensor"), lax.axis_index("dp")]
    ).astype(jnp.int32)
    freqs = jnp.asarray(FREQS).reshape(HALF, 1)
    send, pair, act, slope, cs = call(
        first_body,
        [
            pltpu.VMEM((8, 2, 208, BLK), BF),
            ((2 * rows, width), BF),
            pltpu.HBM((rows, 1024), BF),
            pltpu.HBM((rows, 1024), BF),
            ((2, 2, HALF, BLK), F32),
        ],
        (
            at, Far(positions), Far(freqs), Far(x), Far(ln_gain), Far(ln_bias), Layer(wq, 0), Far(bq),
            Layer(w_up, 0), Far(b_up),
            Layer(w_down, 0), Layer(w_out, 0), Raw(wq), Raw(w_out),
        ),
        "norm_qkv_feed",
        scratch=[
            pltpu.VMEM((64, 256), BF),
            pltpu.VMEM((64, 256), BF),
            pltpu.SemaphoreType.DMA((2,)),
        ],
        smem_first=True,
    )
    pair_other = swap(pair)
    recv = both(send)
    ctx_send, lse, ctx, start, pieces = call(
        attend_body,
        [((8, 2, HEAD, BLK), BF), ((1, 1024), F32), pltpu.HBM((HEAD, 1024), F32), ((1, 1024), jnp.int32),
            pltpu.HBM((8, 2 * HEAD, BLK), BF),
        ],
        (at, recv),
        "attend",
        smem_first=True,
    )
    others = lax.all_gather(pieces, "dp")
    recv_ctx = both(ctx_send)
    stream, send, grads_a, parts, d_b_up1, d_sum1 = call(
        middle_body,
        [
            pltpu.HBM((rows, width), F32),
            ((8, 256, BLK), BF),
            pltpu.HBM((8, 512, 256), BF),
            ((2 * rows, width), BF),
            ((1, 1024), F32),
            ((1, width), F32),
        ],
        (
            at, Far(x), pair, pair_other, recv_ctx, Layer(w_out, 0), out_bias, ln_gain, ln_bias,
            Layer(wq, 1), bq, Layer(w_up, 1), b_up, Layer(w_down, 1), Layer(w_out, 1), Far(cot), cs,
        ),
        "middle",
        scratch=[pltpu.VMEM((rows, 1024), BF), pltpu.VMEM((rows, 1024), BF)],
        smem_first=True,
    )
    sums_a = lax.psum_scatter(grads_a, "dp", scatter_dimension=0)
    parts_other = swap(parts)
    recv_both = exchange(send, "context")
    (both_send,) = call(
        attend_both_body,
        [((8, 2, 256, BLK), BF)],
        (recv_both, start, After(parts_other)),
        "attend_both",
        scratch=[pltpu.VMEM((HEAD, 1024), F32), pltpu.VMEM((HEAD, 1024), F32)],
    )
    recv_grad = both(both_send)
    block_out, g, send, grads_b, part_g, d_b_up0, d_b_qkv1, d_norm1, d_sum0 = call(
        turn_point_body,
        [
            pltpu.HBM((rows, width), F32),
            pltpu.HBM((rows, width), F32),
            pltpu.VMEM((8, 192, BLK), BF),
            pltpu.HBM((8, 832, 256), BF),
            ((rows, width), BF),
            ((1, 1024), F32),
            ((3, 256), F32),
            ((4, width), F32),
            ((1, width), F32),
        ],
        (
            at, Far(stream), parts, parts_other, recv_grad, Layer(w_out, 1), Layer(wq, 1),
            Quarter(others, 1), out_bias, ln_gain, ln_bias, Far(cot), cs, Far(x), Far(act), Far(slope),
            Layer(w_up, 0), Layer(w_down, 0), Layer(w_out, 0), recv_ctx, Far(sums_a),
        ),
        "turn_point",
        smem_first=True,
    )
    sums_b = lax.psum_scatter(grads_b, "dp", scatter_dimension=0)
    part_g_other = swap(part_g)
    recv_d = exchange(send, "context")
    (back_send,) = call(
        attend_back_body,
        [((8, 2, 320, BLK), BF)],
        (at, recv, recv_d, start, lse, ctx, After(part_g_other)),
        "attend_back",
        smem_first=True,
        scratch=[pltpu.VMEM((HEAD, 1024), F32), pltpu.VMEM((HEAD, 1024), F32)],
    )
    recv_grad0 = both(back_send)
    in_grad, grads_c, sums_a, _, _ = call(
        last_body,
        [
            pltpu.HBM((rows, width), F32),
            ((8, 208, 256), BF),
            pltpu.HBM((512, 256), BF),
            ((3, 256), F32),
            ((4, width), F32),
        ],
        (
            at, Far(x), Far(g), part_g, part_g_other, recv_grad0, Layer(wq, 0), Quarter(others, 0), cs,
            ln_gain, ln_bias, d_b_up0, d_b_up1, d_b_qkv1, d_norm1, d_sum0, d_sum1,
        ),
        "last",
        smem_first=True,
    )
    mixed, sums_a = call(
        mix_body,
        [((8, 136, 256), BF), pltpu.HBM((512, 256), BF)],
        (exchange(grads_c, "dp"), Far(sums_b), Far(sums_a)),
        "mix",
    )
    full_a = lax.all_gather(sums_a, "dp")
    (summed,) = call(sum_body, [((8, 136, 256), BF)], (exchange(mixed, "context"),), "sum")
    full_bc = lax.all_gather(exchange(summed, "context"), "dp")
    g_up, g_down, g_qkv, g_out, g_b_up, g_b_qkv, g_sum, g_gain, g_bias = unpack(full_a, full_bc)
    return (
        block_out.reshape(tokens_in.shape),
        in_grad.reshape(tokens_in.shape),
        jnp.transpose(g_qkv, (0, 2, 1, 3)),
        jnp.transpose(g_b_qkv, (1, 0, 2)),
        g_out,
        g_up,
        g_b_up,
        g_down,
        g_sum,
        g_gain,
        g_bias,
    )


def solution(mesh):
    return jax.shard_map(
        shards,
        mesh=mesh,
        in_specs=(
            P("dp", "context", None),
            P("dp", "context", None),
            P("dp", "context"),
            P(None, None, None, "tensor"),
            P(None, None, "tensor"),
            P(None, "tensor", None),
            P(None, None, "tensor"),
            P(None, "tensor"),
            P(None, "tensor", None),
            P(),
            P(),
            P(),
        ),
        out_specs=(
            P("dp", "context", None),
            P("dp", "context", None),
            P(None, None, None, "tensor"),
            P(None, None, "tensor"),
            P(None, "tensor", None),
            P(None, None, "tensor"),
            P(None, "tensor"),
            P(None, "tensor", None),
            P(),
            P(),
            P(),
        ),
        check_vma=False,
    )
```

```python
from functools import partial

import numpy as np

import jax
import jax.numpy as jnp
from jax import lax
from jax.experimental import pallas as pl
from jax.experimental.pallas import tpu as pltpu
from jax.sharding import PartitionSpec as P

EPS = 1e-05
HALF = 8
HEAD = 64
BLK = 128
CHUNK = 256
NEG = -1e30
BF = jnp.bfloat16
F32 = jnp.float32

FREQS = (10000.0 ** (-np.arange(HALF, dtype=np.float64) * 2.0 / 16.0)).astype(np.float32)


def mm(a, b, ca=1, cb=0):
    return lax.dot_general(a, b, (((ca,), (cb,)), ((), ())), preferred_element_type=F32)


class After:
    def __init__(self, array):
        self.array = array

    def spec(self):
        return pl.BlockSpec(memory_space=pl.ANY)


class Layer:
    def __init__(self, array, index):
        self.array, self.index = far(array), index

    def spec(self):
        rest = self.array.shape[1:]
        place = (self.index,) + (0,) * len(rest)
        return pl.BlockSpec((None,) + rest, lambda i: place)


class Far:
    def __init__(self, array):
        self.array = far(array)

    def spec(self):
        return whole(self.array.shape)


Kept = type(pltpu.HBM((8, 128), F32))


def far(array):
    return pltpu.with_memory_space_constraint(array, pltpu.HBM)


class Fetch:
    def __init__(self, array, layer=None):
        self.array, self.layer = far(array), layer
        self.shape = array.shape if layer is None else array.shape[1:]

    def spec(self):
        return pl.BlockSpec(memory_space=pltpu.HBM)

    def source(self, ref):
        return ref if self.layer is None else ref.at[self.layer]


class Lazy:
    def __init__(self, ref, copy):
        self.ref, self.copy, self.shape = ref, copy, ref.shape

    def __getitem__(self, index):
        if self.copy is not None:
            self.copy.wait()
            self.copy = None
        return self.ref[index]


class Store:
    def __init__(self, shape, dtype):
        self.shape, self.dtype = shape, dtype


class Out:
    def __init__(self, ref, target, sems, copies):
        self.ref, self.target, self.sems, self.copies, self.done = ref, target, sems, copies, False

    def __setitem__(self, index, value):
        self.ref[index] = value

    def __getitem__(self, index):
        return self.ref[index]

    def flush(self, *place):
        source, target = self.ref, self.target
        if place:
            source, target = source.at[place], target.at[place]
        copy = pltpu.make_async_copy(source, target, self.sems.at[len(self.copies)])
        copy.start()
        self.copies.append(copy)
        self.done = True


FLUSHES = 40


def flush(ref, *place):
    if isinstance(ref, Out):
        ref.flush(*place)


def whole(shape):
    return pl.BlockSpec(shape, lambda i: (0,) * len(shape))


def call(body, out_shape, args, name, scratch=(), smem_first=False):
    own = (Layer, Far, After, Fetch)
    specs = [a.spec() if isinstance(a, own) else whole(a.shape) for a in args]
    fetched = [i for i, a in enumerate(args) if isinstance(a, Fetch)]
    stored = [i for i, o in enumerate(out_shape) if isinstance(o, Store)]
    plans = list(args)
    arrays = [a.array if isinstance(a, own) else a for a in args]
    if smem_first:
        specs[0] = pl.BlockSpec(memory_space=pltpu.SMEM)
    shapes, out_specs = [], []
    for o in out_shape:
        if isinstance(o, Store):
            shapes.append(pltpu.HBM(o.shape, o.dtype))
            out_specs.append(pl.BlockSpec(memory_space=pltpu.HBM))
        else:
            shapes.append(o if isinstance(o, Kept) else jax.ShapeDtypeStruct(*o))
            out_specs.append(whole(o.shape if isinstance(o, Kept) else o[0]))
    buffers = [pltpu.VMEM(plans[i].shape, arrays[i].dtype) for i in fetched]
    buffers += [pltpu.VMEM(out_shape[i].shape, out_shape[i].dtype) for i in stored]
    sems = []
    if fetched:
        sems.append(pltpu.SemaphoreType.DMA((len(fetched),)))
    if stored:
        sems.append(pltpu.SemaphoreType.DMA((FLUSHES,)))
    n_in, n_out, n_scratch = len(args), len(out_shape), len(scratch)

    def run(*refs):
        ins, outs = list(refs[:n_in]), list(refs[n_in : n_in + n_out])
        rest = list(refs[n_in + n_out :])
        mine, rest = rest[:n_scratch], rest[n_scratch:]
        for k, i in enumerate(fetched):
            copy = pltpu.make_async_copy(
                plans[i].source(ins[i]), rest[k], rest[len(buffers)].at[k]
            )
            copy.start()
            ins[i] = Lazy(rest[k], copy)
        copies = []
        for k, i in enumerate(stored):
            outs[i] = Out(rest[len(fetched) + k], outs[i], rest[-1], copies)
        body(*ins, *outs, *mine)
        for i in fetched:
            if ins[i].copy is not None:
                ins[i].copy.wait()
        for i in stored:
            if not outs[i].done:
                outs[i].flush()
        for copy in copies:
            copy.wait()

    return pl.pallas_call(
        run,
        grid=(1,),
        out_shape=shapes,
        in_specs=specs,
        out_specs=out_specs,
        scratch_shapes=list(scratch) + buffers + sems,
        compiler_params=pltpu.CompilerParams(vmem_limit_bytes=40 * 1024 * 1024),
        name=name,
    )(*arrays)


def norm_rows(x):
    mean = jnp.mean(x, -1, keepdims=True)
    cen = x - mean
    inv = lax.rsqrt(jnp.mean(cen * cen, -1, keepdims=True) + EPS)
    return cen * inv, inv


def turn(t, cos, sin):
    a, b = t[:HALF], t[HALF : 2 * HALF]
    return jnp.concatenate([a * cos - b * sin, b * cos + a * sin, t[2 * HALF :]], 0)


def turn_back(u, cos, sin):
    a, b = u[:HALF], u[HALF : 2 * HALF]
    return jnp.concatenate([a * cos + b * sin, b * cos - a * sin, u[2 * HALF :]], 0)


def send_qkv(send, attn_in, w_qkv, b_qkv, layer, cs):
    for e in range(3):
        turned = (mm(attn_in, w_qkv[e]) + b_qkv[e, layer : layer + 1]).T
        for s in range(2):
            cos, sin = cs[s, 0], cs[s, 1]
            for h in range(4):
                j = s * 4 + h
                part = turned[h * HEAD : (h + 1) * HEAD, s * BLK : (s + 1) * BLK]
                if e < 2:
                    part = turn(part, cos, sin)
                if e == 0:
                    part = part * (HEAD**-0.5)
                send[j, e * HEAD : (e + 1) * HEAD, :] = part.astype(BF)


def feed_forward(mlp_in, w_up, b_up, layer, w_down, act, slope):
    width = w_up.shape[1]
    total = None
    for c in range(0, width, 256):
        cols = slice(c, c + 256)
        pre = mm(mlp_in, w_up[:, cols]) + b_up[layer : layer + 1, cols]
        cdf = 0.5 + 0.5 * lax.erf(pre * np.float32(0.7071067811865476))
        a = (pre * cdf).astype(BF)
        act[:, cols] = a
        tail = pre * (jnp.exp(-0.5 * pre * pre) * np.float32(0.3989422804014327))
        slope[:, cols] = (cdf + tail).astype(BF)
        term = mm(a, w_down[cols, :])
        total = term if total is None else total + term
    return total


def feed_back(g_b, act, slope, mlp_in, w_up, w_down, d_up, d_down, d_b_up):
    width = w_up.shape[1]
    total = None
    mlp_t = mlp_in.T
    for c in range(0, width, 256):
        cols = slice(c, c + 256)
        d_act = mm(g_b, w_down[cols, :], 1, 1)
        d_pre = d_act * slope[:, cols].astype(F32)
        d_pre_b = d_pre.astype(BF)
        d_b_up[:, cols] = jnp.sum(d_pre_b.astype(F32), 0, keepdims=True)
        d_up(c // 256, mm(mlp_t, d_pre_b))
        d_down(c, mm(act[:, cols].T, g_b))
        term = mm(d_pre_b, w_up[:, cols], 1, 1)
        total = term if total is None else total + term
    return total


def pack_up(out, row):
    def put(c, value):
        for p in range(8):
            out[p, row + 64 * c : row + 64 * (c + 1), :] = value[64 * p : 64 * (p + 1)].astype(BF)
        if c % 2 == 1:
            flush(out, slice(None), slice(row + 64 * (c - 1), row + 64 * (c + 1)))

    return put


def pack_down(out, row):
    def put(c, value):
        for half in range(2):
            for k in range(2):
                out[c // 128 + k, row + 128 * half : row + 128 * (half + 1), :] = value[
                    128 * k : 128 * (k + 1), 256 * half : 256 * (half + 1)
                ].astype(BF)
        if c % 512 == 256:
            flush(out, slice(c // 128 - 2, c // 128 + 2), slice(row, row + 256))

    return put


def pack_qkv(out, row):
    def put(e, value):
        for p in range(8):
            out[p, row + 64 * e : row + 64 * (e + 1), :] = value[64 * p : 64 * (p + 1)].astype(BF)

    return put


def own_ctx(t, recv):
    full = jnp.concatenate([gather_ctx(recv, s) for s in range(2)], 1)
    return jnp.where(t == 0, full[0:256], full[256:512])


def pack_out(out, row, ctx, upstream):
    value = mm(ctx, upstream)
    for p in range(8):
        for half in range(2):
            out[p, row + 32 * half : row + 32 * (half + 1), :] = value[
                32 * p : 32 * (p + 1), 256 * half : 256 * (half + 1)
            ].astype(BF)


def first_body(
    at, pos, freqs, x, gain, bias, w_qkv, b_qkv, w_up, b_up, w_down, w_out,
    send, pair, act, slope, cs,
):
    pair[256:512] = w_out[...]
    for s in range(2):
        p = pos[s : s + 1, :].astype(F32)
        angle = freqs[...] * p
        cs[s, 0] = jnp.cos(angle)
        cs[s, 1] = jnp.sin(angle)
    normed, _ = norm_rows(x[...])
    attn_in = (normed * gain[0, 0:1] + bias[0, 0:1]).astype(BF)
    mlp_in = (normed * gain[0, 1:2] + bias[0, 1:2]).astype(BF)
    send_qkv(send, attn_in, w_qkv, b_qkv, 0, cs)
    row = lax.broadcasted_iota(jnp.int32, (16, BLK), 0)
    token = at[0] * BLK + lax.broadcasted_iota(jnp.int32, (1, BLK), 1)
    for s in range(2):
        start = jnp.maximum(token - pos[s : s + 1, :], 0)
        high = (start // 8).astype(F32)
        low = (start % 8).astype(F32)
        block = jnp.where(row == 0, high, jnp.where(row == 1, low, 0.0)).astype(BF)
        for h in range(4):
            send[s * 4 + h, 3 * HEAD : 3 * HEAD + 16, :] = block
    pair[0:256] = feed_forward(mlp_in, w_up, b_up, 0, w_down, act, slope).astype(BF)


def load_rows(recv, lo, hi):
    return jnp.concatenate([recv[i, lo:hi, :] for i in range(8)], 1)


def starts_of(recv):
    rows = load_rows(recv, 3 * HEAD, 3 * HEAD + 16).astype(F32)
    return rows[0:1] * 8.0 + rows[1:2]


def visible_of(start, c, length):
    key = lax.broadcasted_iota(jnp.int32, (length, CHUNK), 0)
    query = lax.broadcasted_iota(jnp.int32, (length, CHUNK), 1) + c * CHUNK
    return (key <= query) & (key >= start[:, c * CHUNK : (c + 1) * CHUNK])


def attend_body(recv, send, lse, ctx, start_out):
    q = load_rows(recv, 0, HEAD)
    k_t = load_rows(recv, HEAD, 2 * HEAD)
    v_t = load_rows(recv, 2 * HEAD, 3 * HEAD)
    k = k_t.T
    start = starts_of(recv).astype(jnp.int32)
    start_out[...] = start
    for c in range(4):
        cols = slice(c * CHUNK, (c + 1) * CHUNK)
        length = (c + 1) * CHUNK
        scores = mm(k[:length], q[:, cols])
        scores = jnp.where(visible_of(start, c, length), scores, NEG)
        peak = jnp.max(scores, 0, keepdims=True)
        shifted = jnp.exp(scores - peak)
        total = jnp.sum(shifted, 0, keepdims=True)
        lse[:, cols] = peak + jnp.log(total)
        out = mm(v_t[:, :length], shifted.astype(BF)) / total
        ctx[:, cols] = out
        for i in range(CHUNK // BLK):
            block = out[:, i * BLK : (i + 1) * BLK].astype(BF)
            for t in range(2):
                send[c * (CHUNK // BLK) + i, t] = block


def attend_both_body(recv, start, _, send, dk, dv):
    q = load_rows(recv, 0, HEAD)
    k_t = load_rows(recv, HEAD, 2 * HEAD)
    v_t = load_rows(recv, 2 * HEAD, 3 * HEAD)
    d_ctx = load_rows(recv, 3 * HEAD, 4 * HEAD)
    k = k_t.T
    v = v_t.T
    dk[...] = jnp.zeros_like(dk)
    dv[...] = jnp.zeros_like(dv)
    for c in range(4):
        cols = slice(c * CHUNK, (c + 1) * CHUNK)
        length = (c + 1) * CHUNK
        scores = mm(k[:length], q[:, cols])
        scores = jnp.where(visible_of(start[...], c, length), scores, NEG)
        peak = jnp.max(scores, 0, keepdims=True)
        shifted = jnp.exp(scores - peak)
        probs = shifted * (1.0 / jnp.sum(shifted, 0, keepdims=True))
        probs_b = probs.astype(BF)
        out = mm(v_t[:, :length], probs_b)
        dq = backward_chunk(q, k_t, v, d_ctx, probs, probs_b, out, cols, length, dk, dv)
        for i in range(CHUNK // BLK):
            b = c * (CHUNK // BLK) + i
            for t in range(2):
                send[b, t, 0:HEAD] = out[:, i * BLK : (i + 1) * BLK].astype(BF)
                send[b, t, HEAD : 2 * HEAD] = dq[:, i * BLK : (i + 1) * BLK].astype(BF)
    put_kv(send, dk, dv, 2 * HEAD)


def backward_chunk(q, k_t, v, d_ctx, probs, probs_b, out, cols, length, dk, dv):
    d_out = d_ctx[:, cols]
    d_probs = mm(v[:length], d_out)
    delta = jnp.sum(d_out.astype(F32) * out, 0, keepdims=True)
    d_scores = (probs * (d_probs - delta)).astype(BF)
    dk[:, :length] += mm(q[:, cols], d_scores, 1, 1)
    dv[:, :length] += mm(d_out, probs_b, 1, 1)
    return mm(k_t[:, :length], d_scores) * (HEAD**-0.5)


def put_kv(send, dk, dv, row):
    for b in range(8):
        for t in range(2):
            send[b, t, row : row + HEAD] = dk[:, b * BLK : (b + 1) * BLK].astype(BF)
            send[b, t, row + HEAD : row + 2 * HEAD] = dv[:, b * BLK : (b + 1) * BLK].astype(BF)


def attend_back_body(recv, recv_d, start, lse, ctx, _, send, dk, dv):
    ride = recv_d[0, 64:192].astype(F32)
    for i in range(1, 8):
        ride = ride + recv_d[i, 64:192].astype(F32)
    ride = ride.astype(BF)
    for b in range(8):
        for t in range(2):
            send[b, t, 192:320] = ride
    q = load_rows(recv, 0, HEAD)
    k_t = load_rows(recv, HEAD, 2 * HEAD)
    v_t = load_rows(recv, 2 * HEAD, 3 * HEAD)
    d_ctx = load_rows(recv_d, 0, HEAD)
    k = k_t.T
    v = v_t.T
    dk[...] = jnp.zeros_like(dk)
    dv[...] = jnp.zeros_like(dv)
    for c in range(4):
        cols = slice(c * CHUNK, (c + 1) * CHUNK)
        length = (c + 1) * CHUNK
        scores = mm(k[:length], q[:, cols])
        scores = jnp.where(visible_of(start[...], c, length), scores, NEG)
        probs = jnp.exp(scores - lse[:, cols])
        probs_b = probs.astype(BF)
        dq = backward_chunk(q, k_t, v, d_ctx, probs, probs_b, ctx[:, cols], cols, length, dk, dv)
        for i in range(CHUNK // BLK):
            for t in range(2):
                send[c * (CHUNK // BLK) + i, t, 0:HEAD] = dq[:, i * BLK : (i + 1) * BLK].astype(BF)
    put_kv(send, dk, dv, HEAD)


def gather_ctx(recv, s):
    return jnp.concatenate([recv[s * 4 + h, t, 0:HEAD, :] for t in range(2) for h in range(4)], 0)


def ordered(t, own, other):
    return jnp.where(t == 0, own, other), jnp.where(t == 0, other, own)


def out_other(others):
    halves = [
        jnp.concatenate([others[3, 64 * p + 32 * c : 64 * p + 32 * (c + 1), :] for p in range(8)], 0)
        for c in range(2)
    ]
    return jnp.concatenate(halves, 1)


def branch_of(t, recv, w_own, w_other):
    first, second = ordered(t, w_own, w_other)
    w = jnp.concatenate([first, second], 0)
    rows = []
    for s in range(2):
        rows.append(mm(gather_ctx(recv, s).T, w))
    return jnp.concatenate(rows, 0)


def middle_body(
    at, x, pair, pair_other, recv, w_out_own, out_bias, gain, bias,
    w_qkv, b_qkv, w_up, b_up, w_down, w_out, cot, cs,
    stream, send, grads, parts, d_b_up, d_sum, act, slope,
):
    branch = pair[0:256].astype(F32) + pair_other[0:256].astype(F32)
    branch = branch + branch_of(at[1], recv, w_out_own[...], pair_other[256:512])
    out = x[...] + branch + out_bias[0, 0:1] + out_bias[0, 1:2]
    stream[...] = out
    normed, _ = norm_rows(out)
    attn_in = (normed * gain[1, 0:1] + bias[1, 0:1]).astype(BF)
    mlp_in = (normed * gain[1, 1:2] + bias[1, 1:2]).astype(BF)
    send_qkv(send, attn_in, w_qkv, b_qkv, 1, cs)
    g_b = cot[...].astype(BF)
    d_ctx = mm(w_out[...], g_b, 1, 1)
    for s in range(2):
        for h in range(4):
            send[s * 4 + h, 3 * HEAD : 4 * HEAD, :] = d_ctx[
                h * HEAD : (h + 1) * HEAD, s * BLK : (s + 1) * BLK
            ].astype(BF)
    d_sum[...] = jnp.sum(cot[...], 0, keepdims=True)
    parts[0:256] = feed_forward(mlp_in, w_up, b_up, 1, w_down, act, slope).astype(BF)
    parts[256:512] = feed_back(
        g_b, act, slope, mlp_in, w_up, w_down, pack_up(grads, 0), pack_down(grads, 256), d_b_up
    ).astype(BF)


def norm_back(
    t, x, g, d_mlp_in, recv, row, w_own, others, cs, gain, bias, layer, d_qkv, d_b_qkv, d_norm
):
    normed, inv = norm_rows(x)
    attn_in = (normed * gain[layer, 0:1] + bias[layer, 0:1]).astype(BF)
    attn_t = attn_in.T
    d_attn_t = None
    for e in range(3):
        halves = []
        for tt in range(2):
            blocks = []
            for h in range(4):
                pieces = []
                for s in range(2):
                    lo = row + e * HEAD
                    u = recv[s * 4 + h, tt, lo : lo + HEAD, :]
                    if e < 2:
                        u = turn_back(u.astype(F32), cs[s, 0], cs[s, 1]).astype(BF)
                    pieces.append(u)
                blocks.append(jnp.concatenate(pieces, 1))
            halves.append(jnp.concatenate(blocks, 0))
        first, second = ordered(t, w_own[e], others[e])
        term = mm(first, halves[0]) + mm(second, halves[1])
        d_attn_t = term if d_attn_t is None else d_attn_t + term
        own = jnp.where(t == 0, halves[0], halves[1])
        d_qkv(e, mm(attn_t, own, 1, 1))
        d_b_qkv[e : e + 1] = mm(jnp.ones((8, own.shape[1]), BF), own, 1, 1)[0:1]
    d_attn_in = d_attn_t.T
    d_norm[0:1] = jnp.sum(d_attn_in * normed, 0, keepdims=True)
    d_norm[1:2] = jnp.sum(d_mlp_in * normed, 0, keepdims=True)
    d_norm[2:3] = jnp.sum(d_attn_in, 0, keepdims=True)
    d_norm[3:4] = jnp.sum(d_mlp_in, 0, keepdims=True)
    d_normed = d_attn_in * gain[layer, 0:1] + d_mlp_in * gain[layer, 1:2]
    return g + inv * (
        d_normed
        - jnp.mean(d_normed, -1, keepdims=True)
        - normed * jnp.mean(d_normed * normed, -1, keepdims=True)
    )


def turn_point_body(
    at, stream, parts, parts_other, recv, w_out, w_qkv, others, out_bias,
    gain, bias, cot, cs, x, act, slope, w_up, w_down, w_out_first, recv_first, sums_a,
    block_out, g_out, send, grads, part, d_b_up, d_b_qkv, d_norm, d_sum,
):
    t = at[1]
    branch = parts[0:256].astype(F32) + parts_other[0:256].astype(F32)
    branch = branch + branch_of(t, recv, w_out[...], out_other(others))
    block_out[...] = stream[...] + branch + out_bias[1, 0:1] + out_bias[1, 1:2]
    d_mlp_in = parts[256:512].astype(F32) + parts_other[256:512].astype(F32)
    g = norm_back(
        t, stream[...], cot[...], d_mlp_in, recv, HEAD, w_qkv, others, cs, gain, bias, 1,
        pack_qkv(grads, 0), d_b_qkv, d_norm,
    )
    g_out[...] = g
    g_b = g.astype(BF)
    d_sum[...] = jnp.sum(g, 0, keepdims=True)
    d_ctx = mm(w_out_first[...], g_b, 1, 1)
    for s in range(2):
        for h in range(4):
            send[s * 4 + h, 0:HEAD] = d_ctx[
                h * HEAD : (h + 1) * HEAD, s * BLK : (s + 1) * BLK
            ].astype(BF)
    for q in range(8):
        for c in range(2):
            send[q, 64 + 64 * c : 128 + 64 * c] = sums_a[
                64 * q : 64 * (q + 1), BLK * c : BLK * (c + 1)
            ]
    pack_out(grads, 704, own_ctx(t, recv), cot[...].astype(BF))
    pack_out(grads, 768, own_ctx(t, recv_first), g_b)
    flush(grads, slice(None), slice(0, 192))
    flush(grads, slice(None), slice(704, 832))
    normed, _ = norm_rows(x[...])
    mlp_in = (normed * gain[0, 1:2] + bias[0, 1:2]).astype(BF)
    part[...] = feed_back(
        g_b, act, slope, mlp_in, w_up, w_down, pack_up(grads, 192), pack_down(grads, 448), d_b_up
    ).astype(BF)


def last_body(
    at, x, g, part, part_other, recv, w_qkv, others, cs, gain, bias,
    d_b_up0, d_b_up1, d_b_qkv1, d_norm1, d_sum0, d_sum1,
    in_grad, grads, sums_a, d_b_qkv0, d_norm0,
):
    d_mlp_in = part[...].astype(F32) + part_other[...].astype(F32)
    in_grad[...] = norm_back(
        at[1], x[...], g[...], d_mlp_in, recv, 0, w_qkv, others, cs, gain, bias, 0,
        pack_qkv(grads, 0), d_b_qkv0, d_norm0,
    )
    for q in range(8):
        both_planes = recv[q, :, 192:320]
        block = jnp.where(at[1] == 0, both_planes[0], both_planes[1])
        for c in range(2):
            sums_a[64 * q : 64 * (q + 1), BLK * c : BLK * (c + 1)] = block[64 * c : 64 * (c + 1)]

    def lanes(ref, row, count):
        return [ref[row : row + 1, 256 * c : 256 * (c + 1)] for c in range(count)]

    def norms(ref):
        return [v for r in range(4) for v in lanes(ref, r, 2)]

    rows = [
        lanes(d_b_up0, 0, 4)
        + lanes(d_b_up1, 0, 4)
        + [v for e in range(3) for ref in (d_b_qkv0, d_b_qkv1) for v in lanes(ref, e, 1)],
        lanes(d_sum0, 0, 2) + lanes(d_sum1, 0, 2) + norms(d_norm0),
        norms(d_norm1),
    ]
    for p in range(8):
        have = rows[p] if p < len(rows) else []
        fill = [jnp.zeros((16 - len(have), 256), F32)]
        grads[p, 192:208, :] = jnp.concatenate(have + fill, 0).astype(BF)


def chunk_body(at, w_qkv, w_out, out):
    for layer in range(2):
        for e in range(3):
            out[layer, e] = w_qkv[layer, e]
        out[layer, 3, 0:32] = w_out[layer, :, 0:256]
        out[layer, 3, 32:64] = w_out[layer, :, 256:512]


def chunk_of(at, wq, w_out):
    return pl.pallas_call(
        chunk_body,
        out_shape=jax.ShapeDtypeStruct((2, 4, 64, 256), BF),
        grid_spec=pltpu.PrefetchScalarGridSpec(
            num_scalar_prefetch=1,
            grid=(1,),
            in_specs=[
                pl.BlockSpec((2, 3, 64, 256), lambda i, at: (0, 0, at[2], 0)),
                pl.BlockSpec((2, 32, 512), lambda i, at: (0, at[2], 0)),
            ],
            out_specs=pl.BlockSpec((2, 4, 64, 256), lambda i, at: (0, 0, 0, 0)),
        ),
        compiler_params=pltpu.CompilerParams(vmem_limit_bytes=40 * 1024 * 1024),
        name="chunk",
    )(at, far(wq), far(w_out))


def hand_on_body(value, _, out):
    out[...] = value[...]


def mix_body(got, early, first, out, first_out):
    total = got[0].astype(F32)
    for i in range(1, 8):
        total = total + got[i].astype(F32)
    for q in range(8):
        tiny = total[192 + 8 * q : 200 + 8 * q] if q < 2 else jnp.zeros((8, 256), F32)
        mine = [early[104 * q : 104 * (q + 1)].astype(F32), total[24 * q : 24 * (q + 1)], tiny]
        out[q] = jnp.concatenate(mine, 0).astype(BF)
    first_out[...] = first[...]


def sum_body(got, out):
    total = got[0].astype(F32)
    for i in range(1, 8):
        total = total + got[i].astype(F32)
    for q in range(8):
        out[q] = total.astype(BF)


def unpack_first_body(first, g_up, g_down):
    for k in range(2):
        for c in range(4):
            cols = slice(256 * c, 256 * (c + 1))
            g_up[0, 64 * k : 64 * (k + 1), cols] = first[k, 64 * c : 64 * (c + 1)].astype(F32)
        for c in range(2):
            rows = first[k, 256 + 128 * c : 256 + 128 * (c + 1)]
            cols = slice(256 * c, 256 * (c + 1))
            g_down[0, 128 * k : 128 * (k + 1), cols] = rows.astype(F32)


def unpack_rest_body(rest, _, __, g_up, g_down, g_qkv, g_out, g_b_up, g_b_qkv, g_sum, g_gain, g_bias):
    p = pl.program_id(0)
    for k in range(2):
        for q in range(8):
            block = rest[k, q].astype(F32)
            for i in range(16):
                value = block[8 * i : 8 * (i + 1)]
                row = 104 * q + 8 * i
                if i >= 13:
                    row = 24 * q + 8 * (i - 13)
                    r = 64 * k + row % 64
                    g_qkv[0, row // 64, r : r + 8] = value
                elif row < 192:
                    r = 64 * k + row % 64
                    g_qkv[1, row // 64, r : r + 8] = value
                elif row < 448:
                    c, r = divmod(row - 192, 64)
                    r += 64 * k
                    g_up[0, r : r + 8, 256 * c : 256 * (c + 1)] = value
                elif row < 704:
                    c, r = divmod(row - 448, 128)
                    r += 128 * k
                    g_down[0, r : r + 8, 256 * c : 256 * (c + 1)] = value
                else:
                    c, r = divmod((row - 704) % 64, 32)
                    r += 32 * k
                    g_out[1 - (row - 704) // 64, r : r + 8, 256 * c : 256 * (c + 1)] = value

    tiny = [jnp.concatenate([rest[k, q].astype(F32)[128:136] for q in range(2)], 0) for k in range(2)]

    @pl.when(p == 0)
    def _():
        for layer in range(2):
            for c in range(4):
                r = 4 * layer + c
                g_b_up[layer : layer + 1, 256 * c : 256 * (c + 1)] = tiny[0][r : r + 1]
        for e in range(3):
            for layer in range(2):
                r = 8 + 2 * e + layer
                g_b_qkv[e, layer : layer + 1, :] = tiny[0][r : r + 1]
        for layer in range(2):
            for c in range(2):
                r = 2 * layer + c
                for which in range(2):
                    g_sum[layer, which : which + 1, 256 * c : 256 * (c + 1)] = tiny[1][r : r + 1]

    def norms(layer, rows, base):
        for which in range(2):
            for c in range(2):
                cols = slice(256 * c, 256 * (c + 1))
                r = base + 2 * which + c
                g_gain[layer, which : which + 1, cols] = rows[r : r + 1]
                g_bias[layer, which : which + 1, cols] = rows[r + 4 : r + 5]

    @pl.when(p == 0)
    def _():
        norms(0, tiny[1], 4)

    @pl.when(p == 1)
    def _():
        norms(1, tiny[0], 0)


UP = (2, 512, 1024)
DOWN = (2, 1024, 512)


def unpack(first, rest):
    def place(layer):
        return [
            pl.BlockSpec((1, 128, 1024), lambda p: (layer, p, 0)),
            pl.BlockSpec((1, 256, 512), lambda p: (layer, p, 0)),
        ]

    params = pltpu.CompilerParams(vmem_limit_bytes=40 * 1024 * 1024)
    g_up, g_down = pl.pallas_call(
        unpack_first_body,
        grid=(4,),
        out_shape=[pltpu.HBM(UP, F32), pltpu.HBM(DOWN, F32)],
        in_specs=[pl.BlockSpec((2, 512, 256), lambda p: (p, 0, 0))],
        out_specs=place(1),
        compiler_params=params,
        name="unpack_first",
    )(far(first))
    outs = [
        ((2, 3, 512, 256), pl.BlockSpec((2, 3, 128, 256), lambda p: (0, 0, p, 0))),
        ((2, 256, 512), pl.BlockSpec((2, 64, 512), lambda p: (0, p, 0))),
        ((2, 1024), whole((2, 1024))),
        ((3, 2, 256), whole((3, 2, 256))),
        ((2, 2, 512), whole((2, 2, 512))),
        ((2, 2, 512), whole((2, 2, 512))),
        ((2, 2, 512), whole((2, 2, 512))),
    ]
    return pl.pallas_call(
        unpack_rest_body,
        grid=(4,),
        out_shape=[pltpu.HBM(shape, F32) for shape in [UP, DOWN] + [o[0] for o in outs]],
        in_specs=[
            pl.BlockSpec((2, 8, 136, 256), lambda p: (p, 0, 0, 0)),
            pl.BlockSpec(memory_space=pl.ANY),
            pl.BlockSpec(memory_space=pl.ANY),
        ],
        out_specs=place(0) + [spec for _, spec in outs],
        input_output_aliases={1: 0, 2: 1},
        compiler_params=params,
        name="unpack_rest",
    )(far(rest), far(g_up), far(g_down))


def swap(value):
    return lax.ppermute(value, "tensor", [(0, 1), (1, 0)])


def exchange(value, axes):
    return lax.all_to_all(value, axes, 0, 0)


def both(value):
    flat = value.reshape((16,) + value.shape[2:])
    return exchange(flat, ("context", "tensor")).reshape(value.shape)


def shards(
    tokens_in, cotangent, positions, w_qkv, b_qkv, w_out, w_up, b_up, w_down, out_bias, ln_gain, ln_bias
):
    rows, width = 256, 512
    x = tokens_in.reshape(rows, width)
    cot = cotangent.reshape(rows, width)
    wq = jnp.transpose(w_qkv, (0, 2, 1, 3))
    bq = jnp.transpose(b_qkv, (1, 0, 2))
    at = jnp.stack(
        [lax.axis_index("context"), lax.axis_index("tensor"), lax.axis_index("dp")]
    ).astype(jnp.int32)
    freqs = jnp.asarray(FREQS).reshape(HALF, 1)
    chunk = swap(chunk_of(at, wq, w_out))
    send, pair, act, slope, cs = call(
        first_body,
        [
            pltpu.VMEM((8, 208, BLK), BF),
            ((2 * rows, width), BF),
            pltpu.HBM((rows, 1024), BF),
            pltpu.HBM((rows, 1024), BF),
            ((2, 2, HALF, BLK), F32),
        ],
        (
            at, positions, freqs, Far(x), ln_gain, ln_bias, Layer(wq, 0), bq, Fetch(w_up, 0), b_up,
            Fetch(w_down, 0), Layer(w_out, 0),
        ),
        "norm_qkv_feed",
        smem_first=True,
    )
    pair_other = swap(pair)
    (chunk,) = call(
        hand_on_body, [pltpu.HBM(chunk.shape, BF)], (chunk, After(send)), "hand_on"
    )
    others = lax.all_gather(chunk, "dp", axis=2, tiled=True)
    recv = exchange(send, "context")
    ctx_send, lse, ctx, start = call(
        attend_body,
        [((8, 2, HEAD, BLK), BF), ((1, 1024), F32), pltpu.HBM((HEAD, 1024), F32), ((1, 1024), jnp.int32)],
        (recv,),
        "attend",
    )
    recv_ctx = both(ctx_send)
    stream, send, grads_a, parts, d_b_up1, d_sum1 = call(
        middle_body,
        [
            pltpu.HBM((rows, width), F32),
            ((8, 256, BLK), BF),
            Store((8, 512, 256), BF),
            ((2 * rows, width), BF),
            ((1, 1024), F32),
            ((1, width), F32),
        ],
        (
            at, Far(x), pair, pair_other, recv_ctx, Layer(w_out, 0), out_bias, ln_gain, ln_bias,
            Layer(wq, 1), bq, Fetch(w_up, 1), b_up, Fetch(w_down, 1), Layer(w_out, 1), Far(cot), cs,
        ),
        "middle",
        scratch=[pltpu.VMEM((rows, 1024), BF), pltpu.VMEM((rows, 1024), BF)],
        smem_first=True,
    )
    sums_a = lax.psum_scatter(grads_a, "dp", scatter_dimension=0)
    parts_other = swap(parts)
    recv_both = exchange(send, "context")
    (both_send,) = call(
        attend_both_body,
        [((8, 2, 256, BLK), BF)],
        (recv_both, start, After(parts_other)),
        "attend_both",
        scratch=[pltpu.VMEM((HEAD, 1024), F32), pltpu.VMEM((HEAD, 1024), F32)],
    )
    recv_grad = both(both_send)
    block_out, g, send, grads_b, part_g, d_b_up0, d_b_qkv1, d_norm1, d_sum0 = call(
        turn_point_body,
        [
            pltpu.HBM((rows, width), F32),
            pltpu.HBM((rows, width), F32),
            pltpu.VMEM((8, 192, BLK), BF),
            Store((8, 832, 256), BF),
            ((rows, width), BF),
            ((1, 1024), F32),
            ((3, 256), F32),
            ((4, width), F32),
            ((1, width), F32),
        ],
        (
            at, Far(stream), parts, parts_other, recv_grad, Layer(w_out, 1), Layer(wq, 1),
            Layer(others, 1), out_bias, ln_gain, ln_bias, Far(cot), cs, Fetch(x), Fetch(act), Fetch(slope),
            Fetch(w_up, 0), Fetch(w_down, 0), Layer(w_out, 0), recv_ctx, Far(sums_a),
        ),
        "turn_point",
        smem_first=True,
    )
    sums_b = lax.psum_scatter(grads_b, "dp", scatter_dimension=0)
    part_g_other = swap(part_g)
    recv_d = exchange(send, "context")
    (back_send,) = call(
        attend_back_body,
        [((8, 2, 320, BLK), BF)],
        (recv, recv_d, start, lse, ctx, After(part_g_other)),
        "attend_back",
        scratch=[pltpu.VMEM((HEAD, 1024), F32), pltpu.VMEM((HEAD, 1024), F32)],
    )
    recv_grad0 = both(back_send)
    in_grad, grads_c, sums_a, _, _ = call(
        last_body,
        [
            pltpu.HBM((rows, width), F32),
            ((8, 208, 256), BF),
            pltpu.HBM((512, 256), BF),
            ((3, 256), F32),
            ((4, width), F32),
        ],
        (
            at, Far(x), Far(g), part_g, part_g_other, recv_grad0, Layer(wq, 0), Layer(others, 0), cs,
            ln_gain, ln_bias, d_b_up0, d_b_up1, d_b_qkv1, d_norm1, d_sum0, d_sum1,
        ),
        "last",
        smem_first=True,
    )
    mixed, sums_a = call(
        mix_body,
        [((8, 136, 256), BF), pltpu.HBM((512, 256), BF)],
        (exchange(grads_c, "dp"), Far(sums_b), Far(sums_a)),
        "mix",
    )
    full_a = lax.all_gather(sums_a, "dp")
    (summed,) = call(sum_body, [((8, 136, 256), BF)], (exchange(mixed, "context"),), "sum")
    full_bc = lax.all_gather(exchange(summed, "context"), "dp")
    g_up, g_down, g_qkv, g_out, g_b_up, g_b_qkv, g_sum, g_gain, g_bias = unpack(full_a, full_bc)
    return (
        block_out.reshape(tokens_in.shape),
        in_grad.reshape(tokens_in.shape),
        jnp.transpose(g_qkv, (0, 2, 1, 3)),
        jnp.transpose(g_b_qkv, (1, 0, 2)),
        g_out,
        g_up,
        g_b_up,
        g_down,
        g_sum,
        g_gain,
        g_bias,
    )


def solution(mesh):
    return jax.shard_map(
        shards,
        mesh=mesh,
        in_specs=(
            P("dp", "context", None),
            P("dp", "context", None),
            P("dp", "context"),
            P(None, None, None, "tensor"),
            P(None, None, "tensor"),
            P(None, "tensor", None),
            P(None, None, "tensor"),
            P(None, "tensor"),
            P(None, "tensor", None),
            P(),
            P(),
            P(),
        ),
        out_specs=(
            P("dp", "context", None),
            P("dp", "context", None),
            P(None, None, None, "tensor"),
            P(None, None, "tensor"),
            P(None, "tensor", None),
            P(None, None, "tensor"),
            P(None, "tensor"),
            P(None, "tensor", None),
            P(),
            P(),
            P(),
        ),
        check_vma=False,
    )
```

```python
from functools import partial

import numpy as np

import jax
import jax.numpy as jnp
from jax import lax
from jax.experimental import pallas as pl
from jax.experimental.pallas import tpu as pltpu
from jax.sharding import PartitionSpec as P

EPS = 1e-05
HALF = 8
HEAD = 64
BLK = 128
CHUNK = 256
NEG = -1e30
BF = jnp.bfloat16
F32 = jnp.float32

FREQS = (10000.0 ** (-np.arange(HALF, dtype=np.float64) * 2.0 / 16.0)).astype(np.float32)


def mm(a, b, ca=1, cb=0):
    return lax.dot_general(a, b, (((ca,), (cb,)), ((), ())), preferred_element_type=F32)


class After:
    def __init__(self, array):
        self.array = array

    def spec(self):
        return pl.BlockSpec(memory_space=pl.ANY)


class Layer:
    def __init__(self, array, index):
        self.array, self.index = far(array), index

    def spec(self):
        rest = self.array.shape[1:]
        place = (self.index,) + (0,) * len(rest)
        return pl.BlockSpec((None,) + rest, lambda i: place)


class Far:
    def __init__(self, array):
        self.array = far(array)

    def spec(self):
        return whole(self.array.shape)


Kept = type(pltpu.HBM((8, 128), F32))


class Near:
    def __init__(self, array):
        self.array = pltpu.with_memory_space_constraint(array, pltpu.VMEM)

    def spec(self):
        return whole(self.array.shape)


def bring(items, after, name):
    pairs = [i if isinstance(i, tuple) else (i, None) for i in items]
    shapes = [a.shape if layer is None else a.shape[1:] for a, layer in pairs]
    count = len(pairs)

    def body(*refs):
        sems = refs[-1]
        copies = []
        for k, (_, layer) in enumerate(pairs):
            source = refs[k] if layer is None else refs[k].at[layer]
            copies.append(pltpu.make_async_copy(source, refs[count + 1 + k], sems.at[k]))
        for copy in copies:
            copy.start()
        for copy in copies:
            copy.wait()

    size = sum(int(np.prod(shape)) * a.dtype.itemsize for (a, _), shape in zip(pairs, shapes))
    outs = pl.pallas_call(
        body,
        out_shape=[pltpu.VMEM(shape, a.dtype) for (a, _), shape in zip(pairs, shapes)],
        in_specs=[pl.BlockSpec(memory_space=pltpu.HBM)] * count
        + [pl.BlockSpec(memory_space=pl.ANY)],
        out_specs=[pl.BlockSpec(memory_space=pltpu.VMEM)] * count,
        scratch_shapes=[pltpu.SemaphoreType.DMA((count,))],
        compiler_params=pltpu.CompilerParams(vmem_limit_bytes=16 * 1024 * 1024),
        cost_estimate=pl.CostEstimate(flops=0, bytes_accessed=2 * size, transcendentals=0),
        name=name,
    )(*[far(a) for a, _ in pairs], after)
    return [Near(o) for o in outs]


def far(array):
    return pltpu.with_memory_space_constraint(array, pltpu.HBM)


def whole(shape):
    return pl.BlockSpec(shape, lambda i: (0,) * len(shape))


def call(body, out_shape, args, name, scratch=(), smem_first=False):
    specs = [
        a.spec() if isinstance(a, (Layer, Far, Near, After)) else whole(a.shape) for a in args
    ]
    args = [a.array if isinstance(a, (Layer, Far, Near, After)) else a for a in args]
    if smem_first:
        specs[0] = pl.BlockSpec(memory_space=pltpu.SMEM)
    return pl.pallas_call(
        body,
        grid=(1,),
        out_shape=[o if isinstance(o, Kept) else jax.ShapeDtypeStruct(*o) for o in out_shape],
        in_specs=specs,
        out_specs=[whole(o.shape if isinstance(o, Kept) else o[0]) for o in out_shape],
        scratch_shapes=list(scratch),
        compiler_params=pltpu.CompilerParams(vmem_limit_bytes=40 * 1024 * 1024),
        name=name,
    )(*args)


def norm_rows(x):
    mean = jnp.mean(x, -1, keepdims=True)
    cen = x - mean
    inv = lax.rsqrt(jnp.mean(cen * cen, -1, keepdims=True) + EPS)
    return cen * inv, inv


def turn(t, cos, sin):
    a, b = t[:HALF], t[HALF : 2 * HALF]
    return jnp.concatenate([a * cos - b * sin, b * cos + a * sin, t[2 * HALF :]], 0)


def turn_back(u, cos, sin):
    a, b = u[:HALF], u[HALF : 2 * HALF]
    return jnp.concatenate([a * cos + b * sin, b * cos - a * sin, u[2 * HALF :]], 0)


def send_qkv(send, attn_in, w_qkv, b_qkv, layer, cs):
    for e in range(3):
        turned = (mm(attn_in, w_qkv[e]) + b_qkv[e, layer : layer + 1]).T
        for s in range(2):
            cos, sin = cs[s, 0], cs[s, 1]
            for h in range(4):
                j = s * 4 + h
                part = turned[h * HEAD : (h + 1) * HEAD, s * BLK : (s + 1) * BLK]
                if e < 2:
                    part = turn(part, cos, sin)
                if e == 0:
                    part = part * (HEAD**-0.5)
                send[j, e * HEAD : (e + 1) * HEAD, :] = part.astype(BF)


def feed_forward(mlp_in, w_up, b_up, layer, w_down, act, slope):
    width = w_up.shape[1]
    total = None
    for c in range(0, width, 256):
        cols = slice(c, c + 256)
        pre = mm(mlp_in, w_up[:, cols]) + b_up[layer : layer + 1, cols]
        cdf = 0.5 + 0.5 * lax.erf(pre * np.float32(0.7071067811865476))
        a = (pre * cdf).astype(BF)
        act[:, cols] = a
        tail = pre * (jnp.exp(-0.5 * pre * pre) * np.float32(0.3989422804014327))
        slope[:, cols] = (cdf + tail).astype(BF)
        term = mm(a, w_down[cols, :])
        total = term if total is None else total + term
    return total


def feed_back(g_b, act, slope, mlp_in, w_up, w_down, d_up, d_down, d_b_up):
    width = w_up.shape[1]
    total = None
    mlp_t = mlp_in.T
    for c in range(0, width, 256):
        cols = slice(c, c + 256)
        d_act = mm(g_b, w_down[cols, :], 1, 1)
        d_pre = d_act * slope[:, cols].astype(F32)
        d_pre_b = d_pre.astype(BF)
        d_b_up[:, cols] = jnp.sum(d_pre_b.astype(F32), 0, keepdims=True)
        d_up(c // 256, mm(mlp_t, d_pre_b))
        d_down(c, mm(act[:, cols].T, g_b))
        term = mm(d_pre_b, w_up[:, cols], 1, 1)
        total = term if total is None else total + term
    return total


def pack_up(out, row):
    def put(c, value):
        for p in range(8):
            out[p, row + 64 * c : row + 64 * (c + 1), :] = value[64 * p : 64 * (p + 1)].astype(BF)

    return put


def pack_down(out, row):
    def put(c, value):
        for half in range(2):
            for k in range(2):
                out[c // 128 + k, row + 128 * half : row + 128 * (half + 1), :] = value[
                    128 * k : 128 * (k + 1), 256 * half : 256 * (half + 1)
                ].astype(BF)

    return put


def pack_qkv(out, row):
    def put(e, value):
        for p in range(8):
            out[p, row + 64 * e : row + 64 * (e + 1), :] = value[64 * p : 64 * (p + 1)].astype(BF)

    return put


def own_ctx(t, recv):
    full = jnp.concatenate([gather_ctx(recv, s) for s in range(2)], 1)
    return jnp.where(t == 0, full[0:256], full[256:512])


def pack_out(out, row, ctx, upstream):
    value = mm(ctx, upstream)
    for p in range(8):
        for half in range(2):
            out[p, row + 32 * half : row + 32 * (half + 1), :] = value[
                32 * p : 32 * (p + 1), 256 * half : 256 * (half + 1)
            ].astype(BF)


def first_body(
    at, pos, freqs, x, gain, bias, w_qkv, b_qkv, w_up, b_up, w_down, w_out,
    send, pair, act, slope, cs,
):
    pair[256:512] = w_out[...]
    for s in range(2):
        p = pos[s : s + 1, :].astype(F32)
        angle = freqs[...] * p
        cs[s, 0] = jnp.cos(angle)
        cs[s, 1] = jnp.sin(angle)
    normed, _ = norm_rows(x[...])
    attn_in = (normed * gain[0, 0:1] + bias[0, 0:1]).astype(BF)
    mlp_in = (normed * gain[0, 1:2] + bias[0, 1:2]).astype(BF)
    send_qkv(send, attn_in, w_qkv, b_qkv, 0, cs)
    row = lax.broadcasted_iota(jnp.int32, (16, BLK), 0)
    token = at[0] * BLK + lax.broadcasted_iota(jnp.int32, (1, BLK), 1)
    for s in range(2):
        start = jnp.maximum(token - pos[s : s + 1, :], 0)
        high = (start // 8).astype(F32)
        low = (start % 8).astype(F32)
        block = jnp.where(row == 0, high, jnp.where(row == 1, low, 0.0)).astype(BF)
        for h in range(4):
            send[s * 4 + h, 3 * HEAD : 3 * HEAD + 16, :] = block
    pair[0:256] = feed_forward(mlp_in, w_up, b_up, 0, w_down, act, slope).astype(BF)


def load_rows(recv, lo, hi):
    return jnp.concatenate([recv[i, lo:hi, :] for i in range(8)], 1)


def starts_of(recv):
    rows = load_rows(recv, 3 * HEAD, 3 * HEAD + 16).astype(F32)
    return rows[0:1] * 8.0 + rows[1:2]


def visible_of(start, c, length):
    key = lax.broadcasted_iota(jnp.int32, (length, CHUNK), 0)
    query = lax.broadcasted_iota(jnp.int32, (length, CHUNK), 1) + c * CHUNK
    return (key <= query) & (key >= start[:, c * CHUNK : (c + 1) * CHUNK])


def attend_body(recv, send, lse, ctx, start_out):
    q = load_rows(recv, 0, HEAD)
    k_t = load_rows(recv, HEAD, 2 * HEAD)
    v_t = load_rows(recv, 2 * HEAD, 3 * HEAD)
    k = k_t.T
    start = starts_of(recv).astype(jnp.int32)
    start_out[...] = start
    for c in range(4):
        cols = slice(c * CHUNK, (c + 1) * CHUNK)
        length = (c + 1) * CHUNK
        scores = mm(k[:length], q[:, cols])
        scores = jnp.where(visible_of(start, c, length), scores, NEG)
        peak = jnp.max(scores, 0, keepdims=True)
        shifted = jnp.exp(scores - peak)
        total = jnp.sum(shifted, 0, keepdims=True)
        lse[:, cols] = peak + jnp.log(total)
        out = mm(v_t[:, :length], shifted.astype(BF)) / total
        ctx[:, cols] = out
        for i in range(CHUNK // BLK):
            block = out[:, i * BLK : (i + 1) * BLK].astype(BF)
            for t in range(2):
                send[c * (CHUNK // BLK) + i, t] = block


def attend_both_body(recv, start, _, send, dk, dv):
    q = load_rows(recv, 0, HEAD)
    k_t = load_rows(recv, HEAD, 2 * HEAD)
    v_t = load_rows(recv, 2 * HEAD, 3 * HEAD)
    d_ctx = load_rows(recv, 3 * HEAD, 4 * HEAD)
    k = k_t.T
    v = v_t.T
    dk[...] = jnp.zeros_like(dk)
    dv[...] = jnp.zeros_like(dv)
    for c in range(4):
        cols = slice(c * CHUNK, (c + 1) * CHUNK)
        length = (c + 1) * CHUNK
        scores = mm(k[:length], q[:, cols])
        scores = jnp.where(visible_of(start[...], c, length), scores, NEG)
        peak = jnp.max(scores, 0, keepdims=True)
        shifted = jnp.exp(scores - peak)
        probs = shifted * (1.0 / jnp.sum(shifted, 0, keepdims=True))
        probs_b = probs.astype(BF)
        out = mm(v_t[:, :length], probs_b)
        dq = backward_chunk(q, k_t, v, d_ctx, probs, probs_b, out, cols, length, dk, dv)
        for i in range(CHUNK // BLK):
            b = c * (CHUNK // BLK) + i
            for t in range(2):
                send[b, t, 0:HEAD] = out[:, i * BLK : (i + 1) * BLK].astype(BF)
                send[b, t, HEAD : 2 * HEAD] = dq[:, i * BLK : (i + 1) * BLK].astype(BF)
    put_kv(send, dk, dv, 2 * HEAD)


def backward_chunk(q, k_t, v, d_ctx, probs, probs_b, out, cols, length, dk, dv):
    d_out = d_ctx[:, cols]
    d_probs = mm(v[:length], d_out)
    delta = jnp.sum(d_out.astype(F32) * out, 0, keepdims=True)
    d_scores = (probs * (d_probs - delta)).astype(BF)
    dk[:, :length] += mm(q[:, cols], d_scores, 1, 1)
    dv[:, :length] += mm(d_out, probs_b, 1, 1)
    return mm(k_t[:, :length], d_scores) * (HEAD**-0.5)


def put_kv(send, dk, dv, row):
    for b in range(8):
        for t in range(2):
            send[b, t, row : row + HEAD] = dk[:, b * BLK : (b + 1) * BLK].astype(BF)
            send[b, t, row + HEAD : row + 2 * HEAD] = dv[:, b * BLK : (b + 1) * BLK].astype(BF)


def attend_back_body(recv, recv_d, start, lse, ctx, _, send, dk, dv):
    ride = recv_d[0, 64:192].astype(F32)
    for i in range(1, 8):
        ride = ride + recv_d[i, 64:192].astype(F32)
    ride = ride.astype(BF)
    for b in range(8):
        for t in range(2):
            send[b, t, 192:320] = ride
    q = load_rows(recv, 0, HEAD)
    k_t = load_rows(recv, HEAD, 2 * HEAD)
    v_t = load_rows(recv, 2 * HEAD, 3 * HEAD)
    d_ctx = load_rows(recv_d, 0, HEAD)
    k = k_t.T
    v = v_t.T
    dk[...] = jnp.zeros_like(dk)
    dv[...] = jnp.zeros_like(dv)
    for c in range(4):
        cols = slice(c * CHUNK, (c + 1) * CHUNK)
        length = (c + 1) * CHUNK
        scores = mm(k[:length], q[:, cols])
        scores = jnp.where(visible_of(start[...], c, length), scores, NEG)
        probs = jnp.exp(scores - lse[:, cols])
        probs_b = probs.astype(BF)
        dq = backward_chunk(q, k_t, v, d_ctx, probs, probs_b, ctx[:, cols], cols, length, dk, dv)
        for i in range(CHUNK // BLK):
            for t in range(2):
                send[c * (CHUNK // BLK) + i, t, 0:HEAD] = dq[:, i * BLK : (i + 1) * BLK].astype(BF)
    put_kv(send, dk, dv, HEAD)


def gather_ctx(recv, s):
    return jnp.concatenate([recv[s * 4 + h, t, 0:HEAD, :] for t in range(2) for h in range(4)], 0)


def ordered(t, own, other):
    return jnp.where(t == 0, own, other), jnp.where(t == 0, other, own)


def out_other(others):
    halves = [
        jnp.concatenate([others[3, 64 * p + 32 * c : 64 * p + 32 * (c + 1), :] for p in range(8)], 0)
        for c in range(2)
    ]
    return jnp.concatenate(halves, 1)


def branch_of(t, recv, w_own, w_other):
    first, second = ordered(t, w_own, w_other)
    w = jnp.concatenate([first, second], 0)
    rows = []
    for s in range(2):
        rows.append(mm(gather_ctx(recv, s).T, w))
    return jnp.concatenate(rows, 0)


def middle_body(
    at, x, pair, pair_other, recv, w_out_own, out_bias, gain, bias,
    w_qkv, b_qkv, w_up, b_up, w_down, w_out, cot, cs,
    stream, send, grads, parts, d_b_up, d_sum, act, slope,
):
    branch = pair[0:256].astype(F32) + pair_other[0:256].astype(F32)
    branch = branch + branch_of(at[1], recv, w_out_own[...], pair_other[256:512])
    out = x[...] + branch + out_bias[0, 0:1] + out_bias[0, 1:2]
    stream[...] = out
    normed, _ = norm_rows(out)
    attn_in = (normed * gain[1, 0:1] + bias[1, 0:1]).astype(BF)
    mlp_in = (normed * gain[1, 1:2] + bias[1, 1:2]).astype(BF)
    send_qkv(send, attn_in, w_qkv, b_qkv, 1, cs)
    g_b = cot[...].astype(BF)
    d_ctx = mm(w_out[...], g_b, 1, 1)
    for s in range(2):
        for h in range(4):
            send[s * 4 + h, 3 * HEAD : 4 * HEAD, :] = d_ctx[
                h * HEAD : (h + 1) * HEAD, s * BLK : (s + 1) * BLK
            ].astype(BF)
    d_sum[...] = jnp.sum(cot[...], 0, keepdims=True)
    parts[0:256] = feed_forward(mlp_in, w_up, b_up, 1, w_down, act, slope).astype(BF)
    parts[256:512] = feed_back(
        g_b, act, slope, mlp_in, w_up, w_down, pack_up(grads, 0), pack_down(grads, 256), d_b_up
    ).astype(BF)


def norm_back(
    t, x, g, d_mlp_in, recv, row, w_own, others, cs, gain, bias, layer, d_qkv, d_b_qkv, d_norm
):
    normed, inv = norm_rows(x)
    attn_in = (normed * gain[layer, 0:1] + bias[layer, 0:1]).astype(BF)
    attn_t = attn_in.T
    d_attn_t = None
    for e in range(3):
        halves = []
        for tt in range(2):
            blocks = []
            for h in range(4):
                pieces = []
                for s in range(2):
                    lo = row + e * HEAD
                    u = recv[s * 4 + h, tt, lo : lo + HEAD, :]
                    if e < 2:
                        u = turn_back(u.astype(F32), cs[s, 0], cs[s, 1]).astype(BF)
                    pieces.append(u)
                blocks.append(jnp.concatenate(pieces, 1))
            halves.append(jnp.concatenate(blocks, 0))
        first, second = ordered(t, w_own[e], others[e])
        term = mm(first, halves[0]) + mm(second, halves[1])
        d_attn_t = term if d_attn_t is None else d_attn_t + term
        own = jnp.where(t == 0, halves[0], halves[1])
        d_qkv(e, mm(attn_t, own, 1, 1))
        d_b_qkv[e : e + 1] = mm(jnp.ones((8, own.shape[1]), BF), own, 1, 1)[0:1]
    d_attn_in = d_attn_t.T
    d_norm[0:1] = jnp.sum(d_attn_in * normed, 0, keepdims=True)
    d_norm[1:2] = jnp.sum(d_mlp_in * normed, 0, keepdims=True)
    d_norm[2:3] = jnp.sum(d_attn_in, 0, keepdims=True)
    d_norm[3:4] = jnp.sum(d_mlp_in, 0, keepdims=True)
    d_normed = d_attn_in * gain[layer, 0:1] + d_mlp_in * gain[layer, 1:2]
    return g + inv * (
        d_normed
        - jnp.mean(d_normed, -1, keepdims=True)
        - normed * jnp.mean(d_normed * normed, -1, keepdims=True)
    )


def turn_point_body(
    at, stream, parts, parts_other, recv, w_out, w_qkv, others, out_bias,
    gain, bias, cot, cs, x, act, slope, w_up, w_down, w_out_first, recv_first, sums_a,
    block_out, g_out, send, grads, part, d_b_up, d_b_qkv, d_norm, d_sum,
):
    t = at[1]
    branch = parts[0:256].astype(F32) + parts_other[0:256].astype(F32)
    branch = branch + branch_of(t, recv, w_out[...], out_other(others))
    block_out[...] = stream[...] + branch + out_bias[1, 0:1] + out_bias[1, 1:2]
    d_mlp_in = parts[256:512].astype(F32) + parts_other[256:512].astype(F32)
    g = norm_back(
        t, stream[...], cot[...], d_mlp_in, recv, HEAD, w_qkv, others, cs, gain, bias, 1,
        pack_qkv(grads, 0), d_b_qkv, d_norm,
    )
    g_out[...] = g
    g_b = g.astype(BF)
    d_sum[...] = jnp.sum(g, 0, keepdims=True)
    d_ctx = mm(w_out_first[...], g_b, 1, 1)
    for s in range(2):
        for h in range(4):
            send[s * 4 + h, 0:HEAD] = d_ctx[
                h * HEAD : (h + 1) * HEAD, s * BLK : (s + 1) * BLK
            ].astype(BF)
    for q in range(8):
        for c in range(2):
            send[q, 64 + 64 * c : 128 + 64 * c] = sums_a[
                64 * q : 64 * (q + 1), BLK * c : BLK * (c + 1)
            ]
    pack_out(grads, 704, own_ctx(t, recv), cot[...].astype(BF))
    pack_out(grads, 768, own_ctx(t, recv_first), g_b)
    normed, _ = norm_rows(x[...])
    mlp_in = (normed * gain[0, 1:2] + bias[0, 1:2]).astype(BF)
    part[...] = feed_back(
        g_b, act, slope, mlp_in, w_up, w_down, pack_up(grads, 192), pack_down(grads, 448), d_b_up
    ).astype(BF)


def last_body(
    at, x, g, part, part_other, recv, w_qkv, others, cs, gain, bias,
    d_b_up0, d_b_up1, d_b_qkv1, d_norm1, d_sum0, d_sum1,
    in_grad, grads, sums_a, d_b_qkv0, d_norm0,
):
    d_mlp_in = part[...].astype(F32) + part_other[...].astype(F32)
    in_grad[...] = norm_back(
        at[1], x[...], g[...], d_mlp_in, recv, 0, w_qkv, others, cs, gain, bias, 0,
        pack_qkv(grads, 0), d_b_qkv0, d_norm0,
    )
    for q in range(8):
        both_planes = recv[q, :, 192:320]
        block = jnp.where(at[1] == 0, both_planes[0], both_planes[1])
        for c in range(2):
            sums_a[64 * q : 64 * (q + 1), BLK * c : BLK * (c + 1)] = block[64 * c : 64 * (c + 1)]

    def lanes(ref, row, count):
        return [ref[row : row + 1, 256 * c : 256 * (c + 1)] for c in range(count)]

    def norms(ref):
        return [v for r in range(4) for v in lanes(ref, r, 2)]

    rows = [
        lanes(d_b_up0, 0, 4)
        + lanes(d_b_up1, 0, 4)
        + [v for e in range(3) for ref in (d_b_qkv0, d_b_qkv1) for v in lanes(ref, e, 1)],
        lanes(d_sum0, 0, 2) + lanes(d_sum1, 0, 2) + norms(d_norm0),
        norms(d_norm1),
    ]
    for p in range(8):
        have = rows[p] if p < len(rows) else []
        fill = [jnp.zeros((16 - len(have), 256), F32)]
        grads[p, 192:208, :] = jnp.concatenate(have + fill, 0).astype(BF)


def chunk_body(at, w_qkv, w_out, out):
    for layer in range(2):
        for e in range(3):
            out[layer, e] = w_qkv[layer, e]
        out[layer, 3, 0:32] = w_out[layer, :, 0:256]
        out[layer, 3, 32:64] = w_out[layer, :, 256:512]


def chunk_of(at, wq, w_out):
    return pl.pallas_call(
        chunk_body,
        out_shape=jax.ShapeDtypeStruct((2, 4, 64, 256), BF),
        grid_spec=pltpu.PrefetchScalarGridSpec(
            num_scalar_prefetch=1,
            grid=(1,),
            in_specs=[
                pl.BlockSpec((2, 3, 64, 256), lambda i, at: (0, 0, at[2], 0)),
                pl.BlockSpec((2, 32, 512), lambda i, at: (0, at[2], 0)),
            ],
            out_specs=pl.BlockSpec((2, 4, 64, 256), lambda i, at: (0, 0, 0, 0)),
        ),
        compiler_params=pltpu.CompilerParams(vmem_limit_bytes=40 * 1024 * 1024),
        name="chunk",
    )(at, far(wq), far(w_out))


def hand_on_body(value, _, out):
    out[...] = value[...]


def mix_body(got, early, first, out, first_out):
    total = got[0].astype(F32)
    for i in range(1, 8):
        total = total + got[i].astype(F32)
    for q in range(8):
        tiny = total[192 + 8 * q : 200 + 8 * q] if q < 2 else jnp.zeros((8, 256), F32)
        mine = [early[104 * q : 104 * (q + 1)].astype(F32), total[24 * q : 24 * (q + 1)], tiny]
        out[q] = jnp.concatenate(mine, 0).astype(BF)
    first_out[...] = first[...]


def sum_body(got, out):
    total = got[0].astype(F32)
    for i in range(1, 8):
        total = total + got[i].astype(F32)
    for q in range(8):
        out[q] = total.astype(BF)


def unpack_first_body(first, g_up, g_down):
    for k in range(2):
        for c in range(4):
            cols = slice(256 * c, 256 * (c + 1))
            g_up[0, 64 * k : 64 * (k + 1), cols] = first[k, 64 * c : 64 * (c + 1)].astype(F32)
        for c in range(2):
            rows = first[k, 256 + 128 * c : 256 + 128 * (c + 1)]
            cols = slice(256 * c, 256 * (c + 1))
            g_down[0, 128 * k : 128 * (k + 1), cols] = rows.astype(F32)


def unpack_rest_body(rest, _, __, g_up, g_down, g_qkv, g_out, g_b_up, g_b_qkv, g_sum, g_gain, g_bias):
    p = pl.program_id(0)
    for k in range(2):
        for q in range(8):
            block = rest[k, q].astype(F32)
            for i in range(16):
                value = block[8 * i : 8 * (i + 1)]
                row = 104 * q + 8 * i
                if i >= 13:
                    row = 24 * q + 8 * (i - 13)
                    r = 64 * k + row % 64
                    g_qkv[0, row // 64, r : r + 8] = value
                elif row < 192:
                    r = 64 * k + row % 64
                    g_qkv[1, row // 64, r : r + 8] = value
                elif row < 448:
                    c, r = divmod(row - 192, 64)
                    r += 64 * k
                    g_up[0, r : r + 8, 256 * c : 256 * (c + 1)] = value
                elif row < 704:
                    c, r = divmod(row - 448, 128)
                    r += 128 * k
                    g_down[0, r : r + 8, 256 * c : 256 * (c + 1)] = value
                else:
                    c, r = divmod((row - 704) % 64, 32)
                    r += 32 * k
                    g_out[1 - (row - 704) // 64, r : r + 8, 256 * c : 256 * (c + 1)] = value

    tiny = [jnp.concatenate([rest[k, q].astype(F32)[128:136] for q in range(2)], 0) for k in range(2)]

    @pl.when(p == 0)
    def _():
        for layer in range(2):
            for c in range(4):
                r = 4 * layer + c
                g_b_up[layer : layer + 1, 256 * c : 256 * (c + 1)] = tiny[0][r : r + 1]
        for e in range(3):
            for layer in range(2):
                r = 8 + 2 * e + layer
                g_b_qkv[e, layer : layer + 1, :] = tiny[0][r : r + 1]
        for layer in range(2):
            for c in range(2):
                r = 2 * layer + c
                for which in range(2):
                    g_sum[layer, which : which + 1, 256 * c : 256 * (c + 1)] = tiny[1][r : r + 1]

    def norms(layer, rows, base):
        for which in range(2):
            for c in range(2):
                cols = slice(256 * c, 256 * (c + 1))
                r = base + 2 * which + c
                g_gain[layer, which : which + 1, cols] = rows[r : r + 1]
                g_bias[layer, which : which + 1, cols] = rows[r + 4 : r + 5]

    @pl.when(p == 0)
    def _():
        norms(0, tiny[1], 4)

    @pl.when(p == 1)
    def _():
        norms(1, tiny[0], 0)


UP = (2, 512, 1024)
DOWN = (2, 1024, 512)


def unpack(first, rest):
    def place(layer):
        return [
            pl.BlockSpec((1, 128, 1024), lambda p: (layer, p, 0)),
            pl.BlockSpec((1, 256, 512), lambda p: (layer, p, 0)),
        ]

    params = pltpu.CompilerParams(vmem_limit_bytes=40 * 1024 * 1024)
    g_up, g_down = pl.pallas_call(
        unpack_first_body,
        grid=(4,),
        out_shape=[pltpu.HBM(UP, F32), pltpu.HBM(DOWN, F32)],
        in_specs=[pl.BlockSpec((2, 512, 256), lambda p: (p, 0, 0))],
        out_specs=place(1),
        compiler_params=params,
        name="unpack_first",
    )(far(first))
    outs = [
        ((2, 3, 512, 256), pl.BlockSpec((2, 3, 128, 256), lambda p: (0, 0, p, 0))),
        ((2, 256, 512), pl.BlockSpec((2, 64, 512), lambda p: (0, p, 0))),
        ((2, 1024), whole((2, 1024))),
        ((3, 2, 256), whole((3, 2, 256))),
        ((2, 2, 512), whole((2, 2, 512))),
        ((2, 2, 512), whole((2, 2, 512))),
        ((2, 2, 512), whole((2, 2, 512))),
    ]
    return pl.pallas_call(
        unpack_rest_body,
        grid=(4,),
        out_shape=[pltpu.HBM(shape, F32) for shape in [UP, DOWN] + [o[0] for o in outs]],
        in_specs=[
            pl.BlockSpec((2, 8, 136, 256), lambda p: (p, 0, 0, 0)),
            pl.BlockSpec(memory_space=pl.ANY),
            pl.BlockSpec(memory_space=pl.ANY),
        ],
        out_specs=place(0) + [spec for _, spec in outs],
        input_output_aliases={1: 0, 2: 1},
        compiler_params=params,
        name="unpack_rest",
    )(far(rest), far(g_up), far(g_down))


def swap(value):
    return lax.ppermute(value, "tensor", [(0, 1), (1, 0)])


def exchange(value, axes):
    return lax.all_to_all(value, axes, 0, 0)


def both(value):
    flat = value.reshape((16,) + value.shape[2:])
    return exchange(flat, ("context", "tensor")).reshape(value.shape)


def shards(
    tokens_in, cotangent, positions, w_qkv, b_qkv, w_out, w_up, b_up, w_down, out_bias, ln_gain, ln_bias
):
    rows, width = 256, 512
    x = tokens_in.reshape(rows, width)
    cot = cotangent.reshape(rows, width)
    wq = jnp.transpose(w_qkv, (0, 2, 1, 3))
    bq = jnp.transpose(b_qkv, (1, 0, 2))
    at = jnp.stack(
        [lax.axis_index("context"), lax.axis_index("tensor"), lax.axis_index("dp")]
    ).astype(jnp.int32)
    freqs = jnp.asarray(FREQS).reshape(HALF, 1)
    chunk = swap(chunk_of(at, wq, w_out))
    send, pair, act, slope, cs = call(
        first_body,
        [
            pltpu.VMEM((8, 208, BLK), BF),
            ((2 * rows, width), BF),
            pltpu.HBM((rows, 1024), BF),
            pltpu.HBM((rows, 1024), BF),
            ((2, 2, HALF, BLK), F32),
        ],
        (
            at, positions, freqs, Far(x), ln_gain, ln_bias, Layer(wq, 0), bq, Layer(w_up, 0), b_up,
            Layer(w_down, 0), Layer(w_out, 0),
        ),
        "norm_qkv_feed",
        smem_first=True,
    )
    pair_other = swap(pair)
    (chunk,) = call(
        hand_on_body, [pltpu.HBM(chunk.shape, BF)], (chunk, After(send)), "hand_on"
    )
    others = lax.all_gather(chunk, "dp", axis=2, tiled=True)
    recv = exchange(send, "context")
    ctx_send, lse, ctx, start = call(
        attend_body,
        [((8, 2, HEAD, BLK), BF), ((1, 1024), F32), pltpu.HBM((HEAD, 1024), F32), ((1, 1024), jnp.int32)],
        (recv,),
        "attend",
    )
    recv_ctx = both(ctx_send)
    x_n, w_out0_n, wq1_n, w_up1_n, w_down1_n, w_out1_n, cot_n = bring(
        [x, (w_out, 0), (wq, 1), (w_up, 1), (w_down, 1), (w_out, 1), cot], ctx_send, "bring_middle"
    )
    stream, send, grads_a, parts, d_b_up1, d_sum1 = call(
        middle_body,
        [
            pltpu.HBM((rows, width), F32),
            ((8, 256, BLK), BF),
            pltpu.HBM((8, 512, 256), BF),
            ((2 * rows, width), BF),
            ((1, 1024), F32),
            ((1, width), F32),
        ],
        (
            at, x_n, pair, pair_other, recv_ctx, w_out0_n, out_bias, ln_gain, ln_bias,
            wq1_n, bq, w_up1_n, b_up, w_down1_n, w_out1_n, cot_n, cs,
        ),
        "middle",
        scratch=[pltpu.VMEM((rows, 1024), BF), pltpu.VMEM((rows, 1024), BF)],
        smem_first=True,
    )
    sums_a = lax.psum_scatter(grads_a, "dp", scatter_dimension=0)
    parts_other = swap(parts)
    recv_both = exchange(send, "context")
    (both_send,) = call(
        attend_both_body,
        [((8, 2, 256, BLK), BF)],
        (recv_both, start, After(parts_other)),
        "attend_both",
        scratch=[pltpu.VMEM((HEAD, 1024), F32), pltpu.VMEM((HEAD, 1024), F32)],
    )
    recv_grad = both(both_send)
    near = bring(
        [
            (w_out, 1), (wq, 1), (others, 1), cot, x, act, slope, (w_up, 0), (w_down, 0), (w_out, 0),
            stream,
        ],
        both_send,
        "bring_turn_point",
    )
    block_out, g, send, grads_b, part_g, d_b_up0, d_b_qkv1, d_norm1, d_sum0 = call(
        turn_point_body,
        [
            pltpu.HBM((rows, width), F32),
            pltpu.HBM((rows, width), F32),
            pltpu.VMEM((8, 192, BLK), BF),
            pltpu.HBM((8, 832, 256), BF),
            ((rows, width), BF),
            ((1, 1024), F32),
            ((3, 256), F32),
            ((4, width), F32),
            ((1, width), F32),
        ],
        (
            at, near[10], parts, parts_other, recv_grad, near[0], near[1], near[2], out_bias, ln_gain,
            ln_bias, near[3], cs, near[4], near[5], near[6], near[7], near[8], near[9], recv_ctx,
            Far(sums_a),
        ),
        "turn_point",
        smem_first=True,
    )
    sums_b = lax.psum_scatter(grads_b, "dp", scatter_dimension=0)
    part_g_other = swap(part_g)
    recv_d = exchange(send, "context")
    (back_send,) = call(
        attend_back_body,
        [((8, 2, 320, BLK), BF)],
        (recv, recv_d, start, lse, ctx, After(part_g_other)),
        "attend_back",
        scratch=[pltpu.VMEM((HEAD, 1024), F32), pltpu.VMEM((HEAD, 1024), F32)],
    )
    recv_grad0 = both(back_send)
    x_n, g_n, wq0_n, others0_n = bring([x, g, (wq, 0), (others, 0)], back_send, "bring_last")
    in_grad, grads_c, sums_a, _, _ = call(
        last_body,
        [
            pltpu.HBM((rows, width), F32),
            ((8, 208, 256), BF),
            pltpu.HBM((512, 256), BF),
            ((3, 256), F32),
            ((4, width), F32),
        ],
        (
            at, x_n, g_n, part_g, part_g_other, recv_grad0, wq0_n, others0_n, cs,
            ln_gain, ln_bias, d_b_up0, d_b_up1, d_b_qkv1, d_norm1, d_sum0, d_sum1,
        ),
        "last",
        smem_first=True,
    )
    mixed, sums_a = call(
        mix_body,
        [((8, 136, 256), BF), pltpu.HBM((512, 256), BF)],
        (exchange(grads_c, "dp"), Far(sums_b), Far(sums_a)),
        "mix",
    )
    full_a = lax.all_gather(sums_a, "dp")
    (summed,) = call(sum_body, [((8, 136, 256), BF)], (exchange(mixed, "context"),), "sum")
    full_bc = lax.all_gather(exchange(summed, "context"), "dp")
    g_up, g_down, g_qkv, g_out, g_b_up, g_b_qkv, g_sum, g_gain, g_bias = unpack(full_a, full_bc)
    return (
        block_out.reshape(tokens_in.shape),
        in_grad.reshape(tokens_in.shape),
        jnp.transpose(g_qkv, (0, 2, 1, 3)),
        jnp.transpose(g_b_qkv, (1, 0, 2)),
        g_out,
        g_up,
        g_b_up,
        g_down,
        g_sum,
        g_gain,
        g_bias,
    )


def solution(mesh):
    return jax.shard_map(
        shards,
        mesh=mesh,
        in_specs=(
            P("dp", "context", None),
            P("dp", "context", None),
            P("dp", "context"),
            P(None, None, None, "tensor"),
            P(None, None, "tensor"),
            P(None, "tensor", None),
            P(None, None, "tensor"),
            P(None, "tensor"),
            P(None, "tensor", None),
            P(),
            P(),
            P(),
        ),
        out_specs=(
            P("dp", "context", None),
            P("dp", "context", None),
            P(None, None, None, "tensor"),
            P(None, None, "tensor"),
            P(None, "tensor", None),
            P(None, None, "tensor"),
            P(None, "tensor"),
            P(None, "tensor", None),
            P(),
            P(),
            P(),
        ),
        check_vma=False,
    )
```

```python
from functools import partial

import numpy as np

import jax
import jax.numpy as jnp
from jax import lax
from jax.experimental import pallas as pl
from jax.experimental.pallas import tpu as pltpu
from jax.sharding import PartitionSpec as P

EPS = 1e-05
HALF = 8
HEAD = 64
BLK = 128
CHUNK = 256
NEG = -1e30
BF = jnp.bfloat16
F32 = jnp.float32

FREQS = (10000.0 ** (-np.arange(HALF, dtype=np.float64) * 2.0 / 16.0)).astype(np.float32)


def mm(a, b, ca=1, cb=0):
    return lax.dot_general(a, b, (((ca,), (cb,)), ((), ())), preferred_element_type=F32)


class After:
    def __init__(self, array):
        self.array = array

    def spec(self):
        return pl.BlockSpec(memory_space=pl.ANY)


class Layer:
    def __init__(self, array, index):
        self.array, self.index = far(array), index

    def spec(self):
        rest = self.array.shape[1:]
        place = (self.index,) + (0,) * len(rest)
        return pl.BlockSpec((None,) + rest, lambda i: place)


class Far:
    def __init__(self, array):
        self.array = far(array)

    def spec(self):
        return whole(self.array.shape)


Kept = type(pltpu.HBM((8, 128), F32))


def far(array):
    return pltpu.with_memory_space_constraint(array, pltpu.HBM)


def whole(shape):
    return pl.BlockSpec(shape, lambda i: (0,) * len(shape))


def call(body, out_shape, args, name, scratch=(), smem_first=False):
    specs = [
        a.spec() if isinstance(a, (Layer, Far, After)) else whole(a.shape) for a in args
    ]
    args = [a.array if isinstance(a, (Layer, Far, After)) else a for a in args]
    if smem_first:
        specs[0] = pl.BlockSpec(memory_space=pltpu.SMEM)
    return pl.pallas_call(
        body,
        grid=(1,),
        out_shape=[o if isinstance(o, Kept) else jax.ShapeDtypeStruct(*o) for o in out_shape],
        in_specs=specs,
        out_specs=[whole(o.shape if isinstance(o, Kept) else o[0]) for o in out_shape],
        scratch_shapes=list(scratch),
        compiler_params=pltpu.CompilerParams(vmem_limit_bytes=40 * 1024 * 1024),
        name=name,
    )(*args)


def norm_rows(x):
    mean = jnp.mean(x, -1, keepdims=True)
    cen = x - mean
    inv = lax.rsqrt(jnp.mean(cen * cen, -1, keepdims=True) + EPS)
    return cen * inv, inv


def turn(t, cos, sin):
    a, b = t[:HALF], t[HALF : 2 * HALF]
    return jnp.concatenate([a * cos - b * sin, b * cos + a * sin, t[2 * HALF :]], 0)


def turn_back(u, cos, sin):
    a, b = u[:HALF], u[HALF : 2 * HALF]
    return jnp.concatenate([a * cos + b * sin, b * cos - a * sin, u[2 * HALF :]], 0)


def send_qkv(send, attn_in, w_qkv, b_qkv, layer, cs):
    for e in range(3):
        turned = (mm(attn_in, w_qkv[e]) + b_qkv[e, layer : layer + 1]).T
        for s in range(2):
            cos, sin = cs[s, 0], cs[s, 1]
            for h in range(4):
                j = s * 4 + h
                part = turned[h * HEAD : (h + 1) * HEAD, s * BLK : (s + 1) * BLK]
                if e < 2:
                    part = turn(part, cos, sin)
                if e == 0:
                    part = part * (HEAD**-0.5)
                send[j, e * HEAD : (e + 1) * HEAD, :] = part.astype(BF)


def feed_forward(mlp_in, w_up, b_up, layer, w_down, act, slope):
    width = w_up.shape[1]
    total = None
    for c in range(0, width, 256):
        cols = slice(c, c + 256)
        pre = mm(mlp_in, w_up[:, cols]) + b_up[layer : layer + 1, cols]
        cdf = 0.5 + 0.5 * lax.erf(pre * np.float32(0.7071067811865476))
        a = (pre * cdf).astype(BF)
        act[:, cols] = a
        tail = pre * (jnp.exp(-0.5 * pre * pre) * np.float32(0.3989422804014327))
        slope[:, cols] = (cdf + tail).astype(BF)
        term = mm(a, w_down[cols, :])
        total = term if total is None else total + term
    return total


def feed_back(g_b, act, slope, mlp_in, w_up, w_down, d_up, d_down, d_b_up):
    width = w_up.shape[1]
    total = None
    mlp_t = mlp_in.T
    for c in range(0, width, 256):
        cols = slice(c, c + 256)
        d_act = mm(g_b, w_down[cols, :], 1, 1)
        d_pre = d_act * slope[:, cols].astype(F32)
        d_pre_b = d_pre.astype(BF)
        d_b_up[:, cols] = jnp.sum(d_pre_b.astype(F32), 0, keepdims=True)
        d_up(c // 256, mm(mlp_t, d_pre_b))
        d_down(c, mm(act[:, cols].T, g_b))
        term = mm(d_pre_b, w_up[:, cols], 1, 1)
        total = term if total is None else total + term
    return total


def pack_up(out, row):
    def put(c, value):
        for p in range(8):
            out[p, row + 64 * c : row + 64 * (c + 1), :] = value[64 * p : 64 * (p + 1)].astype(BF)

    return put


def pack_down(out, row):
    def put(c, value):
        for half in range(2):
            for k in range(2):
                out[c // 128 + k, row + 128 * half : row + 128 * (half + 1), :] = value[
                    128 * k : 128 * (k + 1), 256 * half : 256 * (half + 1)
                ].astype(BF)

    return put


def pack_qkv(out, row):
    def put(e, value):
        for p in range(8):
            out[p, row + 64 * e : row + 64 * (e + 1), :] = value[64 * p : 64 * (p + 1)].astype(BF)

    return put


def own_ctx(t, recv):
    full = jnp.concatenate([gather_ctx(recv, s) for s in range(2)], 1)
    return jnp.where(t == 0, full[0:256], full[256:512])


def pack_out(out, row, ctx, upstream):
    value = mm(ctx, upstream)
    for p in range(8):
        for half in range(2):
            out[p, row + 32 * half : row + 32 * (half + 1), :] = value[
                32 * p : 32 * (p + 1), 256 * half : 256 * (half + 1)
            ].astype(BF)


def first_body(at, pos, freqs, x, gain, bias, w_qkv, b_qkv, send, cs):
    for s in range(2):
        p = pos[s : s + 1, :].astype(F32)
        angle = freqs[...] * p
        cs[s, 0] = jnp.cos(angle)
        cs[s, 1] = jnp.sin(angle)
    normed, _ = norm_rows(x[...])
    attn_in = (normed * gain[0, 0:1] + bias[0, 0:1]).astype(BF)
    send_qkv(send, attn_in, w_qkv, b_qkv, 0, cs)
    row = lax.broadcasted_iota(jnp.int32, (16, BLK), 0)
    token = at[0] * BLK + lax.broadcasted_iota(jnp.int32, (1, BLK), 1)
    for s in range(2):
        start = jnp.maximum(token - pos[s : s + 1, :], 0)
        high = (start // 8).astype(F32)
        low = (start % 8).astype(F32)
        block = jnp.where(row == 0, high, jnp.where(row == 1, low, 0.0)).astype(BF)
        for h in range(4):
            send[s * 4 + h, 3 * HEAD : 3 * HEAD + 16, :] = block


def feed_body(x, gain, bias, w_up, b_up, w_down, w_out, _, pair, act, slope):
    normed, _ = norm_rows(x[...])
    mlp_in = (normed * gain[0, 1:2] + bias[0, 1:2]).astype(BF)
    pair[256:512] = w_out[...]
    pair[0:256] = feed_forward(mlp_in, w_up, b_up, 0, w_down, act, slope).astype(BF)


def load_rows(recv, lo, hi):
    return jnp.concatenate([recv[i, lo:hi, :] for i in range(8)], 1)


def starts_of(recv):
    rows = load_rows(recv, 3 * HEAD, 3 * HEAD + 16).astype(F32)
    return rows[0:1] * 8.0 + rows[1:2]


def masked(scores, start, c, length):
    own = start[:, c * CHUNK : (c + 1) * CHUNK]
    past = length - CHUNK
    key = lax.broadcasted_iota(jnp.int32, (CHUNK, CHUNK), 0)
    query = lax.broadcasted_iota(jnp.int32, (CHUNK, CHUNK), 1)
    near = jnp.where((key <= query) & (key + past >= own), scores[past:], NEG)
    if past == 0:
        return near
    key = lax.broadcasted_iota(jnp.int32, (past, CHUNK), 0)
    return jnp.concatenate([jnp.where(key >= own, scores[:past], NEG), near], 0)


def attend_body(recv, send, lse, ctx, start_out):
    q = load_rows(recv, 0, HEAD)
    k_t = load_rows(recv, HEAD, 2 * HEAD)
    v_t = load_rows(recv, 2 * HEAD, 3 * HEAD)
    k = k_t.T
    start = starts_of(recv).astype(jnp.int32)
    start_out[...] = start
    for c in range(4):
        cols = slice(c * CHUNK, (c + 1) * CHUNK)
        length = (c + 1) * CHUNK
        scores = mm(k[:length], q[:, cols])
        scores = masked(scores, start, c, length)
        peak = jnp.max(scores, 0, keepdims=True)
        shifted = jnp.exp(scores - peak)
        total = jnp.sum(shifted, 0, keepdims=True)
        lse[:, cols] = peak + jnp.log(total)
        out = mm(v_t[:, :length], shifted.astype(BF)) / total
        ctx[:, cols] = out
        for i in range(CHUNK // BLK):
            block = out[:, i * BLK : (i + 1) * BLK].astype(BF)
            for t in range(2):
                send[c * (CHUNK // BLK) + i, t] = block


def attend_both_body(recv, start, _, send, dk, dv):
    q = load_rows(recv, 0, HEAD)
    k_t = load_rows(recv, HEAD, 2 * HEAD)
    v_t = load_rows(recv, 2 * HEAD, 3 * HEAD)
    d_ctx = load_rows(recv, 3 * HEAD, 4 * HEAD)
    k = k_t.T
    v = v_t.T
    dk[...] = jnp.zeros_like(dk)
    dv[...] = jnp.zeros_like(dv)
    for c in range(4):
        cols = slice(c * CHUNK, (c + 1) * CHUNK)
        length = (c + 1) * CHUNK
        scores = mm(k[:length], q[:, cols])
        scores = masked(scores, start[...], c, length)
        peak = jnp.max(scores, 0, keepdims=True)
        shifted = jnp.exp(scores - peak)
        probs = shifted * (1.0 / jnp.sum(shifted, 0, keepdims=True))
        probs_b = probs.astype(BF)
        out = mm(v_t[:, :length], probs_b)
        dq = backward_chunk(q, k_t, v, d_ctx, probs, probs_b, out, cols, length, dk, dv)
        for i in range(CHUNK // BLK):
            b = c * (CHUNK // BLK) + i
            for t in range(2):
                send[b, t, 0:HEAD] = out[:, i * BLK : (i + 1) * BLK].astype(BF)
                send[b, t, HEAD : 2 * HEAD] = dq[:, i * BLK : (i + 1) * BLK].astype(BF)
    put_kv(send, dk, dv, 2 * HEAD)


def backward_chunk(q, k_t, v, d_ctx, probs, probs_b, out, cols, length, dk, dv):
    d_out = d_ctx[:, cols]
    d_probs = mm(v[:length], d_out)
    delta = jnp.sum(d_out.astype(F32) * out, 0, keepdims=True)
    d_scores = (probs * (d_probs - delta)).astype(BF)
    dk[:, :length] += mm(q[:, cols], d_scores, 1, 1)
    dv[:, :length] += mm(d_out, probs_b, 1, 1)
    return mm(k_t[:, :length], d_scores) * (HEAD**-0.5)


def put_kv(send, dk, dv, row):
    for b in range(8):
        for t in range(2):
            send[b, t, row : row + HEAD] = dk[:, b * BLK : (b + 1) * BLK].astype(BF)
            send[b, t, row + HEAD : row + 2 * HEAD] = dv[:, b * BLK : (b + 1) * BLK].astype(BF)


def attend_back_body(recv, recv_d, start, lse, ctx, _, send, dk, dv):
    ride = recv_d[0, 64:192].astype(F32)
    for i in range(1, 8):
        ride = ride + recv_d[i, 64:192].astype(F32)
    ride = ride.astype(BF)
    for b in range(8):
        for t in range(2):
            send[b, t, 192:320] = ride
    q = load_rows(recv, 0, HEAD)
    k_t = load_rows(recv, HEAD, 2 * HEAD)
    v_t = load_rows(recv, 2 * HEAD, 3 * HEAD)
    d_ctx = load_rows(recv_d, 0, HEAD)
    k = k_t.T
    v = v_t.T
    dk[...] = jnp.zeros_like(dk)
    dv[...] = jnp.zeros_like(dv)
    for c in range(4):
        cols = slice(c * CHUNK, (c + 1) * CHUNK)
        length = (c + 1) * CHUNK
        scores = mm(k[:length], q[:, cols])
        scores = masked(scores, start[...], c, length)
        probs = jnp.exp(scores - lse[:, cols])
        probs_b = probs.astype(BF)
        dq = backward_chunk(q, k_t, v, d_ctx, probs, probs_b, ctx[:, cols], cols, length, dk, dv)
        for i in range(CHUNK // BLK):
            for t in range(2):
                send[c * (CHUNK // BLK) + i, t, 0:HEAD] = dq[:, i * BLK : (i + 1) * BLK].astype(BF)
    put_kv(send, dk, dv, HEAD)


def gather_ctx(recv, s):
    return jnp.concatenate([recv[s * 4 + h, t, 0:HEAD, :] for t in range(2) for h in range(4)], 0)


def ordered(t, own, other):
    return jnp.where(t == 0, own, other), jnp.where(t == 0, other, own)


def out_other(others):
    halves = [
        jnp.concatenate([others[3, 64 * p + 32 * c : 64 * p + 32 * (c + 1), :] for p in range(8)], 0)
        for c in range(2)
    ]
    return jnp.concatenate(halves, 1)


def branch_of(t, recv, w_own, w_other):
    first, second = ordered(t, w_own, w_other)
    w = jnp.concatenate([first, second], 0)
    rows = []
    for s in range(2):
        rows.append(mm(gather_ctx(recv, s).T, w))
    return jnp.concatenate(rows, 0)


def middle_body(
    at, x, pair, pair_other, recv, w_out_own, out_bias, gain, bias,
    w_qkv, b_qkv, w_up, b_up, w_down, w_out, cot, cs,
    stream, send, grads, parts, d_b_up, d_sum, act, slope,
):
    branch = pair[0:256].astype(F32) + pair_other[0:256].astype(F32)
    branch = branch + branch_of(at[1], recv, w_out_own[...], pair_other[256:512])
    out = x[...] + branch + out_bias[0, 0:1] + out_bias[0, 1:2]
    stream[...] = out
    normed, _ = norm_rows(out)
    attn_in = (normed * gain[1, 0:1] + bias[1, 0:1]).astype(BF)
    mlp_in = (normed * gain[1, 1:2] + bias[1, 1:2]).astype(BF)
    send_qkv(send, attn_in, w_qkv, b_qkv, 1, cs)
    g_b = cot[...].astype(BF)
    d_ctx = mm(w_out[...], g_b, 1, 1)
    for s in range(2):
        for h in range(4):
            send[s * 4 + h, 3 * HEAD : 4 * HEAD, :] = d_ctx[
                h * HEAD : (h + 1) * HEAD, s * BLK : (s + 1) * BLK
            ].astype(BF)
    d_sum[...] = jnp.sum(cot[...], 0, keepdims=True)
    parts[0:256] = feed_forward(mlp_in, w_up, b_up, 1, w_down, act, slope).astype(BF)
    parts[256:512] = feed_back(
        g_b, act, slope, mlp_in, w_up, w_down, pack_up(grads, 0), pack_down(grads, 256), d_b_up
    ).astype(BF)


def norm_back(
    t, x, g, d_mlp_in, recv, row, w_own, others, cs, gain, bias, layer, d_qkv, d_b_qkv, d_norm
):
    normed, inv = norm_rows(x)
    attn_in = (normed * gain[layer, 0:1] + bias[layer, 0:1]).astype(BF)
    attn_t = attn_in.T
    d_attn_t = None
    for e in range(3):
        halves = []
        for tt in range(2):
            blocks = []
            for h in range(4):
                pieces = []
                for s in range(2):
                    lo = row + e * HEAD
                    u = recv[s * 4 + h, tt, lo : lo + HEAD, :]
                    if e < 2:
                        u = turn_back(u.astype(F32), cs[s, 0], cs[s, 1]).astype(BF)
                    pieces.append(u)
                blocks.append(jnp.concatenate(pieces, 1))
            halves.append(jnp.concatenate(blocks, 0))
        first, second = ordered(t, w_own[e], others[e])
        term = mm(first, halves[0]) + mm(second, halves[1])
        d_attn_t = term if d_attn_t is None else d_attn_t + term
        own = jnp.where(t == 0, halves[0], halves[1])
        d_qkv(e, mm(attn_t, own, 1, 1))
        d_b_qkv[e : e + 1] = mm(jnp.ones((8, own.shape[1]), BF), own, 1, 1)[0:1]
    d_attn_in = d_attn_t.T
    d_norm[0:1] = jnp.sum(d_attn_in * normed, 0, keepdims=True)
    d_norm[1:2] = jnp.sum(d_mlp_in * normed, 0, keepdims=True)
    d_norm[2:3] = jnp.sum(d_attn_in, 0, keepdims=True)
    d_norm[3:4] = jnp.sum(d_mlp_in, 0, keepdims=True)
    d_normed = d_attn_in * gain[layer, 0:1] + d_mlp_in * gain[layer, 1:2]
    return g + inv * (
        d_normed
        - jnp.mean(d_normed, -1, keepdims=True)
        - normed * jnp.mean(d_normed * normed, -1, keepdims=True)
    )


def turn_point_body(
    at, stream, parts, parts_other, recv, w_out, w_qkv, others, out_bias,
    gain, bias, cot, cs, x, act, slope, w_up, w_down, w_out_first, recv_first, sums_a,
    block_out, g_out, send, grads, part, d_b_up, d_b_qkv, d_norm, d_sum,
):
    t = at[1]
    branch = parts[0:256].astype(F32) + parts_other[0:256].astype(F32)
    branch = branch + branch_of(t, recv, w_out[...], out_other(others))
    block_out[...] = stream[...] + branch + out_bias[1, 0:1] + out_bias[1, 1:2]
    d_mlp_in = parts[256:512].astype(F32) + parts_other[256:512].astype(F32)
    g = norm_back(
        t, stream[...], cot[...], d_mlp_in, recv, HEAD, w_qkv, others, cs, gain, bias, 1,
        pack_qkv(grads, 0), d_b_qkv, d_norm,
    )
    g_out[...] = g
    g_b = g.astype(BF)
    d_sum[...] = jnp.sum(g, 0, keepdims=True)
    d_ctx = mm(w_out_first[...], g_b, 1, 1)
    for s in range(2):
        for h in range(4):
            send[s * 4 + h, 0:HEAD] = d_ctx[
                h * HEAD : (h + 1) * HEAD, s * BLK : (s + 1) * BLK
            ].astype(BF)
    for q in range(8):
        for c in range(2):
            send[q, 64 + 64 * c : 128 + 64 * c] = sums_a[
                64 * q : 64 * (q + 1), BLK * c : BLK * (c + 1)
            ]
    pack_out(grads, 704, own_ctx(t, recv), cot[...].astype(BF))
    pack_out(grads, 768, own_ctx(t, recv_first), g_b)
    normed, _ = norm_rows(x[...])
    mlp_in = (normed * gain[0, 1:2] + bias[0, 1:2]).astype(BF)
    part[...] = feed_back(
        g_b, act, slope, mlp_in, w_up, w_down, pack_up(grads, 192), pack_down(grads, 448), d_b_up
    ).astype(BF)


def last_body(
    at, x, g, part, part_other, recv, w_qkv, others, cs, gain, bias,
    d_b_up0, d_b_up1, d_b_qkv1, d_norm1, d_sum0, d_sum1,
    in_grad, grads, sums_a, d_b_qkv0, d_norm0,
):
    d_mlp_in = part[...].astype(F32) + part_other[...].astype(F32)
    in_grad[...] = norm_back(
        at[1], x[...], g[...], d_mlp_in, recv, 0, w_qkv, others, cs, gain, bias, 0,
        pack_qkv(grads, 0), d_b_qkv0, d_norm0,
    )
    for q in range(8):
        both_planes = recv[q, :, 192:320]
        block = jnp.where(at[1] == 0, both_planes[0], both_planes[1])
        for c in range(2):
            sums_a[64 * q : 64 * (q + 1), BLK * c : BLK * (c + 1)] = block[64 * c : 64 * (c + 1)]

    def lanes(ref, row, count):
        return [ref[row : row + 1, 256 * c : 256 * (c + 1)] for c in range(count)]

    def norms(ref):
        return [v for r in range(4) for v in lanes(ref, r, 2)]

    rows = [
        lanes(d_b_up0, 0, 4)
        + lanes(d_b_up1, 0, 4)
        + [v for e in range(3) for ref in (d_b_qkv0, d_b_qkv1) for v in lanes(ref, e, 1)],
        lanes(d_sum0, 0, 2) + lanes(d_sum1, 0, 2) + norms(d_norm0),
        norms(d_norm1),
    ]
    for p in range(8):
        have = rows[p] if p < len(rows) else []
        fill = [jnp.zeros((16 - len(have), 256), F32)]
        grads[p, 192:208, :] = jnp.concatenate(have + fill, 0).astype(BF)


def chunk_body(at, w_qkv, w_out, out):
    for layer in range(2):
        for e in range(3):
            out[layer, e] = w_qkv[layer, e]
        out[layer, 3, 0:32] = w_out[layer, :, 0:256]
        out[layer, 3, 32:64] = w_out[layer, :, 256:512]


def chunk_of(at, wq, w_out):
    return pl.pallas_call(
        chunk_body,
        out_shape=jax.ShapeDtypeStruct((2, 4, 64, 256), BF),
        grid_spec=pltpu.PrefetchScalarGridSpec(
            num_scalar_prefetch=1,
            grid=(1,),
            in_specs=[
                pl.BlockSpec((2, 3, 64, 256), lambda i, at: (0, 0, at[2], 0)),
                pl.BlockSpec((2, 32, 512), lambda i, at: (0, at[2], 0)),
            ],
            out_specs=pl.BlockSpec((2, 4, 64, 256), lambda i, at: (0, 0, 0, 0)),
        ),
        compiler_params=pltpu.CompilerParams(vmem_limit_bytes=40 * 1024 * 1024),
        name="chunk",
    )(at, far(wq), far(w_out))


def hand_on_body(value, _, out):
    out[...] = value[...]


def mix_body(got, early, first, out, first_out):
    total = got[0].astype(F32)
    for i in range(1, 8):
        total = total + got[i].astype(F32)
    for q in range(8):
        tiny = total[192 + 8 * q : 200 + 8 * q] if q < 2 else jnp.zeros((8, 256), F32)
        mine = [early[104 * q : 104 * (q + 1)].astype(F32), total[24 * q : 24 * (q + 1)], tiny]
        out[q] = jnp.concatenate(mine, 0).astype(BF)
    first_out[...] = first[...]


def sum_body(got, out):
    total = got[0].astype(F32)
    for i in range(1, 8):
        total = total + got[i].astype(F32)
    for q in range(8):
        out[q] = total.astype(BF)


def unpack_first_body(first, g_up, g_down):
    for k in range(2):
        for c in range(4):
            cols = slice(256 * c, 256 * (c + 1))
            g_up[0, 64 * k : 64 * (k + 1), cols] = first[k, 64 * c : 64 * (c + 1)].astype(F32)
        for c in range(2):
            rows = first[k, 256 + 128 * c : 256 + 128 * (c + 1)]
            cols = slice(256 * c, 256 * (c + 1))
            g_down[0, 128 * k : 128 * (k + 1), cols] = rows.astype(F32)


def unpack_rest_body(rest, _, __, g_up, g_down, g_qkv, g_out, g_b_up, g_b_qkv, g_sum, g_gain, g_bias):
    p = pl.program_id(0)
    for k in range(2):
        for q in range(8):
            block = rest[k, q].astype(F32)
            for i in range(16):
                value = block[8 * i : 8 * (i + 1)]
                row = 104 * q + 8 * i
                if i >= 13:
                    row = 24 * q + 8 * (i - 13)
                    r = 64 * k + row % 64
                    g_qkv[0, row // 64, r : r + 8] = value
                elif row < 192:
                    r = 64 * k + row % 64
                    g_qkv[1, row // 64, r : r + 8] = value
                elif row < 448:
                    c, r = divmod(row - 192, 64)
                    r += 64 * k
                    g_up[0, r : r + 8, 256 * c : 256 * (c + 1)] = value
                elif row < 704:
                    c, r = divmod(row - 448, 128)
                    r += 128 * k
                    g_down[0, r : r + 8, 256 * c : 256 * (c + 1)] = value
                else:
                    c, r = divmod((row - 704) % 64, 32)
                    r += 32 * k
                    g_out[1 - (row - 704) // 64, r : r + 8, 256 * c : 256 * (c + 1)] = value

    tiny = [jnp.concatenate([rest[k, q].astype(F32)[128:136] for q in range(2)], 0) for k in range(2)]

    @pl.when(p == 0)
    def _():
        for layer in range(2):
            for c in range(4):
                r = 4 * layer + c
                g_b_up[layer : layer + 1, 256 * c : 256 * (c + 1)] = tiny[0][r : r + 1]
        for e in range(3):
            for layer in range(2):
                r = 8 + 2 * e + layer
                g_b_qkv[e, layer : layer + 1, :] = tiny[0][r : r + 1]
        for layer in range(2):
            for c in range(2):
                r = 2 * layer + c
                for which in range(2):
                    g_sum[layer, which : which + 1, 256 * c : 256 * (c + 1)] = tiny[1][r : r + 1]

    def norms(layer, rows, base):
        for which in range(2):
            for c in range(2):
                cols = slice(256 * c, 256 * (c + 1))
                r = base + 2 * which + c
                g_gain[layer, which : which + 1, cols] = rows[r : r + 1]
                g_bias[layer, which : which + 1, cols] = rows[r + 4 : r + 5]

    @pl.when(p == 0)
    def _():
        norms(0, tiny[1], 4)

    @pl.when(p == 1)
    def _():
        norms(1, tiny[0], 0)


UP = (2, 512, 1024)
DOWN = (2, 1024, 512)


def unpack(first, rest):
    def place(layer):
        return [
            pl.BlockSpec((1, 128, 1024), lambda p: (layer, p, 0)),
            pl.BlockSpec((1, 256, 512), lambda p: (layer, p, 0)),
        ]

    params = pltpu.CompilerParams(vmem_limit_bytes=40 * 1024 * 1024)
    g_up, g_down = pl.pallas_call(
        unpack_first_body,
        grid=(4,),
        out_shape=[pltpu.HBM(UP, F32), pltpu.HBM(DOWN, F32)],
        in_specs=[pl.BlockSpec((2, 512, 256), lambda p: (p, 0, 0))],
        out_specs=place(1),
        compiler_params=params,
        name="unpack_first",
    )(far(first))
    outs = [
        ((2, 3, 512, 256), pl.BlockSpec((2, 3, 128, 256), lambda p: (0, 0, p, 0))),
        ((2, 256, 512), pl.BlockSpec((2, 64, 512), lambda p: (0, p, 0))),
        ((2, 1024), whole((2, 1024))),
        ((3, 2, 256), whole((3, 2, 256))),
        ((2, 2, 512), whole((2, 2, 512))),
        ((2, 2, 512), whole((2, 2, 512))),
        ((2, 2, 512), whole((2, 2, 512))),
    ]
    return pl.pallas_call(
        unpack_rest_body,
        grid=(4,),
        out_shape=[pltpu.HBM(shape, F32) for shape in [UP, DOWN] + [o[0] for o in outs]],
        in_specs=[
            pl.BlockSpec((2, 8, 136, 256), lambda p: (p, 0, 0, 0)),
            pl.BlockSpec(memory_space=pl.ANY),
            pl.BlockSpec(memory_space=pl.ANY),
        ],
        out_specs=place(0) + [spec for _, spec in outs],
        input_output_aliases={1: 0, 2: 1},
        compiler_params=params,
        name="unpack_rest",
    )(far(rest), far(g_up), far(g_down))


def swap(value):
    return lax.ppermute(value, "tensor", [(0, 1), (1, 0)])


def exchange(value, axes):
    return lax.all_to_all(value, axes, 0, 0)


def both(value):
    flat = value.reshape((16,) + value.shape[2:])
    return exchange(flat, ("context", "tensor")).reshape(value.shape)


def shards(
    tokens_in, cotangent, positions, w_qkv, b_qkv, w_out, w_up, b_up, w_down, out_bias, ln_gain, ln_bias
):
    rows, width = 256, 512
    x = tokens_in.reshape(rows, width)
    cot = cotangent.reshape(rows, width)
    wq = jnp.transpose(w_qkv, (0, 2, 1, 3))
    bq = jnp.transpose(b_qkv, (1, 0, 2))
    at = jnp.stack(
        [lax.axis_index("context"), lax.axis_index("tensor"), lax.axis_index("dp")]
    ).astype(jnp.int32)
    freqs = jnp.asarray(FREQS).reshape(HALF, 1)
    chunk = swap(chunk_of(at, wq, w_out))
    send, cs = call(
        first_body,
        [pltpu.VMEM((8, 208, BLK), BF), ((2, 2, HALF, BLK), F32)],
        (at, positions, freqs, Far(x), ln_gain, ln_bias, Layer(wq, 0), bq),
        "norm_qkv",
        smem_first=True,
    )
    pair, act, slope = call(
        feed_body,
        [
            ((2 * rows, width), BF),
            pltpu.HBM((rows, 1024), BF),
            pltpu.HBM((rows, 1024), BF),
        ],
        (
            Far(x), ln_gain, ln_bias, Layer(w_up, 0), b_up, Layer(w_down, 0), Layer(w_out, 0),
            After(send),
        ),
        "feed",
    )
    pair_other = swap(pair)
    (chunk,) = call(
        hand_on_body, [pltpu.HBM(chunk.shape, BF)], (chunk, After(act)), "hand_on"
    )
    others = lax.all_gather(chunk, "dp", axis=2, tiled=True)
    recv = exchange(send, "context")
    ctx_send, lse, ctx, start = call(
        attend_body,
        [((8, 2, HEAD, BLK), BF), ((1, 1024), F32), pltpu.HBM((HEAD, 1024), F32), ((1, 1024), jnp.int32)],
        (recv,),
        "attend",
    )
    recv_ctx = both(ctx_send)
    stream, send, grads_a, parts, d_b_up1, d_sum1 = call(
        middle_body,
        [
            pltpu.HBM((rows, width), F32),
            ((8, 256, BLK), BF),
            pltpu.HBM((8, 512, 256), BF),
            ((2 * rows, width), BF),
            ((1, 1024), F32),
            ((1, width), F32),
        ],
        (
            at, Far(x), pair, pair_other, recv_ctx, Layer(w_out, 0), out_bias, ln_gain, ln_bias,
            Layer(wq, 1), bq, Layer(w_up, 1), b_up, Layer(w_down, 1), Layer(w_out, 1), Far(cot), cs,
        ),
        "middle",
        scratch=[pltpu.VMEM((rows, 1024), BF), pltpu.VMEM((rows, 1024), BF)],
        smem_first=True,
    )
    sums_a = lax.psum_scatter(grads_a, "dp", scatter_dimension=0)
    parts_other = swap(parts)
    recv_both = exchange(send, "context")
    (both_send,) = call(
        attend_both_body,
        [((8, 2, 256, BLK), BF)],
        (recv_both, start, After(parts_other)),
        "attend_both",
        scratch=[pltpu.VMEM((HEAD, 1024), F32), pltpu.VMEM((HEAD, 1024), F32)],
    )
    recv_grad = both(both_send)
    block_out, g, send, grads_b, part_g, d_b_up0, d_b_qkv1, d_norm1, d_sum0 = call(
        turn_point_body,
        [
            pltpu.HBM((rows, width), F32),
            pltpu.HBM((rows, width), F32),
            pltpu.VMEM((8, 192, BLK), BF),
            pltpu.HBM((8, 832, 256), BF),
            ((rows, width), BF),
            ((1, 1024), F32),
            ((3, 256), F32),
            ((4, width), F32),
            ((1, width), F32),
        ],
        (
            at, Far(stream), parts, parts_other, recv_grad, Layer(w_out, 1), Layer(wq, 1),
            Layer(others, 1), out_bias, ln_gain, ln_bias, Far(cot), cs, Far(x), Far(act), Far(slope),
            Layer(w_up, 0), Layer(w_down, 0), Layer(w_out, 0), recv_ctx, Far(sums_a),
        ),
        "turn_point",
        smem_first=True,
    )
    sums_b = lax.psum_scatter(grads_b, "dp", scatter_dimension=0)
    part_g_other = swap(part_g)
    recv_d = exchange(send, "context")
    (back_send,) = call(
        attend_back_body,
        [((8, 2, 320, BLK), BF)],
        (recv, recv_d, start, lse, ctx, After(part_g_other)),
        "attend_back",
        scratch=[pltpu.VMEM((HEAD, 1024), F32), pltpu.VMEM((HEAD, 1024), F32)],
    )
    recv_grad0 = both(back_send)
    in_grad, grads_c, sums_a, _, _ = call(
        last_body,
        [
            pltpu.HBM((rows, width), F32),
            ((8, 208, 256), BF),
            pltpu.HBM((512, 256), BF),
            ((3, 256), F32),
            ((4, width), F32),
        ],
        (
            at, Far(x), Far(g), part_g, part_g_other, recv_grad0, Layer(wq, 0), Layer(others, 0), cs,
            ln_gain, ln_bias, d_b_up0, d_b_up1, d_b_qkv1, d_norm1, d_sum0, d_sum1,
        ),
        "last",
        smem_first=True,
    )
    mixed, sums_a = call(
        mix_body,
        [((8, 136, 256), BF), pltpu.HBM((512, 256), BF)],
        (exchange(grads_c, "dp"), Far(sums_b), Far(sums_a)),
        "mix",
    )
    full_a = lax.all_gather(sums_a, "dp")
    (summed,) = call(sum_body, [((8, 136, 256), BF)], (exchange(mixed, "context"),), "sum")
    full_bc = lax.all_gather(exchange(summed, "context"), "dp")
    g_up, g_down, g_qkv, g_out, g_b_up, g_b_qkv, g_sum, g_gain, g_bias = unpack(full_a, full_bc)
    return (
        block_out.reshape(tokens_in.shape),
        in_grad.reshape(tokens_in.shape),
        jnp.transpose(g_qkv, (0, 2, 1, 3)),
        jnp.transpose(g_b_qkv, (1, 0, 2)),
        g_out,
        g_up,
        g_b_up,
        g_down,
        g_sum,
        g_gain,
        g_bias,
    )


def solution(mesh):
    return jax.shard_map(
        shards,
        mesh=mesh,
        in_specs=(
            P("dp", "context", None),
            P("dp", "context", None),
            P("dp", "context"),
            P(None, None, None, "tensor"),
            P(None, None, "tensor"),
            P(None, "tensor", None),
            P(None, None, "tensor"),
            P(None, "tensor"),
            P(None, "tensor", None),
            P(),
            P(),
            P(),
        ),
        out_specs=(
            P("dp", "context", None),
            P("dp", "context", None),
            P(None, None, None, "tensor"),
            P(None, None, "tensor"),
            P(None, "tensor", None),
            P(None, None, "tensor"),
            P(None, "tensor"),
            P(None, "tensor", None),
            P(),
            P(),
            P(),
        ),
        check_vma=False,
    )
```

```python
from functools import partial

import numpy as np

import jax
import jax.numpy as jnp
from jax import lax
from jax.experimental import pallas as pl
from jax.experimental.pallas import tpu as pltpu
from jax.sharding import PartitionSpec as P

EPS = 1e-05
HALF = 8
HEAD = 64
BLK = 128
CHUNK = 256
NEG = -1e30
BF = jnp.bfloat16
F32 = jnp.float32

FREQS = (10000.0 ** (-np.arange(HALF, dtype=np.float64) * 2.0 / 16.0)).astype(np.float32)


def mm(a, b, ca=1, cb=0):
    return lax.dot_general(a, b, (((ca,), (cb,)), ((), ())), preferred_element_type=F32)


class After:
    def __init__(self, array):
        self.array = array

    def spec(self):
        return pl.BlockSpec(memory_space=pl.ANY)


class Layer:
    def __init__(self, array, index):
        self.array, self.index = far(array), index

    def spec(self):
        rest = self.array.shape[1:]
        place = (self.index,) + (0,) * len(rest)
        return pl.BlockSpec((None,) + rest, lambda i: place)


class Far:
    def __init__(self, array):
        self.array = far(array)

    def spec(self):
        return whole(self.array.shape)


Kept = type(pltpu.HBM((8, 128), F32))


def far(array):
    return pltpu.with_memory_space_constraint(array, pltpu.HBM)


def whole(shape):
    return pl.BlockSpec(shape, lambda i: (0,) * len(shape))


def call(body, out_shape, args, name, scratch=(), smem_first=False):
    specs = [
        a.spec() if isinstance(a, (Layer, Far, After)) else whole(a.shape) for a in args
    ]
    args = [a.array if isinstance(a, (Layer, Far, After)) else a for a in args]
    if smem_first:
        specs[0] = pl.BlockSpec(memory_space=pltpu.SMEM)
    return pl.pallas_call(
        body,
        grid=(1,),
        out_shape=[o if isinstance(o, Kept) else jax.ShapeDtypeStruct(*o) for o in out_shape],
        in_specs=specs,
        out_specs=[whole(o.shape if isinstance(o, Kept) else o[0]) for o in out_shape],
        scratch_shapes=list(scratch),
        compiler_params=pltpu.CompilerParams(vmem_limit_bytes=40 * 1024 * 1024),
        name=name,
    )(*args)


def norm_rows(x):
    mean = jnp.mean(x, -1, keepdims=True)
    cen = x - mean
    inv = lax.rsqrt(jnp.mean(cen * cen, -1, keepdims=True) + EPS)
    return cen * inv, inv


def turn(t, cos, sin):
    a, b = t[:HALF], t[HALF : 2 * HALF]
    return jnp.concatenate([a * cos - b * sin, b * cos + a * sin, t[2 * HALF :]], 0)


def turn_back(u, cos, sin):
    a, b = u[:HALF], u[HALF : 2 * HALF]
    return jnp.concatenate([a * cos + b * sin, b * cos - a * sin, u[2 * HALF :]], 0)


def send_qkv(send, attn_in, w_qkv, b_qkv, layer, cs):
    for e in range(3):
        turned = (mm(attn_in, w_qkv[e]) + b_qkv[e, layer : layer + 1]).T
        for s in range(2):
            cos, sin = cs[s, 0], cs[s, 1]
            for h in range(4):
                j = s * 4 + h
                part = turned[h * HEAD : (h + 1) * HEAD, s * BLK : (s + 1) * BLK]
                if e < 2:
                    part = turn(part, cos, sin)
                if e == 0:
                    part = part * (HEAD**-0.5)
                send[j, e * HEAD : (e + 1) * HEAD, :] = part.astype(BF)


def feed_forward(mlp_in, w_up, b_up, layer, w_down, act, slope):
    width = w_up.shape[1]
    total = None
    for c in range(0, width, 256):
        cols = slice(c, c + 256)
        pre = mm(mlp_in, w_up[:, cols]) + b_up[layer : layer + 1, cols]
        cdf = 0.5 + 0.5 * lax.erf(pre * np.float32(0.7071067811865476))
        a = (pre * cdf).astype(BF)
        act[:, cols] = a
        tail = pre * (jnp.exp(-0.5 * pre * pre) * np.float32(0.3989422804014327))
        slope[:, cols] = (cdf + tail).astype(BF)
        term = mm(a, w_down[cols, :])
        total = term if total is None else total + term
    return total


def feed_back(g_b, act, slope, mlp_in, w_up, w_down, d_up, d_down, d_b_up):
    width = w_up.shape[1]
    total = None
    mlp_t = mlp_in.T
    for c in range(0, width, 256):
        cols = slice(c, c + 256)
        d_act = mm(g_b, w_down[cols, :], 1, 1)
        d_pre = d_act * slope[:, cols].astype(F32)
        d_pre_b = d_pre.astype(BF)
        d_b_up[:, cols] = jnp.sum(d_pre_b.astype(F32), 0, keepdims=True)
        d_up(c // 256, mm(mlp_t, d_pre_b))
        d_down(c, mm(act[:, cols].T, g_b))
        term = mm(d_pre_b, w_up[:, cols], 1, 1)
        total = term if total is None else total + term
    return total


def pack_up(out, row):
    def put(c, value):
        for p in range(8):
            out[p, row + 64 * c : row + 64 * (c + 1), :] = value[64 * p : 64 * (p + 1)].astype(BF)

    return put


def pack_down(out, row):
    def put(c, value):
        for half in range(2):
            for k in range(2):
                out[c // 128 + k, row + 128 * half : row + 128 * (half + 1), :] = value[
                    128 * k : 128 * (k + 1), 256 * half : 256 * (half + 1)
                ].astype(BF)

    return put


def pack_qkv(out, row):
    def put(e, value):
        for p in range(8):
            out[p, row + 64 * e : row + 64 * (e + 1), :] = value[64 * p : 64 * (p + 1)].astype(BF)

    return put


def own_ctx(t, recv):
    full = jnp.concatenate([gather_ctx(recv, s) for s in range(2)], 1)
    return jnp.where(t == 0, full[0:256], full[256:512])


def pack_out(out, row, ctx, upstream):
    value = mm(ctx, upstream)
    for p in range(8):
        for half in range(2):
            out[p, row + 32 * half : row + 32 * (half + 1), :] = value[
                32 * p : 32 * (p + 1), 256 * half : 256 * (half + 1)
            ].astype(BF)


def first_body(at, pos, freqs, x, gain, bias, w_qkv, b_qkv, send, cs):
    for s in range(2):
        p = pos[s : s + 1, :].astype(F32)
        angle = freqs[...] * p
        cs[s, 0] = jnp.cos(angle)
        cs[s, 1] = jnp.sin(angle)
    normed, _ = norm_rows(x[...])
    attn_in = (normed * gain[0, 0:1] + bias[0, 0:1]).astype(BF)
    send_qkv(send, attn_in, w_qkv, b_qkv, 0, cs)
    row = lax.broadcasted_iota(jnp.int32, (16, BLK), 0)
    token = at[0] * BLK + lax.broadcasted_iota(jnp.int32, (1, BLK), 1)
    for s in range(2):
        start = jnp.maximum(token - pos[s : s + 1, :], 0)
        high = (start // 8).astype(F32)
        low = (start % 8).astype(F32)
        block = jnp.where(row == 0, high, jnp.where(row == 1, low, 0.0)).astype(BF)
        for h in range(4):
            send[s * 4 + h, 3 * HEAD : 3 * HEAD + 16, :] = block


def feed_body(x, gain, bias, w_up, b_up, w_down, w_out, _, pair, act, slope):
    normed, _ = norm_rows(x[...])
    mlp_in = (normed * gain[0, 1:2] + bias[0, 1:2]).astype(BF)
    pair[256:512] = w_out[...]
    pair[0:256] = feed_forward(mlp_in, w_up, b_up, 0, w_down, act, slope).astype(BF)


def load_rows(recv, lo, hi):
    return jnp.concatenate([recv[i, lo:hi, :] for i in range(8)], 1)


def starts_of(recv):
    rows = load_rows(recv, 3 * HEAD, 3 * HEAD + 16).astype(F32)
    return rows[0:1] * 8.0 + rows[1:2]


def masked(scores, start, c, length):
    own = start[:, c * CHUNK : (c + 1) * CHUNK]
    past = length - CHUNK
    key = lax.broadcasted_iota(jnp.int32, (CHUNK, CHUNK), 0)
    query = lax.broadcasted_iota(jnp.int32, (CHUNK, CHUNK), 1)
    near = jnp.where((key <= query) & (key + past >= own), scores[past:], NEG)
    if past == 0:
        return near
    key = lax.broadcasted_iota(jnp.int32, (past, CHUNK), 0)
    return jnp.concatenate([jnp.where(key >= own, scores[:past], NEG), near], 0)


def attend_body(recv, send, lse, ctx, start_out):
    q = load_rows(recv, 0, HEAD)
    k_t = load_rows(recv, HEAD, 2 * HEAD)
    v_t = load_rows(recv, 2 * HEAD, 3 * HEAD)
    k = k_t.T
    start = starts_of(recv).astype(jnp.int32)
    start_out[...] = start
    for c in range(4):
        cols = slice(c * CHUNK, (c + 1) * CHUNK)
        length = (c + 1) * CHUNK
        scores = mm(k[:length], q[:, cols])
        scores = masked(scores, start, c, length)
        peak = jnp.max(scores, 0, keepdims=True)
        shifted = jnp.exp(scores - peak)
        total = jnp.sum(shifted, 0, keepdims=True)
        lse[:, cols] = peak + jnp.log(total)
        out = mm(v_t[:, :length], shifted.astype(BF)) / total
        ctx[:, cols] = out
        for i in range(CHUNK // BLK):
            block = out[:, i * BLK : (i + 1) * BLK].astype(BF)
            for t in range(2):
                send[c * (CHUNK // BLK) + i, t] = block


def attend_both_body(recv, start, _, send, dk, dv):
    q = load_rows(recv, 0, HEAD)
    k_t = load_rows(recv, HEAD, 2 * HEAD)
    v_t = load_rows(recv, 2 * HEAD, 3 * HEAD)
    d_ctx = load_rows(recv, 3 * HEAD, 4 * HEAD)
    k = k_t.T
    v = v_t.T
    dk[...] = jnp.zeros_like(dk)
    dv[...] = jnp.zeros_like(dv)
    for c in range(4):
        cols = slice(c * CHUNK, (c + 1) * CHUNK)
        length = (c + 1) * CHUNK
        scores = mm(k[:length], q[:, cols])
        scores = masked(scores, start[...], c, length)
        peak = jnp.max(scores, 0, keepdims=True)
        shifted = jnp.exp(scores - peak)
        probs = shifted * (1.0 / jnp.sum(shifted, 0, keepdims=True))
        probs_b = probs.astype(BF)
        out = mm(v_t[:, :length], probs_b)
        dq = backward_chunk(q, k_t, v, d_ctx, probs, probs_b, out, cols, length, dk, dv)
        for i in range(CHUNK // BLK):
            b = c * (CHUNK // BLK) + i
            for t in range(2):
                send[b, t, 0:HEAD] = out[:, i * BLK : (i + 1) * BLK].astype(BF)
                send[b, t, HEAD : 2 * HEAD] = dq[:, i * BLK : (i + 1) * BLK].astype(BF)
    put_kv(send, dk, dv, 2 * HEAD)


def backward_chunk(q, k_t, v, d_ctx, probs, probs_b, out, cols, length, dk, dv):
    d_out = d_ctx[:, cols]
    d_probs = mm(v[:length], d_out)
    delta = jnp.sum(d_out.astype(F32) * out, 0, keepdims=True)
    d_scores = (probs * (d_probs - delta)).astype(BF)
    dk[:, :length] += mm(q[:, cols], d_scores, 1, 1)
    dv[:, :length] += mm(d_out, probs_b, 1, 1)
    return mm(k_t[:, :length], d_scores) * (HEAD**-0.5)


def put_kv(send, dk, dv, row):
    for b in range(8):
        for t in range(2):
            send[b, t, row : row + HEAD] = dk[:, b * BLK : (b + 1) * BLK].astype(BF)
            send[b, t, row + HEAD : row + 2 * HEAD] = dv[:, b * BLK : (b + 1) * BLK].astype(BF)


def attend_back_body(recv, recv_d, start, lse, ctx, _, send, dk, dv):
    ride = recv_d[0, 64:192].astype(F32)
    for i in range(1, 8):
        ride = ride + recv_d[i, 64:192].astype(F32)
    ride = ride.astype(BF)
    for b in range(8):
        for t in range(2):
            send[b, t, 192:320] = ride
    q = load_rows(recv, 0, HEAD)
    k_t = load_rows(recv, HEAD, 2 * HEAD)
    v_t = load_rows(recv, 2 * HEAD, 3 * HEAD)
    d_ctx = load_rows(recv_d, 0, HEAD)
    k = k_t.T
    v = v_t.T
    dk[...] = jnp.zeros_like(dk)
    dv[...] = jnp.zeros_like(dv)
    for c in range(4):
        cols = slice(c * CHUNK, (c + 1) * CHUNK)
        length = (c + 1) * CHUNK
        scores = mm(k[:length], q[:, cols])
        scores = masked(scores, start[...], c, length)
        probs = jnp.exp(scores - lse[:, cols])
        probs_b = probs.astype(BF)
        dq = backward_chunk(q, k_t, v, d_ctx, probs, probs_b, ctx[:, cols], cols, length, dk, dv)
        for i in range(CHUNK // BLK):
            for t in range(2):
                send[c * (CHUNK // BLK) + i, t, 0:HEAD] = dq[:, i * BLK : (i + 1) * BLK].astype(BF)
    put_kv(send, dk, dv, HEAD)


def gather_ctx(recv, s):
    return jnp.concatenate([recv[s * 4 + h, t, 0:HEAD, :] for t in range(2) for h in range(4)], 0)


def ordered(t, own, other):
    return jnp.where(t == 0, own, other), jnp.where(t == 0, other, own)


def out_other(others):
    halves = [
        jnp.concatenate([others[3, 64 * p + 32 * c : 64 * p + 32 * (c + 1), :] for p in range(8)], 0)
        for c in range(2)
    ]
    return jnp.concatenate(halves, 1)


def branch_of(t, recv, w_own, w_other):
    first, second = ordered(t, w_own, w_other)
    w = jnp.concatenate([first, second], 0)
    rows = []
    for s in range(2):
        rows.append(mm(gather_ctx(recv, s).T, w))
    return jnp.concatenate(rows, 0)


def middle_body(
    at, x, pair, pair_other, recv, w_out_own, out_bias, gain, bias,
    w_qkv, b_qkv, w_up, b_up, w_down, w_out, cot, cs,
    stream, send, grads, parts, d_b_up, d_sum, act, slope,
):
    branch = pair[0:256].astype(F32) + pair_other[0:256].astype(F32)
    branch = branch + branch_of(at[1], recv, w_out_own[...], pair_other[256:512])
    out = x[...] + branch + out_bias[0, 0:1] + out_bias[0, 1:2]
    stream[...] = out
    normed, _ = norm_rows(out)
    attn_in = (normed * gain[1, 0:1] + bias[1, 0:1]).astype(BF)
    mlp_in = (normed * gain[1, 1:2] + bias[1, 1:2]).astype(BF)
    send_qkv(send, attn_in, w_qkv, b_qkv, 1, cs)
    g_b = cot[...].astype(BF)
    d_ctx = mm(w_out[...], g_b, 1, 1)
    for s in range(2):
        for h in range(4):
            send[s * 4 + h, 3 * HEAD : 4 * HEAD, :] = d_ctx[
                h * HEAD : (h + 1) * HEAD, s * BLK : (s + 1) * BLK
            ].astype(BF)
    d_sum[...] = jnp.sum(cot[...], 0, keepdims=True)
    parts[0:256] = feed_forward(mlp_in, w_up, b_up, 1, w_down, act, slope).astype(BF)
    parts[256:512] = feed_back(
        g_b, act, slope, mlp_in, w_up, w_down, pack_up(grads, 0), pack_down(grads, 256), d_b_up
    ).astype(BF)


def norm_back(
    t, x, g, d_mlp_in, recv, row, w_own, others, cs, gain, bias, layer, d_qkv, d_b_qkv, d_norm
):
    normed, inv = norm_rows(x)
    attn_in = (normed * gain[layer, 0:1] + bias[layer, 0:1]).astype(BF)
    attn_t = attn_in.T
    d_attn_t = None
    for e in range(3):
        halves = []
        for tt in range(2):
            blocks = []
            for h in range(4):
                pieces = []
                for s in range(2):
                    lo = row + e * HEAD
                    u = recv[s * 4 + h, tt, lo : lo + HEAD, :]
                    if e < 2:
                        u = turn_back(u.astype(F32), cs[s, 0], cs[s, 1]).astype(BF)
                    pieces.append(u)
                blocks.append(jnp.concatenate(pieces, 1))
            halves.append(jnp.concatenate(blocks, 0))
        first, second = ordered(t, w_own[e], others[e])
        term = mm(first, halves[0]) + mm(second, halves[1])
        d_attn_t = term if d_attn_t is None else d_attn_t + term
        own = jnp.where(t == 0, halves[0], halves[1])
        d_qkv(e, mm(attn_t, own, 1, 1))
        d_b_qkv[e : e + 1] = mm(jnp.ones((8, own.shape[1]), BF), own, 1, 1)[0:1]
    d_attn_in = d_attn_t.T
    d_norm[0:1] = jnp.sum(d_attn_in * normed, 0, keepdims=True)
    d_norm[1:2] = jnp.sum(d_mlp_in * normed, 0, keepdims=True)
    d_norm[2:3] = jnp.sum(d_attn_in, 0, keepdims=True)
    d_norm[3:4] = jnp.sum(d_mlp_in, 0, keepdims=True)
    d_normed = d_attn_in * gain[layer, 0:1] + d_mlp_in * gain[layer, 1:2]
    return g + inv * (
        d_normed
        - jnp.mean(d_normed, -1, keepdims=True)
        - normed * jnp.mean(d_normed * normed, -1, keepdims=True)
    )


def turn_point_body(
    at, stream, parts, parts_other, recv, w_out, w_qkv, others, out_bias,
    gain, bias, cot, cs, x, act, slope, w_up, w_down, w_out_first, recv_first, sums_a,
    block_out, g_out, send, grads, part, d_b_up, d_b_qkv, d_norm, d_sum,
):
    t = at[1]
    branch = parts[0:256].astype(F32) + parts_other[0:256].astype(F32)
    branch = branch + branch_of(t, recv, w_out[...], out_other(others))
    block_out[...] = stream[...] + branch + out_bias[1, 0:1] + out_bias[1, 1:2]
    d_mlp_in = parts[256:512].astype(F32) + parts_other[256:512].astype(F32)
    g = norm_back(
        t, stream[...], cot[...], d_mlp_in, recv, HEAD, w_qkv, others, cs, gain, bias, 1,
        pack_qkv(grads, 0), d_b_qkv, d_norm,
    )
    g_out[...] = g
    g_b = g.astype(BF)
    d_sum[...] = jnp.sum(g, 0, keepdims=True)
    d_ctx = mm(w_out_first[...], g_b, 1, 1)
    for s in range(2):
        for h in range(4):
            send[s * 4 + h, 0:HEAD] = d_ctx[
                h * HEAD : (h + 1) * HEAD, s * BLK : (s + 1) * BLK
            ].astype(BF)
    for q in range(8):
        for c in range(2):
            send[q, 64 + 64 * c : 128 + 64 * c] = sums_a[
                64 * q : 64 * (q + 1), BLK * c : BLK * (c + 1)
            ]
    pack_out(grads, 704, own_ctx(t, recv), cot[...].astype(BF))
    pack_out(grads, 768, own_ctx(t, recv_first), g_b)
    normed, _ = norm_rows(x[...])
    mlp_in = (normed * gain[0, 1:2] + bias[0, 1:2]).astype(BF)
    part[...] = feed_back(
        g_b, act, slope, mlp_in, w_up, w_down, pack_up(grads, 192), pack_down(grads, 448), d_b_up
    ).astype(BF)


def last_body(
    at, x, g, part, part_other, recv, w_qkv, others, cs, gain, bias,
    d_b_up0, d_b_up1, d_b_qkv1, d_norm1, d_sum0, d_sum1,
    in_grad, grads, sums_a, d_b_qkv0, d_norm0,
):
    d_mlp_in = part[...].astype(F32) + part_other[...].astype(F32)
    in_grad[...] = norm_back(
        at[1], x[...], g[...], d_mlp_in, recv, 0, w_qkv, others, cs, gain, bias, 0,
        pack_qkv(grads, 0), d_b_qkv0, d_norm0,
    )
    for q in range(8):
        both_planes = recv[q, :, 192:320]
        block = jnp.where(at[1] == 0, both_planes[0], both_planes[1])
        for c in range(2):
            sums_a[64 * q : 64 * (q + 1), BLK * c : BLK * (c + 1)] = block[64 * c : 64 * (c + 1)]

    def lanes(ref, row, count):
        return [ref[row : row + 1, 256 * c : 256 * (c + 1)] for c in range(count)]

    def norms(ref):
        return [v for r in range(4) for v in lanes(ref, r, 2)]

    rows = [
        lanes(d_b_up0, 0, 4)
        + lanes(d_b_up1, 0, 4)
        + [v for e in range(3) for ref in (d_b_qkv0, d_b_qkv1) for v in lanes(ref, e, 1)],
        lanes(d_sum0, 0, 2) + lanes(d_sum1, 0, 2) + norms(d_norm0),
        norms(d_norm1),
    ]
    for p in range(8):
        have = rows[p] if p < len(rows) else []
        fill = [jnp.zeros((16 - len(have), 256), F32)]
        grads[p, 192:208, :] = jnp.concatenate(have + fill, 0).astype(BF)


def chunk_body(at, w_qkv, w_out, out):
    for layer in range(2):
        for e in range(3):
            out[layer, e] = w_qkv[layer, e]
        out[layer, 3, 0:32] = w_out[layer, :, 0:256]
        out[layer, 3, 32:64] = w_out[layer, :, 256:512]


def chunk_of(at, wq, w_out):
    return pl.pallas_call(
        chunk_body,
        out_shape=jax.ShapeDtypeStruct((2, 4, 64, 256), BF),
        grid_spec=pltpu.PrefetchScalarGridSpec(
            num_scalar_prefetch=1,
            grid=(1,),
            in_specs=[
                pl.BlockSpec((2, 3, 64, 256), lambda i, at: (0, 0, at[2], 0)),
                pl.BlockSpec((2, 32, 512), lambda i, at: (0, at[2], 0)),
            ],
            out_specs=pl.BlockSpec((2, 4, 64, 256), lambda i, at: (0, 0, 0, 0)),
        ),
        compiler_params=pltpu.CompilerParams(vmem_limit_bytes=40 * 1024 * 1024),
        name="chunk",
    )(at, far(wq), far(w_out))


def hand_on_body(value, _, out):
    out[...] = value[...]


def mix_body(got, early, first, out, first_out):
    total = got[0].astype(F32)
    for i in range(1, 8):
        total = total + got[i].astype(F32)
    for q in range(8):
        tiny = total[192 + 8 * q : 200 + 8 * q] if q < 2 else jnp.zeros((8, 256), F32)
        mine = [early[104 * q : 104 * (q + 1)].astype(F32), total[24 * q : 24 * (q + 1)], tiny]
        out[q] = jnp.concatenate(mine, 0).astype(BF)
    first_out[...] = first[...]


def sum_body(got, out):
    total = got[0].astype(F32)
    for i in range(1, 8):
        total = total + got[i].astype(F32)
    for q in range(8):
        out[q] = total.astype(BF)


def unpack_first_body(first, g_up, g_down):
    for k in range(2):
        for c in range(4):
            cols = slice(256 * c, 256 * (c + 1))
            g_up[0, 64 * k : 64 * (k + 1), cols] = first[k, 64 * c : 64 * (c + 1)].astype(F32)
        for c in range(2):
            rows = first[k, 256 + 128 * c : 256 + 128 * (c + 1)]
            cols = slice(256 * c, 256 * (c + 1))
            g_down[0, 128 * k : 128 * (k + 1), cols] = rows.astype(F32)


def unpack_rest_body(rest, _, __, g_up, g_down, g_qkv, g_out, g_b_up, g_b_qkv, g_sum, g_gain, g_bias):
    p = pl.program_id(0)
    for k in range(2):
        for q in range(8):
            block = rest[k, q].astype(F32)
            for i in range(16):
                value = block[8 * i : 8 * (i + 1)]
                row = 104 * q + 8 * i
                if i >= 13:
                    row = 24 * q + 8 * (i - 13)
                    r = 64 * k + row % 64
                    g_qkv[0, row // 64, r : r + 8] = value
                elif row < 192:
                    r = 64 * k + row % 64
                    g_qkv[1, row // 64, r : r + 8] = value
                elif row < 448:
                    c, r = divmod(row - 192, 64)
                    r += 64 * k
                    g_up[0, r : r + 8, 256 * c : 256 * (c + 1)] = value
                elif row < 704:
                    c, r = divmod(row - 448, 128)
                    r += 128 * k
                    g_down[0, r : r + 8, 256 * c : 256 * (c + 1)] = value
                else:
                    c, r = divmod((row - 704) % 64, 32)
                    r += 32 * k
                    g_out[1 - (row - 704) // 64, r : r + 8, 256 * c : 256 * (c + 1)] = value

    tiny = [jnp.concatenate([rest[k, q].astype(F32)[128:136] for q in range(2)], 0) for k in range(2)]

    @pl.when(p == 0)
    def _():
        for layer in range(2):
            for c in range(4):
                r = 4 * layer + c
                g_b_up[layer : layer + 1, 256 * c : 256 * (c + 1)] = tiny[0][r : r + 1]
        for e in range(3):
            for layer in range(2):
                r = 8 + 2 * e + layer
                g_b_qkv[e, layer : layer + 1, :] = tiny[0][r : r + 1]
        for layer in range(2):
            for c in range(2):
                r = 2 * layer + c
                for which in range(2):
                    g_sum[layer, which : which + 1, 256 * c : 256 * (c + 1)] = tiny[1][r : r + 1]

    def norms(layer, rows, base):
        for which in range(2):
            for c in range(2):
                cols = slice(256 * c, 256 * (c + 1))
                r = base + 2 * which + c
                g_gain[layer, which : which + 1, cols] = rows[r : r + 1]
                g_bias[layer, which : which + 1, cols] = rows[r + 4 : r + 5]

    @pl.when(p == 0)
    def _():
        norms(0, tiny[1], 4)

    @pl.when(p == 1)
    def _():
        norms(1, tiny[0], 0)


UP = (2, 512, 1024)
DOWN = (2, 1024, 512)


def unpack(first, rest):
    def place(layer):
        return [
            pl.BlockSpec((1, 128, 1024), lambda p: (layer, p, 0)),
            pl.BlockSpec((1, 256, 512), lambda p: (layer, p, 0)),
        ]

    params = pltpu.CompilerParams(vmem_limit_bytes=40 * 1024 * 1024)
    g_up, g_down = pl.pallas_call(
        unpack_first_body,
        grid=(4,),
        out_shape=[pltpu.HBM(UP, F32), pltpu.HBM(DOWN, F32)],
        in_specs=[pl.BlockSpec((2, 512, 256), lambda p: (p, 0, 0))],
        out_specs=place(1),
        compiler_params=params,
        name="unpack_first",
    )(far(first))
    outs = [
        ((2, 3, 512, 256), pl.BlockSpec((2, 3, 128, 256), lambda p: (0, 0, p, 0))),
        ((2, 256, 512), pl.BlockSpec((2, 64, 512), lambda p: (0, p, 0))),
        ((2, 1024), whole((2, 1024))),
        ((3, 2, 256), whole((3, 2, 256))),
        ((2, 2, 512), whole((2, 2, 512))),
        ((2, 2, 512), whole((2, 2, 512))),
        ((2, 2, 512), whole((2, 2, 512))),
    ]
    return pl.pallas_call(
        unpack_rest_body,
        grid=(4,),
        out_shape=[pltpu.HBM(shape, F32) for shape in [UP, DOWN] + [o[0] for o in outs]],
        in_specs=[
            pl.BlockSpec((2, 8, 136, 256), lambda p: (p, 0, 0, 0)),
            pl.BlockSpec(memory_space=pl.ANY),
            pl.BlockSpec(memory_space=pl.ANY),
        ],
        out_specs=place(0) + [spec for _, spec in outs],
        input_output_aliases={1: 0, 2: 1},
        compiler_params=params,
        name="unpack_rest",
    )(far(rest), far(g_up), far(g_down))


def swap(value):
    return lax.ppermute(value, "tensor", [(0, 1), (1, 0)])


def exchange(value, axes):
    return lax.all_to_all(value, axes, 0, 0)


def both(value):
    flat = value.reshape((16,) + value.shape[2:])
    return exchange(flat, ("context", "tensor")).reshape(value.shape)


def shards(
    tokens_in, cotangent, positions, w_qkv, b_qkv, w_out, w_up, b_up, w_down, out_bias, ln_gain, ln_bias
):
    rows, width = 256, 512
    x = tokens_in.reshape(rows, width)
    cot = cotangent.reshape(rows, width)
    wq = jnp.transpose(w_qkv, (0, 2, 1, 3))
    bq = jnp.transpose(b_qkv, (1, 0, 2))
    at = jnp.stack(
        [lax.axis_index("context"), lax.axis_index("tensor"), lax.axis_index("dp")]
    ).astype(jnp.int32)
    freqs = jnp.asarray(FREQS).reshape(HALF, 1)
    chunk = swap(chunk_of(at, wq, w_out))
    send, cs = call(
        first_body,
        [pltpu.VMEM((8, 208, BLK), BF), ((2, 2, HALF, BLK), F32)],
        (at, positions, freqs, Far(x), ln_gain, ln_bias, Layer(wq, 0), bq),
        "norm_qkv",
        smem_first=True,
    )
    pair, act, slope = call(
        feed_body,
        [
            ((2 * rows, width), BF),
            pltpu.HBM((rows, 1024), BF),
            pltpu.HBM((rows, 1024), BF),
        ],
        (
            Far(x), ln_gain, ln_bias, Layer(w_up, 0), b_up, Layer(w_down, 0), Layer(w_out, 0),
            After(send),
        ),
        "feed",
    )
    pair_other = swap(pair)
    recv = exchange(send, "context")
    (chunk,) = call(
        hand_on_body, [pltpu.HBM(chunk.shape, BF)], (chunk, After(recv)), "hand_on"
    )
    others = lax.all_gather(chunk, "dp", axis=2, tiled=True)
    ctx_send, lse, ctx, start = call(
        attend_body,
        [((8, 2, HEAD, BLK), BF), ((1, 1024), F32), pltpu.HBM((HEAD, 1024), F32), ((1, 1024), jnp.int32)],
        (recv,),
        "attend",
    )
    recv_ctx = both(ctx_send)
    stream, send, grads_a, parts, d_b_up1, d_sum1 = call(
        middle_body,
        [
            pltpu.HBM((rows, width), F32),
            ((8, 256, BLK), BF),
            pltpu.HBM((8, 512, 256), BF),
            ((2 * rows, width), BF),
            ((1, 1024), F32),
            ((1, width), F32),
        ],
        (
            at, Far(x), pair, pair_other, recv_ctx, Layer(w_out, 0), out_bias, ln_gain, ln_bias,
            Layer(wq, 1), bq, Layer(w_up, 1), b_up, Layer(w_down, 1), Layer(w_out, 1), Far(cot), cs,
        ),
        "middle",
        scratch=[pltpu.VMEM((rows, 1024), BF), pltpu.VMEM((rows, 1024), BF)],
        smem_first=True,
    )
    sums_a = lax.psum_scatter(grads_a, "dp", scatter_dimension=0)
    parts_other = swap(parts)
    recv_both = exchange(send, "context")
    (both_send,) = call(
        attend_both_body,
        [((8, 2, 256, BLK), BF)],
        (recv_both, start, After(parts_other)),
        "attend_both",
        scratch=[pltpu.VMEM((HEAD, 1024), F32), pltpu.VMEM((HEAD, 1024), F32)],
    )
    recv_grad = both(both_send)
    block_out, g, send, grads_b, part_g, d_b_up0, d_b_qkv1, d_norm1, d_sum0 = call(
        turn_point_body,
        [
            pltpu.HBM((rows, width), F32),
            pltpu.HBM((rows, width), F32),
            pltpu.VMEM((8, 192, BLK), BF),
            pltpu.HBM((8, 832, 256), BF),
            ((rows, width), BF),
            ((1, 1024), F32),
            ((3, 256), F32),
            ((4, width), F32),
            ((1, width), F32),
        ],
        (
            at, Far(stream), parts, parts_other, recv_grad, Layer(w_out, 1), Layer(wq, 1),
            Layer(others, 1), out_bias, ln_gain, ln_bias, Far(cot), cs, Far(x), Far(act), Far(slope),
            Layer(w_up, 0), Layer(w_down, 0), Layer(w_out, 0), recv_ctx, Far(sums_a),
        ),
        "turn_point",
        smem_first=True,
    )
    sums_b = lax.psum_scatter(grads_b, "dp", scatter_dimension=0)
    part_g_other = swap(part_g)
    recv_d = exchange(send, "context")
    (back_send,) = call(
        attend_back_body,
        [((8, 2, 320, BLK), BF)],
        (recv, recv_d, start, lse, ctx, After(part_g_other)),
        "attend_back",
        scratch=[pltpu.VMEM((HEAD, 1024), F32), pltpu.VMEM((HEAD, 1024), F32)],
    )
    recv_grad0 = both(back_send)
    in_grad, grads_c, sums_a, _, _ = call(
        last_body,
        [
            pltpu.HBM((rows, width), F32),
            ((8, 208, 256), BF),
            pltpu.HBM((512, 256), BF),
            ((3, 256), F32),
            ((4, width), F32),
        ],
        (
            at, Far(x), Far(g), part_g, part_g_other, recv_grad0, Layer(wq, 0), Layer(others, 0), cs,
            ln_gain, ln_bias, d_b_up0, d_b_up1, d_b_qkv1, d_norm1, d_sum0, d_sum1,
        ),
        "last",
        smem_first=True,
    )
    mixed, sums_a = call(
        mix_body,
        [((8, 136, 256), BF), pltpu.HBM((512, 256), BF)],
        (exchange(grads_c, "dp"), Far(sums_b), Far(sums_a)),
        "mix",
    )
    full_a = lax.all_gather(sums_a, "dp")
    (summed,) = call(sum_body, [((8, 136, 256), BF)], (exchange(mixed, "context"),), "sum")
    full_bc = lax.all_gather(exchange(summed, "context"), "dp")
    g_up, g_down, g_qkv, g_out, g_b_up, g_b_qkv, g_sum, g_gain, g_bias = unpack(full_a, full_bc)
    return (
        block_out.reshape(tokens_in.shape),
        in_grad.reshape(tokens_in.shape),
        jnp.transpose(g_qkv, (0, 2, 1, 3)),
        jnp.transpose(g_b_qkv, (1, 0, 2)),
        g_out,
        g_up,
        g_b_up,
        g_down,
        g_sum,
        g_gain,
        g_bias,
    )


def solution(mesh):
    return jax.shard_map(
        shards,
        mesh=mesh,
        in_specs=(
            P("dp", "context", None),
            P("dp", "context", None),
            P("dp", "context"),
            P(None, None, None, "tensor"),
            P(None, None, "tensor"),
            P(None, "tensor", None),
            P(None, None, "tensor"),
            P(None, "tensor"),
            P(None, "tensor", None),
            P(),
            P(),
            P(),
        ),
        out_specs=(
            P("dp", "context", None),
            P("dp", "context", None),
            P(None, None, None, "tensor"),
            P(None, None, "tensor"),
            P(None, "tensor", None),
            P(None, None, "tensor"),
            P(None, "tensor"),
            P(None, "tensor", None),
            P(),
            P(),
            P(),
        ),
        check_vma=False,
    )
```

```python
from functools import partial

import numpy as np

import jax
import jax.numpy as jnp
from jax import lax
from jax.experimental import pallas as pl
from jax.experimental.pallas import tpu as pltpu
from jax.sharding import PartitionSpec as P

EPS = 1e-05
HALF = 8
HEAD = 64
BLK = 128
CHUNK = 256
NEG = -1e30
BF = jnp.bfloat16
F32 = jnp.float32

FREQS = (10000.0 ** (-np.arange(HALF, dtype=np.float64) * 2.0 / 16.0)).astype(np.float32)


def mm(a, b, ca=1, cb=0):
    return lax.dot_general(a, b, (((ca,), (cb,)), ((), ())), preferred_element_type=F32)


class After:
    def __init__(self, array):
        self.array = array

    def spec(self):
        return pl.BlockSpec(memory_space=pl.ANY)


class Layer:
    def __init__(self, array, index):
        self.array, self.index = far(array), index

    def spec(self):
        rest = self.array.shape[1:]
        place = (self.index,) + (0,) * len(rest)
        return pl.BlockSpec((None,) + rest, lambda i: place)


class Far:
    def __init__(self, array):
        self.array = far(array)

    def spec(self):
        return whole(self.array.shape)


Kept = type(pltpu.HBM((8, 128), F32))


def far(array):
    return pltpu.with_memory_space_constraint(array, pltpu.HBM)


def whole(shape):
    return pl.BlockSpec(shape, lambda i: (0,) * len(shape))


def call(body, out_shape, args, name, scratch=(), smem_first=False):
    specs = [
        a.spec() if isinstance(a, (Layer, Far, After)) else whole(a.shape) for a in args
    ]
    args = [a.array if isinstance(a, (Layer, Far, After)) else a for a in args]
    if smem_first:
        specs[0] = pl.BlockSpec(memory_space=pltpu.SMEM)
    return pl.pallas_call(
        body,
        grid=(1,),
        out_shape=[o if isinstance(o, Kept) else jax.ShapeDtypeStruct(*o) for o in out_shape],
        in_specs=specs,
        out_specs=[whole(o.shape if isinstance(o, Kept) else o[0]) for o in out_shape],
        scratch_shapes=list(scratch),
        compiler_params=pltpu.CompilerParams(vmem_limit_bytes=40 * 1024 * 1024),
        name=name,
    )(*args)


def norm_rows(x):
    mean = jnp.mean(x, -1, keepdims=True)
    cen = x - mean
    inv = lax.rsqrt(jnp.mean(cen * cen, -1, keepdims=True) + EPS)
    return cen * inv, inv


def turn(t, cos, sin):
    a, b = t[:HALF], t[HALF : 2 * HALF]
    return jnp.concatenate([a * cos - b * sin, b * cos + a * sin, t[2 * HALF :]], 0)


def turn_back(u, cos, sin):
    a, b = u[:HALF], u[HALF : 2 * HALF]
    return jnp.concatenate([a * cos + b * sin, b * cos - a * sin, u[2 * HALF :]], 0)


def send_qkv(send, attn_in, w_qkv, b_qkv, layer, cs):
    for e in range(3):
        turned = (mm(attn_in, w_qkv[e]) + b_qkv[e, layer : layer + 1]).T
        for s in range(2):
            cos, sin = cs[s, 0], cs[s, 1]
            for h in range(4):
                j = s * 4 + h
                part = turned[h * HEAD : (h + 1) * HEAD, s * BLK : (s + 1) * BLK]
                if e < 2:
                    part = turn(part, cos, sin)
                if e == 0:
                    part = part * (HEAD**-0.5)
                send[j, e * HEAD : (e + 1) * HEAD, :] = part.astype(BF)


def feed_forward(mlp_in, w_up, b_up, layer, w_down, act, slope):
    width = w_up.shape[1]
    total = None
    for c in range(0, width, 256):
        cols = slice(c, c + 256)
        pre = mm(mlp_in, w_up[:, cols]) + b_up[layer : layer + 1, cols]
        cdf = 0.5 + 0.5 * lax.erf(pre * np.float32(0.7071067811865476))
        a = (pre * cdf).astype(BF)
        act[:, cols] = a
        tail = pre * (jnp.exp(-0.5 * pre * pre) * np.float32(0.3989422804014327))
        slope[:, cols] = (cdf + tail).astype(BF)
        term = mm(a, w_down[cols, :])
        total = term if total is None else total + term
    return total


def feed_back(g_b, act, slope, mlp_in, w_up, w_down, d_up, d_down, d_b_up):
    width = w_up.shape[1]
    total = None
    mlp_t = mlp_in.T
    for c in range(0, width, 256):
        cols = slice(c, c + 256)
        d_act = mm(g_b, w_down[cols, :], 1, 1)
        d_pre = d_act * slope[:, cols].astype(F32)
        d_pre_b = d_pre.astype(BF)
        d_b_up[:, cols] = jnp.sum(d_pre_b.astype(F32), 0, keepdims=True)
        d_up(c // 256, mm(mlp_t, d_pre_b))
        d_down(c, mm(act[:, cols].T, g_b))
        term = mm(d_pre_b, w_up[:, cols], 1, 1)
        total = term if total is None else total + term
    return total


def pack_up(out, row):
    def put(c, value):
        for p in range(8):
            out[p, row + 64 * c : row + 64 * (c + 1), :] = value[64 * p : 64 * (p + 1)].astype(BF)

    return put


def pack_down(out, row):
    def put(c, value):
        for half in range(2):
            for k in range(2):
                out[c // 128 + k, row + 128 * half : row + 128 * (half + 1), :] = value[
                    128 * k : 128 * (k + 1), 256 * half : 256 * (half + 1)
                ].astype(BF)

    return put


def pack_qkv(out, row):
    def put(e, value):
        for p in range(8):
            out[p, row + 64 * e : row + 64 * (e + 1), :] = value[64 * p : 64 * (p + 1)].astype(BF)

    return put


def own_ctx(t, recv):
    full = jnp.concatenate([gather_ctx(recv, s) for s in range(2)], 1)
    return jnp.where(t == 0, full[0:256], full[256:512])


def pack_out(out, row, ctx, upstream):
    value = mm(ctx, upstream)
    for p in range(8):
        for half in range(2):
            out[p, row + 32 * half : row + 32 * (half + 1), :] = value[
                32 * p : 32 * (p + 1), 256 * half : 256 * (half + 1)
            ].astype(BF)


def first_body(
    at, pos, freqs, x, gain, bias, w_qkv, b_qkv, w_up, b_up, w_down, w_out,
    send, pair, act, slope, cs,
):
    pair[256:512] = w_out[...]
    for s in range(2):
        p = pos[s : s + 1, :].astype(F32)
        angle = freqs[...] * p
        cs[s, 0] = jnp.cos(angle)
        cs[s, 1] = jnp.sin(angle)
    normed, _ = norm_rows(x[...])
    attn_in = (normed * gain[0, 0:1] + bias[0, 0:1]).astype(BF)
    mlp_in = (normed * gain[0, 1:2] + bias[0, 1:2]).astype(BF)
    send_qkv(send, attn_in, w_qkv, b_qkv, 0, cs)
    row = lax.broadcasted_iota(jnp.int32, (16, BLK), 0)
    token = at[0] * BLK + lax.broadcasted_iota(jnp.int32, (1, BLK), 1)
    for s in range(2):
        start = jnp.maximum(token - pos[s : s + 1, :], 0)
        high = (start // 8).astype(F32)
        low = (start % 8).astype(F32)
        block = jnp.where(row == 0, high, jnp.where(row == 1, low, 0.0)).astype(BF)
        for h in range(4):
            send[s * 4 + h, 3 * HEAD : 3 * HEAD + 16, :] = block
    pair[0:256] = feed_forward(mlp_in, w_up, b_up, 0, w_down, act, slope).astype(BF)


def load_rows(recv, lo, hi):
    return jnp.concatenate([recv[i, lo:hi, :] for i in range(8)], 1)


def starts_of(recv):
    rows = load_rows(recv, 3 * HEAD, 3 * HEAD + 16).astype(F32)
    return rows[0:1] * 8.0 + rows[1:2]


def visible_of(start, c, length):
    key = lax.broadcasted_iota(jnp.int32, (length, CHUNK), 0)
    query = lax.broadcasted_iota(jnp.int32, (length, CHUNK), 1) + c * CHUNK
    return (key <= query) & (key >= start[:, c * CHUNK : (c + 1) * CHUNK])


def attend_body(recv, send, lse, ctx, start_out):
    q = load_rows(recv, 0, HEAD)
    k_t = load_rows(recv, HEAD, 2 * HEAD)
    v_t = load_rows(recv, 2 * HEAD, 3 * HEAD)
    k = k_t.T
    start = starts_of(recv).astype(jnp.int32)
    start_out[...] = start
    for c in range(4):
        cols = slice(c * CHUNK, (c + 1) * CHUNK)
        length = (c + 1) * CHUNK
        scores = mm(k[:length], q[:, cols])
        scores = jnp.where(visible_of(start, c, length), scores, NEG)
        peak = jnp.max(scores, 0, keepdims=True)
        shifted = jnp.exp(scores - peak)
        total = jnp.sum(shifted, 0, keepdims=True)
        lse[:, cols] = peak + jnp.log(total)
        out = mm(v_t[:, :length], shifted.astype(BF)) / total
        ctx[:, cols] = out
        for i in range(CHUNK // BLK):
            block = out[:, i * BLK : (i + 1) * BLK].astype(BF)
            for t in range(2):
                send[c * (CHUNK // BLK) + i, t] = block


def attend_both_body(recv, start, _, send, dk, dv):
    q = load_rows(recv, 0, HEAD)
    k_t = load_rows(recv, HEAD, 2 * HEAD)
    v_t = load_rows(recv, 2 * HEAD, 3 * HEAD)
    d_ctx = load_rows(recv, 3 * HEAD, 4 * HEAD)
    k = k_t.T
    v = v_t.T
    dk[...] = jnp.zeros_like(dk)
    dv[...] = jnp.zeros_like(dv)
    for c in range(4):
        cols = slice(c * CHUNK, (c + 1) * CHUNK)
        length = (c + 1) * CHUNK
        scores = mm(k[:length], q[:, cols])
        scores = jnp.where(visible_of(start[...], c, length), scores, NEG)
        peak = jnp.max(scores, 0, keepdims=True)
        shifted = jnp.exp(scores - peak)
        probs = shifted * (1.0 / jnp.sum(shifted, 0, keepdims=True))
        probs_b = probs.astype(BF)
        out = mm(v_t[:, :length], probs_b)
        dq = backward_chunk(q, k_t, v, d_ctx, probs, probs_b, out, cols, length, dk, dv)
        for i in range(CHUNK // BLK):
            b = c * (CHUNK // BLK) + i
            for t in range(2):
                send[b, t, 0:HEAD] = out[:, i * BLK : (i + 1) * BLK].astype(BF)
                send[b, t, HEAD : 2 * HEAD] = dq[:, i * BLK : (i + 1) * BLK].astype(BF)
    put_kv(send, dk, dv, 2 * HEAD)


def backward_chunk(q, k_t, v, d_ctx, probs, probs_b, out, cols, length, dk, dv):
    d_out = d_ctx[:, cols]
    d_probs = mm(v[:length], d_out)
    delta = jnp.sum(d_out.astype(F32) * out, 0, keepdims=True)
    d_scores = (probs * (d_probs - delta)).astype(BF)
    dk[:, :length] += mm(q[:, cols], d_scores, 1, 1)
    dv[:, :length] += mm(d_out, probs_b, 1, 1)
    return mm(k_t[:, :length], d_scores) * (HEAD**-0.5)


def put_kv(send, dk, dv, row):
    for b in range(8):
        for t in range(2):
            send[b, t, row : row + HEAD] = dk[:, b * BLK : (b + 1) * BLK].astype(BF)
            send[b, t, row + HEAD : row + 2 * HEAD] = dv[:, b * BLK : (b + 1) * BLK].astype(BF)


def attend_back_body(recv, recv_d, start, lse, ctx, _, send, dk, dv):
    ride = recv_d[0, 64:192].astype(F32)
    for i in range(1, 8):
        ride = ride + recv_d[i, 64:192].astype(F32)
    ride = ride.astype(BF)
    for b in range(8):
        for t in range(2):
            send[b, t, 192:320] = ride
    q = load_rows(recv, 0, HEAD)
    k_t = load_rows(recv, HEAD, 2 * HEAD)
    v_t = load_rows(recv, 2 * HEAD, 3 * HEAD)
    d_ctx = load_rows(recv_d, 0, HEAD)
    k = k_t.T
    v = v_t.T
    dk[...] = jnp.zeros_like(dk)
    dv[...] = jnp.zeros_like(dv)
    for c in range(4):
        cols = slice(c * CHUNK, (c + 1) * CHUNK)
        length = (c + 1) * CHUNK
        scores = mm(k[:length], q[:, cols])
        scores = jnp.where(visible_of(start[...], c, length), scores, NEG)
        probs = jnp.exp(scores - lse[:, cols])
        probs_b = probs.astype(BF)
        dq = backward_chunk(q, k_t, v, d_ctx, probs, probs_b, ctx[:, cols], cols, length, dk, dv)
        for i in range(CHUNK // BLK):
            for t in range(2):
                send[c * (CHUNK // BLK) + i, t, 0:HEAD] = dq[:, i * BLK : (i + 1) * BLK].astype(BF)
    put_kv(send, dk, dv, HEAD)


def gather_ctx(recv, s):
    return jnp.concatenate([recv[s * 4 + h, t, 0:HEAD, :] for t in range(2) for h in range(4)], 0)


def ordered(t, own, other):
    return jnp.where(t == 0, own, other), jnp.where(t == 0, other, own)


def out_other(others):
    halves = [
        jnp.concatenate([others[3, 64 * p + 32 * c : 64 * p + 32 * (c + 1), :] for p in range(8)], 0)
        for c in range(2)
    ]
    return jnp.concatenate(halves, 1)


def branch_of(t, recv, w_own, w_other):
    first, second = ordered(t, w_own, w_other)
    w = jnp.concatenate([first, second], 0)
    rows = []
    for s in range(2):
        rows.append(mm(gather_ctx(recv, s).T, w))
    return jnp.concatenate(rows, 0)


def middle_body(
    at, x, pair, pair_other, recv, w_out_own, out_bias, gain, bias,
    w_qkv, b_qkv, w_up, b_up, w_down, w_out, cot, cs,
    stream, send, grads, parts, d_b_up, d_sum, act, slope,
):
    branch = pair[0:256].astype(F32) + pair_other[0:256].astype(F32)
    branch = branch + branch_of(at[1], recv, w_out_own[...], pair_other[256:512])
    out = x[...] + branch + out_bias[0, 0:1] + out_bias[0, 1:2]
    stream[...] = out
    normed, _ = norm_rows(out)
    attn_in = (normed * gain[1, 0:1] + bias[1, 0:1]).astype(BF)
    mlp_in = (normed * gain[1, 1:2] + bias[1, 1:2]).astype(BF)
    send_qkv(send, attn_in, w_qkv, b_qkv, 1, cs)
    g_b = cot[...].astype(BF)
    d_ctx = mm(w_out[...], g_b, 1, 1)
    for s in range(2):
        for h in range(4):
            send[s * 4 + h, 3 * HEAD : 4 * HEAD, :] = d_ctx[
                h * HEAD : (h + 1) * HEAD, s * BLK : (s + 1) * BLK
            ].astype(BF)
    d_sum[...] = jnp.sum(cot[...], 0, keepdims=True)
    parts[0:256] = feed_forward(mlp_in, w_up, b_up, 1, w_down, act, slope).astype(BF)
    parts[256:512] = feed_back(
        g_b, act, slope, mlp_in, w_up, w_down, pack_up(grads, 0), pack_down(grads, 256), d_b_up
    ).astype(BF)


def norm_back(
    t, x, g, d_mlp_in, recv, row, w_own, others, cs, gain, bias, layer, d_qkv, d_b_qkv, d_norm
):
    normed, inv = norm_rows(x)
    attn_in = (normed * gain[layer, 0:1] + bias[layer, 0:1]).astype(BF)
    attn_t = attn_in.T
    d_attn_t = None
    for e in range(3):
        halves = []
        for tt in range(2):
            blocks = []
            for h in range(4):
                pieces = []
                for s in range(2):
                    lo = row + e * HEAD
                    u = recv[s * 4 + h, tt, lo : lo + HEAD, :]
                    if e < 2:
                        u = turn_back(u.astype(F32), cs[s, 0], cs[s, 1]).astype(BF)
                    pieces.append(u)
                blocks.append(jnp.concatenate(pieces, 1))
            halves.append(jnp.concatenate(blocks, 0))
        first, second = ordered(t, w_own[e], others[e])
        term = mm(first, halves[0]) + mm(second, halves[1])
        d_attn_t = term if d_attn_t is None else d_attn_t + term
        own = jnp.where(t == 0, halves[0], halves[1])
        d_qkv(e, mm(attn_t, own, 1, 1))
        d_b_qkv[e : e + 1] = mm(jnp.ones((8, own.shape[1]), BF), own, 1, 1)[0:1]
    d_attn_in = d_attn_t.T
    d_norm[0:1] = jnp.sum(d_attn_in * normed, 0, keepdims=True)
    d_norm[1:2] = jnp.sum(d_mlp_in * normed, 0, keepdims=True)
    d_norm[2:3] = jnp.sum(d_attn_in, 0, keepdims=True)
    d_norm[3:4] = jnp.sum(d_mlp_in, 0, keepdims=True)
    d_normed = d_attn_in * gain[layer, 0:1] + d_mlp_in * gain[layer, 1:2]
    return g + inv * (
        d_normed
        - jnp.mean(d_normed, -1, keepdims=True)
        - normed * jnp.mean(d_normed * normed, -1, keepdims=True)
    )


def turn_point_body(
    at, stream, parts, parts_other, recv, w_out, w_qkv, others, out_bias,
    gain, bias, cot, cs, x, act, slope, w_up, w_down, w_out_first, recv_first, sums_a,
    block_out, g_out, send, grads, part, d_b_up, d_b_qkv, d_norm, d_sum,
):
    t = at[1]
    branch = parts[0:256].astype(F32) + parts_other[0:256].astype(F32)
    branch = branch + branch_of(t, recv, w_out[...], out_other(others))
    block_out[...] = stream[...] + branch + out_bias[1, 0:1] + out_bias[1, 1:2]
    d_mlp_in = parts[256:512].astype(F32) + parts_other[256:512].astype(F32)
    g = norm_back(
        t, stream[...], cot[...], d_mlp_in, recv, HEAD, w_qkv, others, cs, gain, bias, 1,
        pack_qkv(grads, 0), d_b_qkv, d_norm,
    )
    g_out[...] = g
    g_b = g.astype(BF)
    d_sum[...] = jnp.sum(g, 0, keepdims=True)
    d_ctx = mm(w_out_first[...], g_b, 1, 1)
    for s in range(2):
        for h in range(4):
            send[s * 4 + h, 0:HEAD] = d_ctx[
                h * HEAD : (h + 1) * HEAD, s * BLK : (s + 1) * BLK
            ].astype(BF)
    for q in range(8):
        for c in range(2):
            send[q, 64 + 64 * c : 128 + 64 * c] = sums_a[
                64 * q : 64 * (q + 1), BLK * c : BLK * (c + 1)
            ]
    pack_out(grads, 704, own_ctx(t, recv), cot[...].astype(BF))
    pack_out(grads, 768, own_ctx(t, recv_first), g_b)
    normed, _ = norm_rows(x[...])
    mlp_in = (normed * gain[0, 1:2] + bias[0, 1:2]).astype(BF)
    part[...] = feed_back(
        g_b, act, slope, mlp_in, w_up, w_down, pack_up(grads, 192), pack_down(grads, 448), d_b_up
    ).astype(BF)


def last_body(
    at, x, g, part, part_other, recv, w_qkv, others, cs, gain, bias,
    d_b_up0, d_b_up1, d_b_qkv1, d_norm1, d_sum0, d_sum1,
    in_grad, grads, sums_a, d_b_qkv0, d_norm0,
):
    d_mlp_in = part[...].astype(F32) + part_other[...].astype(F32)
    in_grad[...] = norm_back(
        at[1], x[...], g[...], d_mlp_in, recv, 0, w_qkv, others, cs, gain, bias, 0,
        pack_qkv(grads, 0), d_b_qkv0, d_norm0,
    )
    for q in range(8):
        both_planes = recv[q, :, 192:320]
        block = jnp.where(at[1] == 0, both_planes[0], both_planes[1])
        for c in range(2):
            sums_a[64 * q : 64 * (q + 1), BLK * c : BLK * (c + 1)] = block[64 * c : 64 * (c + 1)]

    def lanes(ref, row, count):
        return [ref[row : row + 1, 256 * c : 256 * (c + 1)] for c in range(count)]

    def norms(ref):
        return [v for r in range(4) for v in lanes(ref, r, 2)]

    rows = [
        lanes(d_b_up0, 0, 4)
        + lanes(d_b_up1, 0, 4)
        + [v for e in range(3) for ref in (d_b_qkv0, d_b_qkv1) for v in lanes(ref, e, 1)],
        lanes(d_sum0, 0, 2) + lanes(d_sum1, 0, 2) + norms(d_norm0),
        norms(d_norm1),
    ]
    for p in range(8):
        have = rows[p] if p < len(rows) else []
        fill = [jnp.zeros((16 - len(have), 256), F32)]
        grads[p, 192:208, :] = jnp.concatenate(have + fill, 0).astype(BF)


def chunk_body(at, w_qkv, w_out, out):
    for layer in range(2):
        for e in range(3):
            out[layer, e] = w_qkv[layer, e]
        out[layer, 3, 0:32] = w_out[layer, :, 0:256]
        out[layer, 3, 32:64] = w_out[layer, :, 256:512]


def chunk_of(at, wq, w_out):
    return pl.pallas_call(
        chunk_body,
        out_shape=jax.ShapeDtypeStruct((2, 4, 64, 256), BF),
        grid_spec=pltpu.PrefetchScalarGridSpec(
            num_scalar_prefetch=1,
            grid=(1,),
            in_specs=[
                pl.BlockSpec((2, 3, 64, 256), lambda i, at: (0, 0, at[2], 0)),
                pl.BlockSpec((2, 32, 512), lambda i, at: (0, at[2], 0)),
            ],
            out_specs=pl.BlockSpec((2, 4, 64, 256), lambda i, at: (0, 0, 0, 0)),
        ),
        compiler_params=pltpu.CompilerParams(vmem_limit_bytes=40 * 1024 * 1024),
        name="chunk",
    )(at, far(wq), far(w_out))


def hand_on_body(value, _, out):
    out[...] = value[...]


def mix_body(got, early, first, out, first_out):
    total = got[0].astype(F32)
    for i in range(1, 8):
        total = total + got[i].astype(F32)
    for q in range(8):
        tiny = total[192 + 8 * q : 200 + 8 * q] if q < 2 else jnp.zeros((8, 256), F32)
        mine = [early[104 * q : 104 * (q + 1)].astype(F32), total[24 * q : 24 * (q + 1)], tiny]
        out[q] = jnp.concatenate(mine, 0).astype(BF)
    first_out[...] = first[...]


def sum_body(got, out):
    total = got[0].astype(F32)
    for i in range(1, 8):
        total = total + got[i].astype(F32)
    for q in range(8):
        out[q] = total.astype(BF)


def unpack_first_body(first, g_up, g_down):
    for k in range(4):
        for c in range(4):
            cols = slice(256 * c, 256 * (c + 1))
            g_up[0, 64 * k : 64 * (k + 1), cols] = first[k, 64 * c : 64 * (c + 1)].astype(F32)
        for c in range(2):
            rows = first[k, 256 + 128 * c : 256 + 128 * (c + 1)]
            cols = slice(256 * c, 256 * (c + 1))
            g_down[0, 128 * k : 128 * (k + 1), cols] = rows.astype(F32)


def unpack_rest_body(rest, _, __, g_up, g_down, g_qkv, g_out, g_b_up, g_b_qkv, g_sum, g_gain, g_bias):
    p = pl.program_id(0)
    for k in range(4):
        for q in range(8):
            block = rest[k, q].astype(F32)
            for i in range(16):
                value = block[8 * i : 8 * (i + 1)]
                row = 104 * q + 8 * i
                if i >= 13:
                    row = 24 * q + 8 * (i - 13)
                    r = 64 * k + row % 64
                    g_qkv[0, row // 64, r : r + 8] = value
                elif row < 192:
                    r = 64 * k + row % 64
                    g_qkv[1, row // 64, r : r + 8] = value
                elif row < 448:
                    c, r = divmod(row - 192, 64)
                    r += 64 * k
                    g_up[0, r : r + 8, 256 * c : 256 * (c + 1)] = value
                elif row < 704:
                    c, r = divmod(row - 448, 128)
                    r += 128 * k
                    g_down[0, r : r + 8, 256 * c : 256 * (c + 1)] = value
                else:
                    c, r = divmod((row - 704) % 64, 32)
                    r += 32 * k
                    g_out[1 - (row - 704) // 64, r : r + 8, 256 * c : 256 * (c + 1)] = value

    tiny = [jnp.concatenate([rest[k, q].astype(F32)[128:136] for q in range(2)], 0) for k in range(3)]

    @pl.when(p == 0)
    def _():
        for layer in range(2):
            for c in range(4):
                r = 4 * layer + c
                g_b_up[layer : layer + 1, 256 * c : 256 * (c + 1)] = tiny[0][r : r + 1]
        for e in range(3):
            for layer in range(2):
                r = 8 + 2 * e + layer
                g_b_qkv[e, layer : layer + 1, :] = tiny[0][r : r + 1]
        for layer in range(2):
            for c in range(2):
                r = 2 * layer + c
                for which in range(2):
                    g_sum[layer, which : which + 1, 256 * c : 256 * (c + 1)] = tiny[1][r : r + 1]

    def norms(layer, rows, base):
        for which in range(2):
            for c in range(2):
                cols = slice(256 * c, 256 * (c + 1))
                r = base + 2 * which + c
                g_gain[layer, which : which + 1, cols] = rows[r : r + 1]
                g_bias[layer, which : which + 1, cols] = rows[r + 4 : r + 5]

    @pl.when(p == 0)
    def _():
        norms(0, tiny[1], 4)
        norms(1, tiny[2], 0)


UP = (2, 512, 1024)
DOWN = (2, 1024, 512)


def unpack(first, rest):
    def place(layer):
        return [
            pl.BlockSpec((1, 256, 1024), lambda p: (layer, p, 0)),
            pl.BlockSpec((1, 512, 512), lambda p: (layer, p, 0)),
        ]

    params = pltpu.CompilerParams(vmem_limit_bytes=40 * 1024 * 1024)
    g_up, g_down = pl.pallas_call(
        unpack_first_body,
        grid=(2,),
        out_shape=[pltpu.HBM(UP, F32), pltpu.HBM(DOWN, F32)],
        in_specs=[pl.BlockSpec((4, 512, 256), lambda p: (p, 0, 0))],
        out_specs=place(1),
        compiler_params=params,
        name="unpack_first",
    )(far(first))
    outs = [
        ((2, 3, 512, 256), pl.BlockSpec((2, 3, 256, 256), lambda p: (0, 0, p, 0))),
        ((2, 256, 512), pl.BlockSpec((2, 128, 512), lambda p: (0, p, 0))),
        ((2, 1024), whole((2, 1024))),
        ((3, 2, 256), whole((3, 2, 256))),
        ((2, 2, 512), whole((2, 2, 512))),
        ((2, 2, 512), whole((2, 2, 512))),
        ((2, 2, 512), whole((2, 2, 512))),
    ]
    return pl.pallas_call(
        unpack_rest_body,
        grid=(2,),
        out_shape=[pltpu.HBM(shape, F32) for shape in [UP, DOWN] + [o[0] for o in outs]],
        in_specs=[
            pl.BlockSpec((4, 8, 136, 256), lambda p: (p, 0, 0, 0)),
            pl.BlockSpec(memory_space=pl.ANY),
            pl.BlockSpec(memory_space=pl.ANY),
        ],
        out_specs=place(0) + [spec for _, spec in outs],
        input_output_aliases={1: 0, 2: 1},
        compiler_params=params,
        name="unpack_rest",
    )(far(rest), far(g_up), far(g_down))


def swap(value):
    return lax.ppermute(value, "tensor", [(0, 1), (1, 0)])


def exchange(value, axes):
    return lax.all_to_all(value, axes, 0, 0)


def both(value):
    flat = value.reshape((16,) + value.shape[2:])
    return exchange(flat, ("context", "tensor")).reshape(value.shape)


def shards(
    tokens_in, cotangent, positions, w_qkv, b_qkv, w_out, w_up, b_up, w_down, out_bias, ln_gain, ln_bias
):
    rows, width = 256, 512
    x = tokens_in.reshape(rows, width)
    cot = cotangent.reshape(rows, width)
    wq = jnp.transpose(w_qkv, (0, 2, 1, 3))
    bq = jnp.transpose(b_qkv, (1, 0, 2))
    at = jnp.stack(
        [lax.axis_index("context"), lax.axis_index("tensor"), lax.axis_index("dp")]
    ).astype(jnp.int32)
    freqs = jnp.asarray(FREQS).reshape(HALF, 1)
    chunk = swap(chunk_of(at, wq, w_out))
    send, pair, act, slope, cs = call(
        first_body,
        [
            pltpu.VMEM((8, 208, BLK), BF),
            ((2 * rows, width), BF),
            pltpu.HBM((rows, 1024), BF),
            pltpu.HBM((rows, 1024), BF),
            ((2, 2, HALF, BLK), F32),
        ],
        (
            at, positions, freqs, Far(x), ln_gain, ln_bias, Layer(wq, 0), bq, Layer(w_up, 0), b_up,
            Layer(w_down, 0), Layer(w_out, 0),
        ),
        "norm_qkv_feed",
        smem_first=True,
    )
    pair_other = swap(pair)
    (chunk,) = call(
        hand_on_body, [pltpu.HBM(chunk.shape, BF)], (chunk, After(send)), "hand_on"
    )
    others = lax.all_gather(chunk, "dp", axis=2, tiled=True)
    recv = exchange(send, "context")
    ctx_send, lse, ctx, start = call(
        attend_body,
        [((8, 2, HEAD, BLK), BF), ((1, 1024), F32), pltpu.HBM((HEAD, 1024), F32), ((1, 1024), jnp.int32)],
        (recv,),
        "attend",
    )
    recv_ctx = both(ctx_send)
    stream, send, grads_a, parts, d_b_up1, d_sum1 = call(
        middle_body,
        [
            pltpu.HBM((rows, width), F32),
            ((8, 256, BLK), BF),
            pltpu.HBM((8, 512, 256), BF),
            ((2 * rows, width), BF),
            ((1, 1024), F32),
            ((1, width), F32),
        ],
        (
            at, Far(x), pair, pair_other, recv_ctx, Layer(w_out, 0), out_bias, ln_gain, ln_bias,
            Layer(wq, 1), bq, Layer(w_up, 1), b_up, Layer(w_down, 1), Layer(w_out, 1), Far(cot), cs,
        ),
        "middle",
        scratch=[pltpu.VMEM((rows, 1024), BF), pltpu.VMEM((rows, 1024), BF)],
        smem_first=True,
    )
    sums_a = lax.psum_scatter(grads_a, "dp", scatter_dimension=0)
    parts_other = swap(parts)
    recv_both = exchange(send, "context")
    (both_send,) = call(
        attend_both_body,
        [((8, 2, 256, BLK), BF)],
        (recv_both, start, After(parts_other)),
        "attend_both",
        scratch=[pltpu.VMEM((HEAD, 1024), F32), pltpu.VMEM((HEAD, 1024), F32)],
    )
    recv_grad = both(both_send)
    block_out, g, send, grads_b, part_g, d_b_up0, d_b_qkv1, d_norm1, d_sum0 = call(
        turn_point_body,
        [
            pltpu.HBM((rows, width), F32),
            pltpu.HBM((rows, width), F32),
            pltpu.VMEM((8, 192, BLK), BF),
            pltpu.HBM((8, 832, 256), BF),
            ((rows, width), BF),
            ((1, 1024), F32),
            ((3, 256), F32),
            ((4, width), F32),
            ((1, width), F32),
        ],
        (
            at, Far(stream), parts, parts_other, recv_grad, Layer(w_out, 1), Layer(wq, 1),
            Layer(others, 1), out_bias, ln_gain, ln_bias, Far(cot), cs, Far(x), Far(act), Far(slope),
            Layer(w_up, 0), Layer(w_down, 0), Layer(w_out, 0), recv_ctx, Far(sums_a),
        ),
        "turn_point",
        smem_first=True,
    )
    sums_b = lax.psum_scatter(grads_b, "dp", scatter_dimension=0)
    part_g_other = swap(part_g)
    recv_d = exchange(send, "context")
    (back_send,) = call(
        attend_back_body,
        [((8, 2, 320, BLK), BF)],
        (recv, recv_d, start, lse, ctx, After(part_g_other)),
        "attend_back",
        scratch=[pltpu.VMEM((HEAD, 1024), F32), pltpu.VMEM((HEAD, 1024), F32)],
    )
    recv_grad0 = both(back_send)
    in_grad, grads_c, sums_a, _, _ = call(
        last_body,
        [
            pltpu.HBM((rows, width), F32),
            ((8, 208, 256), BF),
            pltpu.HBM((512, 256), BF),
            ((3, 256), F32),
            ((4, width), F32),
        ],
        (
            at, Far(x), Far(g), part_g, part_g_other, recv_grad0, Layer(wq, 0), Layer(others, 0), cs,
            ln_gain, ln_bias, d_b_up0, d_b_up1, d_b_qkv1, d_norm1, d_sum0, d_sum1,
        ),
        "last",
        smem_first=True,
    )
    mixed, sums_a = call(
        mix_body,
        [((8, 136, 256), BF), pltpu.HBM((512, 256), BF)],
        (exchange(grads_c, "dp"), Far(sums_b), Far(sums_a)),
        "mix",
    )
    full_a = lax.all_gather(sums_a, "dp")
    (summed,) = call(sum_body, [((8, 136, 256), BF)], (exchange(mixed, "context"),), "sum")
    full_bc = lax.all_gather(exchange(summed, "context"), "dp")
    g_up, g_down, g_qkv, g_out, g_b_up, g_b_qkv, g_sum, g_gain, g_bias = unpack(full_a, full_bc)
    return (
        block_out.reshape(tokens_in.shape),
        in_grad.reshape(tokens_in.shape),
        jnp.transpose(g_qkv, (0, 2, 1, 3)),
        jnp.transpose(g_b_qkv, (1, 0, 2)),
        g_out,
        g_up,
        g_b_up,
        g_down,
        g_sum,
        g_gain,
        g_bias,
    )


def solution(mesh):
    return jax.shard_map(
        shards,
        mesh=mesh,
        in_specs=(
            P("dp", "context", None),
            P("dp", "context", None),
            P("dp", "context"),
            P(None, None, None, "tensor"),
            P(None, None, "tensor"),
            P(None, "tensor", None),
            P(None, None, "tensor"),
            P(None, "tensor"),
            P(None, "tensor", None),
            P(),
            P(),
            P(),
        ),
        out_specs=(
            P("dp", "context", None),
            P("dp", "context", None),
            P(None, None, None, "tensor"),
            P(None, None, "tensor"),
            P(None, "tensor", None),
            P(None, None, "tensor"),
            P(None, "tensor"),
            P(None, "tensor", None),
            P(),
            P(),
            P(),
        ),
        check_vma=False,
    )
```

```python
from functools import partial

import numpy as np

import jax
import jax.numpy as jnp
from jax import lax
from jax.experimental import pallas as pl
from jax.experimental.pallas import tpu as pltpu
from jax.sharding import PartitionSpec as P

EPS = 1e-05
HALF = 8
HEAD = 64
BLK = 128
CHUNK = 256
NEG = -1e30
BF = jnp.bfloat16
F32 = jnp.float32

FREQS = (10000.0 ** (-np.arange(HALF, dtype=np.float64) * 2.0 / 16.0)).astype(np.float32)


def mm(a, b, ca=1, cb=0):
    return lax.dot_general(a, b, (((ca,), (cb,)), ((), ())), preferred_element_type=F32)


class After:
    def __init__(self, array):
        self.array = array

    def spec(self):
        return pl.BlockSpec(memory_space=pl.ANY)


class Layer:
    def __init__(self, array, index):
        self.array, self.index = far(array), index

    def spec(self):
        rest = self.array.shape[1:]
        place = (self.index,) + (0,) * len(rest)
        return pl.BlockSpec((None,) + rest, lambda i: place)


class Far:
    def __init__(self, array):
        self.array = far(array)

    def spec(self):
        return whole(self.array.shape)


Kept = type(pltpu.HBM((8, 128), F32))


def far(array):
    return pltpu.with_memory_space_constraint(array, pltpu.HBM)


def whole(shape):
    return pl.BlockSpec(shape, lambda i: (0,) * len(shape))


def call(body, out_shape, args, name, scratch=(), smem_first=False):
    specs = [
        a.spec() if isinstance(a, (Layer, Far, After)) else whole(a.shape) for a in args
    ]
    args = [a.array if isinstance(a, (Layer, Far, After)) else a for a in args]
    if smem_first:
        specs[0] = pl.BlockSpec(memory_space=pltpu.SMEM)
    return pl.pallas_call(
        body,
        grid=(1,),
        out_shape=[o if isinstance(o, Kept) else jax.ShapeDtypeStruct(*o) for o in out_shape],
        in_specs=specs,
        out_specs=[whole(o.shape if isinstance(o, Kept) else o[0]) for o in out_shape],
        scratch_shapes=list(scratch),
        compiler_params=pltpu.CompilerParams(vmem_limit_bytes=40 * 1024 * 1024),
        name=name,
    )(*args)


def norm_rows(x):
    mean = jnp.mean(x, -1, keepdims=True)
    cen = x - mean
    inv = lax.rsqrt(jnp.mean(cen * cen, -1, keepdims=True) + EPS)
    return cen * inv, inv


def turn(t, cos, sin):
    a, b = t[:HALF], t[HALF : 2 * HALF]
    return jnp.concatenate([a * cos - b * sin, b * cos + a * sin, t[2 * HALF :]], 0)


def turn_back(u, cos, sin):
    a, b = u[:HALF], u[HALF : 2 * HALF]
    return jnp.concatenate([a * cos + b * sin, b * cos - a * sin, u[2 * HALF :]], 0)


def send_qkv(send, attn_in, w_qkv, b_qkv, layer, cs):
    for e in range(3):
        turned = (mm(attn_in, w_qkv[e]) + b_qkv[e, layer : layer + 1]).T
        for s in range(2):
            cos, sin = cs[s, 0], cs[s, 1]
            for h in range(4):
                j = s * 4 + h
                part = turned[h * HEAD : (h + 1) * HEAD, s * BLK : (s + 1) * BLK]
                if e < 2:
                    part = turn(part, cos, sin)
                if e == 0:
                    part = part * (HEAD**-0.5)
                send[j, e * HEAD : (e + 1) * HEAD, :] = part.astype(BF)


def feed_forward(mlp_in, w_up, b_up, layer, w_down, act, slope):
    width = w_up.shape[1]
    total = None
    for c in range(0, width, 256):
        cols = slice(c, c + 256)
        pre = mm(mlp_in, w_up[:, cols]) + b_up[layer : layer + 1, cols]
        cdf = 0.5 + 0.5 * lax.erf(pre * np.float32(0.7071067811865476))
        a = (pre * cdf).astype(BF)
        act[:, cols] = a
        tail = pre * (jnp.exp(-0.5 * pre * pre) * np.float32(0.3989422804014327))
        slope[:, cols] = (cdf + tail).astype(BF)
        term = mm(a, w_down[cols, :])
        total = term if total is None else total + term
    return total


def feed_back(g_b, act, slope, mlp_in, w_up, w_down, d_up, d_down, d_b_up):
    width = w_up.shape[1]
    total = None
    mlp_t = mlp_in.T
    for c in range(0, width, 256):
        cols = slice(c, c + 256)
        d_act = mm(g_b, w_down[cols, :], 1, 1)
        d_pre = d_act * slope[:, cols].astype(F32)
        d_pre_b = d_pre.astype(BF)
        d_b_up[:, cols] = jnp.sum(d_pre_b.astype(F32), 0, keepdims=True)
        d_up(c // 256, mm(mlp_t, d_pre_b))
        d_down(c, mm(act[:, cols].T, g_b))
        term = mm(d_pre_b, w_up[:, cols], 1, 1)
        total = term if total is None else total + term
    return total


def pack_up(out, row):
    def put(c, value):
        for p in range(8):
            out[p, row + 64 * c : row + 64 * (c + 1), :] = value[64 * p : 64 * (p + 1)].astype(BF)

    return put


def pack_down(out, row):
    def put(c, value):
        for half in range(2):
            for k in range(2):
                out[c // 128 + k, row + 128 * half : row + 128 * (half + 1), :] = value[
                    128 * k : 128 * (k + 1), 256 * half : 256 * (half + 1)
                ].astype(BF)

    return put


def pack_qkv(out, row):
    def put(e, value):
        for p in range(8):
            out[p, row + 64 * e : row + 64 * (e + 1), :] = value[64 * p : 64 * (p + 1)].astype(BF)

    return put


def own_ctx(t, recv):
    full = jnp.concatenate([gather_ctx(recv, s) for s in range(2)], 1)
    return jnp.where(t == 0, full[0:256], full[256:512])


def pack_out(out, row, ctx, upstream):
    value = mm(ctx, upstream)
    for p in range(8):
        for half in range(2):
            out[p, row + 32 * half : row + 32 * (half + 1), :] = value[
                32 * p : 32 * (p + 1), 256 * half : 256 * (half + 1)
            ].astype(BF)


def first_body(
    at, pos, freqs, x, gain, bias, w_qkv, b_qkv, w_up, b_up, w_down, w_out,
    send, pair, act, slope, cs,
):
    pair[256:512] = w_out[...]
    for s in range(2):
        p = pos[s : s + 1, :].astype(F32)
        angle = freqs[...] * p
        cs[s, 0] = jnp.cos(angle)
        cs[s, 1] = jnp.sin(angle)
    normed, _ = norm_rows(x[...])
    attn_in = (normed * gain[0, 0:1] + bias[0, 0:1]).astype(BF)
    mlp_in = (normed * gain[0, 1:2] + bias[0, 1:2]).astype(BF)
    send_qkv(send, attn_in, w_qkv, b_qkv, 0, cs)
    row = lax.broadcasted_iota(jnp.int32, (16, BLK), 0)
    token = at[0] * BLK + lax.broadcasted_iota(jnp.int32, (1, BLK), 1)
    for s in range(2):
        start = jnp.maximum(token - pos[s : s + 1, :], 0)
        high = (start // 8).astype(F32)
        low = (start % 8).astype(F32)
        block = jnp.where(row == 0, high, jnp.where(row == 1, low, 0.0)).astype(BF)
        for h in range(4):
            send[s * 4 + h, 3 * HEAD : 3 * HEAD + 16, :] = block
    pair[0:256] = feed_forward(mlp_in, w_up, b_up, 0, w_down, act, slope).astype(BF)


def load_rows(recv, lo, hi):
    return jnp.concatenate([recv[i, lo:hi, :] for i in range(8)], 1)


def starts_of(recv):
    rows = load_rows(recv, 3 * HEAD, 3 * HEAD + 16).astype(F32)
    return rows[0:1] * 8.0 + rows[1:2]


def visible_of(start, c, length):
    key = lax.broadcasted_iota(jnp.int32, (length, CHUNK), 0)
    query = lax.broadcasted_iota(jnp.int32, (length, CHUNK), 1) + c * CHUNK
    return (key <= query) & (key >= start[:, c * CHUNK : (c + 1) * CHUNK])


def attend_body(recv, send, lse, ctx, start_out):
    q = load_rows(recv, 0, HEAD)
    k_t = load_rows(recv, HEAD, 2 * HEAD)
    v_t = load_rows(recv, 2 * HEAD, 3 * HEAD)
    k = k_t.T
    start = starts_of(recv).astype(jnp.int32)
    start_out[...] = start
    for c in range(4):
        cols = slice(c * CHUNK, (c + 1) * CHUNK)
        length = (c + 1) * CHUNK
        scores = mm(k[:length], q[:, cols])
        scores = jnp.where(visible_of(start, c, length), scores, NEG)
        peak = jnp.max(scores, 0, keepdims=True)
        shifted = jnp.exp(scores - peak)
        total = jnp.sum(shifted, 0, keepdims=True)
        lse[:, cols] = peak + jnp.log(total)
        out = mm(v_t[:, :length], shifted.astype(BF)) / total
        ctx[:, cols] = out
        for i in range(CHUNK // BLK):
            block = out[:, i * BLK : (i + 1) * BLK].astype(BF)
            for t in range(2):
                send[c * (CHUNK // BLK) + i, t] = block


def attend_both_body(recv, start, _, send, dk, dv):
    q = load_rows(recv, 0, HEAD)
    k_t = load_rows(recv, HEAD, 2 * HEAD)
    v_t = load_rows(recv, 2 * HEAD, 3 * HEAD)
    d_ctx = load_rows(recv, 3 * HEAD, 4 * HEAD)
    k = k_t.T
    v = v_t.T
    dk[...] = jnp.zeros_like(dk)
    dv[...] = jnp.zeros_like(dv)
    for c in range(4):
        cols = slice(c * CHUNK, (c + 1) * CHUNK)
        length = (c + 1) * CHUNK
        scores = mm(k[:length], q[:, cols])
        scores = jnp.where(visible_of(start[...], c, length), scores, NEG)
        peak = jnp.max(scores, 0, keepdims=True)
        shifted = jnp.exp(scores - peak)
        probs = shifted * (1.0 / jnp.sum(shifted, 0, keepdims=True))
        probs_b = probs.astype(BF)
        out = mm(v_t[:, :length], probs_b)
        dq = backward_chunk(q, k_t, v, d_ctx, probs, probs_b, out, cols, length, dk, dv)
        for i in range(CHUNK // BLK):
            b = c * (CHUNK // BLK) + i
            for t in range(2):
                send[b, t, 0:HEAD] = out[:, i * BLK : (i + 1) * BLK].astype(BF)
                send[b, t, HEAD : 2 * HEAD] = dq[:, i * BLK : (i + 1) * BLK].astype(BF)
    put_kv(send, dk, dv, 2 * HEAD)


def backward_chunk(q, k_t, v, d_ctx, probs, probs_b, out, cols, length, dk, dv):
    d_out = d_ctx[:, cols]
    d_probs = mm(v[:length], d_out)
    delta = jnp.sum(d_out.astype(F32) * out, 0, keepdims=True)
    d_scores = (probs * (d_probs - delta)).astype(BF)
    dk[:, :length] += mm(q[:, cols], d_scores, 1, 1)
    dv[:, :length] += mm(d_out, probs_b, 1, 1)
    return mm(k_t[:, :length], d_scores) * (HEAD**-0.5)


def put_kv(send, dk, dv, row):
    for b in range(8):
        for t in range(2):
            send[b, t, row : row + HEAD] = dk[:, b * BLK : (b + 1) * BLK].astype(BF)
            send[b, t, row + HEAD : row + 2 * HEAD] = dv[:, b * BLK : (b + 1) * BLK].astype(BF)


def attend_back_body(recv, recv_d, start, lse, ctx, _, send, dk, dv):
    ride = recv_d[0, 64:192].astype(F32)
    for i in range(1, 8):
        ride = ride + recv_d[i, 64:192].astype(F32)
    ride = ride.astype(BF)
    for b in range(8):
        for t in range(2):
            send[b, t, 192:320] = ride
    q = load_rows(recv, 0, HEAD)
    k_t = load_rows(recv, HEAD, 2 * HEAD)
    v_t = load_rows(recv, 2 * HEAD, 3 * HEAD)
    d_ctx = load_rows(recv_d, 0, HEAD)
    k = k_t.T
    v = v_t.T
    dk[...] = jnp.zeros_like(dk)
    dv[...] = jnp.zeros_like(dv)
    for c in range(4):
        cols = slice(c * CHUNK, (c + 1) * CHUNK)
        length = (c + 1) * CHUNK
        scores = mm(k[:length], q[:, cols])
        scores = jnp.where(visible_of(start[...], c, length), scores, NEG)
        probs = jnp.exp(scores - lse[:, cols])
        probs_b = probs.astype(BF)
        dq = backward_chunk(q, k_t, v, d_ctx, probs, probs_b, ctx[:, cols], cols, length, dk, dv)
        for i in range(CHUNK // BLK):
            for t in range(2):
                send[c * (CHUNK // BLK) + i, t, 0:HEAD] = dq[:, i * BLK : (i + 1) * BLK].astype(BF)
    put_kv(send, dk, dv, HEAD)


def gather_ctx(recv, s):
    return jnp.concatenate([recv[s * 4 + h, t, 0:HEAD, :] for t in range(2) for h in range(4)], 0)


def ordered(t, own, other):
    return jnp.where(t == 0, own, other), jnp.where(t == 0, other, own)


def out_other(others):
    halves = [
        jnp.concatenate([others[3, 64 * p + 32 * c : 64 * p + 32 * (c + 1), :] for p in range(8)], 0)
        for c in range(2)
    ]
    return jnp.concatenate(halves, 1)


def branch_of(t, recv, w_own, w_other):
    first, second = ordered(t, w_own, w_other)
    w = jnp.concatenate([first, second], 0)
    rows = []
    for s in range(2):
        rows.append(mm(gather_ctx(recv, s).T, w))
    return jnp.concatenate(rows, 0)


def middle_body(
    at, x, pair, pair_other, recv, w_out_own, out_bias, gain, bias,
    w_qkv, b_qkv, w_up, b_up, w_down, w_out, cot, cs,
    stream, send, grads, parts, d_b_up, d_sum, act, slope,
):
    branch = pair[0:256].astype(F32) + pair_other[0:256].astype(F32)
    branch = branch + branch_of(at[1], recv, w_out_own[...], pair_other[256:512])
    out = x[...] + branch + out_bias[0, 0:1] + out_bias[0, 1:2]
    stream[...] = out
    normed, _ = norm_rows(out)
    attn_in = (normed * gain[1, 0:1] + bias[1, 0:1]).astype(BF)
    mlp_in = (normed * gain[1, 1:2] + bias[1, 1:2]).astype(BF)
    send_qkv(send, attn_in, w_qkv, b_qkv, 1, cs)
    g_b = cot[...].astype(BF)
    d_ctx = mm(w_out[...], g_b, 1, 1)
    for s in range(2):
        for h in range(4):
            send[s * 4 + h, 3 * HEAD : 4 * HEAD, :] = d_ctx[
                h * HEAD : (h + 1) * HEAD, s * BLK : (s + 1) * BLK
            ].astype(BF)
    d_sum[...] = jnp.sum(cot[...], 0, keepdims=True)
    parts[0:256] = feed_forward(mlp_in, w_up, b_up, 1, w_down, act, slope).astype(BF)
    parts[256:512] = feed_back(
        g_b, act, slope, mlp_in, w_up, w_down, pack_up(grads, 0), pack_down(grads, 256), d_b_up
    ).astype(BF)


def norm_back(
    t, x, g, d_mlp_in, recv, row, w_own, others, cs, gain, bias, layer, d_qkv, d_b_qkv, d_norm
):
    normed, inv = norm_rows(x)
    attn_in = (normed * gain[layer, 0:1] + bias[layer, 0:1]).astype(BF)
    attn_t = attn_in.T
    d_attn_t = None
    for e in range(3):
        halves = []
        for tt in range(2):
            blocks = []
            for h in range(4):
                pieces = []
                for s in range(2):
                    lo = row + e * HEAD
                    u = recv[s * 4 + h, tt, lo : lo + HEAD, :]
                    if e < 2:
                        u = turn_back(u.astype(F32), cs[s, 0], cs[s, 1]).astype(BF)
                    pieces.append(u)
                blocks.append(jnp.concatenate(pieces, 1))
            halves.append(jnp.concatenate(blocks, 0))
        first, second = ordered(t, w_own[e], others[e])
        term = mm(first, halves[0]) + mm(second, halves[1])
        d_attn_t = term if d_attn_t is None else d_attn_t + term
        own = jnp.where(t == 0, halves[0], halves[1])
        d_qkv(e, mm(attn_t, own, 1, 1))
        d_b_qkv[e : e + 1] = mm(jnp.ones((8, own.shape[1]), BF), own, 1, 1)[0:1]
    d_attn_in = d_attn_t.T
    d_norm[0:1] = jnp.sum(d_attn_in * normed, 0, keepdims=True)
    d_norm[1:2] = jnp.sum(d_mlp_in * normed, 0, keepdims=True)
    d_norm[2:3] = jnp.sum(d_attn_in, 0, keepdims=True)
    d_norm[3:4] = jnp.sum(d_mlp_in, 0, keepdims=True)
    d_normed = d_attn_in * gain[layer, 0:1] + d_mlp_in * gain[layer, 1:2]
    return g + inv * (
        d_normed
        - jnp.mean(d_normed, -1, keepdims=True)
        - normed * jnp.mean(d_normed * normed, -1, keepdims=True)
    )


def turn_point_body(
    at, stream, parts, parts_other, recv, w_out, w_qkv, others, out_bias,
    gain, bias, cot, cs, x, act, slope, w_up, w_down, w_out_first, recv_first, sums_a,
    block_out, g_out, send, grads, part, d_b_up, d_b_qkv, d_norm, d_sum,
):
    t = at[1]
    branch = parts[0:256].astype(F32) + parts_other[0:256].astype(F32)
    branch = branch + branch_of(t, recv, w_out[...], out_other(others))
    block_out[...] = stream[...] + branch + out_bias[1, 0:1] + out_bias[1, 1:2]
    d_mlp_in = parts[256:512].astype(F32) + parts_other[256:512].astype(F32)
    g = norm_back(
        t, stream[...], cot[...], d_mlp_in, recv, HEAD, w_qkv, others, cs, gain, bias, 1,
        pack_qkv(grads, 0), d_b_qkv, d_norm,
    )
    g_out[...] = g
    g_b = g.astype(BF)
    d_sum[...] = jnp.sum(g, 0, keepdims=True)
    d_ctx = mm(w_out_first[...], g_b, 1, 1)
    for s in range(2):
        for h in range(4):
            send[s * 4 + h, 0:HEAD] = d_ctx[
                h * HEAD : (h + 1) * HEAD, s * BLK : (s + 1) * BLK
            ].astype(BF)
    for q in range(8):
        for c in range(2):
            send[q, 64 + 64 * c : 128 + 64 * c] = sums_a[
                64 * q : 64 * (q + 1), BLK * c : BLK * (c + 1)
            ]
    pack_out(grads, 704, own_ctx(t, recv), cot[...].astype(BF))
    pack_out(grads, 768, own_ctx(t, recv_first), g_b)
    normed, _ = norm_rows(x[...])
    mlp_in = (normed * gain[0, 1:2] + bias[0, 1:2]).astype(BF)
    part[...] = feed_back(
        g_b, act, slope, mlp_in, w_up, w_down, pack_up(grads, 192), pack_down(grads, 448), d_b_up
    ).astype(BF)


def last_body(
    at, x, g, part, part_other, recv, w_qkv, others, cs, gain, bias,
    d_b_up0, d_b_up1, d_b_qkv1, d_norm1, d_sum0, d_sum1,
    in_grad, grads, sums_a, d_b_qkv0, d_norm0,
):
    d_mlp_in = part[...].astype(F32) + part_other[...].astype(F32)
    in_grad[...] = norm_back(
        at[1], x[...], g[...], d_mlp_in, recv, 0, w_qkv, others, cs, gain, bias, 0,
        pack_qkv(grads, 0), d_b_qkv0, d_norm0,
    )
    for q in range(8):
        both_planes = recv[q, :, 192:320]
        block = jnp.where(at[1] == 0, both_planes[0], both_planes[1])
        for c in range(2):
            sums_a[64 * q : 64 * (q + 1), BLK * c : BLK * (c + 1)] = block[64 * c : 64 * (c + 1)]

    def lanes(ref, row, count):
        return [ref[row : row + 1, 256 * c : 256 * (c + 1)] for c in range(count)]

    def norms(ref):
        return [v for r in range(4) for v in lanes(ref, r, 2)]

    rows = [
        lanes(d_b_up0, 0, 4)
        + lanes(d_b_up1, 0, 4)
        + [v for e in range(3) for ref in (d_b_qkv0, d_b_qkv1) for v in lanes(ref, e, 1)],
        lanes(d_sum0, 0, 2) + lanes(d_sum1, 0, 2) + norms(d_norm0),
        norms(d_norm1),
    ]
    for p in range(8):
        have = rows[p] if p < len(rows) else []
        fill = [jnp.zeros((16 - len(have), 256), F32)]
        grads[p, 192:208, :] = jnp.concatenate(have + fill, 0).astype(BF)


def chunk_body(at, w_qkv, w_out, out, buffer, sems):
    rows = pl.ds(pl.multiple_of(at[2] * 64, 64), 64)
    less = pl.ds(pl.multiple_of(at[2] * 32, 32), 32)
    copies = [
        pltpu.make_async_copy(w_qkv.at[:, :, rows], out.at[:, 0:3], sems.at[0]),
        pltpu.make_async_copy(w_out.at[:, less], buffer, sems.at[1]),
    ]
    for copy in copies:
        copy.start()
    for copy in copies:
        copy.wait()
    for layer in range(2):
        out[layer, 3, 0:32] = buffer[layer, :, 0:256]
        out[layer, 3, 32:64] = buffer[layer, :, 256:512]


def chunk_of(at, wq, w_out):
    return pl.pallas_call(
        chunk_body,
        out_shape=pltpu.VMEM((2, 4, 64, 256), BF),
        in_specs=[
            pl.BlockSpec(memory_space=pltpu.SMEM),
            pl.BlockSpec(memory_space=pltpu.HBM),
            pl.BlockSpec(memory_space=pltpu.HBM),
        ],
        out_specs=pl.BlockSpec(memory_space=pltpu.VMEM),
        scratch_shapes=[pltpu.VMEM((2, 32, 512), BF), pltpu.SemaphoreType.DMA((2,))],
        compiler_params=pltpu.CompilerParams(vmem_limit_bytes=40 * 1024 * 1024),
        name="chunk",
    )(at, far(wq), far(w_out))


def hand_on_body(value, _, out):
    out[...] = value[...]


def mix_body(got, early, first, out, first_out):
    total = got[0].astype(F32)
    for i in range(1, 8):
        total = total + got[i].astype(F32)
    for q in range(8):
        tiny = total[192 + 8 * q : 200 + 8 * q] if q < 2 else jnp.zeros((8, 256), F32)
        mine = [early[104 * q : 104 * (q + 1)].astype(F32), total[24 * q : 24 * (q + 1)], tiny]
        out[q] = jnp.concatenate(mine, 0).astype(BF)
    first_out[...] = first[...]


def sum_body(got, out):
    total = got[0].astype(F32)
    for i in range(1, 8):
        total = total + got[i].astype(F32)
    for q in range(8):
        out[q] = total.astype(BF)


def unpack_first_body(first, g_up, g_down):
    for k in range(4):
        for c in range(4):
            cols = slice(256 * c, 256 * (c + 1))
            g_up[0, 64 * k : 64 * (k + 1), cols] = first[k, 64 * c : 64 * (c + 1)].astype(F32)
        for c in range(2):
            rows = first[k, 256 + 128 * c : 256 + 128 * (c + 1)]
            cols = slice(256 * c, 256 * (c + 1))
            g_down[0, 128 * k : 128 * (k + 1), cols] = rows.astype(F32)


def unpack_rest_body(rest, _, __, g_up, g_down, g_qkv, g_out, g_b_up, g_b_qkv, g_sum, g_gain, g_bias):
    p = pl.program_id(0)
    for k in range(4):
        for q in range(8):
            block = rest[k, q].astype(F32)
            for i in range(16):
                value = block[8 * i : 8 * (i + 1)]
                row = 104 * q + 8 * i
                if i >= 13:
                    row = 24 * q + 8 * (i - 13)
                    r = 64 * k + row % 64
                    g_qkv[0, row // 64, r : r + 8] = value
                elif row < 192:
                    r = 64 * k + row % 64
                    g_qkv[1, row // 64, r : r + 8] = value
                elif row < 448:
                    c, r = divmod(row - 192, 64)
                    r += 64 * k
                    g_up[0, r : r + 8, 256 * c : 256 * (c + 1)] = value
                elif row < 704:
                    c, r = divmod(row - 448, 128)
                    r += 128 * k
                    g_down[0, r : r + 8, 256 * c : 256 * (c + 1)] = value
                else:
                    c, r = divmod((row - 704) % 64, 32)
                    r += 32 * k
                    g_out[1 - (row - 704) // 64, r : r + 8, 256 * c : 256 * (c + 1)] = value

    tiny = [jnp.concatenate([rest[k, q].astype(F32)[128:136] for q in range(2)], 0) for k in range(3)]

    @pl.when(p == 0)
    def _():
        for layer in range(2):
            for c in range(4):
                r = 4 * layer + c
                g_b_up[layer : layer + 1, 256 * c : 256 * (c + 1)] = tiny[0][r : r + 1]
        for e in range(3):
            for layer in range(2):
                r = 8 + 2 * e + layer
                g_b_qkv[e, layer : layer + 1, :] = tiny[0][r : r + 1]
        for layer in range(2):
            for c in range(2):
                r = 2 * layer + c
                for which in range(2):
                    g_sum[layer, which : which + 1, 256 * c : 256 * (c + 1)] = tiny[1][r : r + 1]

    def norms(layer, rows, base):
        for which in range(2):
            for c in range(2):
                cols = slice(256 * c, 256 * (c + 1))
                r = base + 2 * which + c
                g_gain[layer, which : which + 1, cols] = rows[r : r + 1]
                g_bias[layer, which : which + 1, cols] = rows[r + 4 : r + 5]

    @pl.when(p == 0)
    def _():
        norms(0, tiny[1], 4)
        norms(1, tiny[2], 0)


UP = (2, 512, 1024)
DOWN = (2, 1024, 512)


def unpack(first, rest):
    def place(layer):
        return [
            pl.BlockSpec((1, 256, 1024), lambda p: (layer, p, 0)),
            pl.BlockSpec((1, 512, 512), lambda p: (layer, p, 0)),
        ]

    params = pltpu.CompilerParams(vmem_limit_bytes=40 * 1024 * 1024)
    g_up, g_down = pl.pallas_call(
        unpack_first_body,
        grid=(2,),
        out_shape=[pltpu.HBM(UP, F32), pltpu.HBM(DOWN, F32)],
        in_specs=[pl.BlockSpec((4, 512, 256), lambda p: (p, 0, 0))],
        out_specs=place(1),
        compiler_params=params,
        name="unpack_first",
    )(far(first))
    outs = [
        ((2, 3, 512, 256), pl.BlockSpec((2, 3, 256, 256), lambda p: (0, 0, p, 0))),
        ((2, 256, 512), pl.BlockSpec((2, 128, 512), lambda p: (0, p, 0))),
        ((2, 1024), whole((2, 1024))),
        ((3, 2, 256), whole((3, 2, 256))),
        ((2, 2, 512), whole((2, 2, 512))),
        ((2, 2, 512), whole((2, 2, 512))),
        ((2, 2, 512), whole((2, 2, 512))),
    ]
    return pl.pallas_call(
        unpack_rest_body,
        grid=(2,),
        out_shape=[pltpu.HBM(shape, F32) for shape in [UP, DOWN] + [o[0] for o in outs]],
        in_specs=[
            pl.BlockSpec((4, 8, 136, 256), lambda p: (p, 0, 0, 0)),
            pl.BlockSpec(memory_space=pl.ANY),
            pl.BlockSpec(memory_space=pl.ANY),
        ],
        out_specs=place(0) + [spec for _, spec in outs],
        input_output_aliases={1: 0, 2: 1},
        compiler_params=params,
        name="unpack_rest",
    )(far(rest), far(g_up), far(g_down))


def swap(value):
    return lax.ppermute(value, "tensor", [(0, 1), (1, 0)])


def exchange(value, axes):
    return lax.all_to_all(value, axes, 0, 0)


def both(value):
    flat = value.reshape((16,) + value.shape[2:])
    return exchange(flat, ("context", "tensor")).reshape(value.shape)


def shards(
    tokens_in, cotangent, positions, w_qkv, b_qkv, w_out, w_up, b_up, w_down, out_bias, ln_gain, ln_bias
):
    rows, width = 256, 512
    x = tokens_in.reshape(rows, width)
    cot = cotangent.reshape(rows, width)
    wq = jnp.transpose(w_qkv, (0, 2, 1, 3))
    bq = jnp.transpose(b_qkv, (1, 0, 2))
    at = jnp.stack(
        [lax.axis_index("context"), lax.axis_index("tensor"), lax.axis_index("dp")]
    ).astype(jnp.int32)
    freqs = jnp.asarray(FREQS).reshape(HALF, 1)
    chunk = swap(chunk_of(at, wq, w_out))
    send, pair, act, slope, cs = call(
        first_body,
        [
            pltpu.VMEM((8, 208, BLK), BF),
            ((2 * rows, width), BF),
            pltpu.HBM((rows, 1024), BF),
            pltpu.HBM((rows, 1024), BF),
            ((2, 2, HALF, BLK), F32),
        ],
        (
            at, positions, freqs, Far(x), ln_gain, ln_bias, Layer(wq, 0), bq, Layer(w_up, 0), b_up,
            Layer(w_down, 0), Layer(w_out, 0),
        ),
        "norm_qkv_feed",
        smem_first=True,
    )
    pair_other = swap(pair)
    (chunk,) = call(
        hand_on_body, [pltpu.HBM(chunk.shape, BF)], (chunk, After(send)), "hand_on"
    )
    others = lax.all_gather(chunk, "dp", axis=2, tiled=True)
    recv = exchange(send, "context")
    ctx_send, lse, ctx, start = call(
        attend_body,
        [((8, 2, HEAD, BLK), BF), ((1, 1024), F32), pltpu.HBM((HEAD, 1024), F32), ((1, 1024), jnp.int32)],
        (recv,),
        "attend",
    )
    recv_ctx = both(ctx_send)
    stream, send, grads_a, parts, d_b_up1, d_sum1 = call(
        middle_body,
        [
            pltpu.HBM((rows, width), F32),
            ((8, 256, BLK), BF),
            pltpu.HBM((8, 512, 256), BF),
            ((2 * rows, width), BF),
            ((1, 1024), F32),
            ((1, width), F32),
        ],
        (
            at, Far(x), pair, pair_other, recv_ctx, Layer(w_out, 0), out_bias, ln_gain, ln_bias,
            Layer(wq, 1), bq, Layer(w_up, 1), b_up, Layer(w_down, 1), Layer(w_out, 1), Far(cot), cs,
        ),
        "middle",
        scratch=[pltpu.VMEM((rows, 1024), BF), pltpu.VMEM((rows, 1024), BF)],
        smem_first=True,
    )
    sums_a = lax.psum_scatter(grads_a, "dp", scatter_dimension=0)
    parts_other = swap(parts)
    recv_both = exchange(send, "context")
    (both_send,) = call(
        attend_both_body,
        [((8, 2, 256, BLK), BF)],
        (recv_both, start, After(parts_other)),
        "attend_both",
        scratch=[pltpu.VMEM((HEAD, 1024), F32), pltpu.VMEM((HEAD, 1024), F32)],
    )
    recv_grad = both(both_send)
    block_out, g, send, grads_b, part_g, d_b_up0, d_b_qkv1, d_norm1, d_sum0 = call(
        turn_point_body,
        [
            pltpu.HBM((rows, width), F32),
            pltpu.HBM((rows, width), F32),
            pltpu.VMEM((8, 192, BLK), BF),
            pltpu.HBM((8, 832, 256), BF),
            ((rows, width), BF),
            ((1, 1024), F32),
            ((3, 256), F32),
            ((4, width), F32),
            ((1, width), F32),
        ],
        (
            at, Far(stream), parts, parts_other, recv_grad, Layer(w_out, 1), Layer(wq, 1),
            Layer(others, 1), out_bias, ln_gain, ln_bias, Far(cot), cs, Far(x), Far(act), Far(slope),
            Layer(w_up, 0), Layer(w_down, 0), Layer(w_out, 0), recv_ctx, Far(sums_a),
        ),
        "turn_point",
        smem_first=True,
    )
    sums_b = lax.psum_scatter(grads_b, "dp", scatter_dimension=0)
    part_g_other = swap(part_g)
    recv_d = exchange(send, "context")
    (back_send,) = call(
        attend_back_body,
        [((8, 2, 320, BLK), BF)],
        (recv, recv_d, start, lse, ctx, After(part_g_other)),
        "attend_back",
        scratch=[pltpu.VMEM((HEAD, 1024), F32), pltpu.VMEM((HEAD, 1024), F32)],
    )
    recv_grad0 = both(back_send)
    in_grad, grads_c, sums_a, _, _ = call(
        last_body,
        [
            pltpu.HBM((rows, width), F32),
            ((8, 208, 256), BF),
            pltpu.HBM((512, 256), BF),
            ((3, 256), F32),
            ((4, width), F32),
        ],
        (
            at, Far(x), Far(g), part_g, part_g_other, recv_grad0, Layer(wq, 0), Layer(others, 0), cs,
            ln_gain, ln_bias, d_b_up0, d_b_up1, d_b_qkv1, d_norm1, d_sum0, d_sum1,
        ),
        "last",
        smem_first=True,
    )
    mixed, sums_a = call(
        mix_body,
        [((8, 136, 256), BF), pltpu.HBM((512, 256), BF)],
        (exchange(grads_c, "dp"), Far(sums_b), Far(sums_a)),
        "mix",
    )
    full_a = lax.all_gather(sums_a, "dp")
    (summed,) = call(sum_body, [((8, 136, 256), BF)], (exchange(mixed, "context"),), "sum")
    full_bc = lax.all_gather(exchange(summed, "context"), "dp")
    g_up, g_down, g_qkv, g_out, g_b_up, g_b_qkv, g_sum, g_gain, g_bias = unpack(full_a, full_bc)
    return (
        block_out.reshape(tokens_in.shape),
        in_grad.reshape(tokens_in.shape),
        jnp.transpose(g_qkv, (0, 2, 1, 3)),
        jnp.transpose(g_b_qkv, (1, 0, 2)),
        g_out,
        g_up,
        g_b_up,
        g_down,
        g_sum,
        g_gain,
        g_bias,
    )


def solution(mesh):
    return jax.shard_map(
        shards,
        mesh=mesh,
        in_specs=(
            P("dp", "context", None),
            P("dp", "context", None),
            P("dp", "context"),
            P(None, None, None, "tensor"),
            P(None, None, "tensor"),
            P(None, "tensor", None),
            P(None, None, "tensor"),
            P(None, "tensor"),
            P(None, "tensor", None),
            P(),
            P(),
            P(),
        ),
        out_specs=(
            P("dp", "context", None),
            P("dp", "context", None),
            P(None, None, None, "tensor"),
            P(None, None, "tensor"),
            P(None, "tensor", None),
            P(None, None, "tensor"),
            P(None, "tensor"),
            P(None, "tensor", None),
            P(),
            P(),
            P(),
        ),
        check_vma=False,
    )
```
